32 devices in a mesh: dp: 16 (over z, y, core), mp: 2 (over x).
Axes of the slice: x: 2, y: 2, z: 4, core: 2. Of those that a mesh axis runs over, the one named last changes fastest.
Arguments:
- layer_in: bfloat16 [16, 256, 2048], P('dp'), may hold values from -36 to 36
- seg_ids: int32 [16, 256], P('dp'), may hold values from 0 to 3, never falling along the last dimension, each value on 1 to 192 neighbouring positions
- w_q: bfloat16 [2048, 2048], P('dp', 'mp'), may hold values from -0.125 to 0.125
- w_k: bfloat16 [2048, 1024], P('dp', 'mp'), may hold values from -0.125 to 0.125
- w_v: bfloat16 [2048, 1024], P('dp', 'mp'), may hold values from -0.125 to 0.125
- w_o: bfloat16 [2048, 2048], P('dp', 'mp'), may hold values from -1 to 1
- w_gate: bfloat16 [2048, 6144], P('dp', 'mp'), may hold values from -0.125 to 0.125
- w_up: bfloat16 [2048, 6144], P('dp', 'mp'), may hold values from -0.125 to 0.125
- w_down: bfloat16 [2048, 6144], P('dp', 'mp'), may hold values from -0.078125 to 0.078125
- attn_gain: float32 [2048], replicated, may hold values from 0.25 to 1.75
- mlp_gain: float32 [2048], replicated, may hold values from 0.25 to 1.75
- q_gain: float32 [128], replicated, may hold values from 0.5 to 1.5
- k_gain: float32 [128], replicated, may hold values from 0.5 to 1.5
- cotangent: bfloat16 [16, 256, 2048], P('dp'), may hold values from -6 to 6
Outputs:
- layer_out: bfloat16 [16, 256, 2048], P('dp')
- in_grad: bfloat16 [16, 256, 2048], P('dp')
- grad_q: float32 [2048, 2048], P('dp', 'mp')
- grad_k: float32 [2048, 1024], P('dp', 'mp')
- grad_v: float32 [2048, 1024], P('dp', 'mp')
- grad_o: float32 [2048, 2048], P('dp', 'mp')
- grad_gate: float32 [2048, 6144], P('dp', 'mp')
- grad_up: float32 [2048, 6144], P('dp', 'mp')
- grad_down: float32 [2048, 6144], P('dp', 'mp')
- grad_attn_gain: float32 [2048], P('dp')
- grad_mlp_gain: float32 [2048], P('dp')
- grad_q_gain: float32 [128], P('dp')
- grad_k_gain: float32 [128], P('dp')
The draws below stay inside these ranges and needn't reach their ends.
Inputs may be any that keep to these rules, and one draw needn't show every extreme that they name: `seg_ids`: along each row the document number never falls; each number 0 to 3 covers 1 to 192 positions of the row, and some covers exactly 192.
All inputs are finite; a program needn't handle non-finite values.
Results may differ from the reference program's by a relative error of at most 0.014.
Values may be sent and summed in bfloat16 or wider, within the bound.
A program may use at most 256 MiB of HBM per device.

```python
import math
import jax
import jax.numpy as jnp
import numpy as np
from jax import lax

D = 2048
HQ = 16
KV = 8
HD = 128
FF = 6144
SEQ = 256
SEGS = 4
MOST = 192
ROWS = 16


def draw_layer_in(key, part):
    base_key = jax.random.fold_in(key, 13)
    key_one, key_two, key_three = jax.random.split(base_key, 3)
    base = jnp.clip(jax.random.normal(key_one, (ROWS, SEQ, D), jnp.float32), -4.0, 4.0)
    row_scale = jnp.exp(jax.random.uniform(key_two, (ROWS, SEQ, 1), jnp.float32, math.log(0.3), math.log(3.0)))
    col_scale = jnp.exp(jax.random.uniform(key_three, (D,), jnp.float32, math.log(0.3), math.log(3.0)))
    return (base * row_scale * col_scale).astype(jnp.bfloat16)


def head_gain(key, salt):
    gain_key = jax.random.fold_in(key, salt)
    return jax.random.uniform(gain_key, (HD,), jnp.float32, 0.5, 1.5)


def draw_q_gain(key, part):
    return head_gain(key, 21)


def draw_k_gain(key, part):
    return head_gain(key, 22)


def spiked(drawn, own_key, source, target, shards_of, factor):
    owner, partner = [(jnp.arange(drawn.shape[axis_at]) // (drawn.shape[axis_at] // shards_of)).reshape([-1 if axis == axis_at else 1 for axis in range(drawn.ndim)]) for axis_at in (source, target)]
    chosen = jax.random.permutation(own_key, shards_of)[partner]
    strong = (owner == chosen) | (owner == (partner + shards_of // 2) % shards_of)
    return jnp.where(strong, factor * drawn, drawn)


def shard_levels(key, dims, cuts, low, top_value):
    def one(dim, shards_of):
        draws = jax.random.uniform(jax.random.fold_in(jax.random.fold_in(key, 6), dim), (shards_of,), jnp.float32, low / len(cuts), top_value / len(cuts))
        return jnp.repeat(jnp.exp(draws), dims[dim] // shards_of).reshape((-1,) + (1,) * (len(dims) - dim - 1))

    loudness = one(*cuts[0])
    for cut in cuts[1:]:
        loudness = loudness * one(*cut)
    return loudness


def split_up(count, total, limit, slope):
    portions = [(1 << 20) // math.isqrt(rank ** slope) + 1 for rank in range(2, count + 1)]
    rest, counts = total - limit - (count - 1), [1] * (count - 1)
    while rest > 0:
        candidates = [i for i in range(count - 1) if counts[i] < limit]
        whole, remaining = sum([portions[i] for i in candidates]), rest
        for i in candidates:
            more = min(limit - counts[i], max(1, remaining * portions[i] // whole), rest)
            counts[i] = counts[i] + more
            rest = rest - more
    return np.array([limit] + counts)


def ragged_sizes(stream_key, count, total, most, slope):
    if count == 2:
        one = jax.random.randint(stream_key, (), max(1, total - most), min(most, total - 1) + 1)
        return jnp.stack([one, total - one])
    tallies = jnp.asarray(split_up(count, total, most, slope), jnp.int32)
    twos = (count - 1) // 2
    donor, taker = tallies[1:1 + 2 * twos:2], tallies[2:2 + 2 * twos:2]
    slack = jnp.minimum(donor - 1, most - taker)
    moved = jax.random.randint(jax.random.fold_in(stream_key, 1), (twos,), 0, 1 << 20) % (slack + 1)
    tallies = tallies.at[1:1 + 2 * twos:2].set(donor - moved).at[2:2 + 2 * twos:2].set(taker + moved)
    return tallies[jax.random.permutation(jax.random.fold_in(stream_key, 2), count)]


def noise(own_key, shape, spread, limit, shards=(), kind=jnp.bfloat16):
    entries = spread * jax.random.normal(own_key, shape, jnp.float32)
    if shards:
        entries = entries * shard_levels(own_key, shape, shards, -0.22, 0.18)
    return jnp.clip(entries, -limit, limit).astype(kind)


def gaussian_with(own_key, shape, deviation, bound, pieces, heavy, held_as=jnp.bfloat16):
    entries = deviation * jax.random.normal(own_key, shape, jnp.float32)
    if pieces:
        entries = entries * shard_levels(own_key, shape, pieces, -0.22, 0.18)
    return jnp.clip(spiked(entries, jax.random.fold_in(own_key, 3), *heavy), -bound, bound).astype(held_as)


def setup_inputs(seed: int = 0) -> dict:
    keys = jax.random.split(jax.random.key(seed), 15)
    return {
        "layer_in": draw_layer_in(jax.random.fold_in(keys[14], 71), 0),
        "seg_ids": jax.vmap(lambda own: jnp.searchsorted(jnp.cumsum(ragged_sizes(own, SEGS, SEQ, MOST, 2)), jnp.arange(SEQ), side="right"))(jax.random.split(keys[1], ROWS)).reshape((ROWS, SEQ)).astype(jnp.int32),
        "w_q": noise(keys[2], (D, HQ * HD), D ** -0.5, 0.125, ((0, 16), (1, 2))),
        "w_k": noise(keys[3], (D, KV * HD), D ** -0.5, 0.125, ((0, 16), (1, 2))),
        "w_v": noise(keys[4], (D, KV * HD), D ** -0.5, 0.125, ((0, 16), (1, 2))),
        "w_o": noise(keys[5], (D, HQ * HD), (HQ * HD // 64) ** -0.5, 1.0, ((0, 16), (1, 2))),
        "w_gate": noise(keys[6], (D, FF), D ** -0.5, 0.125, ((0, 16), (1, 2))),
        "w_up": noise(keys[7], (D, FF), D ** -0.5, 0.125, ((0, 16), (1, 2))),
        "w_down": noise(keys[8], (D, FF), FF ** -0.5, 0.078125, ((0, 16), (1, 2))),
        "attn_gain": jnp.clip(1.0 + 0.15 * jax.random.normal(keys[9], (D,), jnp.float32), 0.25, 1.75),
        "mlp_gain": jnp.clip(1.0 + 0.15 * jax.random.normal(keys[10], (D,), jnp.float32), 0.25, 1.75),
        "q_gain": draw_q_gain(jax.random.fold_in(keys[14], 71), 0),
        "k_gain": draw_k_gain(jax.random.fold_in(keys[14], 71), 0),
        "cotangent": gaussian_with(keys[13], (ROWS, SEQ, D), 1.0, 6.0, ((0, 16),), (0, 2, 16, 2.0)),
    }


EPSILON = 1e-06
ROPE_BASE = 1000000.0
MASKED = -1e+30

def matmul(left_op, right_op):
    return jnp.dot(left_op, right_op, preferred_element_type=jnp.float32)

def batched(pattern, left_op, right_op):
    return jnp.einsum(pattern, left_op.astype(jnp.float32), right_op.astype(jnp.float32))

def rms_norm(values, gain_vec):
    inv_rms = lax.rsqrt(lax.optimization_barrier(jnp.mean(values * values, axis=-1, keepdims=True)) + EPSILON)
    return (values * inv_rms * gain_vec, inv_rms)

def norm_back(grad_norm, values, inv_rms, gain_vec):
    scaled = grad_norm * gain_vec
    cubed = inv_rms * inv_rms * inv_rms
    grad_values = inv_rms * scaled - values * cubed * lax.optimization_barrier(jnp.mean(scaled * values, axis=-1, keepdims=True))
    return (grad_values, grad_norm * values * inv_rms)

def rope_tables(seg_row, head_dim):
    seq_len = seg_row.shape[0]
    row_index = jnp.arange(seq_len, dtype=jnp.int32)
    previous = jnp.concatenate([jnp.full((1,), -1, jnp.int32), seg_row[:-1].astype(jnp.int32)])
    starts = lax.cummax(jnp.where(seg_row.astype(jnp.int32) != previous, row_index, jnp.int32(0)), axis=0)
    position = (row_index - starts).astype(jnp.float32)
    frequency = ROPE_BASE ** (-jnp.arange(0, head_dim, 2).astype(jnp.float32) / head_dim)
    angles = position[:, None] * frequency[None, :]
    return (jnp.cos(angles), jnp.sin(angles))

def rope_apply(values, cosine_table, sine_table):
    half_dim = values.shape[-1] // 2
    first_half = values[..., :half_dim]
    second_half = values[..., half_dim:]
    cos_wide = cosine_table[:, None, :]
    sin_wide = sine_table[:, None, :]
    return jnp.concatenate([first_half * cos_wide - second_half * sin_wide, second_half * cos_wide + first_half * sin_wide], axis=-1)

def rope_back(grads, cosine_table, sine_table):
    half_dim = grads.shape[-1] // 2
    first_half = grads[..., :half_dim]
    second_half = grads[..., half_dim:]
    cos_wide = cosine_table[:, None, :]
    sin_wide = sine_table[:, None, :]
    return jnp.concatenate([first_half * cos_wide + second_half * sin_wide, second_half * cos_wide - first_half * sin_wide], axis=-1)

def score_block(queries_half, keys_half, seg_row, group_size):
    seq_len, num_heads, head_dim = queries_half.shape
    kv_heads = keys_half.shape[1]
    grouped = queries_half.reshape(seq_len, kv_heads, group_size, head_dim)
    scores = batched('qkgd,skd->kgqs', grouped, keys_half) * (1.0 / math.sqrt(head_dim))
    row_index = jnp.arange(seq_len, dtype=jnp.int32)
    allowed = (seg_row[:, None] == seg_row[None, :]) & (row_index[None, :] <= row_index[:, None])
    return (jnp.where(allowed[None, None], scores, MASKED), grouped)

def attend(queries_half, keys_half, values_half, seg_row, group_size):
    seq_len = queries_half.shape[0]
    scores, grouped = score_block(queries_half, keys_half, seg_row, group_size)
    row_max = lax.optimization_barrier(jnp.max(scores, axis=-1, keepdims=True))
    log_total = row_max + jnp.log(lax.optimization_barrier(jnp.sum(jnp.exp(scores - row_max), axis=-1, keepdims=True)))
    probs_half = jnp.exp(scores - log_total).astype(jnp.bfloat16)
    context = batched('kgqs,skd->qkgd', probs_half, values_half)
    return (context.reshape(seq_len, -1).astype(jnp.bfloat16), log_total)

def attend_back(queries_half, keys_half, values_half, seg_row, group_size, log_total, context_half, grad_context_half):
    seq_len, num_heads, head_dim = queries_half.shape
    kv_heads = keys_half.shape[1]
    scores, grouped = score_block(queries_half, keys_half, seg_row, group_size)
    probs_full = jnp.exp(scores - log_total)
    probs_half = probs_full.astype(jnp.bfloat16)
    grad_grouped = grad_context_half.reshape(seq_len, kv_heads, group_size, head_dim)
    context_grouped = context_half.reshape(seq_len, kv_heads, group_size, head_dim)
    grad_probs = batched('qkgd,skd->kgqs', grad_grouped, values_half)
    delta_sum = jnp.einsum('qkgd,qkgd->kgq', grad_grouped.astype(jnp.float32), context_grouped.astype(jnp.float32))[..., None]
    grad_scores = (probs_full * (grad_probs - delta_sum) * (1.0 / math.sqrt(head_dim))).astype(jnp.bfloat16)
    grad_queries = batched('kgqs,skd->qkgd', grad_scores, keys_half).reshape(seq_len, num_heads, head_dim)
    grad_keys = batched('kgqs,qkgd->skd', grad_scores, grouped)
    grad_values = batched('kgqs,qkgd->skd', probs_half, grad_grouped)
    return (grad_queries, grad_keys, grad_values)

def layer_pass(row_in, seg_row, row_cot, w_q, w_k, w_v, w_o, w_gate, w_up, w_down, attn_gain, mlp_gain, q_gain, k_gain):
    head_dim = q_gain.shape[0]
    group_size = w_q.shape[1] // w_k.shape[1]
    seq_len = row_in.shape[0]
    residual = row_in.astype(jnp.float32)
    normed_full, scale_one = rms_norm(residual, attn_gain)
    normed_one = normed_full.astype(jnp.bfloat16)
    query_raw = matmul(normed_one, w_q).reshape(seq_len, -1, head_dim)
    key_raw = matmul(normed_one, w_k).reshape(seq_len, -1, head_dim)
    values_half = matmul(normed_one, w_v).astype(jnp.bfloat16).reshape(seq_len, -1, head_dim)
    cosine_table, sine_table = rope_tables(seg_row, head_dim)
    query_norm, scale_q = rms_norm(query_raw, q_gain)
    key_norm, scale_k = rms_norm(key_raw, k_gain)
    queries_half = rope_apply(query_norm, cosine_table, sine_table).astype(jnp.bfloat16)
    keys_half = rope_apply(key_norm, cosine_table, sine_table).astype(jnp.bfloat16)
    context_half, log_total = attend(queries_half, keys_half, values_half, seg_row, group_size)
    mid = residual + matmul(context_half, w_o.T)
    normed_mid, scale_two = rms_norm(mid, mlp_gain)
    normed_two = normed_mid.astype(jnp.bfloat16)
    gate_pre = matmul(normed_two, w_gate)
    up_pre = matmul(normed_two, w_up)
    sigmoid_gate = jax.nn.sigmoid(gate_pre)
    silu_val = gate_pre * sigmoid_gate
    act_half = (silu_val * up_pre).astype(jnp.bfloat16)
    out_row = (mid + matmul(act_half, w_down.T)).astype(jnp.bfloat16)
    grad_act = matmul(row_cot, w_down)
    grad_down = matmul(row_cot.T, act_half)
    grad_gate_pre = (grad_act * up_pre * sigmoid_gate * (1.0 + gate_pre * (1.0 - sigmoid_gate))).astype(jnp.bfloat16)
    grad_up_pre = (grad_act * silu_val).astype(jnp.bfloat16)
    grad_gate = matmul(normed_two.T, grad_gate_pre)
    grad_up = matmul(normed_two.T, grad_up_pre)
    grad_normed_two = matmul(grad_gate_pre, w_gate.T) + matmul(grad_up_pre, w_up.T)
    grad_mid_norm, gain_two_terms = norm_back(grad_normed_two, mid, scale_two, mlp_gain)
    grad_mid = row_cot.astype(jnp.float32) + grad_mid_norm
    grad_mid_half = grad_mid.astype(jnp.bfloat16)
    grad_o = matmul(grad_mid_half.T, context_half)
    grad_context_half = matmul(grad_mid_half, w_o).astype(jnp.bfloat16)
    grad_queries, grad_keys, grad_values = attend_back(queries_half, keys_half, values_half, seg_row, group_size, log_total, context_half, grad_context_half)
    grad_query_raw, q_gain_terms = norm_back(rope_back(grad_queries, cosine_table, sine_table), query_raw, scale_q, q_gain)
    grad_key_raw, k_gain_terms = norm_back(rope_back(grad_keys, cosine_table, sine_table), key_raw, scale_k, k_gain)
    query_grad_half = grad_query_raw.reshape(seq_len, -1).astype(jnp.bfloat16)
    key_grad_half = grad_key_raw.reshape(seq_len, -1).astype(jnp.bfloat16)
    value_grad_half = grad_values.reshape(seq_len, -1).astype(jnp.bfloat16)
    grad_normed_one = matmul(query_grad_half, w_q.T) + matmul(key_grad_half, w_k.T) + matmul(value_grad_half, w_v.T)
    grad_res_norm, gain_one_terms = norm_back(grad_normed_one, residual, scale_one, attn_gain)
    in_grad_row = (grad_mid + grad_res_norm).astype(jnp.bfloat16)
    new_terms = (matmul(normed_one.T, query_grad_half), matmul(normed_one.T, key_grad_half), matmul(normed_one.T, value_grad_half), grad_o, grad_gate, grad_up, grad_down, lax.optimization_barrier(jnp.sum(gain_one_terms, axis=0)), lax.optimization_barrier(jnp.sum(gain_two_terms, axis=0)), lax.optimization_barrier(jnp.sum(q_gain_terms, axis=(0, 1))), lax.optimization_barrier(jnp.sum(k_gain_terms, axis=(0, 1))))
    return (out_row, in_grad_row, new_terms)

def reference(layer_in, seg_ids, w_q, w_k, w_v, w_o, w_gate, w_up, w_down, attn_gain, mlp_gain, q_gain, k_gain, cotangent):

    def scan_step(sums_carry, row_pack):
        row_in, seg_row, row_cot = row_pack
        out_row, in_grad_row, new_terms = layer_pass(row_in, seg_row, row_cot, w_q, w_k, w_v, w_o, w_gate, w_up, w_down, attn_gain, mlp_gain, q_gain, k_gain)
        return (tuple((old + new for old, new in zip(sums_carry, new_terms))), (out_row, in_grad_row))
    initial = tuple((jnp.zeros(shape_tuple, jnp.float32) for shape_tuple in (w_q.shape, w_k.shape, w_v.shape, w_o.shape, w_gate.shape, w_up.shape, w_down.shape, attn_gain.shape, mlp_gain.shape, q_gain.shape, k_gain.shape)))
    sums_carry, stacked = lax.scan(scan_step, initial, (layer_in, seg_ids, cotangent))
    return (stacked[0], stacked[1], sums_carry[0], sums_carry[1], sums_carry[2], sums_carry[3], sums_carry[4], sums_carry[5], sums_carry[6], sums_carry[7], sums_carry[8], sums_carry[9], sums_carry[10])
```

```python
import functools
import math

import jax
import jax.numpy as jnp
from jax import lax
from jax.experimental import pallas as pl
from jax.experimental.pallas import tpu as pltpu
from jax.sharding import PartitionSpec as P

EPSILON = 1e-06
ROPE_BASE = 1000000.0
MASKED = -1e30


def matmul(left_op, right_op):
    return jnp.dot(left_op, right_op, preferred_element_type=jnp.float32)


def batched(pattern, left_op, right_op):
    return jnp.einsum(pattern, left_op, right_op, preferred_element_type=jnp.float32)


def rms_norm(values, gain_vec):
    inv_rms = lax.rsqrt(jnp.mean(values * values, axis=-1, keepdims=True) + EPSILON)
    return (values * inv_rms * gain_vec, inv_rms)


def norm_back(grad_norm, values, inv_rms, gain_vec):
    scaled = grad_norm * gain_vec
    cubed = inv_rms * inv_rms * inv_rms
    grad_values = inv_rms * scaled - values * cubed * jnp.mean(
        scaled * values, axis=-1, keepdims=True
    )
    return (grad_values, grad_norm * values * inv_rms)


def rope_tables(seg_row, head_dim):
    seq_len = seg_row.shape[0]
    row_index = jnp.arange(seq_len, dtype=jnp.int32)
    previous = jnp.concatenate([jnp.full((1,), -1, jnp.int32), seg_row[:-1]])
    starts = lax.cummax(jnp.where(seg_row != previous, row_index, jnp.int32(0)), axis=0)
    position = (row_index - starts).astype(jnp.float32)
    frequency = ROPE_BASE ** (-jnp.arange(0, head_dim, 2).astype(jnp.float32) / head_dim)
    angles = position[:, None] * frequency[None, :]
    return (jnp.cos(angles), jnp.sin(angles))


def rope_apply(values, cosine_table, sine_table):
    half_dim = values.shape[-1] // 2
    first_half = values[..., :half_dim]
    second_half = values[..., half_dim:]
    cos_wide = cosine_table[:, None, :]
    sin_wide = sine_table[:, None, :]
    return jnp.concatenate(
        [
            first_half * cos_wide - second_half * sin_wide,
            second_half * cos_wide + first_half * sin_wide,
        ],
        axis=-1,
    )


def rope_back(grads, cosine_table, sine_table):
    half_dim = grads.shape[-1] // 2
    first_half = grads[..., :half_dim]
    second_half = grads[..., half_dim:]
    cos_wide = cosine_table[:, None, :]
    sin_wide = sine_table[:, None, :]
    return jnp.concatenate(
        [
            first_half * cos_wide + second_half * sin_wide,
            second_half * cos_wide - first_half * sin_wide,
        ],
        axis=-1,
    )


def score_block(queries_half, keys_half, seg_row, group_size):
    seq_len, num_heads, head_dim = queries_half.shape
    kv_heads = keys_half.shape[1]
    grouped = queries_half.reshape(seq_len, kv_heads, group_size, head_dim)
    scores = batched("qkgd,skd->kgqs", grouped, keys_half) * (1.0 / math.sqrt(head_dim))
    row_index = jnp.arange(seq_len, dtype=jnp.int32)
    allowed = (seg_row[:, None] == seg_row[None, :]) & (row_index[None, :] <= row_index[:, None])
    return (jnp.where(allowed[None, None], scores, MASKED), grouped)


def attend(queries_half, keys_half, values_half, seg_row, group_size):
    seq_len = queries_half.shape[0]
    scores, grouped = score_block(queries_half, keys_half, seg_row, group_size)
    row_max = jnp.max(scores, axis=-1, keepdims=True)
    log_total = row_max + jnp.log(jnp.sum(jnp.exp(scores - row_max), axis=-1, keepdims=True))
    probs_half = jnp.exp(scores - log_total).astype(jnp.bfloat16)
    context = batched("kgqs,skd->qkgd", probs_half, values_half)
    return (context.reshape(seq_len, -1).astype(jnp.bfloat16), log_total)


def attend_back(
    queries_half,
    keys_half,
    values_half,
    seg_row,
    group_size,
    log_total,
    context_half,
    grad_context_half,
):
    seq_len, num_heads, head_dim = queries_half.shape
    kv_heads = keys_half.shape[1]
    scores, grouped = score_block(queries_half, keys_half, seg_row, group_size)
    probs_full = jnp.exp(scores - log_total)
    probs_half = probs_full.astype(jnp.bfloat16)
    grad_grouped = grad_context_half.reshape(seq_len, kv_heads, group_size, head_dim)
    context_grouped = context_half.reshape(seq_len, kv_heads, group_size, head_dim)
    grad_probs = batched("qkgd,skd->kgqs", grad_grouped, values_half)
    delta_sum = jnp.einsum(
        "qkgd,qkgd->kgq", grad_grouped.astype(jnp.float32), context_grouped.astype(jnp.float32)
    )[..., None]
    grad_scores = (probs_full * (grad_probs - delta_sum) * (1.0 / math.sqrt(head_dim))).astype(
        jnp.bfloat16
    )
    grad_queries = batched("kgqs,skd->qkgd", grad_scores, keys_half).reshape(
        seq_len, num_heads, head_dim
    )
    grad_keys = batched("kgqs,qkgd->skd", grad_scores, grouped)
    grad_values = batched("kgqs,qkgd->skd", probs_half, grad_grouped)
    return (grad_queries, grad_keys, grad_values)


MESH = pl.DeviceIdType.MESH
ANY = pl.BlockSpec(memory_space=pl.ANY)
VMEM = pl.BlockSpec(memory_space=pltpu.VMEM)
DEPTH = 4
CORES = 2
HALVES = 2


class Place:
    def __init__(self, dp_size):
        self.wide = dp_size // (DEPTH * CORES)
        here = lax.axis_index("dp")
        self.x = lax.axis_index("mp")
        self.z = lax.div(here, jnp.int32(self.wide * CORES))
        self.y = lax.rem(lax.div(here, jnp.int32(CORES)), jnp.int32(self.wide))
        self.c = lax.rem(here, jnp.int32(CORES))

    def device(self, z=None, y=None, c=None, x=None):
        z = self.z if z is None else z
        y = self.y if y is None else y
        c = self.c if c is None else c
        x = self.x if x is None else x
        return ((z * self.wide + y) * CORES + c, x)

    def z_off(self, step):
        return lax.rem(self.z + DEPTH + step, jnp.int32(DEPTH))

    def y_off(self, step):
        return lax.rem(self.y + self.wide + step, jnp.int32(self.wide))


def snake(z, side):
    odd = lax.rem(side, jnp.int32(2))
    return side * DEPTH + z + odd * (DEPTH - 1 - 2 * z)


def unsnake(index, size):
    index = lax.rem(index + 2 * size, jnp.int32(size))
    side = lax.div(index, jnp.int32(DEPTH))
    rest = lax.rem(index, jnp.int32(DEPTH))
    return rest + lax.rem(side, jnp.int32(2)) * (DEPTH - 1 - 2 * rest), side


class Mail:
    def __init__(self, send_sems, recv_sems):
        self.send_sems, self.recv_sems = send_sems, recv_sems
        self.count = 0
        self.open = []

    def send(self, source, target, device):
        copy = pltpu.make_async_remote_copy(
            source,
            target,
            self.send_sems.at[self.count],
            self.recv_sems.at[self.count],
            device_id=device,
            device_id_type=MESH,
        )
        self.count += 1
        copy.start()
        self.open.append(copy)
        return copy

    def finish(self):
        for copy in self.open:
            copy.wait_send()


def meet(devices):
    barrier = pltpu.get_barrier_semaphore()
    for device in devices:
        pl.semaphore_signal(barrier, inc=1, device_id=device, device_id_type=MESH)
    pl.semaphore_wait(barrier, len(devices))


def receive(copies):
    for copy in copies:
        copy.wait_recv()


def own_copies(pairs, sems):
    copies = [
        pltpu.make_async_copy(source, target, sems.at[i]) for i, (source, target) in enumerate(pairs)
    ]
    for copy in copies:
        copy.start()
    return copies


def gather_kernel(
    dp_size, w_q, w_k, w_v, w_o, w_g, w_u, w_d, cot,
    o_q, o_k, o_v, o_o, o_g, o_u, o_d, o_c, own_sems, send_sems, recv_sems,
):
    at = Place(dp_size)
    z, y, c, x = at.z, at.y, at.c, at.x
    ring = DEPTH * at.wide
    loop = DEPTH * HALVES
    spot, seat = snake(z, y), snake(z, x)
    ring_z, ring_y = unsnake(spot + 1, ring)
    back_z, back_y = unsnake(spot - 1, ring)
    ahead, behind = at.device(z=ring_z, y=ring_y), at.device(z=back_z, y=back_y)
    loop_z, loop_x = unsnake(seat + 1, loop)
    tail_z, tail_x = unsnake(seat - 1, loop)
    after, before = at.device(z=loop_z, x=loop_x), at.device(z=tail_z, x=tail_x)
    sibling = at.device(c=1 - c)
    z_peers = [at.device(z=at.z_off(k)) for k in range(1, DEPTH)]
    y_peers = [at.device(y=at.y_off(j)) for j in range(1, at.wide)]
    meet([ahead, behind, after, before, sibling] + z_peers + y_peers)

    mail = Mail(send_sems, recv_sems)
    part = w_g.shape[1] // DEPTH
    tokens = cot.shape[0] // HALVES
    strip = tokens // 2
    ffn = ((w_g, o_g), (w_u, o_u), (w_d, o_d))
    attn = ((w_q, o_q), (w_k, o_k), (w_v, o_v), (w_o, o_o))

    def columns(index):
        return pl.ds(pl.multiple_of(index * part, part), part)

    mine = own_copies(
        [(weight, out.at[z, y, c]) for weight, out in attn]
        + [(weight.at[:, columns(z)], out.at[z, y, c]) for weight, out in ffn]
        + [(cot.at[pl.ds(pl.multiple_of(x * tokens, tokens), tokens)], o_c.at[z, x])],
        own_sems,
    )

    to_sibling = []
    rounds = [
        mail.send(weight, out.at[z, y, c], ahead if i < 2 else behind)
        for i, (weight, out) in enumerate(attn)
    ]
    turns = [
        mail.send(
            cot.at[pl.ds(pl.multiple_of(x * tokens + i * strip, strip), strip)],
            o_c.at[z, x, pl.ds(i * strip, strip)],
            after if i == 0 else before,
        )
        for i in range(2)
    ]
    spread = {}
    for k in range(1, DEPTH):
        target = at.z_off(k)
        spread[k] = [
            mail.send(weight.at[:, columns(target)], out.at[z, y, c], z_peers[k - 1])
            for weight, out in ffn
        ]
    crossing = {}
    for j in range(1, at.wide):
        crossing[0, j] = [
            mail.send(weight.at[:, columns(z)], out.at[z, y, c], y_peers[j - 1])
            for weight, out in ffn
        ]
    to_sibling += [mail.send(weight, out.at[z, y, c], sibling) for weight, out in attn]
    to_sibling += [
        mail.send(weight.at[:, columns(z)], out.at[z, y, c], sibling) for weight, out in ffn
    ]

    for step in range(max(ring, loop) - 1):
        if step < ring - 1:
            receive(rounds)
            one_z, one_y = unsnake(spot - 1 - step, ring)
            two_z, two_y = unsnake(spot + 1 + step, ring)
            places = [(one_z, one_y)] * 2 + [(two_z, two_y)] * 2
            blocks = [out.at[pz, py, c] for (_, out), (pz, py) in zip(attn, places)]
            if step < ring - 2:
                rounds = [
                    mail.send(block, block, ahead if i < 2 else behind)
                    for i, block in enumerate(blocks)
                ]
            to_sibling += [mail.send(block, block, sibling) for block in blocks]
        if step < loop - 1:
            receive(turns)
            one_z, one_x = unsnake(seat - 1 - step, loop)
            two_z, two_x = unsnake(seat + 1 + step, loop)
            if step < loop - 2:
                first = o_c.at[one_z, one_x, pl.ds(0, strip)]
                second = o_c.at[two_z, two_x, pl.ds(strip, strip)]
                turns = [mail.send(first, first, after), mail.send(second, second, before)]
        k = step - 1
        if 1 <= k < DEPTH:
            receive(spread[k])
            source = at.z_off(-k)
            blocks = [out.at[source, y, c] for _, out in ffn]
            for j in range(1, at.wide):
                crossing[k, j] = [mail.send(block, block, y_peers[j - 1]) for block in blocks]
            to_sibling += [mail.send(block, block, sibling) for block in blocks]
        k = step - 3
        if 0 <= k < DEPTH:
            source = at.z_off(-k)
            for j in range(1, at.wide):
                receive(crossing[k, j])
                blocks = [out.at[source, at.y_off(-j), c] for _, out in ffn]
                to_sibling += [mail.send(block, block, sibling) for block in blocks]
    receive(to_sibling)
    mail.finish()
    for copy in mine:
        copy.wait()


def gather_copies(dp_size):
    wide = dp_size // (DEPTH * CORES)
    ring, loop = DEPTH * wide, DEPTH * HALVES
    return 4 * (ring - 1) + 2 * (loop - 1) + 9 + 3 * DEPTH * (wide - 1) + 4 * ring + 3 * ring


def gather(dp_size, w_q, w_k, w_v, w_o, w_g, w_u, w_d, cot):
    wide = dp_size // (DEPTH * CORES)
    rows = w_q.shape[0]
    grid = (DEPTH, wide, CORES, rows)
    part = w_g.shape[1] // DEPTH
    half = jnp.bfloat16
    shapes = [jax.ShapeDtypeStruct(grid + (w.shape[1],), half) for w in (w_q, w_k, w_v, w_o)]
    shapes += [jax.ShapeDtypeStruct(grid + (part,), half)] * 3
    shapes += [jax.ShapeDtypeStruct((DEPTH, HALVES, cot.shape[0] // HALVES, cot.shape[1]), half)]
    copies = gather_copies(dp_size)
    return pl.pallas_call(
        functools.partial(gather_kernel, dp_size),
        out_shape=shapes,
        in_specs=[ANY] * 8,
        out_specs=[ANY] * 8,
        scratch_shapes=[
            pltpu.SemaphoreType.DMA((8,)),
            pltpu.SemaphoreType.DMA((copies,)),
            pltpu.SemaphoreType.DMA((copies,)),
        ],
        compiler_params=pltpu.CompilerParams(collective_id=0, has_side_effects=True),
    )(w_q, w_k, w_v, w_o, w_g, w_u, w_d, cot)


def middle_kernel(
    dp_size, partial, row_in, gain, mid, o_n, outgoing, incoming, normed, own_sems, send_sems, recv_sems
):
    at = Place(dp_size)
    z, x = at.z, at.x
    loop = DEPTH * HALVES
    seat = snake(z, x)
    loop_z, loop_x = unsnake(seat + 1, loop)
    tail_z, tail_x = unsnake(seat - 1, loop)
    after, before = at.device(z=loop_z, x=loop_x), at.device(z=tail_z, x=tail_x)
    other = at.device(x=1 - x)
    tokens = mid.shape[0]
    strip = tokens // 2
    kept = pl.ds(pl.multiple_of(x * tokens, tokens), tokens)
    given = pl.ds(pl.multiple_of((1 - x) * tokens, tokens), tokens)
    outgoing[...] = partial[given, :].astype(jnp.bfloat16)
    meet([after, before, other])
    mail = Mail(send_sems, recv_sems)
    swap = mail.send(outgoing, incoming, other)
    swap.wait_recv()
    values = row_in[kept, :].astype(jnp.float32) + (
        partial[kept, :] + incoming[...].astype(jnp.float32)
    )
    mid[...] = values
    inv_rms = lax.rsqrt(jnp.mean(values * values, axis=-1, keepdims=True) + EPSILON)
    normed[...] = (values * inv_rms * gain[...]).astype(jnp.bfloat16)
    mine = own_copies([(normed, o_n.at[z, x])], own_sems)
    turns = [
        mail.send(
            normed.at[pl.ds(i * strip, strip)],
            o_n.at[z, x, pl.ds(i * strip, strip)],
            after if i == 0 else before,
        )
        for i in range(2)
    ]
    for step in range(loop - 1):
        receive(turns)
        one_z, one_x = unsnake(seat - 1 - step, loop)
        two_z, two_x = unsnake(seat + 1 + step, loop)
        if step < loop - 2:
            first = o_n.at[one_z, one_x, pl.ds(0, strip)]
            second = o_n.at[two_z, two_x, pl.ds(strip, strip)]
            turns = [mail.send(first, first, after), mail.send(second, second, before)]
    mail.finish()
    for copy in mine:
        copy.wait()


def middle(dp_size, partial, row_in, gain):
    tokens, width = partial.shape[0] // HALVES, partial.shape[1]
    copies = 1 + 2 * (DEPTH * HALVES - 1)
    return pl.pallas_call(
        functools.partial(middle_kernel, dp_size),
        out_shape=[
            jax.ShapeDtypeStruct((tokens, width), jnp.float32),
            jax.ShapeDtypeStruct((DEPTH, HALVES, tokens, width), jnp.bfloat16),
        ],
        in_specs=[VMEM] * 3,
        out_specs=[VMEM, ANY],
        scratch_shapes=[
            pltpu.VMEM((tokens, width), jnp.bfloat16),
            pltpu.VMEM((tokens, width), jnp.bfloat16),
            pltpu.VMEM((tokens, width), jnp.bfloat16),
            pltpu.SemaphoreType.DMA((1,)),
            pltpu.SemaphoreType.DMA((copies,)),
            pltpu.SemaphoreType.DMA((copies,)),
        ],
        compiler_params=pltpu.CompilerParams(
            collective_id=1, has_side_effects=True, vmem_limit_bytes=40 * 2**20
        ),
    )(partial, row_in, gain[None, :])


def add_into(target, *others):
    total = target[...].astype(jnp.float32)
    for other in others:
        total = total + other[...].astype(jnp.float32)
    target[...] = total.astype(target.dtype)


def ffn_reduce_kernel(
    dp_size, p_n, p_o, g_g, g_u, g_d, mid, cot, gain,
    o_m, o_h, o_l, o_t, w_g, w_u, w_d,
    r_n, r_o, c_g, c_u, c_d, y_g, y_u, y_d, z_g, z_u, z_d, send_sems, recv_sems,
):
    at = Place(dp_size)
    z, y, c, x = at.z, at.y, at.c, at.x
    loop = DEPTH * HALVES
    seat = snake(z, x)
    loop_z, loop_x = unsnake(seat + 1, loop)
    tail_z, tail_x = unsnake(seat - 1, loop)
    after, before = at.device(z=loop_z, x=loop_x), at.device(z=tail_z, x=tail_x)
    other = at.device(x=1 - x)
    sibling = at.device(c=1 - c)
    z_peers = [at.device(z=at.z_off(k)) for k in range(1, DEPTH)]
    y_peers = [at.device(y=at.y_off(j)) for j in range(1, at.wide)]
    meet([after, before, other, sibling] + z_peers + y_peers)
    mail = Mail(send_sems, recv_sems)
    tokens = mid.shape[0]
    strip = tokens // 2
    part = w_g.shape[1] // DEPTH
    strips = (pl.ds(0, strip), pl.ds(strip, strip))
    grads = ((g_g, c_g, y_g, z_g, w_g), (g_u, c_u, y_u, z_u, w_u), (g_d, c_d, y_d, z_d, w_d))

    def block(array, i, step):
        shift = -1 - step if i == 0 else 1 + step
        bz, bx = unsnake(seat + shift, loop)
        return array.at[bz, bx, strips[i]]

    def ring_start(array, landing):
        return [
            mail.send(block(array, i, 0), landing.at[0, i], after if i == 0 else before)
            for i in range(2)
        ]

    def ring_step(turns, array, landing, step):
        receive(turns)
        turns = []
        for i in range(2):
            add_into(landing.at[step, i], block(array, i, step + 1))
            turns.append(
                mail.send(landing.at[step, i], landing.at[step + 1, i], after if i == 0 else before)
            )
        return turns

    turns_n = ring_start(p_n, r_n)
    order = [(k, at.z_off(k)) for k in (2, 1, 3, 0)]
    to_core = {
        k: [mail.send(grad.at[to, :, 1 - c], land.at[to], sibling) for grad, land, *_ in grads]
        for k, to in order
    }
    turns_o = ring_start(p_o, r_o)
    to_y, to_z = {}, {}

    def core_stage(k, to):
        receive(to_core[k])
        for grad, land, *_ in grads:
            for row in range(at.wide):
                add_into(land.at[to, row], grad.at[to, row, c])
        to_y[k] = [
            mail.send(land.at[to, at.y_off(j)], arrive.at[j - 1, to], y_peers[j - 1])
            for j in range(1, at.wide)
            for _, land, arrive, *_ in grads
        ]

    def y_stage(k, to):
        receive(to_y[k])
        for _, land, arrive, *_ in grads:
            add_into(land.at[to, y], *[arrive.at[j - 1, to] for j in range(1, at.wide)])
        if k > 0:
            to_z[k] = [
                mail.send(land.at[to, y], last.at[k - 1], z_peers[k - 1])
                for _, land, _, last, _ in grads
            ]

    def final_norm():
        receive(turns_n)
        gain_sum = jnp.zeros(o_t.shape, jnp.float32)
        kept = pl.multiple_of(x * tokens, tokens)
        for i in range(2):
            grad_norm = r_n[loop - 2, i].astype(jnp.float32) + p_n[z, x, strips[i]].astype(jnp.float32)
            values = mid[strips[i], :]
            inv_rms = lax.rsqrt(jnp.mean(values * values, axis=-1, keepdims=True) + EPSILON)
            grad_values, terms = norm_back(grad_norm, values, inv_rms, gain[...])
            gain_sum = gain_sum + jnp.sum(terms, axis=0, keepdims=True)
            rows = pl.ds(pl.multiple_of(kept + i * strip, strip), strip)
            total = cot[rows, :].astype(jnp.float32) + grad_values
            o_m[strips[i], :] = total
            o_h[rows, :] = total.astype(jnp.bfloat16)
        o_t[...] = gain_sum
        rows = pl.ds(kept, tokens)
        return mail.send(o_h.at[rows], o_h.at[rows], other)

    for step in range(loop - 2):
        turns_n = ring_step(turns_n, p_n, r_n, step)
        if step < DEPTH:
            core_stage(*order[step])
        if 2 <= step:
            y_stage(*order[step - 2])
        turns_o = ring_step(turns_o, p_o, r_o, step)
    swap_h = final_norm()
    receive(turns_o)
    kept = pl.multiple_of(x * tokens, tokens)
    for i in range(2):
        rows = pl.ds(pl.multiple_of(kept + i * strip, strip), strip)
        total = r_o[loop - 2, i].astype(jnp.float32) + p_o[z, x, strips[i]].astype(jnp.float32)
        o_l[rows, :] = (mid[strips[i], :] + total).astype(jnp.bfloat16)
    rows = pl.ds(kept, tokens)
    swap_l = mail.send(o_l.at[rows], o_l.at[rows], other)
    for _, land, _, last, out in grads:
        for k in range(DEPTH):
            source = at.z_off(-k)
            columns = pl.ds(pl.multiple_of(source * part, part), part)
            if k == 0:
                out[:, columns] = land[z, y].astype(jnp.float32)
    for k in range(1, DEPTH):
        receive(to_z[k])
        source = at.z_off(-k)
        columns = pl.ds(pl.multiple_of(source * part, part), part)
        for _, _, _, last, out in grads:
            out[:, columns] = last[k - 1].astype(jnp.float32)
    receive([swap_h, swap_l])
    mail.finish()


def ffn_reduce(dp_size, p_n, p_o, g_g, g_u, g_d, mid, cot, gain):
    wide = dp_size // (DEPTH * CORES)
    tokens, width = mid.shape
    loop = DEPTH * HALVES
    rows, part = g_g.shape[-2:]
    copies = 4 * (loop - 1) + 3 * DEPTH + 3 * DEPTH * (wide - 1) + 9 + 2
    half = jnp.bfloat16
    return pl.pallas_call(
        functools.partial(ffn_reduce_kernel, dp_size),
        out_shape=[
            jax.ShapeDtypeStruct((tokens, width), jnp.float32),
            jax.ShapeDtypeStruct((HALVES * tokens, width), half),
            jax.ShapeDtypeStruct((HALVES * tokens, width), half),
            jax.ShapeDtypeStruct((1, width), jnp.float32),
        ]
        + [jax.ShapeDtypeStruct((rows, part * DEPTH), jnp.float32)] * 3,
        in_specs=[VMEM] * 8,
        out_specs=[VMEM] * 7,
        scratch_shapes=[pltpu.VMEM((loop - 1, 2, tokens // 2, width), half)] * 2
        + [pltpu.VMEM((DEPTH, wide, rows, part), half)] * 3
        + [pltpu.VMEM((wide - 1, DEPTH, rows, part), half)] * 3
        + [pltpu.VMEM((DEPTH - 1, rows, part), half)] * 3
        + [pltpu.SemaphoreType.DMA((copies,)), pltpu.SemaphoreType.DMA((copies,))],
        compiler_params=pltpu.CompilerParams(
            collective_id=2, has_side_effects=True, vmem_limit_bytes=58 * 2**20
        ),
    )(p_n, p_o, g_g, g_u, g_d, mid, cot, gain[None, :])


def attn_reduce_kernel(
    dp_size, g_q, g_k, g_v, g_o, partial, row_in, grad_mid, gain,
    o_i, w_q, w_k, w_v, w_o,
    outgoing, incoming, c_q, c_k, c_v, c_o, r_q, r_k, r_v, r_o, send_sems, recv_sems,
):
    at = Place(dp_size)
    z, y, c, x = at.z, at.y, at.c, at.x
    ring = DEPTH * at.wide
    spot = snake(z, y)
    ring_z, ring_y = unsnake(spot + 1, ring)
    back_z, back_y = unsnake(spot - 1, ring)
    ahead, behind = at.device(z=ring_z, y=ring_y), at.device(z=back_z, y=back_y)
    other = at.device(x=1 - x)
    sibling = at.device(c=1 - c)
    tokens = grad_mid.shape[0]
    kept = pl.ds(pl.multiple_of(x * tokens, tokens), tokens)
    given = pl.ds(pl.multiple_of((1 - x) * tokens, tokens), tokens)
    outgoing[...] = partial[given, :].astype(jnp.bfloat16)
    meet([ahead, behind, other, sibling])
    mail = Mail(send_sems, recv_sems)
    sets = ((g_q, c_q, r_q, w_q), (g_k, c_k, r_k, w_k), (g_v, c_v, r_v, w_v), (g_o, c_o, r_o, w_o))

    def spot_of(i, step):
        return unsnake(spot + (-1 - step if i < 2 else 1 + step), ring)

    to_core = []
    for step in range(ring):
        row = []
        for i, (grad, land, _, _) in enumerate(sets):
            bz, by = spot_of(i, step)
            row.append(mail.send(grad.at[bz, by, 1 - c], land.at[bz, by], sibling))
        to_core.append(row)
    swap = mail.send(outgoing, incoming, other)
    turns = []
    for step in range(ring):
        receive(to_core[step])
        if step > 0:
            receive(turns)
        turns = []
        for i, (grad, land, arrive, out) in enumerate(sets):
            bz, by = spot_of(i, step)
            terms = [grad[bz, by, c].astype(jnp.float32), land[bz, by].astype(jnp.float32)]
            if step > 0:
                terms.append(arrive[step - 1].astype(jnp.float32))
            total = sum(terms[1:], terms[0])
            if step < ring - 1:
                land[bz, by] = total.astype(jnp.bfloat16)
                turns.append(
                    mail.send(land.at[bz, by], arrive.at[step], ahead if i < 2 else behind)
                )
            else:
                out[...] = total
        if step == 1:
            swap.wait_recv()
            grad_norm = partial[kept, :] + incoming[...].astype(jnp.float32)
            values = row_in[kept, :].astype(jnp.float32)
            inv_rms = lax.rsqrt(jnp.mean(values * values, axis=-1, keepdims=True) + EPSILON)
            grad_values, _ = norm_back(grad_norm, values, inv_rms, gain[...])
            o_i[kept, :] = (grad_mid[...] + grad_values).astype(jnp.bfloat16)
            swap_back = mail.send(o_i.at[kept], o_i.at[kept], other)
    swap_back.wait_recv()
    mail.finish()


def attn_reduce(dp_size, grads, partial, row_in, grad_mid, gain):
    wide = dp_size // (DEPTH * CORES)
    ring = DEPTH * wide
    tokens, width = grad_mid.shape
    half = jnp.bfloat16
    rows = grads[0].shape[-2]
    cols = [grad.shape[-1] for grad in grads]
    copies = 4 * ring + 4 * (ring - 1) + 2
    return pl.pallas_call(
        functools.partial(attn_reduce_kernel, dp_size),
        out_shape=[jax.ShapeDtypeStruct((HALVES * tokens, width), half)]
        + [jax.ShapeDtypeStruct((rows, col), jnp.float32) for col in cols],
        in_specs=[VMEM] * 8,
        out_specs=[VMEM] * 5,
        scratch_shapes=[pltpu.VMEM((tokens, width), half)] * 2
        + [pltpu.VMEM((DEPTH, wide, rows, col), half) for col in cols]
        + [pltpu.VMEM((ring - 1, rows, col), half) for col in cols]
        + [pltpu.SemaphoreType.DMA((copies,)), pltpu.SemaphoreType.DMA((copies,))],
        compiler_params=pltpu.CompilerParams(
            collective_id=3, has_side_effects=True, vmem_limit_bytes=58 * 2**20
        ),
    )(*grads, partial, row_in, grad_mid, gain[None, :])


def body(
    dp_size,
    layer_in,
    seg_ids,
    w_q,
    w_k,
    w_v,
    w_o,
    w_gate,
    w_up,
    w_down,
    attn_gain,
    mlp_gain,
    q_gain,
    k_gain,
    cotangent,
):
    head_dim = q_gain.shape[0]
    group_size = w_q.shape[1] // w_k.shape[1]
    rows = w_q.shape[0]
    width = rows * dp_size
    wide = dp_size // (DEPTH * CORES)
    row_in = layer_in[0]
    seg_row = seg_ids[0]
    row_cot = cotangent[0]
    seq_len = row_in.shape[0]
    gathered = gather(dp_size, w_q, w_k, w_v, w_o, w_gate, w_up, w_down, row_cot)
    full_q, full_k, full_v, full_o, part_gate, part_up, part_down = [
        array.reshape(width, -1) for array in gathered[:7]
    ]
    cots = gathered[7].reshape(-1, width)

    residual = row_in.astype(jnp.float32)
    normed_full, scale_one = rms_norm(residual, attn_gain)
    normed_one = normed_full.astype(jnp.bfloat16)
    query_raw = matmul(normed_one, full_q).reshape(seq_len, -1, head_dim)
    key_raw = matmul(normed_one, full_k).reshape(seq_len, -1, head_dim)
    values_half = matmul(normed_one, full_v).astype(jnp.bfloat16).reshape(seq_len, -1, head_dim)
    cosine_table, sine_table = rope_tables(seg_row, head_dim)
    query_norm, scale_q = rms_norm(query_raw, q_gain)
    key_norm, scale_k = rms_norm(key_raw, k_gain)
    queries_half = rope_apply(query_norm, cosine_table, sine_table).astype(jnp.bfloat16)
    keys_half = rope_apply(key_norm, cosine_table, sine_table).astype(jnp.bfloat16)
    context_half, log_total = attend(queries_half, keys_half, values_half, seg_row, group_size)

    mid, normed = middle(dp_size, matmul(context_half, full_o.T), row_in, mlp_gain)
    normed_two = normed.reshape(-1, width)
    gate_pre = matmul(normed_two, part_gate)
    up_pre = matmul(normed_two, part_up)
    sigmoid_gate = jax.nn.sigmoid(gate_pre)
    silu_val = gate_pre * sigmoid_gate
    act_half = (silu_val * up_pre).astype(jnp.bfloat16)
    out_part = matmul(act_half, part_down.T).astype(jnp.bfloat16)
    grad_act = matmul(cots, part_down)
    grad_gate_pre = (
        grad_act * up_pre * sigmoid_gate * (1.0 + gate_pre * (1.0 - sigmoid_gate))
    ).astype(jnp.bfloat16)
    grad_up_pre = (grad_act * silu_val).astype(jnp.bfloat16)
    norm_part = (
        matmul(grad_gate_pre, part_gate.T) + matmul(grad_up_pre, part_up.T)
    ).astype(jnp.bfloat16)
    grads = [
        matmul(left.T, right).astype(jnp.bfloat16).reshape(DEPTH, wide, CORES, rows, -1)
        for left, right in (
            (normed_two, grad_gate_pre),
            (normed_two, grad_up_pre),
            (cots, act_half),
        )
    ]
    shape = (DEPTH, HALVES, seq_len // HALVES, width)
    grad_mid, grad_mid_half, out_row, gain_two, grad_gate, grad_up, grad_down = ffn_reduce(
        dp_size, norm_part.reshape(shape), out_part.reshape(shape), *grads, mid, row_cot, mlp_gain
    )

    grad_o = matmul(grad_mid_half.T, context_half)
    grad_context_half = matmul(grad_mid_half, full_o).astype(jnp.bfloat16)
    grad_queries, grad_keys, grad_values = attend_back(
        queries_half,
        keys_half,
        values_half,
        seg_row,
        group_size,
        log_total,
        context_half,
        grad_context_half,
    )
    grad_query_raw, q_gain_terms = norm_back(
        rope_back(grad_queries, cosine_table, sine_table), query_raw, scale_q, q_gain
    )
    grad_key_raw, k_gain_terms = norm_back(
        rope_back(grad_keys, cosine_table, sine_table), key_raw, scale_k, k_gain
    )
    query_grad_half = grad_query_raw.reshape(seq_len, -1).astype(jnp.bfloat16)
    key_grad_half = grad_key_raw.reshape(seq_len, -1).astype(jnp.bfloat16)
    value_grad_half = grad_values.reshape(seq_len, -1).astype(jnp.bfloat16)
    normed_part = (
        matmul(query_grad_half, full_q.T)
        + matmul(key_grad_half, full_k.T)
        + matmul(value_grad_half, full_v.T)
    )
    grads = [
        matmul(left.T, right).astype(jnp.bfloat16).reshape(DEPTH, wide, CORES, rows, -1)
        for left, right in (
            (normed_one, query_grad_half),
            (normed_one, key_grad_half),
            (normed_one, value_grad_half),
        )
    ] + [grad_o.astype(jnp.bfloat16).reshape(DEPTH, wide, CORES, rows, -1)]
    in_grad, grad_q, grad_k, grad_v, grad_o = attn_reduce(
        dp_size, grads, normed_part, row_in, grad_mid, attn_gain
    )

    gain_one = jnp.sum(normed_part * residual * scale_one, axis=0)
    gains = [gain_one, gain_two[0], jnp.sum(q_gain_terms, axis=(0, 1)), jnp.sum(k_gain_terms, axis=(0, 1))]
    sizes = [gain.shape[0] for gain in gains]
    summed = lax.psum(jnp.concatenate(gains), ("dp", "mp"))
    gain_outs = []
    start = 0
    for size in sizes:
        share = size // dp_size
        gain_outs.append(
            lax.dynamic_slice(summed, (start + lax.axis_index("dp") * share,), (share,))
        )
        start += size
    return (
        out_row[None],
        in_grad[None],
        grad_q,
        grad_k,
        grad_v,
        grad_o,
        grad_gate,
        grad_up,
        grad_down,
        *gain_outs,
    )


def solution(mesh):
    return jax.shard_map(
        functools.partial(body, mesh.shape["dp"]),
        mesh=mesh,
        in_specs=(
            P("dp", None, None),
            P("dp", None),
            P("dp", "mp"),
            P("dp", "mp"),
            P("dp", "mp"),
            P("dp", "mp"),
            P("dp", "mp"),
            P("dp", "mp"),
            P("dp", "mp"),
            P(),
            P(),
            P(),
            P(),
            P("dp", None, None),
        ),
        out_specs=(
            P("dp", None, None),
            P("dp", None, None),
            P("dp", "mp"),
            P("dp", "mp"),
            P("dp", "mp"),
            P("dp", "mp"),
            P("dp", "mp"),
            P("dp", "mp"),
            P("dp", "mp"),
            P("dp"),
            P("dp"),
            P("dp"),
            P("dp"),
        ),
        check_vma=False,
    )
```

```python
import functools
import math

import jax
import jax.numpy as jnp
from jax import lax
from jax.experimental import pallas as pl
from jax.experimental.pallas import tpu as pltpu
from jax.sharding import PartitionSpec as P

EPSILON = 1e-06
ROPE_BASE = 1000000.0
MASKED = -1e30


def matmul(left_op, right_op):
    return jnp.dot(left_op, right_op, preferred_element_type=jnp.float32)


def rms_norm(values, gain_vec):
    inv_rms = lax.rsqrt(jnp.mean(values * values, axis=-1, keepdims=True) + EPSILON)
    return (values * inv_rms * gain_vec, inv_rms)


def norm_back(grad_norm, values, inv_rms, gain_vec):
    scaled = grad_norm * gain_vec
    cubed = inv_rms * inv_rms * inv_rms
    grad_values = inv_rms * scaled - values * cubed * jnp.mean(
        scaled * values, axis=-1, keepdims=True
    )
    return (grad_values, grad_norm * values * inv_rms)


MESH = pl.DeviceIdType.MESH
ANY = pl.BlockSpec(memory_space=pl.ANY)
VMEM = pl.BlockSpec(memory_space=pltpu.VMEM)
DEPTH = 4
CORES = 2
HALVES = 2


class Place:
    def __init__(self, dp_size):
        self.wide = dp_size // (DEPTH * CORES)
        here = lax.axis_index("dp")
        self.x = lax.axis_index("mp")
        self.z = lax.div(here, jnp.int32(self.wide * CORES))
        self.y = lax.rem(lax.div(here, jnp.int32(CORES)), jnp.int32(self.wide))
        self.c = lax.rem(here, jnp.int32(CORES))

    def device(self, z=None, y=None, c=None, x=None):
        z = self.z if z is None else z
        y = self.y if y is None else y
        c = self.c if c is None else c
        x = self.x if x is None else x
        return ((z * self.wide + y) * CORES + c, x)

    def z_off(self, step):
        return lax.rem(self.z + DEPTH + step, jnp.int32(DEPTH))

    def y_off(self, step):
        return lax.rem(self.y + self.wide + step, jnp.int32(self.wide))


def snake(z, side):
    odd = lax.rem(side, jnp.int32(2))
    return side * DEPTH + z + odd * (DEPTH - 1 - 2 * z)


def unsnake(index, size):
    index = lax.rem(index + 2 * size, jnp.int32(size))
    side = lax.div(index, jnp.int32(DEPTH))
    rest = lax.rem(index, jnp.int32(DEPTH))
    return rest + lax.rem(side, jnp.int32(2)) * (DEPTH - 1 - 2 * rest), side


class Mail:
    def __init__(self, send_sems, recv_sems):
        self.send_sems, self.recv_sems = send_sems, recv_sems
        self.count = 0
        self.open = []

    def send(self, source, target, device):
        copy = pltpu.make_async_remote_copy(
            source,
            target,
            self.send_sems.at[self.count],
            self.recv_sems.at[self.count],
            device_id=device,
            device_id_type=MESH,
        )
        self.count += 1
        copy.start()
        self.open.append(copy)
        return copy

    def finish(self):
        for copy in self.open:
            copy.wait_send()


def meet(devices):
    barrier = pltpu.get_barrier_semaphore()
    for device in devices:
        pl.semaphore_signal(barrier, inc=1, device_id=device, device_id_type=MESH)
    pl.semaphore_wait(barrier, len(devices))


def receive(copies):
    for copy in copies:
        copy.wait_recv()


def own_copies(pairs, sems):
    copies = [
        pltpu.make_async_copy(source, target, sems.at[i]) for i, (source, target) in enumerate(pairs)
    ]
    for copy in copies:
        copy.start()
    return copies


def dot_nt(left_op, right_op):
    return lax.dot_general(
        left_op, right_op, (((1,), (1,)), ((), ())), preferred_element_type=jnp.float32
    )


def dot_tn(left_op, right_op):
    return lax.dot_general(
        left_op, right_op, (((0,), (0,)), ((), ())), preferred_element_type=jnp.float32
    )


def turned(values):
    return pltpu.roll(values, values.shape[-1] // 2, axis=values.ndim - 1)


def document_tables(seg_col, seg_row, head_dim):
    seq_len = seg_col.shape[0]
    rows = lax.broadcasted_iota(jnp.int32, (seq_len, seq_len), 0)
    cols = lax.broadcasted_iota(jnp.int32, (seq_len, seq_len), 1)
    same = seg_col == seg_row
    bias = jnp.where(same & (cols <= rows), 0.0, MASKED)
    before = jnp.where(same & (cols < rows), 1.0, 0.0)
    position = jnp.sum(before, axis=-1, keepdims=True)
    lane = lax.broadcasted_iota(jnp.int32, (1, head_dim), 1)
    half_dim = head_dim // 2
    slot = jnp.where(lane < half_dim, lane, lane - half_dim).astype(jnp.float32)
    frequency = jnp.exp(slot * (-2.0 * math.log(ROPE_BASE) / head_dim))
    angles = position * frequency
    sine = jnp.sin(angles)
    return bias, jnp.cos(angles), jnp.where(lane < half_dim, -sine, sine)


def matmul_tiles(left, right, write, tile=256):
    @pl.loop(0, right.shape[1] // tile)
    def _(index):
        columns = pl.ds(pl.multiple_of(index * tile, tile), tile)
        write(columns, matmul(left[...], right[:, columns]))


def forward_kernel(
    dp_size, w_q, w_k, w_v, w_o, w_g, w_u, w_d, cot, row_in, seg_col, seg_row,
    gain_one, gain_two, q_gain, k_gain,
    o_q, o_k, o_v, o_o, o_g, o_u, o_d, o_c, o_n,
    mid, normed_one, query_raw, key_raw, values_half, queries, keys, context, log_total,
    cosine, sine, bias,
    f_q, f_k, f_v, f_o, outgoing, incoming, normed, own_sems, send_sems, recv_sems,
):
    at = Place(dp_size)
    z, y, c, x = at.z, at.y, at.c, at.x
    ring = DEPTH * at.wide
    loop = DEPTH * HALVES
    spot, seat = snake(z, y), snake(z, x)
    ring_z, ring_y = unsnake(spot + 1, ring)
    back_z, back_y = unsnake(spot - 1, ring)
    ahead, behind = at.device(z=ring_z, y=ring_y), at.device(z=back_z, y=back_y)
    loop_z, loop_x = unsnake(seat + 1, loop)
    tail_z, tail_x = unsnake(seat - 1, loop)
    after, before = at.device(z=loop_z, x=loop_x), at.device(z=tail_z, x=tail_x)
    sibling, other = at.device(c=1 - c), at.device(x=1 - x)
    z_peers = [at.device(z=at.z_off(k)) for k in range(1, DEPTH)]
    y_peers = [at.device(y=at.y_off(j)) for j in range(1, at.wide)]
    meet([ahead, behind, after, before, sibling, other] + z_peers + y_peers)

    mail = Mail(send_sems, recv_sems)
    rows = w_q.shape[0]
    head_dim = q_gain.shape[1]
    part = w_g.shape[1] // DEPTH
    tokens = mid.shape[0]
    strip = tokens // 2
    ffn = ((w_g, o_g), (w_u, o_u), (w_d, o_d))
    attn = ((w_q, f_q), (w_k, f_k), (w_v, f_v), (w_o, f_o))

    def block_rows(bz, by, bc):
        return pl.ds(pl.multiple_of(((bz * at.wide + by) * CORES + bc) * rows, rows), rows)

    def columns(index):
        return pl.ds(pl.multiple_of(index * part, part), part)

    here = block_rows(z, y, c)
    rounds = [
        mail.send(weight, out.at[here], ahead if i < 2 else behind)
        for i, (weight, out) in enumerate(attn)
    ]
    attn_sibling = [mail.send(weight, out.at[here], sibling) for weight, out in attn]
    to_sibling = []
    mine = own_copies([(weight, out.at[here]) for weight, out in attn], own_sems)
    own_ffn = [
        pltpu.make_async_copy(weight.at[:, columns(z)], out.at[here], own_sems.at[4 + i])
        for i, (weight, out) in enumerate(ffn)
    ]
    own_ffn.append(
        pltpu.make_async_copy(
            cot.at[pl.ds(pl.multiple_of(x * tokens, tokens), tokens)], o_c.at[z, x], own_sems.at[7]
        )
    )
    for copy in own_ffn:
        copy.start()

    residual = row_in[...].astype(jnp.float32)
    normed_full, _ = rms_norm(residual, gain_one[...])
    normed_one[...] = normed_full.astype(jnp.bfloat16)
    bias_values, cosine[...], sine[...] = document_tables(seg_col[...], seg_row[...], head_dim)
    bias[...] = bias_values

    spread, crossing, state = {}, {}, {}

    def start_spread():
        for k in range(1, DEPTH):
            target = at.z_off(k)
            spread[k] = [
                mail.send(weight.at[:, columns(target)], out.at[here], z_peers[k - 1])
                for weight, out in ffn
            ]
        for j in range(1, at.wide):
            crossing[0, j] = [
                mail.send(weight.at[:, columns(z)], out.at[here], y_peers[j - 1])
                for weight, out in ffn
            ]
        to_sibling.extend(
            mail.send(weight.at[:, columns(z)], out.at[here], sibling) for weight, out in ffn
        )

    def start_turns(name, first, second, out):
        state[name] = [
            mail.send(first, out.at[z, x, pl.ds(0, strip)], after),
            mail.send(second, out.at[z, x, pl.ds(strip, strip)], before),
        ]

    def turn(name, out, step):
        receive(state[name])
        one_z, one_x = unsnake(seat - 1 - step, loop)
        two_z, two_x = unsnake(seat + 1 + step, loop)
        if step < loop - 2:
            first = out.at[one_z, one_x, pl.ds(0, strip)]
            second = out.at[two_z, two_x, pl.ds(strip, strip)]
            state[name] = [mail.send(first, first, after), mail.send(second, second, before)]

    def forward_spread(k):
        receive(spread[k])
        source = block_rows(at.z_off(-k), y, c)
        blocks = [out.at[source] for _, out in ffn]
        for j in range(1, at.wide):
            crossing[k, j] = [mail.send(block, block, y_peers[j - 1]) for block in blocks]
        to_sibling.extend(mail.send(block, block, sibling) for block in blocks)

    def forward_crossing(k):
        for j in range(1, at.wide):
            receive(crossing[k, j])
            source = block_rows(at.z_off(-k), at.y_off(-j), c)
            blocks = [out.at[source] for _, out in ffn]
            to_sibling.extend(mail.send(block, block, sibling) for block in blocks)

    for step in range(ring - 1):
        receive(rounds)
        one_z, one_y = unsnake(spot - 1 - step, ring)
        two_z, two_y = unsnake(spot + 1 + step, ring)
        places = [block_rows(one_z, one_y, c)] * 2 + [block_rows(two_z, two_y, c)] * 2
        blocks = [out.at[place] for (_, out), place in zip(attn, places)]
        if step < ring - 2:
            rounds = [
                mail.send(block, block, ahead if i < 2 else behind)
                for i, block in enumerate(blocks)
            ]
        attn_sibling += [mail.send(block, block, sibling) for block in blocks]
        if step == ring - 4:
            start_spread()
    cot_start = pl.multiple_of(x * tokens, tokens)
    start_turns(
        "cot", cot.at[pl.ds(cot_start, strip)], cot.at[pl.ds(cot_start + strip, strip)], o_c
    )
    for copy in mine:
        copy.wait()
    receive(attn_sibling)
    saved = [
        pltpu.make_async_copy(full, out, own_sems.at[i])
        for i, (full, out) in enumerate(((f_q, o_q), (f_k, o_k), (f_v, o_v), (f_o, o_o)))
    ]
    for copy in saved:
        copy.start()

    def write_query(cols, block):
        query_raw[:, cols] = block

    def write_key(cols, block):
        key_raw[:, cols] = block

    def write_value(cols, block):
        values_half[:, cols] = block.astype(jnp.bfloat16)

    matmul_tiles(normed_one, f_q, write_query)
    matmul_tiles(normed_one, f_k, write_key)
    matmul_tiles(normed_one, f_v, write_value)
    turn("cot", o_c, 0)

    def rotated(raw, gain):
        unit, _ = rms_norm(raw, gain)
        return (unit * cosine[...] + turned(unit) * sine[...]).astype(jnp.bfloat16)

    kv_heads = key_raw.shape[1] // head_dim
    group = query_raw.shape[1] // key_raw.shape[1]
    for j in range(kv_heads):
        kv_cols = pl.ds(j * head_dim, head_dim)
        keys[:, kv_cols] = rotated(key_raw[:, kv_cols], k_gain[...])
        for g in range(group):
            head = j * group + g
            cols = pl.ds(head * head_dim, head_dim)
            queries[:, cols] = rotated(query_raw[:, cols], q_gain[...])
            scores = dot_nt(queries[:, cols], keys[:, kv_cols]) * (1.0 / math.sqrt(head_dim))
            scores = scores + bias[...]
            row_max = jnp.max(scores, axis=-1, keepdims=True)
            weights = jnp.exp(scores - row_max)
            total = jnp.sum(weights, axis=-1, keepdims=True)
            log_total[:, head : head + 1] = row_max + jnp.log(total)
            probs = (weights * (1.0 / total)).astype(jnp.bfloat16)
            context[:, cols] = matmul(probs, values_half[:, kv_cols]).astype(jnp.bfloat16)
        if j == kv_heads // 2 - 1:
            turn("cot", o_c, 1)

    given = pl.ds(pl.multiple_of((1 - x) * tokens, tokens), tokens)
    kept = pl.ds(pl.multiple_of(x * tokens, tokens), tokens)
    width = row_in.shape[1]
    tile = 256

    def project(token_rows, target):
        @pl.loop(0, width // tile)
        def _(index):
            cols = pl.ds(pl.multiple_of(index * tile, tile), tile)
            block = dot_nt(context[token_rows, :], f_o[cols, :])
            target[:, cols] = block.astype(target.dtype)

    project(given, outgoing)
    swap = mail.send(outgoing, incoming, other)
    project(kept, mid)
    turn("cot", o_c, 2)
    forward_spread(1)
    forward_spread(2)
    swap.wait_recv()
    total = row_in[kept, :].astype(jnp.float32) + (mid[...] + incoming[...].astype(jnp.float32))
    mid[...] = total
    normed_mid, _ = rms_norm(total, gain_two[...])
    normed[...] = normed_mid.astype(jnp.bfloat16)
    last = pltpu.make_async_copy(normed, o_n.at[z, x], own_sems.at[8])
    last.start()
    start_turns("mid", normed.at[pl.ds(0, strip)], normed.at[pl.ds(strip, strip)], o_n)
    forward_spread(3)
    for step in range(loop - 1):
        turn("mid", o_n, step)
        if step + 3 < loop - 1:
            turn("cot", o_c, step + 3)
        if step < DEPTH:
            forward_crossing(step)
    receive(to_sibling)
    mail.finish()
    for copy in own_ffn + saved + [last]:
        copy.wait()


def forward(dp_size, weights, cot, row_in, seg_row, gains):
    w_q, w_k, w_v, w_o, w_g, w_u, w_d = weights
    wide = dp_size // (DEPTH * CORES)
    seq_len, width = row_in.shape
    head_dim = gains[2].shape[1]
    tokens = seq_len // HALVES
    part = w_g.shape[1] // DEPTH
    ring, loop = DEPTH * wide, DEPTH * HALVES
    half, full = jnp.bfloat16, jnp.float32
    attn_cols = [w.shape[1] for w in (w_q, w_k, w_v, w_o)]
    shapes = [jax.ShapeDtypeStruct((width, cols), half) for cols in attn_cols]
    shapes += [jax.ShapeDtypeStruct((width, part), half)] * 3
    shapes += [jax.ShapeDtypeStruct((DEPTH, HALVES, tokens, width), half)] * 2
    q_cols, kv_cols = attn_cols[0], attn_cols[1]
    for cols, kind in (
        (width, half), (q_cols, full), (kv_cols, full), (kv_cols, half), (q_cols, half),
        (kv_cols, half), (q_cols, half), (head_dim, full), (head_dim, full), (head_dim, full),
        (seq_len, full),
    ):
        shapes.append(jax.ShapeDtypeStruct((seq_len, cols), kind))
    shapes.insert(9, jax.ShapeDtypeStruct((tokens, width), full))
    copies = 4 * (ring - 1) + 4 * (loop - 1) + 1 + 9 + 3 * DEPTH * (wide - 1) + 4 * ring + 3 * ring
    return pl.pallas_call(
        functools.partial(forward_kernel, dp_size),
        out_shape=shapes,
        in_specs=[ANY] * 8 + [VMEM] * 7,
        out_specs=[ANY] * 9 + [VMEM] * 12,
        scratch_shapes=[pltpu.VMEM((width, cols), half) for cols in attn_cols]
        + [pltpu.VMEM((tokens, width), half)] * 3
        + [
            pltpu.SemaphoreType.DMA((9,)),
            pltpu.SemaphoreType.DMA((copies,)),
            pltpu.SemaphoreType.DMA((copies,)),
        ],
        compiler_params=pltpu.CompilerParams(
            collective_id=0, has_side_effects=True, vmem_limit_bytes=56 * 2**20
        ),
    )(w_q, w_k, w_v, w_o, w_g, w_u, w_d, cot, row_in, seg_row[:, None], seg_row[None, :], *gains)


def add_into(target, *others):
    total = target[...].astype(jnp.float32)
    for other in others:
        total = total + other[...].astype(jnp.float32)
    target[...] = total.astype(target.dtype)


def backward_kernel(
    dp_size, p_n, p_o, g_g, g_u, g_d, w_q, w_k, w_v, w_o,
    mid, cot, gain_two, row_in, normed_one, query_raw, key_raw, values_half, queries, keys,
    context, log_total, cosine, sine, bias, q_gain, k_gain,
    a_q, a_k, a_v, a_o,
    o_m, o_l, o_t, o_s, o_x, o_y, o_p, d_g, d_u, d_d,
    r_n, r_o, c_g, c_u, c_d, s_g, s_u, s_d, y_g, y_u, y_d, z_g, z_u, z_d,
    f_q, f_k, f_v, f_o, mid_half, context_grad, query_grad, key_grad, value_grad, flipped,
    own_sems, send_sems, recv_sems,
):
    at = Place(dp_size)
    z, y, c, x = at.z, at.y, at.c, at.x
    loop = DEPTH * HALVES
    seat = snake(z, x)
    loop_z, loop_x = unsnake(seat + 1, loop)
    tail_z, tail_x = unsnake(seat - 1, loop)
    after, before = at.device(z=loop_z, x=loop_x), at.device(z=tail_z, x=tail_x)
    other = at.device(x=1 - x)
    sibling = at.device(c=1 - c)
    z_peers = [at.device(z=at.z_off(k)) for k in range(1, DEPTH)]
    y_peers = [at.device(y=at.y_off(j)) for j in range(1, at.wide)]
    grads = (
        (g_g, c_g, s_g, y_g, z_g, d_g),
        (g_u, c_u, s_u, y_u, z_u, d_u),
        (g_d, c_d, s_d, y_d, z_d, d_d),
    )
    own_parts = [
        pltpu.make_async_copy(grad.at[:, :, c], own, own_sems.at[4 + i])
        for i, (grad, _, own, *_) in enumerate(grads)
    ]
    loads = [
        pltpu.make_async_copy(weight, full, own_sems.at[i])
        for i, (weight, full) in enumerate(((w_q, f_q), (w_k, f_k), (w_v, f_v), (w_o, f_o)))
    ]
    for copy in own_parts + loads:
        copy.start()
    meet([after, before, other, sibling] + z_peers + y_peers)
    mail = Mail(send_sems, recv_sems)
    tokens = mid.shape[0]
    strip = tokens // 2
    part = d_g.shape[1] // DEPTH
    strips = (pl.ds(0, strip), pl.ds(strip, strip))
    kept = pl.multiple_of(x * tokens, tokens)
    state = {}

    def block(array, i, step):
        shift = -1 - step if i == 0 else 1 + step
        bz, bx = unsnake(seat + shift, loop)
        return array.at[bz, bx, strips[i]]

    def ring_start(name, array, landing):
        state[name] = [
            mail.send(block(array, i, 0), landing.at[0, i], after if i == 0 else before)
            for i in range(2)
        ]

    def ring_step(name, array, landing, step):
        receive(state[name])
        turns = []
        for i in range(2):
            add_into(landing.at[step, i], block(array, i, step + 1))
            turns.append(
                mail.send(landing.at[step, i], landing.at[step + 1, i], after if i == 0 else before)
            )
        state[name] = turns

    ring_start("norm", p_n, r_n)
    order = [(k, at.z_off(k)) for k in (2, 1, 3, 0)]
    to_core = {
        k: [mail.send(grad.at[to, :, 1 - c], land.at[to], sibling) for grad, land, *_ in grads]
        for k, to in order
    }
    to_y, to_z = {}, {}

    def core_stage(k, to):
        receive(to_core[k])
        for _, land, own, *_ in grads:
            add_into(own.at[to], land.at[to])
        to_y[k] = [
            mail.send(own.at[to, at.y_off(j)], arrive.at[j - 1, to], y_peers[j - 1])
            for j in range(1, at.wide)
            for _, _, own, arrive, *_ in grads
        ]

    def y_stage(k, to):
        receive(to_y[k])
        for _, _, own, arrive, *_ in grads:
            add_into(own.at[to, y], *[arrive.at[j - 1, to] for j in range(1, at.wide)])
        if k > 0:
            to_z[k] = [
                mail.send(own.at[to, y], last.at[k - 1], z_peers[k - 1])
                for _, _, own, _, last, _ in grads
            ]

    for step in range(loop - 2):
        ring_step("norm", p_n, r_n, step)
        if step == 0:
            for copy in own_parts:
                copy.wait()
        if step < DEPTH:
            core_stage(*order[step])
        if step == loop - 3:
            y_stage(*order[0])
    receive(state["norm"])
    gain_sum = jnp.zeros(o_t.shape, jnp.float32)
    for i in range(2):
        grad_norm = r_n[loop - 2, i].astype(jnp.float32) + p_n[z, x, strips[i]].astype(jnp.float32)
        values = mid[strips[i], :]
        inv_rms = lax.rsqrt(jnp.mean(values * values, axis=-1, keepdims=True) + EPSILON)
        grad_values, terms = norm_back(grad_norm, values, inv_rms, gain_two[...])
        gain_sum = gain_sum + jnp.sum(terms, axis=0, keepdims=True)
        rows = pl.ds(pl.multiple_of(kept + i * strip, strip), strip)
        total = cot[rows, :].astype(jnp.float32) + grad_values
        o_m[strips[i], :] = total
        mid_half[rows, :] = total.astype(jnp.bfloat16)
    o_t[...] = gain_sum
    kept_rows = pl.ds(kept, tokens)
    swap_h = mail.send(mid_half.at[kept_rows], mid_half.at[kept_rows], other)
    ring_start("out", p_o, r_o)
    y_stage(*order[1])
    y_stage(*order[2])
    flipped[...] = normed_one[...].T
    for copy in loads:
        copy.wait()
    swap_h.wait_recv()

    def write_context(cols, value):
        context_grad[:, cols] = value.astype(jnp.bfloat16)

    matmul_tiles(mid_half, f_o, write_context)
    ring_step("out", p_o, r_o, 0)

    width = row_in.shape[1]
    tile = 256

    @pl.loop(0, width // tile)
    def _(index):
        rows = pl.ds(pl.multiple_of(index * tile, tile), tile)
        f_o[rows, :] = dot_tn(mid_half[:, rows], context[...]).astype(jnp.bfloat16)

    store_o = pltpu.make_async_copy(f_o, a_o, own_sems.at[3])
    store_o.start()
    y_stage(*order[3])

    head_dim = q_gain.shape[1]
    kv_heads = key_raw.shape[1] // head_dim
    group = query_raw.shape[1] // key_raw.shape[1]
    scale = 1.0 / math.sqrt(head_dim)

    def raw_grad(grad, raw, gain):
        back = grad * cosine[...] - turned(grad) * sine[...]
        inv_rms = lax.rsqrt(jnp.mean(raw * raw, axis=-1, keepdims=True) + EPSILON)
        grad_raw, terms = norm_back(back, raw, inv_rms, gain)
        return grad_raw.astype(jnp.bfloat16), jnp.sum(terms, axis=0, keepdims=True)

    q_sum = jnp.zeros(o_x.shape, jnp.float32)
    k_sum = jnp.zeros(o_y.shape, jnp.float32)
    for j in range(kv_heads):
        kv_cols = pl.ds(j * head_dim, head_dim)
        key_total = jnp.zeros((row_in.shape[0], head_dim), jnp.float32)
        value_total = jnp.zeros((row_in.shape[0], head_dim), jnp.float32)
        for g in range(group):
            head = j * group + g
            cols = pl.ds(head * head_dim, head_dim)
            scores = dot_nt(queries[:, cols], keys[:, kv_cols]) * scale + bias[...]
            probs = jnp.exp(scores - log_total[:, head : head + 1])
            grad_context = context_grad[:, cols]
            grad_probs = dot_nt(grad_context, values_half[:, kv_cols])
            delta = jnp.sum(
                grad_context.astype(jnp.float32) * context[:, cols].astype(jnp.float32),
                axis=-1,
                keepdims=True,
            )
            grad_scores = (probs * (grad_probs - delta) * scale).astype(jnp.bfloat16)
            grad_query, terms = raw_grad(
                matmul(grad_scores, keys[:, kv_cols]), query_raw[:, cols], q_gain[...]
            )
            query_grad[:, cols] = grad_query
            q_sum = q_sum + terms
            key_total = key_total + dot_tn(grad_scores, queries[:, cols])
            value_total = value_total + dot_tn(probs.astype(jnp.bfloat16), grad_context)
        grad_key, terms = raw_grad(key_total, key_raw[:, kv_cols], k_gain[...])
        key_grad[:, kv_cols] = grad_key
        k_sum = k_sum + terms
        value_grad[:, kv_cols] = value_total.astype(jnp.bfloat16)
        if j % 2 == 1:
            ring_step("out", p_o, r_o, 1 + j // 2)
    o_x[...] = q_sum
    o_y[...] = k_sum

    @pl.loop(0, width // tile)
    def _(index):
        rows = pl.ds(pl.multiple_of(index * tile, tile), tile)
        total = dot_nt(query_grad[...], f_q[rows, :])
        total = total + dot_nt(key_grad[...], f_k[rows, :])
        o_p[:, rows] = total + dot_nt(value_grad[...], f_v[rows, :])

    ring_step("out", p_o, r_o, 3)
    values = row_in[...].astype(jnp.float32)
    inv_rms = lax.rsqrt(jnp.mean(values * values, axis=-1, keepdims=True) + EPSILON)
    o_s[...] = jnp.sum(o_p[...] * values * inv_rms, axis=0, keepdims=True)

    @pl.loop(0, width // tile)
    def _(index):
        rows = pl.ds(pl.multiple_of(index * tile, tile), tile)
        lhs = flipped[rows, :]
        f_q[rows, :] = matmul(lhs, query_grad[...]).astype(jnp.bfloat16)
        f_k[rows, :] = matmul(lhs, key_grad[...]).astype(jnp.bfloat16)
        f_v[rows, :] = matmul(lhs, value_grad[...]).astype(jnp.bfloat16)

    stores = [
        pltpu.make_async_copy(full, out, own_sems.at[i])
        for i, (full, out) in enumerate(((f_q, a_q), (f_k, a_k), (f_v, a_v)))
    ]
    for copy in stores:
        copy.start()
    for step in range(4, loop - 2):
        ring_step("out", p_o, r_o, step)
    for _, _, own, _, _, out in grads:
        out[:, pl.ds(pl.multiple_of(z * part, part), part)] = own[z, y].astype(jnp.float32)
    for k in range(1, DEPTH):
        receive(to_z[k])
        columns = pl.ds(pl.multiple_of(at.z_off(-k) * part, part), part)
        for _, _, _, _, last, out in grads:
            out[:, columns] = last[k - 1].astype(jnp.float32)
    receive(state["out"])
    for i in range(2):
        rows = pl.ds(pl.multiple_of(kept + i * strip, strip), strip)
        total = r_o[loop - 2, i].astype(jnp.float32) + p_o[z, x, strips[i]].astype(jnp.float32)
        o_l[rows, :] = (mid[strips[i], :] + total).astype(jnp.bfloat16)
    swap_l = mail.send(o_l.at[kept_rows], o_l.at[kept_rows], other)
    swap_l.wait_recv()
    mail.finish()
    for copy in stores + [store_o]:
        copy.wait()


def backward(dp_size, parts, grads, weights, mid, cot, gain_two, saved, gains):
    wide = dp_size // (DEPTH * CORES)
    tokens, width = mid.shape
    seq_len = HALVES * tokens
    loop = DEPTH * HALVES
    rows, part = grads[0].shape[-2:]
    half, full = jnp.bfloat16, jnp.float32
    attn_cols = [w.shape[1] for w in weights]
    head_dim = gains[0].shape[1]
    copies = 4 * (loop - 1) + 3 * DEPTH + 3 * DEPTH * (wide - 1) + 9 + 2
    shapes = [jax.ShapeDtypeStruct((width, cols), half) for cols in attn_cols]
    shapes += [
        jax.ShapeDtypeStruct((tokens, width), full),
        jax.ShapeDtypeStruct((seq_len, width), half),
        jax.ShapeDtypeStruct((1, width), full),
        jax.ShapeDtypeStruct((1, width), full),
        jax.ShapeDtypeStruct((1, head_dim), full),
        jax.ShapeDtypeStruct((1, head_dim), full),
        jax.ShapeDtypeStruct((seq_len, width), full),
    ]
    shapes += [jax.ShapeDtypeStruct((rows, part * DEPTH), full)] * 3
    return pl.pallas_call(
        functools.partial(backward_kernel, dp_size),
        out_shape=shapes,
        in_specs=[VMEM] * 2 + [ANY] * 7 + [VMEM] * (3 + len(saved) + 2),
        out_specs=[ANY] * 4 + [VMEM] * 10,
        scratch_shapes=[pltpu.VMEM((loop - 1, 2, tokens // 2, width), half)] * 2
        + [pltpu.VMEM((DEPTH, wide, rows, part), half)] * 6
        + [pltpu.VMEM((wide - 1, DEPTH, rows, part), half)] * 3
        + [pltpu.VMEM((DEPTH - 1, rows, part), half)] * 3
        + [pltpu.VMEM((width, cols), half) for cols in attn_cols]
        + [pltpu.VMEM((seq_len, width), half)]
        + [pltpu.VMEM((seq_len, cols), half) for cols in (attn_cols[0],) + tuple(attn_cols[:3])]
        + [pltpu.VMEM((width, seq_len), half)]
        + [
            pltpu.SemaphoreType.DMA((7,)),
            pltpu.SemaphoreType.DMA((copies,)),
            pltpu.SemaphoreType.DMA((copies,)),
        ],
        compiler_params=pltpu.CompilerParams(
            collective_id=1, has_side_effects=True, vmem_limit_bytes=63 * 2**20
        ),
    )(*parts, *grads, *weights, mid, cot, gain_two, *saved, *gains)


def attn_reduce_kernel(
    dp_size, g_q, g_k, g_v, g_o, partial, row_in, grad_mid, gain, t_a, t_m, t_q, t_k,
    o_i, sums, w_q, w_k, w_v, w_o,
    gathering, arriving, outgoing, incoming, c_q, c_k, c_v, c_o, r_q, r_k, r_v, r_o, send_sems, recv_sems,
):
    at = Place(dp_size)
    z, y, c, x = at.z, at.y, at.c, at.x
    ring = DEPTH * at.wide
    spot = snake(z, y)
    ring_z, ring_y = unsnake(spot + 1, ring)
    back_z, back_y = unsnake(spot - 1, ring)
    ahead, behind = at.device(z=ring_z, y=ring_y), at.device(z=back_z, y=back_y)
    other = at.device(x=1 - x)
    sibling = at.device(c=1 - c)
    tokens = grad_mid.shape[0]
    kept = pl.ds(pl.multiple_of(x * tokens, tokens), tokens)
    given = pl.ds(pl.multiple_of((1 - x) * tokens, tokens), tokens)
    outgoing[...] = partial[given, :].astype(jnp.bfloat16)
    head_dim = t_q.shape[1]
    gathering[...] = jnp.zeros(gathering.shape, jnp.float32)
    for i, term in enumerate((t_a, t_m)):
        gathering[0, i : i + 1, :] = term[...]
    for i, term in enumerate((t_q, t_k)):
        gathering[0, i + 2 : i + 3, :head_dim] = term[...]
    pairs = pair_devices(at)
    meet([ahead, behind, other, sibling] + pairs)
    mail = Mail(send_sems, recv_sems)
    sets = ((g_q, c_q, r_q, w_q), (g_k, c_k, r_k, w_k), (g_v, c_v, r_v, w_v), (g_o, c_o, r_o, w_o))

    def spot_of(i, step):
        return unsnake(spot + (-1 - step if i < 2 else 1 + step), ring)

    to_core = []
    for step in range(ring):
        row = []
        for i, (grad, land, _, _) in enumerate(sets):
            bz, by = spot_of(i, step)
            row.append(mail.send(grad.at[bz, by, 1 - c], land.at[bz, by], sibling))
        to_core.append(row)
    swap = mail.send(outgoing, incoming, other)
    exchange = mail.send(gathering.at[0], arriving.at[0], pairs[0])
    turns = []
    for step in range(ring):
        receive(to_core[step])
        if step > 0:
            receive(turns)
        turns = []
        for i, (grad, land, arrive, out) in enumerate(sets):
            bz, by = spot_of(i, step)
            terms = [grad[bz, by, c].astype(jnp.float32), land[bz, by].astype(jnp.float32)]
            if step > 0:
                terms.append(arrive[step - 1].astype(jnp.float32))
            total = sum(terms[1:], terms[0])
            if step < ring - 1:
                land[bz, by] = total.astype(jnp.bfloat16)
                turns.append(
                    mail.send(land.at[bz, by], arrive.at[step], ahead if i < 2 else behind)
                )
            else:
                out[...] = total
        if 1 <= step <= len(pairs):
            exchange.wait_recv()
            total = gathering[step - 1] + arriving[step - 1]
            if step < len(pairs):
                gathering[step] = total
                exchange = mail.send(gathering.at[step], arriving.at[step], pairs[step])
            else:
                sums[...] = total
        if step == 1:
            swap.wait_recv()
            grad_norm = partial[kept, :] + incoming[...].astype(jnp.float32)
            values = row_in[kept, :].astype(jnp.float32)
            inv_rms = lax.rsqrt(jnp.mean(values * values, axis=-1, keepdims=True) + EPSILON)
            grad_values, _ = norm_back(grad_norm, values, inv_rms, gain[...])
            o_i[kept, :] = (grad_mid[...] + grad_values).astype(jnp.bfloat16)
            swap_back = mail.send(o_i.at[kept], o_i.at[kept], other)
    swap_back.wait_recv()
    mail.finish()


def pair_devices(at):
    def flip(index, bit):
        return index + bit - 2 * bit * lax.rem(lax.div(index, jnp.int32(bit)), jnp.int32(2))

    bits = [1 << i for i in range(at.wide.bit_length() - 1)]
    return (
        [at.device(c=1 - at.c), at.device(x=1 - at.x)]
        + [at.device(y=flip(at.y, bit)) for bit in bits]
        + [at.device(z=flip(at.z, bit)) for bit in (1, 2)]
    )


def attn_reduce(dp_size, grads, partial, row_in, grad_mid, gain, terms):
    wide = dp_size // (DEPTH * CORES)
    ring = DEPTH * wide
    tokens, width = grad_mid.shape
    half = jnp.bfloat16
    rows = grads[0].shape[-2]
    cols = [grad.shape[-1] for grad in grads]
    pairs = 4 + wide.bit_length() - 1
    copies = 4 * ring + 4 * (ring - 1) + 2 + pairs
    return pl.pallas_call(
        functools.partial(attn_reduce_kernel, dp_size),
        out_shape=[
            jax.ShapeDtypeStruct((HALVES * tokens, width), half),
            jax.ShapeDtypeStruct((8, width), jnp.float32),
        ]
        + [jax.ShapeDtypeStruct((rows, col), jnp.float32) for col in cols],
        in_specs=[VMEM] * 12,
        out_specs=[VMEM] * 6,
        scratch_shapes=[pltpu.VMEM((pairs, 8, width), jnp.float32)] * 2
        + [pltpu.VMEM((tokens, width), half)] * 2
        + [pltpu.VMEM((DEPTH, wide, rows, col), half) for col in cols]
        + [pltpu.VMEM((ring - 1, rows, col), half) for col in cols]
        + [pltpu.SemaphoreType.DMA((copies,)), pltpu.SemaphoreType.DMA((copies,))],
        compiler_params=pltpu.CompilerParams(
            collective_id=2, has_side_effects=True, vmem_limit_bytes=58 * 2**20
        ),
    )(*grads, partial, row_in, grad_mid, gain, *terms)


def body(
    dp_size,
    layer_in,
    seg_ids,
    w_q,
    w_k,
    w_v,
    w_o,
    w_gate,
    w_up,
    w_down,
    attn_gain,
    mlp_gain,
    q_gain,
    k_gain,
    cotangent,
):
    rows = w_q.shape[0]
    width = rows * dp_size
    wide = dp_size // (DEPTH * CORES)
    row_in = layer_in[0]
    row_cot = cotangent[0]
    seq_len = row_in.shape[0]
    gains = [gain[None, :] for gain in (attn_gain, mlp_gain, q_gain, k_gain)]
    outs = forward(
        dp_size, (w_q, w_k, w_v, w_o, w_gate, w_up, w_down), row_cot, row_in, seg_ids[0], gains
    )
    attn_full, (part_gate, part_up, part_down), (cots, normed_two), mid = (
        outs[:4], outs[4:7], outs[7:9], outs[9],
    )
    saved = outs[10:]
    cots, normed_two = cots.reshape(-1, width), normed_two.reshape(-1, width)

    gate_pre = matmul(normed_two, part_gate)
    up_pre = matmul(normed_two, part_up)
    sigmoid_gate = jax.nn.sigmoid(gate_pre)
    silu_val = gate_pre * sigmoid_gate
    act_half = (silu_val * up_pre).astype(jnp.bfloat16)
    out_part = matmul(act_half, part_down.T).astype(jnp.bfloat16)
    grad_act = matmul(cots, part_down)
    grad_gate_pre = (
        grad_act * up_pre * sigmoid_gate * (1.0 + gate_pre * (1.0 - sigmoid_gate))
    ).astype(jnp.bfloat16)
    grad_up_pre = (grad_act * silu_val).astype(jnp.bfloat16)
    norm_part = (
        matmul(grad_gate_pre, part_gate.T) + matmul(grad_up_pre, part_up.T)
    ).astype(jnp.bfloat16)
    grads = [
        matmul(left.T, right).astype(jnp.bfloat16).reshape(DEPTH, wide, CORES, rows, -1)
        for left, right in (
            (normed_two, grad_gate_pre),
            (normed_two, grad_up_pre),
            (cots, act_half),
        )
    ]
    shape = (DEPTH, HALVES, seq_len // HALVES, width)
    parts = (norm_part.reshape(shape), out_part.reshape(shape))
    outs = backward(
        dp_size, parts, grads, attn_full, mid, row_cot, gains[1], [row_in] + list(saved), gains[2:]
    )
    attn_grads = [grad.reshape(DEPTH, wide, CORES, rows, -1) for grad in outs[:4]]
    grad_mid, out_row, gain_two, gain_one, q_sum, k_sum, normed_part = outs[4:11]
    grad_gate, grad_up, grad_down = outs[11:]
    in_grad, sums, grad_q, grad_k, grad_v, grad_o = attn_reduce(
        dp_size, attn_grads, normed_part, row_in, grad_mid, gains[0],
        (gain_one, gain_two, q_sum, k_sum),
    )
    gain_outs = []
    for i, size in enumerate((width, width, q_gain.shape[0], k_gain.shape[0])):
        share = size // dp_size
        gain_outs.append(lax.dynamic_slice(sums[i], (lax.axis_index("dp") * share,), (share,)))
    return (
        out_row[None],
        in_grad[None],
        grad_q,
        grad_k,
        grad_v,
        grad_o,
        grad_gate,
        grad_up,
        grad_down,
        *gain_outs,
    )


def solution(mesh):
    return jax.shard_map(
        functools.partial(body, mesh.shape["dp"]),
        mesh=mesh,
        in_specs=(
            P("dp", None, None),
            P("dp", None),
            P("dp", "mp"),
            P("dp", "mp"),
            P("dp", "mp"),
            P("dp", "mp"),
            P("dp", "mp"),
            P("dp", "mp"),
            P("dp", "mp"),
            P(),
            P(),
            P(),
            P(),
            P("dp", None, None),
        ),
        out_specs=(
            P("dp", None, None),
            P("dp", None, None),
            P("dp", "mp"),
            P("dp", "mp"),
            P("dp", "mp"),
            P("dp", "mp"),
            P("dp", "mp"),
            P("dp", "mp"),
            P("dp", "mp"),
            P("dp"),
            P("dp"),
            P("dp"),
            P("dp"),
        ),
        check_vma=False,
    )
```

```python
import functools
import math

import jax
import jax.numpy as jnp
from jax import lax
from jax.experimental import pallas as pl
from jax.experimental.pallas import tpu as pltpu
from jax.sharding import PartitionSpec as P

EPSILON = 1e-06
ROPE_BASE = 1000000.0
MASKED = -1e30


def matmul(left_op, right_op):
    return jnp.dot(left_op, right_op, preferred_element_type=jnp.float32)


def rms_norm(values, gain_vec):
    inv_rms = lax.rsqrt(jnp.mean(values * values, axis=-1, keepdims=True) + EPSILON)
    return (values * inv_rms * gain_vec, inv_rms)


def norm_back(grad_norm, values, inv_rms, gain_vec):
    scaled = grad_norm * gain_vec
    cubed = inv_rms * inv_rms * inv_rms
    grad_values = inv_rms * scaled - values * cubed * jnp.mean(
        scaled * values, axis=-1, keepdims=True
    )
    return (grad_values, grad_norm * values * inv_rms)


MESH = pl.DeviceIdType.MESH
ANY = pl.BlockSpec(memory_space=pl.ANY)
VMEM = pl.BlockSpec(memory_space=pltpu.VMEM)
DEPTH = 4
CORES = 2
HALVES = 2
UP, DOWN = 0, 1
TILE = 256


def split(index, size):
    size = jnp.int32(size)
    return lax.div(index, size), lax.rem(index, size)


class Place:
    def __init__(self, dp_size):
        self.wide = dp_size // (DEPTH * CORES)
        self.x = lax.axis_index("mp")
        rest, self.c = split(lax.axis_index("dp"), CORES)
        self.z, self.y = split(rest, self.wide)

    def device(self, z=None, y=None, c=None, x=None):
        z = self.z if z is None else z
        y = self.y if y is None else y
        c = self.c if c is None else c
        x = self.x if x is None else x
        return ((z * self.wide + y) * CORES + c, x)

    def z_off(self, step):
        return lax.rem(self.z + DEPTH + step, jnp.int32(DEPTH))

    def y_off(self, step):
        return lax.rem(self.y + self.wide + step, jnp.int32(self.wide))

    def rows(self, z, y, c, count):
        return pl.ds(pl.multiple_of(((z * self.wide + y) * CORES + c) * count, count), count)

    def line(self):
        return [self.device(z=self.z_off(1)), self.device(z=self.z_off(-1))]

    def z_peers(self):
        return [self.device(z=self.z_off(k)) for k in range(1, DEPTH)]

    def y_peers(self):
        return [self.device(y=self.y_off(j)) for j in range(1, self.wide)]

    def order(self):
        low = 1 - lax.div(self.z, jnp.int32(2))
        return [3 * low, 1 + low, low * (1 - self.z) + (1 - low) * (5 - self.z), self.z]


def guarded(when, action):
    if when is None:
        action()
    else:
        pl.when(when)(action)


class Mail:
    def __init__(self, send_sems, recv_sems):
        self.send_sems, self.recv_sems = send_sems, recv_sems
        self.count = 0
        self.open = []

    def reserve(self, count):
        first = self.count
        self.count += count
        return first

    def describe(self, source, target, device, slot):
        return pltpu.make_async_remote_copy(
            source,
            target,
            self.send_sems.at[slot],
            self.recv_sems.at[slot],
            device_id=device,
            device_id_type=MESH,
        )

    def make(self, source, target, device, when=None, slot=None):
        copy = self.describe(source, target, device, self.reserve(1) if slot is None else slot)
        self.open.append((copy, when))
        return copy

    def send(self, source, target, device, when=None):
        copy = self.make(source, target, device, when)
        guarded(when, copy.start)
        return copy

    def finish(self):
        for copy, when in self.open:
            guarded(when, copy.wait_send)


def meet(devices):
    barrier = pltpu.get_barrier_semaphore()
    for device in devices:
        pl.semaphore_signal(barrier, inc=1, device_id=device, device_id_type=MESH)
    pl.semaphore_wait(barrier, len(devices))


def receive(copies):
    for copy in copies:
        copy.wait_recv()


def start_all(copies):
    for copy in copies:
        copy.start()


class LineGather:
    def __init__(self, mail, at, own, place, sides, sibling=None, share_own=True):
        self.mail, self.at, self.place = mail, at, place
        self.sides, self.sibling = sides, sibling
        self.neighbours = at.line()
        self.open_end = [at.z < DEPTH - 1, at.z > 0]
        pairs = list(zip(own, place(at.z, 0)))
        self.hops = [
            [mail.send(source, target, self.neighbours[way], self.open_end[way]) for source, target in pairs]
            for way in (UP, DOWN)
        ]
        self.over, self.cores = {}, []
        if share_own:
            self.over["own"] = [
                [mail.send(source, target, side) for source, target in pairs] for side in sides
            ]
        if sibling is not None:
            self.cores.append(
                (None, [mail.send(source, target, sibling) for source, target in pairs])
            )

    def where(self, way, step):
        z = self.at.z
        if way == UP:
            return z >= step + 1, self.at.z_off(-1 - step)
        return z + 1 + step < DEPTH, self.at.z_off(1 + step)

    def step(self, step):
        for way in (UP, DOWN):
            got, index = self.where(way, step)
            refs = self.place(index, 0)
            arrived = self.hops[way]
            onward = []
            if step < DEPTH - 2:
                more = got & self.open_end[way]
                onward = [self.mail.make(ref, ref, self.neighbours[way], more) for ref in refs]
            over = [[self.mail.make(ref, ref, side, got) for ref in refs] for side in self.sides]
            cores = []
            if self.sibling is not None:
                cores = [self.mail.make(ref, ref, self.sibling, got) for ref in refs]

            def pass_on(way=way, arrived=arrived, onward=onward, over=over, cores=cores):
                receive(arrived)
                pl.when(self.open_end[way])(lambda: start_all(onward))
                for copies in over:
                    start_all(copies)
                start_all(cores)

            pl.when(got)(pass_on)
            self.hops[way] = onward
            self.over[way, step] = over
            if cores:
                self.cores.append((got, cores))

    def side_step(self, key):
        got, index = (None, self.at.z) if key == "own" else self.where(*key)
        cores = []
        for j in range(1, len(self.sides) + 1):
            if self.sibling is not None:
                refs = self.place(index, j)
                cores += [self.mail.make(ref, ref, self.sibling, got) for ref in refs]

        def pass_on():
            for copies in self.over[key]:
                receive(copies)
            start_all(cores)

        guarded(got, pass_on)
        if cores:
            self.cores.append((got, cores))

    def side_steps(self, step):
        self.side_step((UP, step))
        self.side_step((DOWN, step))

    def finish(self):
        for got, cores in self.cores:
            guarded(got, lambda cores=cores: receive(cores))


class LineReduce:
    slots = 2 * (DEPTH - 1)

    def __init__(self, mail, at, pieces, part, land):
        self.mail, self.at, self.pieces, self.part, self.land = mail, at, pieces, part, land
        self.base = mail.reserve(self.slots * pieces)

    def copies(self, index, sources, device):
        slots = [self.base + index * self.pieces + i for i in range(self.pieces)]
        return [
            self.mail.describe(source, target, device, slot)
            for source, target, slot in zip(sources, self.land(index), slots)
        ]

    def pass_on(self, turn):
        z = self.at.z
        low = 1 - lax.div(z, jnp.int32(2))
        up = low if turn < 2 else 1 - lax.rem(z, jnp.int32(2))
        target = self.at.order()[turn]
        index = up * (target - 1) + (1 - up) * (DEPTH - 1 + target)
        device = self.at.device(z=z + 2 * up - 1)
        sources = self.part(target)
        copies = self.copies(index, sources, device)
        has_in = up * jnp.where(z > 0, 1, 0) + (1 - up) * jnp.where(z < DEPTH - 1, 1, 0)

        @pl.when(has_in > 0)
        def _():
            receive(copies)
            for source, landed in zip(sources, self.land(index)):
                add_into(source, landed)

        start_all(copies)
        self.mail.open += [(copy, None) for copy in copies]

    def last(self, use):
        z = self.at.z
        sources = self.part(z)
        for when, index, neighbour in (
            (z > 0, lax.max(z - 1, 0), self.at.z_off(-1)),
            (z < DEPTH - 1, lax.min(DEPTH - 1 + z, self.slots - 1), self.at.z_off(1)),
        ):
            copies = self.copies(index, sources, self.at.device(z=neighbour))

            @pl.when(when)
            def _(copies=copies, index=index):
                receive(copies)
                for i, landed in enumerate(self.land(index)):
                    use(i, landed)


def own_copies(pairs, sems, first=0):
    copies = [
        pltpu.make_async_copy(source, target, sems.at[first + i])
        for i, (source, target) in enumerate(pairs)
    ]
    start_all(copies)
    return copies


def finish_own(copies):
    for copy in copies:
        copy.wait()


def add_into(target, *others):
    total = target[...].astype(jnp.float32)
    for other in others:
        total = total + other[...].astype(jnp.float32)
    target[...] = total.astype(target.dtype)


def dot_nt(left_op, right_op):
    return lax.dot_general(
        left_op, right_op, (((1,), (1,)), ((), ())), preferred_element_type=jnp.float32
    )


def dot_tn(left_op, right_op):
    return lax.dot_general(
        left_op, right_op, (((0,), (0,)), ((), ())), preferred_element_type=jnp.float32
    )


def turned(values):
    return pltpu.roll(values, values.shape[-1] // 2, axis=values.ndim - 1)


def document_tables(seg_col, seg_row, head_dim):
    seq_len = seg_col.shape[0]
    rows = lax.broadcasted_iota(jnp.int32, (seq_len, seq_len), 0)
    cols = lax.broadcasted_iota(jnp.int32, (seq_len, seq_len), 1)
    same = seg_col == seg_row
    bias = jnp.where(same & (cols <= rows), 0.0, MASKED)
    before = jnp.where(same & (cols < rows), 1.0, 0.0)
    position = jnp.sum(before, axis=-1, keepdims=True)
    lane = lax.broadcasted_iota(jnp.int32, (1, head_dim), 1)
    half_dim = head_dim // 2
    slot = jnp.where(lane < half_dim, lane, lane - half_dim).astype(jnp.float32)
    frequency = jnp.exp(slot * (-2.0 * math.log(ROPE_BASE) / head_dim))
    angles = position * frequency
    sine = jnp.sin(angles)
    return bias, jnp.cos(angles), jnp.where(lane < half_dim, -sine, sine)


def matmul_tiles(left, right, write, tile=256):
    @pl.loop(0, right.shape[1] // tile)
    def _(index):
        columns = pl.ds(pl.multiple_of(index * tile, tile), tile)
        write(columns, matmul(left[...], right[:, columns]))


def forward_kernel(
    dp_size, w_q, w_k, w_v, w_o, w_g, w_u, w_d, cot, row_in, seg_col, seg_row,
    gain_one, gain_two, q_gain, k_gain,
    o_attn, o_ffn, o_c, o_n,
    mid, normed_one, query_raw, key_raw, values_half, queries, keys, context, log_total,
    cosine, sine, bias,
    full, outgoing, incoming, normed, own_sems, send_sems, recv_sems,
):
    at = Place(dp_size)
    z, y, c, x = at.z, at.y, at.c, at.x
    sibling, other = at.device(c=1 - c), at.device(x=1 - x)
    z_peers, y_peers = at.z_peers(), at.y_peers()
    meet([sibling, other] + z_peers + y_peers)

    mail = Mail(send_sems, recv_sems)
    rows = w_q.shape[0]
    head_dim = q_gain.shape[1]
    part = w_g.shape[1] // DEPTH
    tokens = mid.shape[0]
    here = at.rows(z, y, c, rows)
    spans, start = [], 0
    for weight in (w_q, w_k, w_v, w_o):
        spans.append(pl.ds(start, weight.shape[1]))
        start += weight.shape[1]
    q_span, k_span, v_span, o_span = spans
    ffn = [(weight, pl.ds(i * part, part)) for i, weight in enumerate((w_g, w_u, w_d))]

    def columns(index):
        return pl.ds(pl.multiple_of(index * part, part), part)

    def half_rows(index):
        return pl.ds(pl.multiple_of(index * tokens, tokens), tokens)

    mine = own_copies(
        [(weight, full.at[here, span]) for weight, span in zip((w_q, w_k, w_v, w_o), spans)],
        own_sems,
    )
    own_ffn = own_copies(
        [(weight.at[:, columns(z)], o_ffn.at[here, span]) for weight, span in ffn]
        + [(cot.at[half_rows(i)], o_c.at[z, i]) for i in range(2)],
        own_sems,
        4,
    )
    finish_own(mine)
    attn = LineGather(
        mail,
        at,
        (full.at[here],),
        lambda zb, j: [full.at[at.rows(zb, at.y_off(-j), c, rows)]],
        y_peers,
        sibling,
    )

    residual = row_in[...].astype(jnp.float32)
    normed_full, _ = rms_norm(residual, gain_one[...])
    normed_one[...] = normed_full.astype(jnp.bfloat16)
    bias_values, cosine[...], sine[...] = document_tables(seg_col[...], seg_row[...], head_dim)
    bias[...] = bias_values

    spread, crossing, to_sibling = {}, {}, []

    def start_spread():
        for k in range(1, DEPTH):
            target = at.z_off(k)
            spread[k] = [
                mail.send(weight.at[:, columns(target)], o_ffn.at[here, span], z_peers[k - 1])
                for weight, span in ffn
            ]
        finish_own(own_ffn)
        block = o_ffn.at[here]
        for j in range(1, at.wide):
            crossing[0, j] = mail.send(block, block, y_peers[j - 1])
        to_sibling.append(mail.send(block, block, sibling))

    def forward_spread(k):
        receive(spread[k])
        block = o_ffn.at[at.rows(at.z_off(-k), y, c, rows)]
        for j in range(1, at.wide):
            crossing[k, j] = mail.send(block, block, y_peers[j - 1])
        to_sibling.append(mail.send(block, block, sibling))

    def forward_crossing(k):
        for j in range(1, at.wide):
            crossing[k, j].wait_recv()
            block = o_ffn.at[at.rows(at.z_off(-k), at.y_off(-j), c, rows)]
            to_sibling.append(mail.send(block, block, sibling))

    def half_place(out):
        return lambda zb, j: [out.at[zb, x if j == 0 else 1 - x]]

    attn.step(0)
    attn.side_step("own")
    attn.step(1)
    start_spread()
    attn.side_steps(0)
    attn.step(2)
    cots = LineGather(
        mail, at, (cot.at[half_rows(x)],), half_place(o_c), [other], share_own=False
    )
    attn.side_steps(1)
    attn.side_steps(2)
    attn.finish()
    saved = own_copies([(full, o_attn)], own_sems)

    def write_query(cols, block):
        query_raw[:, cols] = block

    def write_key(cols, block):
        key_raw[:, cols] = block

    def write_value(cols, block):
        values_half[:, cols] = block.astype(jnp.bfloat16)

    matmul_tiles(normed_one, full.at[:, q_span], write_query)
    matmul_tiles(normed_one, full.at[:, k_span], write_key)
    matmul_tiles(normed_one, full.at[:, v_span], write_value)
    cots.step(0)
    forward_spread(1)

    def rotated(raw, gain):
        unit, _ = rms_norm(raw, gain)
        return (unit * cosine[...] + turned(unit) * sine[...]).astype(jnp.bfloat16)

    kv_heads = key_raw.shape[1] // head_dim
    group = query_raw.shape[1] // key_raw.shape[1]
    for j in range(kv_heads):
        kv_cols = pl.ds(j * head_dim, head_dim)
        keys[:, kv_cols] = rotated(key_raw[:, kv_cols], k_gain[...])
        for g in range(group):
            head = j * group + g
            cols = pl.ds(head * head_dim, head_dim)
            queries[:, cols] = rotated(query_raw[:, cols], q_gain[...])
            scores = dot_nt(queries[:, cols], keys[:, kv_cols]) * (1.0 / math.sqrt(head_dim))
            scores = scores + bias[...]
            row_max = jnp.max(scores, axis=-1, keepdims=True)
            weights = jnp.exp(scores - row_max)
            total = jnp.sum(weights, axis=-1, keepdims=True)
            log_total[:, head : head + 1] = row_max + jnp.log(total)
            probs = (weights * (1.0 / total)).astype(jnp.bfloat16)
            context[:, cols] = matmul(probs, values_half[:, kv_cols]).astype(jnp.bfloat16)
        if j == kv_heads // 2 - 1:
            cots.step(1)
            forward_spread(3)

    given, kept = half_rows(1 - x), half_rows(x)
    width = row_in.shape[1]

    def project(token_rows, target):
        @pl.loop(0, width // TILE)
        def _(index):
            cols = pl.ds(pl.multiple_of(index * TILE, TILE), TILE)
            block = dot_nt(context[token_rows, :], full[cols, o_span])
            target[:, cols] = block.astype(target.dtype)

    project(given, outgoing)
    swap = mail.send(outgoing, incoming, other)
    project(kept, mid)
    forward_spread(2)
    cots.step(2)
    swap.wait_recv()
    total = row_in[kept, :].astype(jnp.float32) + (mid[...] + incoming[...].astype(jnp.float32))
    mid[...] = total
    normed_mid, _ = rms_norm(total, gain_two[...])
    normed[...] = normed_mid.astype(jnp.bfloat16)
    last = own_copies([(normed, o_n.at[z, x])], own_sems, 9)
    norms = LineGather(mail, at, (normed,), half_place(o_n), [other])
    cots.side_steps(0)
    forward_crossing(0)
    norms.step(0)
    forward_crossing(1)
    norms.step(1)
    forward_crossing(3)
    cots.side_steps(1)
    norms.step(2)
    forward_crossing(2)
    cots.side_steps(2)
    norms.side_step("own")
    for step in range(DEPTH - 1):
        norms.side_steps(step)
    receive(to_sibling)
    mail.finish()
    finish_own(saved + last)


def forward(dp_size, weights, cot, row_in, seg_row, gains):
    w_q, w_k, w_v, w_o, w_g, w_u, w_d = weights
    wide = dp_size // (DEPTH * CORES)
    seq_len, width = row_in.shape
    head_dim = gains[2].shape[1]
    tokens = seq_len // HALVES
    part = w_g.shape[1] // DEPTH
    half, whole = jnp.bfloat16, jnp.float32
    attn_cols = [w.shape[1] for w in (w_q, w_k, w_v, w_o)]
    shapes = [jax.ShapeDtypeStruct((width, cols), half) for cols in (sum(attn_cols), 3 * part)]
    shapes += [jax.ShapeDtypeStruct((DEPTH, HALVES, tokens, width), half)] * 2
    q_cols, kv_cols = attn_cols[0], attn_cols[1]
    for cols, kind in (
        (width, half), (q_cols, whole), (kv_cols, whole), (kv_cols, half), (q_cols, half),
        (kv_cols, half), (q_cols, half), (head_dim, whole), (head_dim, whole), (head_dim, whole),
        (seq_len, whole),
    ):
        shapes.append(jax.ShapeDtypeStruct((seq_len, cols), kind))
    shapes.insert(4, jax.ShapeDtypeStruct((tokens, width), whole))
    hops = 2 * (DEPTH - 1)
    spots = 1 + hops
    copies = (hops + spots * (2 * wide - 1)) + 2 * (2 * hops + 1) + 1
    copies += 9 + DEPTH * (2 * wide - 1)
    return pl.pallas_call(
        functools.partial(forward_kernel, dp_size),
        out_shape=shapes,
        in_specs=[ANY] * 8 + [VMEM] * 7,
        out_specs=[ANY] * 4 + [VMEM] * 12,
        scratch_shapes=[pltpu.VMEM((width, sum(attn_cols)), half)]
        + [pltpu.VMEM((tokens, width), half)] * 3
        + [
            pltpu.SemaphoreType.DMA((10,)),
            pltpu.SemaphoreType.DMA((copies,)),
            pltpu.SemaphoreType.DMA((copies,)),
        ],
        compiler_params=pltpu.CompilerParams(
            collective_id=0, has_side_effects=True, vmem_limit_bytes=56 * 2**20
        ),
    )(w_q, w_k, w_v, w_o, w_g, w_u, w_d, cot, row_in, seg_row[:, None], seg_row[None, :], *gains)


def mlp_kernel(
    dp_size, weights, n_all, c_all, mid, cot, gain,
    o_m, o_h, o_l, o_t, shares,
    full, x_n, x_c, hidden, p_n, p_o, h_n, h_o, l_n, l_o, from_core, from_y,
    own_sems, send_sems, recv_sems,
):
    at = Place(dp_size)
    z, y, c, x = at.z, at.y, at.c, at.x
    other, sibling = at.device(x=1 - x), at.device(c=1 - c)
    y_peers = at.y_peers()
    order = at.order()
    tokens = mid.shape[0]
    block_rows = HALVES * tokens
    rows = from_core.shape[2]
    part = full.shape[1] // 3
    gate_up, down = pl.ds(0, 2 * part), pl.ds(2 * part, part)
    width = mid.shape[1]

    def band(index, size):
        return pl.ds(pl.multiple_of(index * size, size), size)

    loads = {}
    for i, name in enumerate("gud"):
        span = pl.ds(i * part, part)
        loads[name] = pltpu.make_async_copy(weights.at[:, span], full.at[:, span], own_sems.at[i])
    for i, index in enumerate(order):
        block = band(index, block_rows)
        loads["n", i] = pltpu.make_async_copy(n_all.at[block], x_n.at[block], own_sems.at[3 + i])
        loads["c", i] = pltpu.make_async_copy(c_all.at[block], x_c.at[block], own_sems.at[7 + i])
    for key in ("g", "u", ("n", 0), "d", ("c", 0)):
        loads[key].start()
    for i in range(1, DEPTH):
        loads["n", i].start()
        loads["c", i].start()
    meet([other, sibling] + at.line() + y_peers)
    mail = Mail(send_sems, recv_sems)

    def half_rows(index, side):
        return band(index * HALVES + side, tokens)

    norm_line = LineReduce(
        mail, at, 1, lambda index: [p_n.at[half_rows(index, x)]], lambda slot: [l_n.at[slot]]
    )
    out_line = LineReduce(
        mail, at, 1, lambda index: [p_o.at[half_rows(index, x)]], lambda slot: [l_o.at[slot]]
    )
    norm_swaps, out_swaps = [], []

    def compute(i):
        block = band(order[i], block_rows)
        if i == 0:
            for name in ("g", "u", "d"):
                loads[name].wait()
        loads["n", i].wait()
        loads["c", i].wait()

        @pl.loop(0, part // TILE)
        def _(index):
            g_cols, u_cols, d_cols = [
                pl.ds(pl.multiple_of(i * part + index * TILE, TILE), TILE) for i in range(3)
            ]
            gate = matmul(x_n[block, :], full[:, g_cols])
            up = matmul(x_n[block, :], full[:, u_cols])
            grad_act = matmul(x_c[block, :], full[:, d_cols])
            sigmoid_gate = 1.0 / (1.0 + jnp.exp(-gate))
            silu_val = gate * sigmoid_gate
            hidden[block, g_cols] = (
                grad_act * up * sigmoid_gate * (1.0 + gate * (1.0 - sigmoid_gate))
            ).astype(jnp.bfloat16)
            hidden[block, u_cols] = (grad_act * silu_val).astype(jnp.bfloat16)
            hidden[block, d_cols] = (silu_val * up).astype(jnp.bfloat16)

        @pl.loop(0, width // TILE)
        def _(index):
            cols = band(index, TILE)
            p_n[block, cols] = dot_nt(hidden[block, gate_up], full[cols, gate_up]).astype(jnp.bfloat16)

        norm_swaps.append(mail.send(p_n.at[half_rows(order[i], 1 - x)], h_n.at[i], other))

        @pl.loop(0, width // TILE)
        def _(index):
            cols = band(index, TILE)
            p_o[block, cols] = dot_nt(hidden[block, down], full[cols, down]).astype(jnp.bfloat16)

    def reduce_step(line, partial, swaps, landed, i):
        swaps[i].wait_recv()
        add_into(partial.at[half_rows(order[i], x)], landed.at[i])
        line.pass_on(i)

    def weight_grads(i):
        @pl.loop(0, width // DEPTH // TILE)
        def _(index):
            cols = pl.ds(pl.multiple_of(order[i] * (width // DEPTH) + index * TILE, TILE), TILE)
            full[cols, gate_up] = matmul(x_n[:, cols].T, hidden[:, gate_up]).astype(jnp.bfloat16)
            full[cols, down] = matmul(x_c[:, cols].T, hidden[:, down]).astype(jnp.bfloat16)

        return [
            mail.send(
                full.at[at.rows(order[i], side, 1 - c, rows)], from_core.at[order[i], side], sibling
            )
            for side in range(at.wide)
        ]

    to_core, to_y = {}, {}

    def core_stage(i):
        receive(to_core[i])
        for side in range(at.wide):
            add_into(full.at[at.rows(order[i], side, c, rows)], from_core.at[order[i], side])
        to_y[i] = [
            mail.send(
                full.at[at.rows(order[i], at.y_off(j), c, rows)],
                from_y.at[j - 1, order[i]],
                y_peers[j - 1],
            )
            for j in range(1, at.wide)
        ]

    def y_stage(i):
        receive(to_y[i])
        total = full[at.rows(order[i], y, c, rows), :].astype(jnp.float32)
        for j in range(1, at.wide):
            total = total + from_y[j - 1, order[i]].astype(jnp.float32)
        shares[order[i]] = total.astype(jnp.bfloat16)

    compute(0)
    compute(1)
    reduce_step(norm_line, p_n, norm_swaps, h_n, 0)
    compute(2)
    compute(3)
    reduce_step(norm_line, p_n, norm_swaps, h_n, 1)
    to_core[0] = weight_grads(0)
    to_core[1] = weight_grads(1)
    core_stage(0)
    reduce_step(norm_line, p_n, norm_swaps, h_n, 2)
    to_core[2] = weight_grads(2)
    core_stage(1)
    to_core[3] = weight_grads(3)
    core_stage(2)
    norm_swaps[3].wait_recv()
    for i in range(DEPTH):
        out_swaps.append(mail.send(p_o.at[half_rows(order[i], 1 - x)], h_o.at[i], other))
    core_stage(3)
    o_m[...] = p_n[half_rows(z, x), :].astype(jnp.float32) + h_n[3].astype(jnp.float32)

    def add_norm(_, landed):
        o_m[...] = o_m[...] + landed[...].astype(jnp.float32)

    norm_line.last(add_norm)
    grad_norm = o_m[...]
    values = mid[...]
    inv_rms = lax.rsqrt(jnp.mean(values * values, axis=-1, keepdims=True) + EPSILON)
    grad_values, terms = norm_back(grad_norm, values, inv_rms, gain[...])
    o_t[...] = jnp.sum(terms, axis=0, keepdims=True)
    kept = band(x, tokens)
    total = cot[kept, :].astype(jnp.float32) + grad_values
    o_m[...] = total
    o_h[kept, :] = total.astype(jnp.bfloat16)
    swap_h = mail.send(o_h.at[kept], o_h.at[kept], other)
    for i in range(DEPTH - 1):
        reduce_step(out_line, p_o, out_swaps, h_o, i)
        y_stage(i)
    y_stage(DEPTH - 1)
    out_swaps[3].wait_recv()
    o_l[...] = mid[...] + (
        p_o[half_rows(z, x), :].astype(jnp.float32) + h_o[3].astype(jnp.float32)
    )

    def add_out(_, landed):
        o_l[...] = o_l[...] + landed[...].astype(jnp.float32)

    out_line.last(add_out)
    swap_h.wait_recv()
    mail.finish()


def mlp(dp_size, weights, normed, cots, mid, cot, gain):
    wide = dp_size // (DEPTH * CORES)
    tokens, width = mid.shape
    cols = weights.shape[1]
    rows = width // dp_size
    every = DEPTH * HALVES * tokens
    half, full = jnp.bfloat16, jnp.float32
    copies = 2 * LineReduce.slots + 2 * DEPTH + DEPTH * (2 * wide - 1) + 1
    shapes = [
        jax.ShapeDtypeStruct((tokens, width), full),
        jax.ShapeDtypeStruct((HALVES * tokens, width), half),
        jax.ShapeDtypeStruct((tokens, width), full),
        jax.ShapeDtypeStruct((1, width), full),
        jax.ShapeDtypeStruct((DEPTH, rows, cols), half),
    ]
    return pl.pallas_call(
        functools.partial(mlp_kernel, dp_size),
        out_shape=shapes,
        in_specs=[ANY] * 3 + [VMEM] * 3,
        out_specs=[VMEM] * 5,
        scratch_shapes=[pltpu.VMEM((width, cols), half)]
        + [pltpu.VMEM((every, width), half)] * 2
        + [pltpu.VMEM((every, cols), half)]
        + [pltpu.VMEM((every, width), half)] * 2
        + [pltpu.VMEM((DEPTH, tokens, width), half)] * 2
        + [pltpu.VMEM((LineReduce.slots, tokens, width), half)] * 2
        + [
            pltpu.VMEM((DEPTH, wide, rows, cols), half),
            pltpu.VMEM((wide - 1, DEPTH, rows, cols), half),
            pltpu.SemaphoreType.DMA((11,)),
            pltpu.SemaphoreType.DMA((copies,)),
            pltpu.SemaphoreType.DMA((copies,)),
        ],
        compiler_params=pltpu.CompilerParams(
            collective_id=1, has_side_effects=True, vmem_limit_bytes=63 * 2**20
        ),
    )(weights, normed, cots, mid, cot, gain)


def pair_devices(at):
    def flip(index, bit):
        return index + bit - 2 * bit * lax.rem(lax.div(index, jnp.int32(bit)), jnp.int32(2))

    bits = [1 << i for i in range(at.wide.bit_length() - 1)]
    return (
        [at.device(c=1 - at.c), at.device(x=1 - at.x)]
        + [at.device(y=flip(at.y, bit)) for bit in bits]
        + [at.device(z=flip(at.z, bit)) for bit in (1, 2)]
    )


def backward_kernel(
    dp_size, shares, weights,
    grad_mid, mid_half, out_half, t_m, gain_one, row_in, normed_one, query_raw, key_raw,
    values_half, queries, keys, context, log_total, cosine, sine, bias, q_gain, k_gain,
    o_l, o_i, sums, d_q, d_k, d_v, d_o, d_g, d_u, d_d,
    full, from_core, from_y, from_z, from_spread, context_grad, raw_half, flipped, partial,
    outgoing, incoming, gathering, arriving, own_sems, send_sems, recv_sems,
):
    at = Place(dp_size)
    z, y, c, x = at.z, at.y, at.c, at.x
    other, sibling = at.device(x=1 - x), at.device(c=1 - c)
    y_peers, z_peers = at.y_peers(), at.z_peers()
    order = at.order()
    pairs = pair_devices(at)
    tokens, width = grad_mid.shape
    rows = d_q.shape[0]
    part = shares.shape[2] // 3
    spans, start = [], 0
    for out in (d_q, d_k, d_v, d_o):
        spans.append(pl.ds(start, out.shape[1]))
        start += out.shape[1]
    q_span, k_span, v_span, o_span = spans
    qkv_span = pl.ds(0, start - d_o.shape[1])
    q_cols, kv_width = d_q.shape[1], d_k.shape[1]
    head_dim = q_gain.shape[1]

    def band(index, size):
        return pl.ds(pl.multiple_of(index * size, size), size)

    kept, given = band(x, tokens), band(1 - x, tokens)
    loads = own_copies(
        [(weights.at[:, span], full.at[:, span]) for span in (o_span, qkv_span)], own_sems
    )
    o_l[kept, :] = out_half[...].astype(jnp.bfloat16)
    meet([other, sibling] + y_peers + z_peers + pairs)
    mail = Mail(send_sems, recv_sems)
    to_z = {
        k: mail.send(shares.at[at.z_off(k)], from_spread.at[k - 1], z_peers[k - 1])
        for k in (2, 1, 3)
    }
    swap_l = mail.send(o_l.at[kept], o_l.at[kept], other)
    flipped[...] = normed_one[...].T
    sets = {"o": (o_span, ((d_o, o_span),)), "qkv": (qkv_span, tuple(zip((d_q, d_k, d_v), spans)))}
    lines = {
        name: LineReduce(
            mail,
            at,
            1,
            lambda index, span=span: [full.at[at.rows(index, y, c, rows), span]],
            lambda slot, span=span: [from_z.at[slot, :, span]],
        )
        for name, (span, _) in sets.items()
    }
    to_core, to_y = {}, {}

    def core_sends(name, i):
        span, _ = sets[name]
        to_core[name, i] = [
            mail.send(
                full.at[at.rows(order[i], side, 1 - c, rows), span],
                from_core.at[order[i], side, :, span],
                sibling,
            )
            for side in range(at.wide)
        ]

    def core_stage(name, i):
        span, _ = sets[name]
        receive(to_core[name, i])
        for side in range(at.wide):
            add_into(
                full.at[at.rows(order[i], side, c, rows), span], from_core.at[order[i], side, :, span]
            )
        to_y[name, i] = [
            mail.send(
                full.at[at.rows(order[i], at.y_off(j), c, rows), span],
                from_y.at[j - 1, order[i], :, span],
                y_peers[j - 1],
            )
            for j in range(1, at.wide)
        ]

    def y_stage(name, i):
        span, outs = sets[name]
        receive(to_y[name, i])
        if i < DEPTH - 1:
            terms = [from_y.at[j - 1, order[i], :, span] for j in range(1, at.wide)]
            add_into(full.at[at.rows(order[i], y, c, rows), span], *terms)
            lines[name].pass_on(i)
            return
        for out, own in outs:
            out[...] = full[at.rows(z, y, c, rows), own].astype(jnp.float32)
            add_into(out, *[from_y.at[j - 1, z, :, own] for j in range(1, at.wide)])

    def finish_line(name):
        span, outs = sets[name]

        def use(_, landed):
            for out, own in outs:
                first = own.start - span.start
                add_into(out, landed.at[:, pl.ds(first, own.size)])

        lines[name].last(use)

    gathering[...] = jnp.zeros(gathering.shape, jnp.float32)
    loads[0].wait()

    def write_context(cols, value):
        context_grad[:, cols] = value.astype(jnp.bfloat16)

    matmul_tiles(mid_half, full.at[:, o_span], write_context)

    quarter = width // DEPTH
    for i in range(DEPTH):

        @pl.loop(0, quarter // TILE)
        def _(index, i=i):
            cols = pl.ds(pl.multiple_of(order[i] * quarter + index * TILE, TILE), TILE)
            full[cols, o_span] = dot_tn(mid_half[:, cols], context[...]).astype(jnp.bfloat16)

        core_sends("o", i)

    kv_heads = key_raw.shape[1] // head_dim
    group = query_raw.shape[1] // key_raw.shape[1]
    scale = 1.0 / math.sqrt(head_dim)

    def raw_grad(grad, raw, gain):
        back = grad * cosine[...] - turned(grad) * sine[...]
        inv_rms = lax.rsqrt(jnp.mean(raw * raw, axis=-1, keepdims=True) + EPSILON)
        grad_raw, terms = norm_back(back, raw, inv_rms, gain)
        return grad_raw.astype(jnp.bfloat16), jnp.sum(terms, axis=0, keepdims=True)

    q_sum = jnp.zeros((1, head_dim), jnp.float32)
    k_sum = jnp.zeros((1, head_dim), jnp.float32)
    for j in range(kv_heads):
        kv_cols = pl.ds(j * head_dim, head_dim)
        key_total = jnp.zeros((row_in.shape[0], head_dim), jnp.float32)
        value_total = jnp.zeros((row_in.shape[0], head_dim), jnp.float32)
        for g in range(group):
            head = j * group + g
            cols = pl.ds(head * head_dim, head_dim)
            scores = dot_nt(queries[:, cols], keys[:, kv_cols]) * scale + bias[...]
            probs = jnp.exp(scores - log_total[:, head : head + 1])
            grad_context = context_grad[:, cols]
            grad_probs = dot_nt(grad_context, values_half[:, kv_cols])
            delta = jnp.sum(
                grad_context.astype(jnp.float32) * context[:, cols].astype(jnp.float32),
                axis=-1,
                keepdims=True,
            )
            grad_scores = (probs * (grad_probs - delta) * scale).astype(jnp.bfloat16)
            grad_query, terms = raw_grad(
                matmul(grad_scores, keys[:, kv_cols]), query_raw[:, cols], q_gain[...]
            )
            raw_half[:, cols] = grad_query
            q_sum = q_sum + terms
            key_total = key_total + dot_tn(grad_scores, queries[:, cols])
            value_total = value_total + dot_tn(probs.astype(jnp.bfloat16), grad_context)
        grad_key, terms = raw_grad(key_total, key_raw[:, kv_cols], k_gain[...])
        raw_half[:, pl.ds(q_cols + j * head_dim, head_dim)] = grad_key
        k_sum = k_sum + terms
        raw_half[:, pl.ds(q_cols + kv_width + j * head_dim, head_dim)] = value_total.astype(
            jnp.bfloat16
        )
        if j < DEPTH:
            core_stage("o", j)
    gathering[0, 2:3, :head_dim] = q_sum
    gathering[0, 3:4, :head_dim] = k_sum
    for j in range(kv_heads, DEPTH):
        core_stage("o", j)
    finish_own(loads[1:])

    def project(token_rows, target):
        @pl.loop(0, width // TILE)
        def _(index):
            cols = band(index, TILE)
            total = dot_nt(raw_half[token_rows, :], full[cols, qkv_span])
            partial[token_rows, cols] = total
            if target is not None:
                target[:, cols] = total.astype(target.dtype)

    project(given, outgoing)
    swap = mail.send(outgoing, incoming, other)
    project(kept, None)
    y_stage("o", 0)
    for i in range(DEPTH):

        @pl.loop(0, quarter // TILE)
        def _(index, i=i):
            cols = pl.ds(pl.multiple_of(order[i] * quarter + index * TILE, TILE), TILE)
            full[cols, qkv_span] = matmul(flipped[cols, :], raw_half[...]).astype(jnp.bfloat16)

        core_sends("qkv", i)
        if i > 0:
            core_stage("qkv", i - 1)
    core_stage("qkv", DEPTH - 1)
    y_stage("o", 1)
    swap.wait_recv()
    grad_norm = partial[kept, :] + incoming[...].astype(jnp.float32)
    values = row_in[kept, :].astype(jnp.float32)
    inv_rms = lax.rsqrt(jnp.mean(values * values, axis=-1, keepdims=True) + EPSILON)
    grad_values, _ = norm_back(grad_norm, values, inv_rms, gain_one[...])
    o_i[kept, :] = (grad_mid[...] + grad_values).astype(jnp.bfloat16)
    swap_back = mail.send(o_i.at[kept], o_i.at[kept], other)

    values = row_in[...].astype(jnp.float32)
    inv_rms = lax.rsqrt(jnp.mean(values * values, axis=-1, keepdims=True) + EPSILON)
    gathering[0, 0:1, :] = jnp.sum(partial[...] * values * inv_rms, axis=0, keepdims=True)
    gathering[0, 1:2, :] = t_m[...]
    exchange = mail.send(gathering.at[0], arriving.at[0], pairs[0])

    def pair_step(step):
        total = gathering[step] + arriving[step]
        if step + 1 < len(pairs):
            gathering[step + 1] = total
            return mail.send(gathering.at[step + 1], arriving.at[step + 1], pairs[step + 1])
        sums[...] = total
        return None

    y_stage("o", 2)
    y_stage("o", 3)
    for step in range(len(pairs)):
        exchange.wait_recv()
        exchange = pair_step(step)
        if step < DEPTH:
            y_stage("qkv", step)
        if step == 1:
            finish_line("o")
    for k in range(DEPTH):
        if k > 0:
            to_z[k].wait_recv()
        for i, out in enumerate((d_g, d_u, d_d)):
            span = pl.ds(i * part, part)
            share = shares[z, :, span] if k == 0 else from_spread[k - 1, :, span]
            out[:, band(at.z_off(-k), part)] = share.astype(jnp.float32)
    finish_line("qkv")
    receive([swap_l, swap_back])
    mail.finish()


def backward(dp_size, shares, weights, cols, grad_mid, mid_half, out_half, gain_terms, saved, gains):
    wide = dp_size // (DEPTH * CORES)
    tokens, width = grad_mid.shape
    seq_len = HALVES * tokens
    part = shares.shape[2] // 3
    rows = width // dp_size
    half, full = jnp.bfloat16, jnp.float32
    every = sum(cols)
    pairs = 4 + wide.bit_length() - 1
    copies = 3 + 3 + 2 * LineReduce.slots + 2 * DEPTH * (2 * wide - 1) + pairs
    shapes = [jax.ShapeDtypeStruct((seq_len, width), half)] * 2
    shapes += [jax.ShapeDtypeStruct((8, width), full)]
    shapes += [jax.ShapeDtypeStruct((rows, col), full) for col in cols]
    shapes += [jax.ShapeDtypeStruct((rows, part * DEPTH), full)] * 3
    inputs = [grad_mid, mid_half, out_half, gain_terms, gains[0], *saved, *gains[2:]]
    return pl.pallas_call(
        functools.partial(backward_kernel, dp_size),
        out_shape=shapes,
        in_specs=[VMEM, ANY] + [VMEM] * len(inputs),
        out_specs=[VMEM] * 10,
        scratch_shapes=[
            pltpu.VMEM((width, every), half),
            pltpu.VMEM((DEPTH, wide, rows, every), half),
            pltpu.VMEM((wide - 1, DEPTH, rows, every), half),
            pltpu.VMEM((LineReduce.slots, rows, every), half),
            pltpu.VMEM((DEPTH - 1, rows, 3 * part), half),
            pltpu.VMEM((seq_len, cols[0]), half),
            pltpu.VMEM((seq_len, every - cols[3]), half),
            pltpu.VMEM((width, seq_len), half),
            pltpu.VMEM((seq_len, width), full),
            pltpu.VMEM((tokens, width), half),
            pltpu.VMEM((tokens, width), half),
            pltpu.VMEM((pairs, 8, width), full),
            pltpu.VMEM((pairs, 8, width), full),
            pltpu.SemaphoreType.DMA((2,)),
            pltpu.SemaphoreType.DMA((copies,)),
            pltpu.SemaphoreType.DMA((copies,)),
        ],
        compiler_params=pltpu.CompilerParams(
            collective_id=2, has_side_effects=True, vmem_limit_bytes=63 * 2**20
        ),
    )(shares, weights, *inputs)


def body(
    dp_size,
    layer_in,
    seg_ids,
    w_q,
    w_k,
    w_v,
    w_o,
    w_gate,
    w_up,
    w_down,
    attn_gain,
    mlp_gain,
    q_gain,
    k_gain,
    cotangent,
):
    row_in = layer_in[0]
    row_cot = cotangent[0]
    width = row_in.shape[1]
    gains = [gain[None, :] for gain in (attn_gain, mlp_gain, q_gain, k_gain)]
    outs = forward(
        dp_size, (w_q, w_k, w_v, w_o, w_gate, w_up, w_down), row_cot, row_in, seg_ids[0], gains
    )
    attn_full, ffn_full, cots, normed, mid = outs[:5]
    saved = outs[5:]
    outs = mlp(
        dp_size, ffn_full, normed.reshape(-1, width), cots.reshape(-1, width), mid, row_cot, gains[1]
    )
    grad_mid, mid_half, out_half, gain_terms, shares = outs
    cols = [weight.shape[1] for weight in (w_q, w_k, w_v, w_o)]
    outs = backward(
        dp_size, shares, attn_full, cols, grad_mid, mid_half, out_half, gain_terms,
        [row_in] + list(saved), gains,
    )
    out_row, in_grad, sums = outs[:3]
    gain_outs = []
    for i, size in enumerate((width, width, q_gain.shape[0], k_gain.shape[0])):
        share = size // dp_size
        gain_outs.append(lax.dynamic_slice(sums[i], (lax.axis_index("dp") * share,), (share,)))
    return (out_row[None], in_grad[None], *outs[3:], *gain_outs)


def solution(mesh):
    return jax.shard_map(
        functools.partial(body, mesh.shape["dp"]),
        mesh=mesh,
        in_specs=(
            P("dp", None, None),
            P("dp", None),
            P("dp", "mp"),
            P("dp", "mp"),
            P("dp", "mp"),
            P("dp", "mp"),
            P("dp", "mp"),
            P("dp", "mp"),
            P("dp", "mp"),
            P(),
            P(),
            P(),
            P(),
            P("dp", None, None),
        ),
        out_specs=(
            P("dp", None, None),
            P("dp", None, None),
            P("dp", "mp"),
            P("dp", "mp"),
            P("dp", "mp"),
            P("dp", "mp"),
            P("dp", "mp"),
            P("dp", "mp"),
            P("dp", "mp"),
            P("dp"),
            P("dp"),
            P("dp"),
            P("dp"),
        ),
        check_vma=False,
    )
```

```python
import functools
import math

import jax
import jax.numpy as jnp
from jax import lax
from jax.experimental import pallas as pl
from jax.experimental.pallas import tpu as pltpu
from jax.sharding import PartitionSpec as P

EPSILON = 1e-06
ROPE_BASE = 1000000.0
MASKED = -1e30


def matmul(left_op, right_op):
    return jnp.dot(left_op, right_op, preferred_element_type=jnp.float32)


def rms_norm(values, gain_vec):
    inv_rms = lax.rsqrt(jnp.mean(values * values, axis=-1, keepdims=True) + EPSILON)
    return (values * inv_rms * gain_vec, inv_rms)


def norm_back(grad_norm, values, inv_rms, gain_vec):
    scaled = grad_norm * gain_vec
    cubed = inv_rms * inv_rms * inv_rms
    grad_values = inv_rms * scaled - values * cubed * jnp.mean(
        scaled * values, axis=-1, keepdims=True
    )
    return (grad_values, grad_norm * values * inv_rms)


MESH = pl.DeviceIdType.MESH
ANY = pl.BlockSpec(memory_space=pl.ANY)
VMEM = pl.BlockSpec(memory_space=pltpu.VMEM)
DEPTH = 4
CORES = 2
HALVES = 2
UP, DOWN = 0, 1
TILE = 256


def split(index, size):
    size = jnp.int32(size)
    return lax.div(index, size), lax.rem(index, size)


class Place:
    def __init__(self, dp_size):
        self.wide = dp_size // (DEPTH * CORES)
        self.x = lax.axis_index("mp")
        rest, self.c = split(lax.axis_index("dp"), CORES)
        self.z, self.y = split(rest, self.wide)

    def device(self, z=None, y=None, c=None, x=None):
        z = self.z if z is None else z
        y = self.y if y is None else y
        c = self.c if c is None else c
        x = self.x if x is None else x
        return ((z * self.wide + y) * CORES + c, x)

    def z_off(self, step):
        return lax.rem(self.z + DEPTH + step, jnp.int32(DEPTH))

    def z_flip(self, bits):
        z = self.z
        if bits == DEPTH - 1:
            return DEPTH - 1 - z
        return z + bits - 2 * bits * lax.rem(lax.div(z, jnp.int32(bits)), jnp.int32(2))

    def y_off(self, step):
        return lax.rem(self.y + self.wide + step, jnp.int32(self.wide))

    def rows(self, z, y, c, count):
        return pl.ds(pl.multiple_of(((z * self.wide + y) * CORES + c) * count, count), count)

    def line(self):
        return [self.device(z=self.z_off(1)), self.device(z=self.z_off(-1))]

    def z_peers(self):
        return [self.device(z=self.z_off(k)) for k in range(1, DEPTH)]

    def y_peers(self):
        return [self.device(y=self.y_off(j)) for j in range(1, self.wide)]

    def order(self):
        low = 1 - lax.div(self.z, jnp.int32(2))
        return [3 * low, 1 + low, low * (1 - self.z) + (1 - low) * (5 - self.z), self.z]


def guarded(when, action):
    if when is None:
        action()
    else:
        pl.when(when)(action)


class Mail:
    def __init__(self, send_sems, recv_sems):
        self.send_sems, self.recv_sems = send_sems, recv_sems
        self.count = 0
        self.open = []

    def reserve(self, count):
        first = self.count
        self.count += count
        return first

    def describe(self, source, target, device, slot):
        return pltpu.make_async_remote_copy(
            source,
            target,
            self.send_sems.at[slot],
            self.recv_sems.at[slot],
            device_id=device,
            device_id_type=MESH,
        )

    def make(self, source, target, device, when=None, slot=None):
        copy = self.describe(source, target, device, self.reserve(1) if slot is None else slot)
        self.open.append((copy, when))
        return copy

    def send(self, source, target, device, when=None):
        copy = self.make(source, target, device, when)
        guarded(when, copy.start)
        return copy

    def finish(self):
        for copy, when in self.open:
            guarded(when, copy.wait_send)


def meet(devices):
    barrier = pltpu.get_barrier_semaphore()
    for device in devices:
        pl.semaphore_signal(barrier, inc=1, device_id=device, device_id_type=MESH)
    pl.semaphore_wait(barrier, len(devices))


def receive(copies):
    for copy in copies:
        copy.wait_recv()


def start_all(copies):
    for copy in copies:
        copy.start()


class LineGather:
    def __init__(self, mail, at, own, place, sides, sibling=None, share_own=True):
        self.mail, self.at, self.place = mail, at, place
        self.sides, self.sibling = sides, sibling
        self.neighbours = at.line()
        self.open_end = [at.z < DEPTH - 1, at.z > 0]
        pairs = list(zip(own, place(at.z, 0)))
        self.hops = [
            [mail.send(source, target, self.neighbours[way], self.open_end[way]) for source, target in pairs]
            for way in (UP, DOWN)
        ]
        self.over, self.cores = {}, []
        if share_own:
            self.over["own"] = [
                [mail.send(source, target, side) for source, target in pairs] for side in sides
            ]
        if sibling is not None:
            self.cores.append(
                (None, [mail.send(source, target, sibling) for source, target in pairs])
            )

    def where(self, way, step):
        z = self.at.z
        if way == UP:
            return z >= step + 1, self.at.z_off(-1 - step)
        return z + 1 + step < DEPTH, self.at.z_off(1 + step)

    def step(self, step):
        for way in (UP, DOWN):
            got, index = self.where(way, step)
            refs = self.place(index, 0)
            arrived = self.hops[way]
            onward = []
            if step < DEPTH - 2:
                more = got & self.open_end[way]
                onward = [self.mail.make(ref, ref, self.neighbours[way], more) for ref in refs]
            over = [[self.mail.make(ref, ref, side, got) for ref in refs] for side in self.sides]
            cores = []
            if self.sibling is not None:
                cores = [self.mail.make(ref, ref, self.sibling, got) for ref in refs]

            def pass_on(way=way, arrived=arrived, onward=onward, over=over, cores=cores):
                receive(arrived)
                pl.when(self.open_end[way])(lambda: start_all(onward))
                for copies in over:
                    start_all(copies)
                start_all(cores)

            pl.when(got)(pass_on)
            self.hops[way] = onward
            self.over[way, step] = over
            if cores:
                self.cores.append((got, cores))

    def side_step(self, key):
        got, index = (None, self.at.z) if key == "own" else self.where(*key)
        cores = []
        for j in range(1, len(self.sides) + 1):
            if self.sibling is not None:
                refs = self.place(index, j)
                cores += [self.mail.make(ref, ref, self.sibling, got) for ref in refs]

        def pass_on():
            for copies in self.over[key]:
                receive(copies)
            start_all(cores)

        guarded(got, pass_on)
        if cores:
            self.cores.append((got, cores))

    def side_steps(self, step):
        self.side_step((UP, step))
        self.side_step((DOWN, step))

    def finish(self):
        for got, cores in self.cores:
            guarded(got, lambda cores=cores: receive(cores))


class LineReduce:
    slots = 2 * (DEPTH - 1)

    def __init__(self, mail, at, pieces, part, land):
        self.mail, self.at, self.pieces, self.part, self.land = mail, at, pieces, part, land
        self.base = mail.reserve(self.slots * pieces)

    def copies(self, index, sources, device):
        slots = [self.base + index * self.pieces + i for i in range(self.pieces)]
        return [
            self.mail.describe(source, target, device, slot)
            for source, target, slot in zip(sources, self.land(index), slots)
        ]

    def pass_on(self, turn):
        z = self.at.z
        low = 1 - lax.div(z, jnp.int32(2))
        up = low if turn < 2 else 1 - lax.rem(z, jnp.int32(2))
        target = self.at.order()[turn]
        index = up * (target - 1) + (1 - up) * (DEPTH - 1 + target)
        device = self.at.device(z=z + 2 * up - 1)
        sources = self.part(target)
        copies = self.copies(index, sources, device)
        has_in = up * jnp.where(z > 0, 1, 0) + (1 - up) * jnp.where(z < DEPTH - 1, 1, 0)

        @pl.when(has_in > 0)
        def _():
            receive(copies)
            for source, landed in zip(sources, self.land(index)):
                add_into(source, landed)

        start_all(copies)
        self.mail.open += [(copy, None) for copy in copies]

    def last(self, use):
        z = self.at.z
        sources = self.part(z)
        for when, index, neighbour in (
            (z > 0, lax.max(z - 1, 0), self.at.z_off(-1)),
            (z < DEPTH - 1, lax.min(DEPTH - 1 + z, self.slots - 1), self.at.z_off(1)),
        ):
            copies = self.copies(index, sources, self.at.device(z=neighbour))

            @pl.when(when)
            def _(copies=copies, index=index):
                receive(copies)
                for i, landed in enumerate(self.land(index)):
                    use(i, landed)


def own_copies(pairs, sems, first=0):
    copies = [
        pltpu.make_async_copy(source, target, sems.at[first + i])
        for i, (source, target) in enumerate(pairs)
    ]
    start_all(copies)
    return copies


def finish_own(copies):
    for copy in copies:
        copy.wait()


def add_into(target, *others):
    total = target[...].astype(jnp.float32)
    for other in others:
        total = total + other[...].astype(jnp.float32)
    target[...] = total.astype(target.dtype)


def dot_nt(left_op, right_op):
    return lax.dot_general(
        left_op, right_op, (((1,), (1,)), ((), ())), preferred_element_type=jnp.float32
    )


def dot_tn(left_op, right_op):
    return lax.dot_general(
        left_op, right_op, (((0,), (0,)), ((), ())), preferred_element_type=jnp.float32
    )


def turned(values):
    return pltpu.roll(values, values.shape[-1] // 2, axis=values.ndim - 1)


def document_tables(seg_col, seg_row, head_dim):
    seq_len = seg_col.shape[0]
    rows = lax.broadcasted_iota(jnp.int32, (seq_len, seq_len), 0)
    cols = lax.broadcasted_iota(jnp.int32, (seq_len, seq_len), 1)
    same = seg_col == seg_row
    bias = jnp.where(same & (cols <= rows), 0.0, MASKED)
    before = jnp.where(same & (cols < rows), 1.0, 0.0)
    position = jnp.sum(before, axis=-1, keepdims=True)
    lane = lax.broadcasted_iota(jnp.int32, (1, head_dim), 1)
    half_dim = head_dim // 2
    slot = jnp.where(lane < half_dim, lane, lane - half_dim).astype(jnp.float32)
    frequency = jnp.exp(slot * (-2.0 * math.log(ROPE_BASE) / head_dim))
    angles = position * frequency
    sine = jnp.sin(angles)
    return bias, jnp.cos(angles), jnp.where(lane < half_dim, -sine, sine)


def matmul_tiles(left, right, write, tile=256):
    @pl.loop(0, right.shape[1] // tile)
    def _(index):
        columns = pl.ds(pl.multiple_of(index * tile, tile), tile)
        write(columns, matmul(left[...], right[:, columns]))


def forward_kernel(
    dp_size, w_q, w_k, w_v, w_o, w_g, w_u, w_d, cot, row_in, seg_col, seg_row,
    gain_one, gain_two, q_gain, k_gain,
    o_attn, o_ffn, o_c, o_n,
    mid, normed_one, query_raw, key_raw, values_half, queries, keys, context, log_total,
    cosine, sine, bias,
    full, own_part, outgoing, incoming, normed, own_sems, send_sems, recv_sems,
):
    at = Place(dp_size)
    z, y, c, x = at.z, at.y, at.c, at.x
    sibling, other = at.device(c=1 - c), at.device(x=1 - x)
    z_peers, y_peers = at.z_peers(), at.y_peers()
    meet([sibling, other] + z_peers + y_peers)

    mail = Mail(send_sems, recv_sems)
    rows = w_q.shape[0]
    head_dim = q_gain.shape[1]
    part = w_g.shape[1] // DEPTH
    tokens = mid.shape[0]
    here = at.rows(z, y, c, rows)
    spans, start = [], 0
    for weight in (w_q, w_k, w_v, w_o):
        spans.append(pl.ds(start, weight.shape[1]))
        start += weight.shape[1]
    q_span, k_span, v_span, o_span = spans
    ffn = [(weight, pl.ds(i * part, part)) for i, weight in enumerate((w_g, w_u, w_d))]

    def columns(index):
        return pl.ds(pl.multiple_of(index * part, part), part)

    def half_rows(index):
        return pl.ds(pl.multiple_of(index * tokens, tokens), tokens)

    mine = own_copies(
        [(weight, full.at[here, span]) for weight, span in zip((w_q, w_k, w_v, w_o), spans)],
        own_sems,
    )
    own_ffn = own_copies(
        [(weight.at[:, columns(z)], own_part.at[:, span]) for weight, span in ffn], own_sems, 4
    )
    own_cot = own_copies([(cot.at[half_rows(i)], o_c.at[z, i]) for i in range(2)], own_sems, 7)
    finish_own(mine)
    attn = LineGather(
        mail,
        at,
        (full.at[here],),
        lambda zb, j: [full.at[at.rows(zb, at.y_off(-j), c, rows)]],
        y_peers,
        sibling,
    )

    residual = row_in[...].astype(jnp.float32)
    normed_full, _ = rms_norm(residual, gain_one[...])
    normed_one[...] = normed_full.astype(jnp.bfloat16)
    bias_values, cosine[...], sine[...] = document_tables(seg_col[...], seg_row[...], head_dim)
    bias[...] = bias_values

    spread, crossing, to_sibling = {}, {}, []

    def start_spread():
        for k in range(1, DEPTH):
            target = at.z_flip(k)
            spread[k] = [
                mail.send(
                    weight.at[:, columns(target)], o_ffn.at[here, span], at.device(z=target)
                )
                for weight, span in ffn
            ]
        block = o_ffn.at[here]
        for j in range(1, at.wide):
            crossing[0, j] = mail.send(own_part, block, y_peers[j - 1])
        to_sibling.append(mail.send(own_part, block, sibling))

    def forward_spread(k):
        receive(spread[k])
        block = o_ffn.at[at.rows(at.z_flip(k), y, c, rows)]
        for j in range(1, at.wide):
            crossing[k, j] = mail.send(block, block, y_peers[j - 1])
        to_sibling.append(mail.send(block, block, sibling))

    def forward_crossing(k):
        for j in range(1, at.wide):
            crossing[k, j].wait_recv()
            block = o_ffn.at[at.rows(at.z_flip(k), at.y_off(-j), c, rows)]
            to_sibling.append(mail.send(block, block, sibling))

    def half_place(out):
        return lambda zb, j: [out.at[zb, x if j == 0 else 1 - x]]

    attn.step(0)
    finish_own(own_ffn)
    own_copy = own_copies([(own_part, o_ffn.at[here])], own_sems, 4)
    attn.side_step("own")
    attn.step(1)
    cots = LineGather(
        mail, at, (cot.at[half_rows(x)],), half_place(o_c), [other], share_own=False
    )
    attn.side_steps(0)
    attn.step(2)
    cots.step(0)
    attn.side_steps(1)
    cots.step(1)
    start_spread()
    attn.side_steps(2)
    attn.finish()
    saved = own_copies([(full, o_attn)], own_sems)

    def write_query(cols, block):
        query_raw[:, cols] = block

    def write_key(cols, block):
        key_raw[:, cols] = block

    def write_value(cols, block):
        values_half[:, cols] = block.astype(jnp.bfloat16)

    matmul_tiles(normed_one, full.at[:, q_span], write_query)
    matmul_tiles(normed_one, full.at[:, k_span], write_key)
    matmul_tiles(normed_one, full.at[:, v_span], write_value)

    def rotated(raw, gain):
        unit, _ = rms_norm(raw, gain)
        return (unit * cosine[...] + turned(unit) * sine[...]).astype(jnp.bfloat16)

    kv_heads = key_raw.shape[1] // head_dim
    group = query_raw.shape[1] // key_raw.shape[1]
    for j in range(kv_heads):
        kv_cols = pl.ds(j * head_dim, head_dim)
        keys[:, kv_cols] = rotated(key_raw[:, kv_cols], k_gain[...])
        for g in range(group):
            head = j * group + g
            cols = pl.ds(head * head_dim, head_dim)
            queries[:, cols] = rotated(query_raw[:, cols], q_gain[...])
            scores = dot_nt(queries[:, cols], keys[:, kv_cols]) * (1.0 / math.sqrt(head_dim))
            scores = scores + bias[...]
            row_max = jnp.max(scores, axis=-1, keepdims=True)
            weights = jnp.exp(scores - row_max)
            total = jnp.sum(weights, axis=-1, keepdims=True)
            log_total[:, head : head + 1] = row_max + jnp.log(total)
            probs = (weights * (1.0 / total)).astype(jnp.bfloat16)
            context[:, cols] = matmul(probs, values_half[:, kv_cols]).astype(jnp.bfloat16)
        if j == kv_heads // 2 - 1:
            cots.step(2)

    given, kept = half_rows(1 - x), half_rows(x)
    width = row_in.shape[1]

    def project(token_rows, target):
        @pl.loop(0, width // TILE)
        def _(index):
            cols = pl.ds(pl.multiple_of(index * TILE, TILE), TILE)
            block = dot_nt(context[token_rows, :], full[cols, o_span])
            target[:, cols] = block.astype(target.dtype)

    project(given, outgoing)
    swap = mail.send(outgoing, incoming, other)
    project(kept, mid)
    swap.wait_recv()
    total = row_in[kept, :].astype(jnp.float32) + (mid[...] + incoming[...].astype(jnp.float32))
    mid[...] = total
    normed_mid, _ = rms_norm(total, gain_two[...])
    normed[...] = normed_mid.astype(jnp.bfloat16)
    last = own_copies([(normed, o_n.at[z, x])], own_sems, 9)
    strip = tokens // 2
    norms = []
    for i in range(2):
        rows_of = pl.ds(i * strip, strip)
        norms.append(
            LineGather(
                mail,
                at,
                (normed.at[rows_of],),
                lambda zb, j, rows_of=rows_of: [o_n.at[zb, x if j == 0 else 1 - x, rows_of]],
                [other],
            )
        )
    forward_spread(1)
    forward_crossing(0)
    for step in range(DEPTH - 1):
        if step < DEPTH - 2:
            forward_spread(step + 2)
        for line in norms:
            line.step(step)
        forward_crossing(step + 1)
    for step in range(DEPTH - 1):
        cots.side_steps(step)
    for line in norms:
        line.side_step("own")
        for step in range(DEPTH - 1):
            line.side_steps(step)
    receive(to_sibling)
    mail.finish()
    finish_own(saved + last + own_cot + own_copy)


def forward(dp_size, weights, cot, row_in, seg_row, gains):
    w_q, w_k, w_v, w_o, w_g, w_u, w_d = weights
    wide = dp_size // (DEPTH * CORES)
    seq_len, width = row_in.shape
    head_dim = gains[2].shape[1]
    tokens = seq_len // HALVES
    part = w_g.shape[1] // DEPTH
    half, whole = jnp.bfloat16, jnp.float32
    attn_cols = [w.shape[1] for w in (w_q, w_k, w_v, w_o)]
    shapes = [jax.ShapeDtypeStruct((width, cols), half) for cols in (sum(attn_cols), 3 * part)]
    shapes += [jax.ShapeDtypeStruct((DEPTH, HALVES, tokens, width), half)] * 2
    q_cols, kv_cols = attn_cols[0], attn_cols[1]
    for cols, kind in (
        (width, half), (q_cols, whole), (kv_cols, whole), (kv_cols, half), (q_cols, half),
        (kv_cols, half), (q_cols, half), (head_dim, whole), (head_dim, whole), (head_dim, whole),
        (seq_len, whole),
    ):
        shapes.append(jax.ShapeDtypeStruct((seq_len, cols), kind))
    shapes.insert(4, jax.ShapeDtypeStruct((tokens, width), whole))
    hops = 2 * (DEPTH - 1)
    spots = 1 + hops
    copies = (hops + spots * (2 * wide - 1)) + 3 * (2 * hops + 1) + 1
    copies += 9 + DEPTH * (2 * wide - 1)
    return pl.pallas_call(
        functools.partial(forward_kernel, dp_size),
        out_shape=shapes,
        in_specs=[ANY] * 7 + [VMEM] * 8,
        out_specs=[ANY] * 4 + [VMEM] * 12,
        scratch_shapes=[pltpu.VMEM((width, sum(attn_cols)), half)]
        + [pltpu.VMEM((w_g.shape[0], 3 * part), half)]
        + [pltpu.VMEM((tokens, width), half)] * 3
        + [
            pltpu.SemaphoreType.DMA((10,)),
            pltpu.SemaphoreType.DMA((copies,)),
            pltpu.SemaphoreType.DMA((copies,)),
        ],
        compiler_params=pltpu.CompilerParams(
            collective_id=0, has_side_effects=True, vmem_limit_bytes=56 * 2**20
        ),
    )(w_q, w_k, w_v, w_o, w_g, w_u, w_d, cot, row_in, seg_row[:, None], seg_row[None, :], *gains)


def mlp_kernel(
    dp_size, weights, n_all, c_all, mid, cot, gain,
    o_m, o_h, o_l, o_t, shares,
    full, x_n, x_c, hidden, p_n, p_o, h_n, h_o, h_l, l_n, l_o, l_z, outgoing, from_core, from_y,
    own_sems, send_sems, recv_sems,
):
    at = Place(dp_size)
    z, y, c, x = at.z, at.y, at.c, at.x
    other, sibling = at.device(x=1 - x), at.device(c=1 - c)
    y_peers = at.y_peers()
    order = at.order()
    tokens = mid.shape[0]
    block_rows = HALVES * tokens
    rows = from_core.shape[2]
    part = full.shape[1] // 3
    gate_up, down = pl.ds(0, 2 * part), pl.ds(2 * part, part)
    width = mid.shape[1]

    def band(index, size):
        return pl.ds(pl.multiple_of(index * size, size), size)

    loads = {}
    for i, name in enumerate("gud"):
        span = pl.ds(i * part, part)
        loads[name] = pltpu.make_async_copy(weights.at[:, span], full.at[:, span], own_sems.at[i])
    for i, index in enumerate(order):
        block = band(index, block_rows)
        loads["n", i] = pltpu.make_async_copy(n_all.at[block], x_n.at[block], own_sems.at[3 + i])
        loads["c", i] = pltpu.make_async_copy(c_all.at[block], x_c.at[block], own_sems.at[7 + i])
    for key in ("g", "u", ("n", 0), "d", ("c", 0)):
        loads[key].start()
    for i in range(1, DEPTH):
        loads["n", i].start()
        loads["c", i].start()
    meet([other, sibling] + at.line() + y_peers)
    mail = Mail(send_sems, recv_sems)

    def half_rows(index, side):
        return band(index * HALVES + side, tokens)

    first, second = pl.ds(0, width // 2), pl.ds(width // 2, width // 2)
    norm_line = LineReduce(
        mail, at, 1, lambda index: [p_n.at[half_rows(index, x)]], lambda slot: [l_n.at[slot]]
    )
    out_line = LineReduce(
        mail, at, 1, lambda index: [p_o.at[half_rows(index, x), first]], lambda slot: [l_o.at[slot]]
    )
    late_line = LineReduce(
        mail, at, 1, lambda index: [p_o.at[band(index, block_rows), second]], lambda slot: [l_z.at[slot]]
    )
    norm_swaps, out_swaps = [], []

    def compute(i):
        block = band(order[i], block_rows)
        if i == 0:
            for name in ("g", "u", "d"):
                loads[name].wait()
        loads["n", i].wait()
        loads["c", i].wait()

        @pl.loop(0, part // TILE)
        def _(index):
            g_cols, u_cols, d_cols = [
                pl.ds(pl.multiple_of(i * part + index * TILE, TILE), TILE) for i in range(3)
            ]
            gate = matmul(x_n[block, :], full[:, g_cols])
            up = matmul(x_n[block, :], full[:, u_cols])
            grad_act = matmul(x_c[block, :], full[:, d_cols])
            sigmoid_gate = 1.0 / (1.0 + jnp.exp(-gate))
            silu_val = gate * sigmoid_gate
            hidden[block, g_cols] = (
                grad_act * up * sigmoid_gate * (1.0 + gate * (1.0 - sigmoid_gate))
            ).astype(jnp.bfloat16)
            hidden[block, u_cols] = (grad_act * silu_val).astype(jnp.bfloat16)
            hidden[block, d_cols] = (silu_val * up).astype(jnp.bfloat16)

        @pl.loop(0, width // TILE)
        def _(index):
            cols = band(index, TILE)
            p_n[block, cols] = dot_nt(hidden[block, gate_up], full[cols, gate_up]).astype(jnp.bfloat16)

        norm_swaps.append(mail.send(p_n.at[half_rows(order[i], 1 - x)], h_n.at[i], other))

    def compute_out(i):
        block = band(order[i], block_rows)

        @pl.loop(0, width // TILE)
        def _(index):
            cols = band(index, TILE)
            p_o[block, cols] = dot_nt(hidden[block, down], full[cols, down]).astype(jnp.bfloat16)

    def norm_step(i):
        norm_swaps[i].wait_recv()
        add_into(p_n.at[half_rows(order[i], x)], h_n.at[i])
        norm_line.pass_on(i)

    def out_step(i):
        out_swaps[i].wait_recv()
        add_into(p_o.at[half_rows(order[i], x), first], h_o.at[i])
        out_line.pass_on(i)

    def weight_grads(span, i):
        left = x_n if span is gate_up else x_c

        @pl.loop(0, width // DEPTH // TILE)
        def _(index):
            cols = pl.ds(pl.multiple_of(order[i] * (width // DEPTH) + index * TILE, TILE), TILE)
            full[cols, span] = matmul(left[:, cols].T, hidden[:, span]).astype(jnp.bfloat16)

        to_core[span.start, i] = [
            mail.send(
                full.at[at.rows(order[i], side, 1 - c, rows), span],
                from_core.at[order[i], side, :, span],
                sibling,
            )
            for side in range(at.wide)
        ]

    to_core, to_y = {}, {}

    def core_stage(span, i):
        receive(to_core[span.start, i])
        for side in range(at.wide):
            add_into(
                full.at[at.rows(order[i], side, c, rows), span], from_core.at[order[i], side, :, span]
            )
        to_y[span.start, i] = [
            mail.send(
                full.at[at.rows(order[i], at.y_off(j), c, rows), span],
                from_y.at[j - 1, order[i], :, span],
                y_peers[j - 1],
            )
            for j in range(1, at.wide)
        ]

    def y_stage(span, i):
        receive(to_y[span.start, i])
        total = full[at.rows(order[i], y, c, rows), span].astype(jnp.float32)
        for j in range(1, at.wide):
            total = total + from_y[j - 1, order[i], :, span].astype(jnp.float32)
        shares[order[i], :, span] = total.astype(jnp.bfloat16)

    compute(0)
    compute(1)
    compute(2)
    norm_step(0)
    compute(3)
    weight_grads(gate_up, 0)
    norm_step(1)
    weight_grads(gate_up, 1)
    core_stage(gate_up, 0)
    weight_grads(gate_up, 2)
    core_stage(gate_up, 1)
    norm_step(2)
    weight_grads(gate_up, 3)
    core_stage(gate_up, 2)
    compute_out(0)
    late_line.pass_on(0)
    core_stage(gate_up, 3)
    compute_out(1)
    late_line.pass_on(1)
    compute_out(2)
    compute_out(3)
    norm_swaps[3].wait_recv()
    for i in range(DEPTH):
        out_swaps.append(
            mail.send(p_o.at[half_rows(order[i], 1 - x), first], h_o.at[i], other)
        )
    weight_grads(down, 0)
    weight_grads(down, 1)
    core_stage(down, 0)
    o_m[...] = p_n[half_rows(z, x), :].astype(jnp.float32) + h_n[3].astype(jnp.float32)

    def add_norm(_, landed):
        o_m[...] = o_m[...] + landed[...].astype(jnp.float32)

    norm_line.last(add_norm)
    grad_norm = o_m[...]
    values = mid[...]
    inv_rms = lax.rsqrt(jnp.mean(values * values, axis=-1, keepdims=True) + EPSILON)
    grad_values, terms = norm_back(grad_norm, values, inv_rms, gain[...])
    o_t[...] = jnp.sum(terms, axis=0, keepdims=True)
    kept = band(x, tokens)
    total = cot[kept, :].astype(jnp.float32) + grad_values
    o_m[...] = total
    o_h[kept, :] = total.astype(jnp.bfloat16)
    swap_h = mail.send(o_h.at[kept], o_h.at[kept], other)
    late_line.pass_on(2)
    weight_grads(down, 2)
    core_stage(down, 1)
    weight_grads(down, 3)
    core_stage(down, 2)
    core_stage(down, 3)
    for i in range(DEPTH - 1):
        out_step(i)
        y_stage(gate_up, i)

    def add_late(_, landed):
        for i in range(HALVES):
            rows_of = band(z * HALVES + i, tokens)
            add_into(p_o.at[rows_of, second], landed.at[pl.ds(i * tokens, tokens)])

    late_line.last(add_late)
    outgoing[...] = p_o[half_rows(z, 1 - x), second]
    swap_l = mail.send(outgoing, h_l, other)
    y_stage(gate_up, DEPTH - 1)
    for i in range(DEPTH):
        y_stage(down, i)
    out_swaps[3].wait_recv()
    o_l[:, first] = mid[:, first] + (
        p_o[half_rows(z, x), first].astype(jnp.float32) + h_o[3].astype(jnp.float32)
    )

    def add_out(_, landed):
        o_l[:, first] = o_l[:, first] + landed[...].astype(jnp.float32)

    out_line.last(add_out)
    swap_l.wait_recv()
    o_l[:, second] = mid[:, second] + (
        p_o[half_rows(z, x), second].astype(jnp.float32) + h_l[...].astype(jnp.float32)
    )
    swap_h.wait_recv()
    mail.finish()


def mlp(dp_size, weights, normed, cots, mid, cot, gain):
    wide = dp_size // (DEPTH * CORES)
    tokens, width = mid.shape
    cols = weights.shape[1]
    rows = width // dp_size
    every = DEPTH * HALVES * tokens
    half, full = jnp.bfloat16, jnp.float32
    copies = 3 * LineReduce.slots + 2 * DEPTH + 2 * DEPTH * (2 * wide - 1) + 2
    shapes = [
        jax.ShapeDtypeStruct((tokens, width), full),
        jax.ShapeDtypeStruct((HALVES * tokens, width), half),
        jax.ShapeDtypeStruct((tokens, width), full),
        jax.ShapeDtypeStruct((1, width), full),
        jax.ShapeDtypeStruct((DEPTH, rows, cols), half),
    ]
    return pl.pallas_call(
        functools.partial(mlp_kernel, dp_size),
        out_shape=shapes,
        in_specs=[ANY] * 3 + [VMEM] * 3,
        out_specs=[VMEM] * 5,
        scratch_shapes=[pltpu.VMEM((width, cols), half)]
        + [pltpu.VMEM((every, width), half)] * 2
        + [pltpu.VMEM((every, cols), half)]
        + [pltpu.VMEM((every, width), half)] * 2
        + [
            pltpu.VMEM((DEPTH, tokens, width), half),
            pltpu.VMEM((DEPTH, tokens, width // 2), half),
            pltpu.VMEM((tokens, width // 2), half),
            pltpu.VMEM((LineReduce.slots, tokens, width), half),
            pltpu.VMEM((LineReduce.slots, tokens, width // 2), half),
            pltpu.VMEM((LineReduce.slots, HALVES * tokens, width // 2), half),
            pltpu.VMEM((tokens, width // 2), half),
        ]
        + [
            pltpu.VMEM((DEPTH, wide, rows, cols), half),
            pltpu.VMEM((wide - 1, DEPTH, rows, cols), half),
            pltpu.SemaphoreType.DMA((11,)),
            pltpu.SemaphoreType.DMA((copies,)),
            pltpu.SemaphoreType.DMA((copies,)),
        ],
        compiler_params=pltpu.CompilerParams(
            collective_id=1, has_side_effects=True, vmem_limit_bytes=63 * 2**20
        ),
    )(weights, normed, cots, mid, cot, gain)


def pair_devices(at):
    def flip(index, bit):
        return index + bit - 2 * bit * lax.rem(lax.div(index, jnp.int32(bit)), jnp.int32(2))

    bits = [1 << i for i in range(at.wide.bit_length() - 1)]
    return (
        [at.device(c=1 - at.c), at.device(x=1 - at.x)]
        + [at.device(y=flip(at.y, bit)) for bit in bits]
        + [at.device(z=flip(at.z, bit)) for bit in (1, 2)]
    )


def backward_kernel(
    dp_size, shares, weights,
    grad_mid, mid_half, out_half, t_m, gain_one, row_in, normed_one, query_raw, key_raw,
    values_half, queries, keys, context, log_total, cosine, sine, bias, q_gain, k_gain,
    o_l, o_i, sums, d_q, d_k, d_v, d_o, d_g, d_u, d_d,
    full, from_core, from_y, from_z, from_spread, context_grad, raw_half, flipped, partial,
    outgoing, incoming, gathering, arriving, own_sems, send_sems, recv_sems,
):
    at = Place(dp_size)
    z, y, c, x = at.z, at.y, at.c, at.x
    other, sibling = at.device(x=1 - x), at.device(c=1 - c)
    y_peers, z_peers = at.y_peers(), at.z_peers()
    order = at.order()
    pairs = pair_devices(at)
    tokens, width = grad_mid.shape
    rows = d_q.shape[0]
    part = shares.shape[2] // 3
    spans, start = [], 0
    for out in (d_q, d_k, d_v, d_o):
        spans.append(pl.ds(start, out.shape[1]))
        start += out.shape[1]
    q_span, k_span, v_span, o_span = spans
    qkv_span = pl.ds(0, start - d_o.shape[1])
    q_cols, kv_width = d_q.shape[1], d_k.shape[1]
    head_dim = q_gain.shape[1]

    def band(index, size):
        return pl.ds(pl.multiple_of(index * size, size), size)

    kept, given = band(x, tokens), band(1 - x, tokens)
    loads = own_copies(
        [(weights.at[:, span], full.at[:, span]) for span in (o_span, qkv_span)], own_sems
    )
    o_l[kept, :] = out_half[...].astype(jnp.bfloat16)
    meet([other, sibling] + y_peers + z_peers + pairs)
    mail = Mail(send_sems, recv_sems)
    to_z = {
        k: mail.send(shares.at[at.z_off(k)], from_spread.at[k - 1], z_peers[k - 1])
        for k in (2, 1, 3)
    }
    swap_l = mail.send(o_l.at[kept], o_l.at[kept], other)
    flipped[...] = normed_one[...].T
    sets = {"o": (o_span, ((d_o, o_span),)), "qkv": (qkv_span, tuple(zip((d_q, d_k, d_v), spans)))}
    lines = {
        name: LineReduce(
            mail,
            at,
            1,
            lambda index, span=span: [full.at[at.rows(index, y, c, rows), span]],
            lambda slot, span=span: [from_z.at[slot, :, span]],
        )
        for name, (span, _) in sets.items()
    }
    to_core, to_y = {}, {}

    def core_sends(name, i):
        span, _ = sets[name]
        to_core[name, i] = [
            mail.send(
                full.at[at.rows(order[i], side, 1 - c, rows), span],
                from_core.at[order[i], side, :, span],
                sibling,
            )
            for side in range(at.wide)
        ]

    def core_stage(name, i):
        span, _ = sets[name]
        receive(to_core[name, i])
        for side in range(at.wide):
            add_into(
                full.at[at.rows(order[i], side, c, rows), span], from_core.at[order[i], side, :, span]
            )
        to_y[name, i] = [
            mail.send(
                full.at[at.rows(order[i], at.y_off(j), c, rows), span],
                from_y.at[j - 1, order[i], :, span],
                y_peers[j - 1],
            )
            for j in range(1, at.wide)
        ]

    def y_stage(name, i):
        span, outs = sets[name]
        receive(to_y[name, i])
        if i < DEPTH - 1:
            terms = [from_y.at[j - 1, order[i], :, span] for j in range(1, at.wide)]
            add_into(full.at[at.rows(order[i], y, c, rows), span], *terms)
            lines[name].pass_on(i)
            return
        for out, own in outs:
            out[...] = full[at.rows(z, y, c, rows), own].astype(jnp.float32)
            add_into(out, *[from_y.at[j - 1, z, :, own] for j in range(1, at.wide)])

    def finish_line(name):
        span, outs = sets[name]

        def use(_, landed):
            for out, own in outs:
                first = own.start - span.start
                add_into(out, landed.at[:, pl.ds(first, own.size)])

        lines[name].last(use)

    gathering[...] = jnp.zeros(gathering.shape, jnp.float32)
    loads[0].wait()

    def write_context(cols, value):
        context_grad[:, cols] = value.astype(jnp.bfloat16)

    matmul_tiles(mid_half, full.at[:, o_span], write_context)

    quarter = width // DEPTH
    for i in range(DEPTH):

        @pl.loop(0, quarter // TILE)
        def _(index, i=i):
            cols = pl.ds(pl.multiple_of(order[i] * quarter + index * TILE, TILE), TILE)
            full[cols, o_span] = dot_tn(mid_half[:, cols], context[...]).astype(jnp.bfloat16)

        core_sends("o", i)

    kv_heads = key_raw.shape[1] // head_dim
    group = query_raw.shape[1] // key_raw.shape[1]
    scale = 1.0 / math.sqrt(head_dim)

    def raw_grad(grad, raw, gain):
        back = grad * cosine[...] - turned(grad) * sine[...]
        inv_rms = lax.rsqrt(jnp.mean(raw * raw, axis=-1, keepdims=True) + EPSILON)
        grad_raw, terms = norm_back(back, raw, inv_rms, gain)
        return grad_raw.astype(jnp.bfloat16), jnp.sum(terms, axis=0, keepdims=True)

    q_sum = jnp.zeros((1, head_dim), jnp.float32)
    k_sum = jnp.zeros((1, head_dim), jnp.float32)
    for j in range(kv_heads):
        kv_cols = pl.ds(j * head_dim, head_dim)
        key_total = jnp.zeros((row_in.shape[0], head_dim), jnp.float32)
        value_total = jnp.zeros((row_in.shape[0], head_dim), jnp.float32)
        for g in range(group):
            head = j * group + g
            cols = pl.ds(head * head_dim, head_dim)
            scores = dot_nt(queries[:, cols], keys[:, kv_cols]) * scale + bias[...]
            probs = jnp.exp(scores - log_total[:, head : head + 1])
            grad_context = context_grad[:, cols]
            grad_probs = dot_nt(grad_context, values_half[:, kv_cols])
            delta = jnp.sum(
                grad_context.astype(jnp.float32) * context[:, cols].astype(jnp.float32),
                axis=-1,
                keepdims=True,
            )
            grad_scores = (probs * (grad_probs - delta) * scale).astype(jnp.bfloat16)
            grad_query, terms = raw_grad(
                matmul(grad_scores, keys[:, kv_cols]), query_raw[:, cols], q_gain[...]
            )
            raw_half[:, cols] = grad_query
            q_sum = q_sum + terms
            key_total = key_total + dot_tn(grad_scores, queries[:, cols])
            value_total = value_total + dot_tn(probs.astype(jnp.bfloat16), grad_context)
        grad_key, terms = raw_grad(key_total, key_raw[:, kv_cols], k_gain[...])
        raw_half[:, pl.ds(q_cols + j * head_dim, head_dim)] = grad_key
        k_sum = k_sum + terms
        raw_half[:, pl.ds(q_cols + kv_width + j * head_dim, head_dim)] = value_total.astype(
            jnp.bfloat16
        )
        if j < DEPTH:
            core_stage("o", j)
    gathering[0, 2:3, :head_dim] = q_sum
    gathering[0, 3:4, :head_dim] = k_sum
    for j in range(kv_heads, DEPTH):
        core_stage("o", j)
    finish_own(loads[1:])

    def project(token_rows, target):
        @pl.loop(0, width // TILE)
        def _(index):
            cols = band(index, TILE)
            total = dot_nt(raw_half[token_rows, :], full[cols, qkv_span])
            partial[token_rows, cols] = total
            if target is not None:
                target[:, cols] = total.astype(target.dtype)

    project(given, outgoing)
    swap = mail.send(outgoing, incoming, other)
    project(kept, None)

    values = row_in[...].astype(jnp.float32)
    inv_rms = lax.rsqrt(jnp.mean(values * values, axis=-1, keepdims=True) + EPSILON)
    gathering[0, 0:1, :] = jnp.sum(partial[...] * values * inv_rms, axis=0, keepdims=True)
    gathering[0, 1:2, :] = t_m[...]
    exchange = [mail.send(gathering.at[0], arriving.at[0], pairs[0])]

    def pair_step():
        step = len(exchange) - 1
        if step == len(pairs):
            return
        exchange[step].wait_recv()
        total = gathering[step] + arriving[step]
        if step + 1 < len(pairs):
            gathering[step + 1] = total
            exchange.append(
                mail.send(gathering.at[step + 1], arriving.at[step + 1], pairs[step + 1])
            )
        else:
            sums[...] = total
            exchange.append(None)

    y_stage("o", 0)
    for i in range(DEPTH):

        @pl.loop(0, quarter // TILE)
        def _(index, i=i):
            cols = pl.ds(pl.multiple_of(order[i] * quarter + index * TILE, TILE), TILE)
            full[cols, qkv_span] = matmul(flipped[cols, :], raw_half[...]).astype(jnp.bfloat16)

        core_sends("qkv", i)
        if i == 0:
            pair_step()
        else:
            core_stage("qkv", i - 1)
    core_stage("qkv", DEPTH - 1)
    y_stage("o", 1)
    pair_step()
    swap.wait_recv()
    grad_norm = partial[kept, :] + incoming[...].astype(jnp.float32)
    values = row_in[kept, :].astype(jnp.float32)
    inv_rms = lax.rsqrt(jnp.mean(values * values, axis=-1, keepdims=True) + EPSILON)
    grad_values, _ = norm_back(grad_norm, values, inv_rms, gain_one[...])
    o_i[kept, :] = (grad_mid[...] + grad_values).astype(jnp.bfloat16)
    swap_back = mail.send(o_i.at[kept], o_i.at[kept], other)

    y_stage("o", 2)
    y_stage("o", 3)
    for i in range(DEPTH - 1):
        y_stage("qkv", i)
        if i > 0:
            pair_step()
    finish_line("o")
    y_stage("qkv", DEPTH - 1)
    while exchange[-1] is not None:
        pair_step()
    for k in range(DEPTH):
        if k > 0:
            to_z[k].wait_recv()
        for i, out in enumerate((d_g, d_u, d_d)):
            span = pl.ds(i * part, part)
            share = shares[z, :, span] if k == 0 else from_spread[k - 1, :, span]
            out[:, band(at.z_off(-k), part)] = share.astype(jnp.float32)
    finish_line("qkv")
    receive([swap_l, swap_back])
    mail.finish()


def backward(dp_size, shares, weights, cols, grad_mid, mid_half, out_half, gain_terms, saved, gains):
    wide = dp_size // (DEPTH * CORES)
    tokens, width = grad_mid.shape
    seq_len = HALVES * tokens
    part = shares.shape[2] // 3
    rows = width // dp_size
    half, full = jnp.bfloat16, jnp.float32
    every = sum(cols)
    pairs = 4 + wide.bit_length() - 1
    copies = 3 + 3 + 2 * LineReduce.slots + 2 * DEPTH * (2 * wide - 1) + pairs
    shapes = [jax.ShapeDtypeStruct((seq_len, width), half)] * 2
    shapes += [jax.ShapeDtypeStruct((8, width), full)]
    shapes += [jax.ShapeDtypeStruct((rows, col), full) for col in cols]
    shapes += [jax.ShapeDtypeStruct((rows, part * DEPTH), full)] * 3
    inputs = [grad_mid, mid_half, out_half, gain_terms, gains[0], *saved, *gains[2:]]
    return pl.pallas_call(
        functools.partial(backward_kernel, dp_size),
        out_shape=shapes,
        in_specs=[VMEM, ANY] + [VMEM] * len(inputs),
        out_specs=[VMEM] * 10,
        scratch_shapes=[
            pltpu.VMEM((width, every), half),
            pltpu.VMEM((DEPTH, wide, rows, every), half),
            pltpu.VMEM((wide - 1, DEPTH, rows, every), half),
            pltpu.VMEM((LineReduce.slots, rows, every), half),
            pltpu.VMEM((DEPTH - 1, rows, 3 * part), half),
            pltpu.VMEM((seq_len, cols[0]), half),
            pltpu.VMEM((seq_len, every - cols[3]), half),
            pltpu.VMEM((width, seq_len), half),
            pltpu.VMEM((seq_len, width), full),
            pltpu.VMEM((tokens, width), half),
            pltpu.VMEM((tokens, width), half),
            pltpu.VMEM((pairs, 8, width), full),
            pltpu.VMEM((pairs, 8, width), full),
            pltpu.SemaphoreType.DMA((2,)),
            pltpu.SemaphoreType.DMA((copies,)),
            pltpu.SemaphoreType.DMA((copies,)),
        ],
        compiler_params=pltpu.CompilerParams(
            collective_id=2, has_side_effects=True, vmem_limit_bytes=63 * 2**20
        ),
    )(shares, weights, *inputs)


def body(
    dp_size,
    layer_in,
    seg_ids,
    w_q,
    w_k,
    w_v,
    w_o,
    w_gate,
    w_up,
    w_down,
    attn_gain,
    mlp_gain,
    q_gain,
    k_gain,
    cotangent,
):
    row_in = layer_in[0]
    row_cot = cotangent[0]
    width = row_in.shape[1]
    gains = [gain[None, :] for gain in (attn_gain, mlp_gain, q_gain, k_gain)]
    outs = forward(
        dp_size, (w_q, w_k, w_v, w_o, w_gate, w_up, w_down), row_cot, row_in, seg_ids[0], gains
    )
    attn_full, ffn_full, cots, normed, mid = outs[:5]
    saved = outs[5:]
    outs = mlp(
        dp_size, ffn_full, normed.reshape(-1, width), cots.reshape(-1, width), mid, row_cot, gains[1]
    )
    grad_mid, mid_half, out_half, gain_terms, shares = outs
    cols = [weight.shape[1] for weight in (w_q, w_k, w_v, w_o)]
    outs = backward(
        dp_size, shares, attn_full, cols, grad_mid, mid_half, out_half, gain_terms,
        [row_in] + list(saved), gains,
    )
    out_row, in_grad, sums = outs[:3]
    gain_outs = []
    for i, size in enumerate((width, width, q_gain.shape[0], k_gain.shape[0])):
        share = size // dp_size
        gain_outs.append(lax.dynamic_slice(sums[i], (lax.axis_index("dp") * share,), (share,)))
    return (out_row[None], in_grad[None], *outs[3:], *gain_outs)


def solution(mesh):
    return jax.shard_map(
        functools.partial(body, mesh.shape["dp"]),
        mesh=mesh,
        in_specs=(
            P("dp", None, None),
            P("dp", None),
            P("dp", "mp"),
            P("dp", "mp"),
            P("dp", "mp"),
            P("dp", "mp"),
            P("dp", "mp"),
            P("dp", "mp"),
            P("dp", "mp"),
            P(),
            P(),
            P(),
            P(),
            P("dp", None, None),
        ),
        out_specs=(
            P("dp", None, None),
            P("dp", None, None),
            P("dp", "mp"),
            P("dp", "mp"),
            P("dp", "mp"),
            P("dp", "mp"),
            P("dp", "mp"),
            P("dp", "mp"),
            P("dp", "mp"),
            P("dp"),
            P("dp"),
            P("dp"),
            P("dp"),
        ),
        check_vma=False,
    )
```

```python
import functools
import math

import jax
import jax.numpy as jnp
from jax import lax
from jax.experimental import pallas as pl
from jax.experimental.pallas import tpu as pltpu
from jax.sharding import PartitionSpec as P

EPSILON = 1e-06
ROPE_BASE = 1000000.0
MASKED = -1e30


def matmul(left_op, right_op):
    return jnp.dot(left_op, right_op, preferred_element_type=jnp.float32)


def rms_norm(values, gain_vec):
    inv_rms = lax.rsqrt(jnp.mean(values * values, axis=-1, keepdims=True) + EPSILON)
    return (values * inv_rms * gain_vec, inv_rms)


def norm_back(grad_norm, values, inv_rms, gain_vec):
    scaled = grad_norm * gain_vec
    cubed = inv_rms * inv_rms * inv_rms
    grad_values = inv_rms * scaled - values * cubed * jnp.mean(
        scaled * values, axis=-1, keepdims=True
    )
    return (grad_values, grad_norm * values * inv_rms)


MESH = pl.DeviceIdType.MESH
ANY = pl.BlockSpec(memory_space=pl.ANY)
VMEM = pl.BlockSpec(memory_space=pltpu.VMEM)
DEPTH = 4
CORES = 2
HALVES = 2
UP, DOWN = 0, 1
TILE = 256


def split(index, size):
    size = jnp.int32(size)
    return lax.div(index, size), lax.rem(index, size)


class Place:
    def __init__(self, dp_size):
        self.wide = dp_size // (DEPTH * CORES)
        self.x = lax.axis_index("mp")
        rest, self.c = split(lax.axis_index("dp"), CORES)
        self.z, self.y = split(rest, self.wide)

    def device(self, z=None, y=None, c=None, x=None):
        z = self.z if z is None else z
        y = self.y if y is None else y
        c = self.c if c is None else c
        x = self.x if x is None else x
        return ((z * self.wide + y) * CORES + c, x)

    def z_off(self, step):
        return lax.rem(self.z + DEPTH + step, jnp.int32(DEPTH))

    def z_flip(self, bits):
        z = self.z
        if bits == DEPTH - 1:
            return DEPTH - 1 - z
        return z + bits - 2 * bits * lax.rem(lax.div(z, jnp.int32(bits)), jnp.int32(2))

    def y_off(self, step):
        return lax.rem(self.y + self.wide + step, jnp.int32(self.wide))

    def rows(self, z, y, c, count):
        return pl.ds(pl.multiple_of(((z * self.wide + y) * CORES + c) * count, count), count)

    def line(self):
        return [self.device(z=self.z_off(1)), self.device(z=self.z_off(-1))]

    def z_peers(self):
        return [self.device(z=self.z_off(k)) for k in range(1, DEPTH)]

    def y_peers(self):
        return [self.device(y=self.y_off(j)) for j in range(1, self.wide)]

    def order(self):
        low = 1 - lax.div(self.z, jnp.int32(2))
        return [3 * low, 1 + low, low * (1 - self.z) + (1 - low) * (5 - self.z), self.z]


def guarded(when, action):
    if when is None:
        action()
    else:
        pl.when(when)(action)


class Mail:
    def __init__(self, send_sems, recv_sems):
        self.send_sems, self.recv_sems = send_sems, recv_sems
        self.count = 0
        self.open = []

    def reserve(self, count):
        first = self.count
        self.count += count
        return first

    def describe(self, source, target, device, slot):
        return pltpu.make_async_remote_copy(
            source,
            target,
            self.send_sems.at[slot],
            self.recv_sems.at[slot],
            device_id=device,
            device_id_type=MESH,
        )

    def make(self, source, target, device, when=None, slot=None):
        copy = self.describe(source, target, device, self.reserve(1) if slot is None else slot)
        self.open.append((copy, when))
        return copy

    def send(self, source, target, device, when=None):
        copy = self.make(source, target, device, when)
        guarded(when, copy.start)
        return copy

    def finish(self):
        for copy, when in self.open:
            guarded(when, copy.wait_send)


def meet(devices):
    barrier = pltpu.get_barrier_semaphore()
    for device in devices:
        pl.semaphore_signal(barrier, inc=1, device_id=device, device_id_type=MESH)
    pl.semaphore_wait(barrier, len(devices))


def receive(copies):
    for copy in copies:
        copy.wait_recv()


def start_all(copies):
    for copy in copies:
        copy.start()


class LineGather:
    def __init__(self, mail, at, own, place, sides, sibling=None, share_own=True):
        self.mail, self.at, self.place = mail, at, place
        self.sides, self.sibling = sides, sibling
        self.neighbours = at.line()
        self.open_end = [at.z < DEPTH - 1, at.z > 0]
        pairs = list(zip(own, place(at.z, 0)))
        self.hops = [
            [mail.send(source, target, self.neighbours[way], self.open_end[way]) for source, target in pairs]
            for way in (UP, DOWN)
        ]
        self.over, self.cores = {}, []
        if share_own:
            self.over["own"] = [
                [mail.send(source, target, side) for source, target in pairs] for side in sides
            ]
        if sibling is not None:
            self.cores.append(
                (None, [mail.send(source, target, sibling) for source, target in pairs])
            )

    def where(self, way, step):
        z = self.at.z
        if way == UP:
            return z >= step + 1, self.at.z_off(-1 - step)
        return z + 1 + step < DEPTH, self.at.z_off(1 + step)

    def step(self, step):
        for way in (UP, DOWN):
            got, index = self.where(way, step)
            refs = self.place(index, 0)
            arrived = self.hops[way]
            onward = []
            if step < DEPTH - 2:
                more = got & self.open_end[way]
                onward = [self.mail.make(ref, ref, self.neighbours[way], more) for ref in refs]
            over = [[self.mail.make(ref, ref, side, got) for ref in refs] for side in self.sides]
            cores = []
            if self.sibling is not None:
                cores = [self.mail.make(ref, ref, self.sibling, got) for ref in refs]

            def pass_on(way=way, arrived=arrived, onward=onward, over=over, cores=cores):
                receive(arrived)
                pl.when(self.open_end[way])(lambda: start_all(onward))
                for copies in over:
                    start_all(copies)
                start_all(cores)

            pl.when(got)(pass_on)
            self.hops[way] = onward
            self.over[way, step] = over
            if cores:
                self.cores.append((got, cores))

    def side_step(self, key):
        got, index = (None, self.at.z) if key == "own" else self.where(*key)
        cores = []
        for j in range(1, len(self.sides) + 1):
            if self.sibling is not None:
                refs = self.place(index, j)
                cores += [self.mail.make(ref, ref, self.sibling, got) for ref in refs]

        def pass_on():
            for copies in self.over[key]:
                receive(copies)
            start_all(cores)

        guarded(got, pass_on)
        if cores:
            self.cores.append((got, cores))

    def side_steps(self, step):
        self.side_step((UP, step))
        self.side_step((DOWN, step))

    def finish(self):
        for got, cores in self.cores:
            guarded(got, lambda cores=cores: receive(cores))


class LineReduce:
    slots = 2 * (DEPTH - 1)

    def __init__(self, mail, at, pieces, part, land):
        self.mail, self.at, self.pieces, self.part, self.land = mail, at, pieces, part, land
        self.base = mail.reserve(self.slots * pieces)

    def copies(self, index, sources, device):
        slots = [self.base + index * self.pieces + i for i in range(self.pieces)]
        return [
            self.mail.describe(source, target, device, slot)
            for source, target, slot in zip(sources, self.land(index), slots)
        ]

    def pass_on(self, turn):
        z = self.at.z
        low = 1 - lax.div(z, jnp.int32(2))
        up = low if turn < 2 else 1 - lax.rem(z, jnp.int32(2))
        target = self.at.order()[turn]
        index = up * (target - 1) + (1 - up) * (DEPTH - 1 + target)
        device = self.at.device(z=z + 2 * up - 1)
        sources = self.part(target)
        copies = self.copies(index, sources, device)
        has_in = up * jnp.where(z > 0, 1, 0) + (1 - up) * jnp.where(z < DEPTH - 1, 1, 0)

        @pl.when(has_in > 0)
        def _():
            receive(copies)
            for source, landed in zip(sources, self.land(index)):
                add_into(source, landed)

        start_all(copies)
        self.mail.open += [(copy, None) for copy in copies]

    def last(self, use):
        z = self.at.z
        sources = self.part(z)
        for when, index, neighbour in (
            (z > 0, lax.max(z - 1, 0), self.at.z_off(-1)),
            (z < DEPTH - 1, lax.min(DEPTH - 1 + z, self.slots - 1), self.at.z_off(1)),
        ):
            copies = self.copies(index, sources, self.at.device(z=neighbour))

            @pl.when(when)
            def _(copies=copies, index=index):
                receive(copies)
                for i, landed in enumerate(self.land(index)):
                    use(i, landed)


def own_copies(pairs, sems, first=0):
    copies = [
        pltpu.make_async_copy(source, target, sems.at[first + i])
        for i, (source, target) in enumerate(pairs)
    ]
    start_all(copies)
    return copies


def finish_own(copies):
    for copy in copies:
        copy.wait()


def add_into(target, *others):
    total = target[...].astype(jnp.float32)
    for other in others:
        total = total + other[...].astype(jnp.float32)
    target[...] = total.astype(target.dtype)


def dot_nt(left_op, right_op):
    return lax.dot_general(
        left_op, right_op, (((1,), (1,)), ((), ())), preferred_element_type=jnp.float32
    )


def dot_tn(left_op, right_op):
    return lax.dot_general(
        left_op, right_op, (((0,), (0,)), ((), ())), preferred_element_type=jnp.float32
    )


def turned(values):
    return pltpu.roll(values, values.shape[-1] // 2, axis=values.ndim - 1)


def document_tables(seg_col, seg_row, head_dim):
    seq_len = seg_col.shape[0]
    rows = lax.broadcasted_iota(jnp.int32, (seq_len, seq_len), 0)
    cols = lax.broadcasted_iota(jnp.int32, (seq_len, seq_len), 1)
    same = seg_col == seg_row
    bias = jnp.where(same & (cols <= rows), 0.0, MASKED)
    before = jnp.where(same & (cols < rows), 1.0, 0.0)
    position = jnp.sum(before, axis=-1, keepdims=True)
    lane = lax.broadcasted_iota(jnp.int32, (1, head_dim), 1)
    half_dim = head_dim // 2
    slot = jnp.where(lane < half_dim, lane, lane - half_dim).astype(jnp.float32)
    frequency = jnp.exp(slot * (-2.0 * math.log(ROPE_BASE) / head_dim))
    angles = position * frequency
    sine = jnp.sin(angles)
    return bias, jnp.cos(angles), jnp.where(lane < half_dim, -sine, sine)


def matmul_tiles(left, right, write, tile=256):
    @pl.loop(0, right.shape[1] // tile)
    def _(index):
        columns = pl.ds(pl.multiple_of(index * tile, tile), tile)
        write(columns, matmul(left[...], right[:, columns]))


SAVED = 11


def forward_kernel(
    dp_size, w_q, w_k, w_v, w_o, w_g, w_u, w_d, cot, row_in, seg_col, seg_row,
    gain_one, gain_two, q_gain, k_gain,
    *refs,
):
    o_attn, o_ffn, o_c, o_n, o_mid = refs[:5]
    stored, held = refs[5 : 5 + SAVED], refs[6 + SAVED : 6 + 2 * SAVED]
    mid = refs[5 + SAVED]
    normed_one, query_raw, key_raw, values_half, queries, keys, context, log_total = held[:8]
    cosine, sine, bias = held[8:]
    full, own_part, outgoing, incoming, normed, own_sems, send_sems, recv_sems = refs[6 + 2 * SAVED :]
    at = Place(dp_size)
    z, y, c, x = at.z, at.y, at.c, at.x
    sibling, other = at.device(c=1 - c), at.device(x=1 - x)
    z_peers, y_peers = at.z_peers(), at.y_peers()
    meet([sibling, other] + z_peers + y_peers)

    mail = Mail(send_sems, recv_sems)
    rows = w_q.shape[0]
    head_dim = q_gain.shape[1]
    part = w_g.shape[1] // DEPTH
    tokens = mid.shape[0]
    here = at.rows(z, y, c, rows)
    spans, start = [], 0
    for weight in (w_q, w_k, w_v, w_o):
        spans.append(pl.ds(start, weight.shape[1]))
        start += weight.shape[1]
    q_span, k_span, v_span, o_span = spans
    ffn = [(weight, pl.ds(i * part, part)) for i, weight in enumerate((w_g, w_u, w_d))]

    def columns(index):
        return pl.ds(pl.multiple_of(index * part, part), part)

    def half_rows(index):
        return pl.ds(pl.multiple_of(index * tokens, tokens), tokens)

    mine = own_copies(
        [(weight, full.at[here, span]) for weight, span in zip((w_q, w_k, w_v, w_o), spans)],
        own_sems,
    )
    own_ffn = own_copies(
        [(weight.at[:, columns(z)], own_part.at[:, span]) for weight, span in ffn], own_sems, 4
    )
    own_cot = own_copies([(cot.at[half_rows(i)], o_c.at[z, i]) for i in range(2)], own_sems, 7)
    finish_own(mine)
    attn = LineGather(
        mail,
        at,
        (full.at[here],),
        lambda zb, j: [full.at[at.rows(zb, at.y_off(-j), c, rows)]],
        y_peers,
        sibling,
    )

    residual = row_in[...].astype(jnp.float32)
    normed_full, _ = rms_norm(residual, gain_one[...])
    normed_one[...] = normed_full.astype(jnp.bfloat16)
    bias_values, cosine[...], sine[...] = document_tables(seg_col[...], seg_row[...], head_dim)
    bias[...] = bias_values

    spread, crossing, to_sibling = {}, {}, []

    def start_spread():
        for k in range(1, DEPTH):
            target = at.z_flip(k)
            spread[k] = [
                mail.send(
                    weight.at[:, columns(target)], o_ffn.at[here, span], at.device(z=target)
                )
                for weight, span in ffn
            ]
        block = o_ffn.at[here]
        for j in range(1, at.wide):
            crossing[0, j] = mail.send(own_part, block, y_peers[j - 1])
        to_sibling.append(mail.send(own_part, block, sibling))

    def forward_spread(k):
        receive(spread[k])
        block = o_ffn.at[at.rows(at.z_flip(k), y, c, rows)]
        for j in range(1, at.wide):
            crossing[k, j] = mail.send(block, block, y_peers[j - 1])
        to_sibling.append(mail.send(block, block, sibling))

    def forward_crossing(k):
        for j in range(1, at.wide):
            crossing[k, j].wait_recv()
            block = o_ffn.at[at.rows(at.z_flip(k), at.y_off(-j), c, rows)]
            to_sibling.append(mail.send(block, block, sibling))

    def half_place(out):
        return lambda zb, j: [out.at[zb, x if j == 0 else 1 - x]]

    attn.step(0)
    finish_own(own_ffn)
    own_copy = own_copies([(own_part, o_ffn.at[here])], own_sems, 4)
    attn.side_step("own")
    attn.step(1)
    cots = LineGather(
        mail, at, (cot.at[half_rows(x)],), half_place(o_c), [other], share_own=False
    )
    attn.side_steps(0)
    attn.step(2)
    cots.step(0)
    attn.side_steps(1)
    cots.step(1)
    start_spread()
    attn.side_steps(2)
    attn.finish()
    saved = own_copies([(full, o_attn)], own_sems)

    def write_query(cols, block):
        query_raw[:, cols] = block

    def write_key(cols, block):
        key_raw[:, cols] = block

    def write_value(cols, block):
        values_half[:, cols] = block.astype(jnp.bfloat16)

    matmul_tiles(normed_one, full.at[:, q_span], write_query)
    matmul_tiles(normed_one, full.at[:, k_span], write_key)
    matmul_tiles(normed_one, full.at[:, v_span], write_value)

    def rotated(raw, gain):
        unit, _ = rms_norm(raw, gain)
        return (unit * cosine[...] + turned(unit) * sine[...]).astype(jnp.bfloat16)

    kv_heads = key_raw.shape[1] // head_dim
    group = query_raw.shape[1] // key_raw.shape[1]
    for j in range(kv_heads):
        kv_cols = pl.ds(j * head_dim, head_dim)
        keys[:, kv_cols] = rotated(key_raw[:, kv_cols], k_gain[...])
        for g in range(group):
            head = j * group + g
            cols = pl.ds(head * head_dim, head_dim)
            queries[:, cols] = rotated(query_raw[:, cols], q_gain[...])
            scores = dot_nt(queries[:, cols], keys[:, kv_cols]) * (1.0 / math.sqrt(head_dim))
            scores = scores + bias[...]
            row_max = jnp.max(scores, axis=-1, keepdims=True)
            weights = jnp.exp(scores - row_max)
            total = jnp.sum(weights, axis=-1, keepdims=True)
            log_total[:, head : head + 1] = row_max + jnp.log(total)
            probs = (weights * (1.0 / total)).astype(jnp.bfloat16)
            context[:, cols] = matmul(probs, values_half[:, kv_cols]).astype(jnp.bfloat16)
        if j == kv_heads // 2 - 1:
            cots.step(2)

    saved += own_copies(list(zip(held, stored)), own_sems, 11)
    given, kept = half_rows(1 - x), half_rows(x)
    width = row_in.shape[1]

    def project(token_rows, target):
        @pl.loop(0, width // TILE)
        def _(index):
            cols = pl.ds(pl.multiple_of(index * TILE, TILE), TILE)
            block = dot_nt(context[token_rows, :], full[cols, o_span])
            target[:, cols] = block.astype(target.dtype)

    project(given, outgoing)
    swap = mail.send(outgoing, incoming, other)
    project(kept, mid)
    swap.wait_recv()
    total = row_in[kept, :].astype(jnp.float32) + (mid[...] + incoming[...].astype(jnp.float32))
    mid[...] = total
    saved += own_copies([(mid, o_mid)], own_sems, 10)
    normed_mid, _ = rms_norm(total, gain_two[...])
    normed[...] = normed_mid.astype(jnp.bfloat16)
    last = own_copies([(normed, o_n.at[z, x])], own_sems, 9)
    strip = tokens // 2
    norms = []
    for i in range(2):
        rows_of = pl.ds(i * strip, strip)
        norms.append(
            LineGather(
                mail,
                at,
                (normed.at[rows_of],),
                lambda zb, j, rows_of=rows_of: [o_n.at[zb, x if j == 0 else 1 - x, rows_of]],
                [other],
            )
        )
    forward_spread(1)
    forward_crossing(0)
    for step in range(DEPTH - 1):
        if step < DEPTH - 2:
            forward_spread(step + 2)
        for line in norms:
            line.step(step)
        forward_crossing(step + 1)
    for step in range(DEPTH - 1):
        cots.side_steps(step)
    for line in norms:
        line.side_step("own")
        for step in range(DEPTH - 1):
            line.side_steps(step)
    receive(to_sibling)
    mail.finish()
    finish_own(saved + last + own_cot + own_copy)


def forward(dp_size, weights, cot, row_in, seg_row, gains):
    w_q, w_k, w_v, w_o, w_g, w_u, w_d = weights
    wide = dp_size // (DEPTH * CORES)
    seq_len, width = row_in.shape
    head_dim = gains[2].shape[1]
    tokens = seq_len // HALVES
    part = w_g.shape[1] // DEPTH
    half, whole = jnp.bfloat16, jnp.float32
    attn_cols = [w.shape[1] for w in (w_q, w_k, w_v, w_o)]
    shapes = [jax.ShapeDtypeStruct((width, cols), half) for cols in (sum(attn_cols), 3 * part)]
    shapes += [jax.ShapeDtypeStruct((DEPTH, HALVES, tokens, width), half)] * 2
    q_cols, kv_cols = attn_cols[0], attn_cols[1]
    for cols, kind in (
        (width, half), (q_cols, whole), (kv_cols, whole), (kv_cols, half), (q_cols, half),
        (kv_cols, half), (q_cols, half), (head_dim, whole), (head_dim, whole), (head_dim, whole),
        (seq_len, whole),
    ):
        shapes.append(jax.ShapeDtypeStruct((seq_len, cols), kind))
    shapes.insert(4, jax.ShapeDtypeStruct((tokens, width), whole))
    hops = 2 * (DEPTH - 1)
    spots = 1 + hops
    copies = (hops + spots * (2 * wide - 1)) + 3 * (2 * hops + 1) + 1
    copies += 9 + DEPTH * (2 * wide - 1)
    return pl.pallas_call(
        functools.partial(forward_kernel, dp_size),
        out_shape=shapes,
        in_specs=[ANY] * 7 + [VMEM] * 8,
        out_specs=[ANY] * (5 + SAVED),
        scratch_shapes=[pltpu.VMEM(shape.shape, shape.dtype) for shape in shapes[4:]]
        + [pltpu.VMEM((width, sum(attn_cols)), half)]
        + [pltpu.VMEM((w_g.shape[0], 3 * part), half)]
        + [pltpu.VMEM((tokens, width), half)] * 3
        + [
            pltpu.SemaphoreType.DMA((11 + SAVED,)),
            pltpu.SemaphoreType.DMA((copies,)),
            pltpu.SemaphoreType.DMA((copies,)),
        ],
        compiler_params=pltpu.CompilerParams(
            collective_id=0, has_side_effects=True, vmem_limit_bytes=56 * 2**20
        ),
    )(w_q, w_k, w_v, w_o, w_g, w_u, w_d, cot, row_in, seg_row[:, None], seg_row[None, :], *gains)


def mlp_kernel(
    dp_size, weights, n_all, c_all, a_mid, a_cot, gain,
    a_m, a_h, a_l, o_t, a_shares,
    mid, cot, o_m, o_h, o_l, o_b, shares, full, x_n, x_c, hidden, p_n, p_o, h_n, h_o, h_l, l_n, l_o, l_z, outgoing, from_core, from_y,
    own_sems, send_sems, recv_sems,
):
    at = Place(dp_size)
    z, y, c, x = at.z, at.y, at.c, at.x
    other, sibling = at.device(x=1 - x), at.device(c=1 - c)
    y_peers = at.y_peers()
    order = at.order()
    tokens = mid.shape[0]
    block_rows = HALVES * tokens
    rows = from_core.shape[2]
    part = full.shape[1] // 3
    gate_up, down = pl.ds(0, 2 * part), pl.ds(2 * part, part)
    width = mid.shape[1]

    def band(index, size):
        return pl.ds(pl.multiple_of(index * size, size), size)

    loads = {}
    for i, name in enumerate("gud"):
        span = pl.ds(i * part, part)
        loads[name] = pltpu.make_async_copy(weights.at[:, span], full.at[:, span], own_sems.at[i])
    for i, index in enumerate(order):
        block = band(index, block_rows)
        loads["n", i] = pltpu.make_async_copy(n_all.at[block], x_n.at[block], own_sems.at[3 + i])
        loads["c", i] = pltpu.make_async_copy(c_all.at[block], x_c.at[block], own_sems.at[7 + i])
    for key in ("g", "u", ("n", 0), "d", ("c", 0)):
        loads[key].start()
    for i in range(1, DEPTH):
        loads["n", i].start()
        loads["c", i].start()
    late = own_copies([(a_mid, mid), (a_cot, cot)], own_sems, 11)
    meet([other, sibling] + at.line() + y_peers)
    mail = Mail(send_sems, recv_sems)

    def half_rows(index, side):
        return band(index * HALVES + side, tokens)

    first, second = pl.ds(0, width // 2), pl.ds(width // 2, width // 2)
    norm_line = LineReduce(
        mail, at, 1, lambda index: [p_n.at[half_rows(index, x)]], lambda slot: [l_n.at[slot]]
    )
    out_line = LineReduce(
        mail, at, 1, lambda index: [p_o.at[half_rows(index, x), first]], lambda slot: [l_o.at[slot]]
    )
    late_line = LineReduce(
        mail, at, 1, lambda index: [p_o.at[band(index, block_rows), second]], lambda slot: [l_z.at[slot]]
    )
    norm_swaps, out_swaps = [], []

    def compute(i):
        block = band(order[i], block_rows)
        if i == 0:
            for name in ("g", "u", "d"):
                loads[name].wait()
        loads["n", i].wait()
        loads["c", i].wait()

        @pl.loop(0, part // TILE)
        def _(index):
            g_cols, u_cols, d_cols = [
                pl.ds(pl.multiple_of(i * part + index * TILE, TILE), TILE) for i in range(3)
            ]
            gate = matmul(x_n[block, :], full[:, g_cols])
            up = matmul(x_n[block, :], full[:, u_cols])
            grad_act = matmul(x_c[block, :], full[:, d_cols])
            sigmoid_gate = 1.0 / (1.0 + jnp.exp(-gate))
            silu_val = gate * sigmoid_gate
            hidden[block, g_cols] = (
                grad_act * up * sigmoid_gate * (1.0 + gate * (1.0 - sigmoid_gate))
            ).astype(jnp.bfloat16)
            hidden[block, u_cols] = (grad_act * silu_val).astype(jnp.bfloat16)
            hidden[block, d_cols] = (silu_val * up).astype(jnp.bfloat16)

        @pl.loop(0, width // TILE)
        def _(index):
            cols = band(index, TILE)
            p_n[block, cols] = dot_nt(hidden[block, gate_up], full[cols, gate_up]).astype(jnp.bfloat16)

        norm_swaps.append(mail.send(p_n.at[half_rows(order[i], 1 - x)], h_n.at[i], other))

    def compute_out(i):
        block = band(order[i], block_rows)

        @pl.loop(0, width // TILE)
        def _(index):
            cols = band(index, TILE)
            p_o[block, cols] = dot_nt(hidden[block, down], full[cols, down]).astype(jnp.bfloat16)

    def norm_step(i):
        norm_swaps[i].wait_recv()
        add_into(p_n.at[half_rows(order[i], x)], h_n.at[i])
        norm_line.pass_on(i)

    def out_step(i):
        out_swaps[i].wait_recv()
        add_into(p_o.at[half_rows(order[i], x), first], h_o.at[i])
        out_line.pass_on(i)

    def weight_grads(span, i):
        left = x_n if span is gate_up else x_c

        @pl.loop(0, width // DEPTH // TILE)
        def _(index):
            cols = pl.ds(pl.multiple_of(order[i] * (width // DEPTH) + index * TILE, TILE), TILE)
            full[cols, span] = matmul(left[:, cols].T, hidden[:, span]).astype(jnp.bfloat16)

        to_core[span.start, i] = [
            mail.send(
                full.at[at.rows(order[i], side, 1 - c, rows), span],
                from_core.at[order[i], side, :, span],
                sibling,
            )
            for side in range(at.wide)
        ]

    to_core, to_y = {}, {}

    def core_stage(span, i):
        receive(to_core[span.start, i])
        for side in range(at.wide):
            add_into(
                full.at[at.rows(order[i], side, c, rows), span], from_core.at[order[i], side, :, span]
            )
        to_y[span.start, i] = [
            mail.send(
                full.at[at.rows(order[i], at.y_off(j), c, rows), span],
                from_y.at[j - 1, order[i], :, span],
                y_peers[j - 1],
            )
            for j in range(1, at.wide)
        ]

    def y_stage(span, i):
        receive(to_y[span.start, i])
        total = full[at.rows(order[i], y, c, rows), span].astype(jnp.float32)
        for j in range(1, at.wide):
            total = total + from_y[j - 1, order[i], :, span].astype(jnp.float32)
        shares[order[i], :, span] = total.astype(jnp.bfloat16)

    compute(0)
    compute(1)
    compute(2)
    norm_step(0)
    compute(3)
    weight_grads(gate_up, 0)
    norm_step(1)
    weight_grads(gate_up, 1)
    core_stage(gate_up, 0)
    weight_grads(gate_up, 2)
    core_stage(gate_up, 1)
    norm_step(2)
    weight_grads(gate_up, 3)
    core_stage(gate_up, 2)
    compute_out(0)
    late_line.pass_on(0)
    core_stage(gate_up, 3)
    compute_out(1)
    late_line.pass_on(1)
    compute_out(2)
    compute_out(3)
    norm_swaps[3].wait_recv()
    for i in range(DEPTH):
        out_swaps.append(
            mail.send(p_o.at[half_rows(order[i], 1 - x), first], h_o.at[i], other)
        )
    weight_grads(down, 0)
    weight_grads(down, 1)
    core_stage(down, 0)
    finish_own(late)
    o_m[...] = p_n[half_rows(z, x), :].astype(jnp.float32) + h_n[3].astype(jnp.float32)

    def add_norm(_, landed):
        o_m[...] = o_m[...] + landed[...].astype(jnp.float32)

    norm_line.last(add_norm)
    grad_norm = o_m[...]
    values = mid[...]
    inv_rms = lax.rsqrt(jnp.mean(values * values, axis=-1, keepdims=True) + EPSILON)
    grad_values, terms = norm_back(grad_norm, values, inv_rms, gain[...])
    o_t[...] = jnp.sum(terms, axis=0, keepdims=True)
    kept = band(x, tokens)
    total = cot[kept, :].astype(jnp.float32) + grad_values
    o_m[...] = total
    o_h[kept, :] = total.astype(jnp.bfloat16)
    swap_h = mail.send(o_h.at[kept], o_h.at[kept], other)
    stores = own_copies([(o_m, a_m)], own_sems, 0)
    late_line.pass_on(2)
    weight_grads(down, 2)
    core_stage(down, 1)
    weight_grads(down, 3)
    core_stage(down, 2)
    core_stage(down, 3)
    for i in range(DEPTH - 1):
        out_step(i)
        y_stage(gate_up, i)

    def add_late(_, landed):
        for i in range(HALVES):
            rows_of = band(z * HALVES + i, tokens)
            add_into(p_o.at[rows_of, second], landed.at[pl.ds(i * tokens, tokens)])

    late_line.last(add_late)
    outgoing[...] = p_o[half_rows(z, 1 - x), second]
    swap_l = mail.send(outgoing, h_l, other)
    y_stage(gate_up, DEPTH - 1)
    for i in range(DEPTH):
        y_stage(down, i)
        stores.extend(own_copies([(shares.at[order[i]], a_shares.at[order[i]])], own_sems, 3 + i))
    out_swaps[3].wait_recv()
    o_l[:, first] = mid[:, first] + (
        p_o[half_rows(z, x), first].astype(jnp.float32) + h_o[3].astype(jnp.float32)
    )

    def add_out(_, landed):
        o_l[:, first] = o_l[:, first] + landed[...].astype(jnp.float32)

    out_line.last(add_out)
    swap_l.wait_recv()
    o_l[:, second] = mid[:, second] + (
        p_o[half_rows(z, x), second].astype(jnp.float32) + h_l[...].astype(jnp.float32)
    )
    o_b[...] = o_l[...].astype(jnp.bfloat16)
    stores += own_copies([(o_b, a_l)], own_sems, 1)
    swap_h.wait_recv()
    stores += own_copies([(o_h, a_h)], own_sems, 2)
    mail.finish()
    finish_own(stores)


def mlp(dp_size, weights, normed, cots, mid, cot, gain):
    wide = dp_size // (DEPTH * CORES)
    tokens, width = mid.shape
    cols = weights.shape[1]
    rows = width // dp_size
    every = DEPTH * HALVES * tokens
    half, full = jnp.bfloat16, jnp.float32
    copies = 3 * LineReduce.slots + 2 * DEPTH + 2 * DEPTH * (2 * wide - 1) + 2
    shapes = [
        jax.ShapeDtypeStruct((tokens, width), full),
        jax.ShapeDtypeStruct((HALVES * tokens, width), half),
        jax.ShapeDtypeStruct((tokens, width), half),
        jax.ShapeDtypeStruct((1, width), full),
        jax.ShapeDtypeStruct((DEPTH, rows, cols), half),
    ]
    return pl.pallas_call(
        functools.partial(mlp_kernel, dp_size),
        out_shape=shapes,
        in_specs=[ANY] * 5 + [VMEM],
        out_specs=[ANY] * 3 + [VMEM, ANY],
        scratch_shapes=[
            pltpu.VMEM((tokens, width), full),
            pltpu.VMEM((HALVES * tokens, width), half),
            pltpu.VMEM((tokens, width), full),
            pltpu.VMEM((HALVES * tokens, width), half),
            pltpu.VMEM((tokens, width), full),
            pltpu.VMEM((tokens, width), half),
            pltpu.VMEM((DEPTH, rows, cols), half),
        ]
        + [pltpu.VMEM((width, cols), half)]
        + [pltpu.VMEM((every, width), half)] * 2
        + [pltpu.VMEM((every, cols), half)]
        + [pltpu.VMEM((every, width), half)] * 2
        + [
            pltpu.VMEM((DEPTH, tokens, width), half),
            pltpu.VMEM((DEPTH, tokens, width // 2), half),
            pltpu.VMEM((tokens, width // 2), half),
            pltpu.VMEM((LineReduce.slots, tokens, width), half),
            pltpu.VMEM((LineReduce.slots, tokens, width // 2), half),
            pltpu.VMEM((LineReduce.slots, HALVES * tokens, width // 2), half),
            pltpu.VMEM((tokens, width // 2), half),
        ]
        + [
            pltpu.VMEM((DEPTH, wide, rows, cols), half),
            pltpu.VMEM((wide - 1, DEPTH, rows, cols), half),
            pltpu.SemaphoreType.DMA((13,)),
            pltpu.SemaphoreType.DMA((copies,)),
            pltpu.SemaphoreType.DMA((copies,)),
        ],
        compiler_params=pltpu.CompilerParams(
            collective_id=1, has_side_effects=True, vmem_limit_bytes=63 * 2**20
        ),
    )(weights, normed, cots, mid, cot, gain)


def backward_kernel(
    dp_size, shares, weights, a_mid, mid_half, a_out, t_m, gain_one, a_row, a_normed, a_query,
    a_key, a_values, a_queries, a_keys, context, a_log, a_cosine, a_sine, a_bias, q_gain, k_gain,
    o_l, o_i, sums, d_q, d_k, d_v, d_o, d_g, d_u, d_d,
    grad_mid, out_half, row_in, normed_one, query_raw, key_raw, values_half, queries, keys,
    log_total, cosine, sine, bias,
    full, head_grads, gains, from_other, totals, core_o, core_h, core_s, y_o, y_h, y_s, z_o, z_h, z_s,
    spare, context_grad, raw_half, raw_head, flipped, partial,
    outgoing, incoming, own_sems, send_sems, recv_sems,
):
    at = Place(dp_size)
    z, y, c, x = at.z, at.y, at.c, at.x
    other, sibling = at.device(x=1 - x), at.device(c=1 - c)
    y_peers, z_peers = at.y_peers(), at.z_peers()
    order = at.order()
    tokens, width = grad_mid.shape
    rows = d_q.shape[0]
    part = shares.shape[2] // 3
    spans, start = [], 0
    for out in (d_q, d_k, d_v, d_o):
        spans.append(pl.ds(start, out.shape[1]))
        start += out.shape[1]
    q_span, k_span, v_span, o_span = spans
    qkv_span = pl.ds(0, start - d_o.shape[1])
    q_cols, kv_width = d_q.shape[1], d_k.shape[1]
    head_dim = q_gain.shape[1]

    def band(index, size):
        return pl.ds(pl.multiple_of(index * size, size), size)

    kept, given = band(x, tokens), band(1 - x, tokens)
    loads = own_copies(
        [(weights.at[:, span], full.at[:, span]) for span in (o_span, qkv_span)], own_sems
    )
    late = own_copies(
        [
            (a_normed, normed_one), (a_query, query_raw), (a_key, key_raw), (a_values, values_half),
            (a_queries, queries), (a_keys, keys), (a_log, log_total), (a_cosine, cosine),
            (a_sine, sine), (a_bias, bias), (a_out, out_half), (a_mid, grad_mid), (a_row, row_in),
        ],
        own_sems,
        2,
    )
    meet([other, sibling] + y_peers + z_peers)
    mail = Mail(send_sems, recv_sems)
    ffn = [(out, pl.ds(i * part, part)) for i, out in enumerate((d_g, d_u, d_d))]
    to_z = [
        mail.send(
            shares.at[at.z_off(k), :, span], out.at[:, band(z, part)], z_peers[k - 1]
        )
        for k in (2, 1, 3)
        for out, span in ffn
    ]
    kv_heads = key_raw.shape[1] // head_dim
    group = query_raw.shape[1] // key_raw.shape[1]
    q_part = group * head_dim

    def block_of(zb, side, core):
        return (zb * at.wide + side) * CORES + core

    class Sums:
        def __init__(self, held, core_land, y_land, z_land, outs):
            self.held, self.core_land, self.y_land, self.outs = held, core_land, y_land, outs
            self.line = LineReduce(
                mail, at, 1, lambda zb: [held(zb, y, c)], lambda slot: [z_land.at[slot]]
            )
            self.to_core, self.to_y = {}, {}

        def core_sends(self, i):
            self.to_core[i] = [
                mail.send(
                    self.held(order[i], side, 1 - c), self.core_land.at[order[i], side], sibling
                )
                for side in range(at.wide)
            ]

        def core_stage(self, i):
            receive(self.to_core[i])
            for side in range(at.wide):
                add_into(self.held(order[i], side, c), self.core_land.at[order[i], side])
            self.to_y[i] = [
                mail.send(
                    self.held(order[i], at.y_off(j), c), self.y_land.at[j - 1, order[i]], y_peers[j - 1]
                )
                for j in range(1, at.wide)
            ]

        def y_stage(self, i):
            receive(self.to_y[i])
            terms = [self.y_land.at[j - 1, order[i]] for j in range(1, at.wide)]
            own = self.held(order[i], y, c)
            if i < DEPTH - 1:
                add_into(own, *terms)
                return
            for out, span in self.outs:
                out[...] = own[:, span].astype(jnp.float32)
                add_into(out, *[term.at[:, span] for term in terms])

        def finish(self):
            def use(_, landed):
                for out, span in self.outs:
                    add_into(out, landed.at[:, span])

            self.line.last(use)

    out_sums = Sums(
        lambda zb, side, core: full.at[at.rows(zb, side, core, rows), o_span],
        core_o, y_o, z_o, [(d_o, pl.ds(0, d_o.shape[1]))],
    )
    head_sums = []
    for j in range(kv_heads):
        kv_cols = pl.ds(j * head_dim, head_dim)
        head_sums.append(
            Sums(
                lambda zb, side, core, j=j: head_grads.at[j, at.rows(zb, side, core, rows)],
                core_h.at[j], y_h.at[j], z_h.at[j],
                [
                    (d_q.at[:, pl.ds(j * q_part, q_part)], pl.ds(0, q_part)),
                    (d_k.at[:, kv_cols], pl.ds(q_part, head_dim)),
                    (d_v.at[:, kv_cols], pl.ds(q_part + head_dim, head_dim)),
                ],
            )
        )
    gain_sums = Sums(
        lambda zb, side, core: totals.at[block_of(zb, side, core)],
        core_s, y_s, z_s, [(sums, pl.ds(0, sums.shape[1]))],
    )

    gains[...] = jnp.zeros(gains.shape, jnp.float32)
    loads[0].wait()

    def write_context(cols, value):
        context_grad[:, cols] = value.astype(jnp.bfloat16)

    matmul_tiles(mid_half, full.at[:, o_span], write_context)

    quarter = width // DEPTH
    for i in range(DEPTH):

        @pl.loop(0, quarter // TILE)
        def _(index, i=i):
            cols = pl.ds(pl.multiple_of(order[i] * quarter + index * TILE, TILE), TILE)
            full[cols, o_span] = dot_tn(mid_half[:, cols], context[...]).astype(jnp.bfloat16)

        out_sums.core_sends(i)
    own_share = own_copies([(shares.at[z], spare)], own_sems, 15)
    for i in range(DEPTH):
        out_sums.core_stage(i)
    finish_own(late)
    finish_own(own_share)
    own_share = own_copies(
        [(spare.at[:, span], out.at[:, band(z, part)]) for out, span in ffn], own_sems, 15
    )
    flipped[...] = normed_one[...].T
    o_l[kept, :] = out_half[...]
    swap_l = mail.send(o_l.at[kept], o_l.at[kept], other)

    scale = 1.0 / math.sqrt(head_dim)

    def raw_grad(grad, raw, gain):
        back = grad * cosine[...] - turned(grad) * sine[...]
        inv_rms = lax.rsqrt(jnp.mean(raw * raw, axis=-1, keepdims=True) + EPSILON)
        grad_raw, terms = norm_back(back, raw, inv_rms, gain)
        return grad_raw.astype(jnp.bfloat16), jnp.sum(terms, axis=0, keepdims=True)

    for j in range(kv_heads):
        q_sum = jnp.zeros((1, head_dim), jnp.float32)
        k_sum = jnp.zeros((1, head_dim), jnp.float32)
        kv_cols = pl.ds(j * head_dim, head_dim)
        key_total = jnp.zeros((row_in.shape[0], head_dim), jnp.float32)
        value_total = jnp.zeros((row_in.shape[0], head_dim), jnp.float32)
        for g in range(group):
            head = j * group + g
            cols = pl.ds(head * head_dim, head_dim)
            scores = dot_nt(queries[:, cols], keys[:, kv_cols]) * scale + bias[...]
            probs = jnp.exp(scores - log_total[:, head : head + 1])
            grad_context = context_grad[:, cols]
            grad_probs = dot_nt(grad_context, values_half[:, kv_cols])
            delta = jnp.sum(
                grad_context.astype(jnp.float32) * context[:, cols].astype(jnp.float32),
                axis=-1,
                keepdims=True,
            )
            grad_scores = (probs * (grad_probs - delta) * scale).astype(jnp.bfloat16)
            grad_query, terms = raw_grad(
                matmul(grad_scores, keys[:, kv_cols]), query_raw[:, cols], q_gain[...]
            )
            raw_half[:, cols] = grad_query
            raw_head[:, pl.ds(g * head_dim, head_dim)] = grad_query
            q_sum = q_sum + terms
            key_total = key_total + dot_tn(grad_scores, queries[:, cols])
            value_total = value_total + dot_tn(probs.astype(jnp.bfloat16), grad_context)
        grad_key, terms = raw_grad(key_total, key_raw[:, kv_cols], k_gain[...])
        grad_value = value_total.astype(jnp.bfloat16)
        raw_half[:, pl.ds(q_cols + j * head_dim, head_dim)] = grad_key
        raw_half[:, pl.ds(q_cols + kv_width + j * head_dim, head_dim)] = grad_value
        raw_head[:, pl.ds(q_part, head_dim)] = grad_key
        raw_head[:, pl.ds(q_part + head_dim, head_dim)] = grad_value
        k_sum = k_sum + terms
        gains[0, 2:3, :head_dim] = gains[0, 2:3, :head_dim] + q_sum
        gains[0, 3:4, :head_dim] = gains[0, 3:4, :head_dim] + k_sum
        for i in range(DEPTH):

            @pl.loop(0, quarter // TILE)
            def _(index, i=i, j=j):
                cols = pl.ds(pl.multiple_of(order[i] * quarter + index * TILE, TILE), TILE)
                head_grads[j, cols, :] = matmul(flipped[cols, :], raw_head[...]).astype(jnp.bfloat16)

            head_sums[j].core_sends(i)
        if 1 <= j < DEPTH:
            out_sums.y_stage(j - 1)
            out_sums.line.pass_on(j - 1)
        if j > 0:
            for i in range(DEPTH):
                head_sums[j - 1].core_stage(i)
    for j in range(max(kv_heads - 1, 0), DEPTH - 1):
        out_sums.y_stage(j)
        out_sums.line.pass_on(j)
    out_sums.y_stage(DEPTH - 1)
    for i in range(DEPTH):
        head_sums[kv_heads - 1].core_stage(i)
    finish_own(loads[1:])

    def project(token_rows, target):
        @pl.loop(0, width // TILE)
        def _(index):
            cols = band(index, TILE)
            total = dot_nt(raw_half[token_rows, :], full[cols, qkv_span])
            partial[token_rows, cols] = total
            if target is not None:
                target[:, cols] = total.astype(target.dtype)

    project(given, outgoing)
    swap = mail.send(outgoing, incoming, other)
    project(kept, None)

    values = row_in[...].astype(jnp.float32)
    inv_rms = lax.rsqrt(jnp.mean(values * values, axis=-1, keepdims=True) + EPSILON)
    gain_terms = jnp.sum(partial[...] * values * inv_rms, axis=0, keepdims=True)
    blocks = gains.shape[0]
    share = width // blocks
    head_terms = gains[0, 2:4, :]
    for index in range(blocks):
        gains[index, 0:1, :share] = gain_terms[:, index * share : (index + 1) * share]
        gains[index, 1:2, :share] = t_m[:, index * share : (index + 1) * share]
        gains[index, 2:4, :] = head_terms
    swap_gains = mail.send(gains, from_other, other)
    swap.wait_recv()
    grad_norm = partial[kept, :] + incoming[...].astype(jnp.float32)
    values = row_in[kept, :].astype(jnp.float32)
    inv_rms = lax.rsqrt(jnp.mean(values * values, axis=-1, keepdims=True) + EPSILON)
    grad_values, _ = norm_back(grad_norm, values, inv_rms, gain_one[...])
    o_i[kept, :] = (grad_mid[...] + grad_values).astype(jnp.bfloat16)
    swap_back = mail.send(o_i.at[kept], o_i.at[kept], other)

    swap_gains.wait_recv()
    totals[...] = gains[...] + from_other[...]
    for i in range(DEPTH):
        gain_sums.core_sends(i)
    for i in range(DEPTH):
        gain_sums.core_stage(i)
    every = head_sums + [gain_sums]
    for index in range(len(every) + DEPTH - 2):
        if index < len(every):
            for i in range(DEPTH):
                every[index].y_stage(i)
        for turn in range(DEPTH - 1):
            if 0 <= index - turn < len(every):
                every[index - turn].line.pass_on(turn)
    out_sums.finish()
    for one in every[:-1]:
        one.finish()
    every[-1].finish()
    receive([swap_l, swap_back] + to_z)
    finish_own(own_share)
    mail.finish()


def backward(dp_size, shares, weights, cols, grad_mid, mid_half, out_half, gain_terms, saved, gains):
    wide = dp_size // (DEPTH * CORES)
    tokens, width = grad_mid.shape
    seq_len = HALVES * tokens
    part = shares.shape[2] // 3
    rows = width // dp_size
    half, full = jnp.bfloat16, jnp.float32
    every = sum(cols)
    kv_heads = cols[1] // gains[2].shape[1]
    head_cols = (every - cols[3]) // kv_heads
    passes = kv_heads + 2
    copies = 9 + 4 + passes * (LineReduce.slots + DEPTH * (2 * wide - 1))
    shapes = [jax.ShapeDtypeStruct((seq_len, width), half)] * 2
    shapes += [jax.ShapeDtypeStruct((8, 128), full)]
    shapes += [jax.ShapeDtypeStruct((rows, col), full) for col in cols]
    shapes += [jax.ShapeDtypeStruct((rows, DEPTH * part), half)] * 3
    lazy = [grad_mid, out_half] + [one for i, one in enumerate(saved) if i != 7]
    inputs = [grad_mid, mid_half, out_half, gain_terms, gains[0], *saved, *gains[2:]]
    return pl.pallas_call(
        functools.partial(backward_kernel, dp_size),
        out_shape=shapes,
        in_specs=[ANY] * 3 + [VMEM, ANY, VMEM, VMEM] + [ANY] * 7 + [VMEM] + [ANY] * 4 + [VMEM] * 2,
        out_specs=[VMEM] * 7 + [ANY] * 3,
        scratch_shapes=[pltpu.VMEM(one.shape, one.dtype) for one in lazy]
        + [
            pltpu.VMEM((width, every), half),
            pltpu.VMEM((kv_heads, width, head_cols), half),
            pltpu.VMEM((dp_size, 8, 128), full),
            pltpu.VMEM((dp_size, 8, 128), full),
            pltpu.VMEM((dp_size, 8, 128), full),
            pltpu.VMEM((DEPTH, wide, rows, cols[3]), half),
            pltpu.VMEM((kv_heads, DEPTH, wide, rows, head_cols), half),
            pltpu.VMEM((DEPTH, wide, 8, 128), full),
            pltpu.VMEM((wide - 1, DEPTH, rows, cols[3]), half),
            pltpu.VMEM((kv_heads, wide - 1, DEPTH, rows, head_cols), half),
            pltpu.VMEM((wide - 1, DEPTH, 8, 128), full),
            pltpu.VMEM((LineReduce.slots, rows, cols[3]), half),
            pltpu.VMEM((kv_heads, LineReduce.slots, rows, head_cols), half),
            pltpu.VMEM((LineReduce.slots, 8, 128), full),
            pltpu.VMEM((rows, 3 * part), half),
            pltpu.VMEM((seq_len, cols[0]), half),
            pltpu.VMEM((seq_len, every - cols[3]), half),
            pltpu.VMEM((seq_len, head_cols), half),
            pltpu.VMEM((width, seq_len), half),
            pltpu.VMEM((seq_len, width), full),
            pltpu.VMEM((tokens, width), half),
            pltpu.VMEM((tokens, width), half),
            pltpu.SemaphoreType.DMA((18,)),
            pltpu.SemaphoreType.DMA((copies,)),
            pltpu.SemaphoreType.DMA((copies,)),
        ],
        compiler_params=pltpu.CompilerParams(
            collective_id=2, has_side_effects=True, vmem_limit_bytes=63 * 2**20
        ),
    )(shares, weights, *inputs)


def body(
    dp_size,
    layer_in,
    seg_ids,
    w_q,
    w_k,
    w_v,
    w_o,
    w_gate,
    w_up,
    w_down,
    attn_gain,
    mlp_gain,
    q_gain,
    k_gain,
    cotangent,
):
    row_in = layer_in[0]
    row_cot = cotangent[0]
    width = row_in.shape[1]
    gains = [gain[None, :] for gain in (attn_gain, mlp_gain, q_gain, k_gain)]
    outs = forward(
        dp_size, (w_q, w_k, w_v, w_o, w_gate, w_up, w_down), row_cot, row_in, seg_ids[0], gains
    )
    attn_full, ffn_full, cots, normed, mid = outs[:5]
    saved = outs[5:]
    outs = mlp(
        dp_size, ffn_full, normed.reshape(-1, width), cots.reshape(-1, width), mid, row_cot, gains[1]
    )
    grad_mid, mid_half, out_half, gain_terms, shares = outs
    cols = [weight.shape[1] for weight in (w_q, w_k, w_v, w_o)]
    outs = backward(
        dp_size, shares, attn_full, cols, grad_mid, mid_half, out_half, gain_terms,
        [row_in] + list(saved), gains,
    )
    out_row, in_grad, sums = outs[:3]
    share = width // dp_size
    gain_outs = [sums[0, :share], sums[1, :share]]
    for i, gain in enumerate((q_gain, k_gain)):
        share = gain.shape[0] // dp_size
        gain_outs.append(lax.dynamic_slice(sums[2 + i], (lax.axis_index("dp") * share,), (share,)))
    ffn_grads = [grad.astype(jnp.float32) for grad in outs[7:]]
    return (out_row[None], in_grad[None], *outs[3:7], *ffn_grads, *gain_outs)


def solution(mesh):
    return jax.shard_map(
        functools.partial(body, mesh.shape["dp"]),
        mesh=mesh,
        in_specs=(
            P("dp", None, None),
            P("dp", None),
            P("dp", "mp"),
            P("dp", "mp"),
            P("dp", "mp"),
            P("dp", "mp"),
            P("dp", "mp"),
            P("dp", "mp"),
            P("dp", "mp"),
            P(),
            P(),
            P(),
            P(),
            P("dp", None, None),
        ),
        out_specs=(
            P("dp", None, None),
            P("dp", None, None),
            P("dp", "mp"),
            P("dp", "mp"),
            P("dp", "mp"),
            P("dp", "mp"),
            P("dp", "mp"),
            P("dp", "mp"),
            P("dp", "mp"),
            P("dp"),
            P("dp"),
            P("dp"),
            P("dp"),
        ),
        check_vma=False,
    )
```

```python
import functools
import math

import jax
import jax.numpy as jnp
from jax import lax
from jax.experimental import pallas as pl
from jax.experimental.pallas import tpu as pltpu
from jax.sharding import PartitionSpec as P

EPSILON = 1e-06
ROPE_BASE = 1000000.0
MASKED = -1e30


def matmul(left_op, right_op):
    return jnp.dot(left_op, right_op, preferred_element_type=jnp.float32)


def rms_norm(values, gain_vec):
    inv_rms = lax.rsqrt(jnp.mean(values * values, axis=-1, keepdims=True) + EPSILON)
    return (values * inv_rms * gain_vec, inv_rms)


def norm_back(grad_norm, values, inv_rms, gain_vec):
    scaled = grad_norm * gain_vec
    cubed = inv_rms * inv_rms * inv_rms
    grad_values = inv_rms * scaled - values * cubed * jnp.mean(
        scaled * values, axis=-1, keepdims=True
    )
    return (grad_values, grad_norm * values * inv_rms)


MESH = pl.DeviceIdType.MESH
ANY = pl.BlockSpec(memory_space=pl.ANY)
VMEM = pl.BlockSpec(memory_space=pltpu.VMEM)
DEPTH = 4
CORES = 2
HALVES = 2
UP, DOWN = 0, 1
TILE = 256


def split(index, size):
    size = jnp.int32(size)
    return lax.div(index, size), lax.rem(index, size)


class Place:
    def __init__(self, dp_size):
        self.wide = dp_size // (DEPTH * CORES)
        self.x = lax.axis_index("mp")
        rest, self.c = split(lax.axis_index("dp"), CORES)
        self.z, self.y = split(rest, self.wide)

    def device(self, z=None, y=None, c=None, x=None):
        z = self.z if z is None else z
        y = self.y if y is None else y
        c = self.c if c is None else c
        x = self.x if x is None else x
        return ((z * self.wide + y) * CORES + c, x)

    def z_off(self, step):
        return lax.rem(self.z + DEPTH + step, jnp.int32(DEPTH))

    def z_flip(self, bits):
        z = self.z
        if bits == DEPTH - 1:
            return DEPTH - 1 - z
        return z + bits - 2 * bits * lax.rem(lax.div(z, jnp.int32(bits)), jnp.int32(2))

    def y_off(self, step):
        return lax.rem(self.y + self.wide + step, jnp.int32(self.wide))

    def rows(self, z, y, c, count):
        return pl.ds(pl.multiple_of(((z * self.wide + y) * CORES + c) * count, count), count)

    def line(self):
        return [self.device(z=self.z_off(1)), self.device(z=self.z_off(-1))]

    def z_peers(self):
        return [self.device(z=self.z_off(k)) for k in range(1, DEPTH)]

    def y_peers(self):
        return [self.device(y=self.y_off(j)) for j in range(1, self.wide)]

    def order(self):
        low = 1 - lax.div(self.z, jnp.int32(2))
        return [3 * low, 1 + low, low * (1 - self.z) + (1 - low) * (5 - self.z), self.z]


def guarded(when, action):
    if when is None:
        action()
    else:
        pl.when(when)(action)


class Mail:
    def __init__(self, send_sems, recv_sems):
        self.send_sems, self.recv_sems = send_sems, recv_sems
        self.count = 0
        self.open = []

    def reserve(self, count):
        first = self.count
        self.count += count
        return first

    def describe(self, source, target, device, slot):
        return pltpu.make_async_remote_copy(
            source,
            target,
            self.send_sems.at[slot],
            self.recv_sems.at[slot],
            device_id=device,
            device_id_type=MESH,
        )

    def make(self, source, target, device, when=None, slot=None):
        copy = self.describe(source, target, device, self.reserve(1) if slot is None else slot)
        self.open.append((copy, when))
        return copy

    def send(self, source, target, device, when=None):
        copy = self.make(source, target, device, when)
        guarded(when, copy.start)
        return copy

    def finish(self):
        for copy, when in self.open:
            guarded(when, copy.wait_send)


def meet(devices):
    barrier = pltpu.get_barrier_semaphore()
    for device in devices:
        pl.semaphore_signal(barrier, inc=1, device_id=device, device_id_type=MESH)
    pl.semaphore_wait(barrier, len(devices))


def receive(copies):
    for copy in copies:
        copy.wait_recv()


def start_all(copies):
    for copy in copies:
        copy.start()


class LineGather:
    def __init__(self, mail, at, own, place, sides, sibling=None, share_own=True):
        self.mail, self.at, self.place = mail, at, place
        self.sides, self.sibling = sides, sibling
        self.neighbours = at.line()
        self.open_end = [at.z < DEPTH - 1, at.z > 0]
        pairs = list(zip(own, place(at.z, 0)))
        self.hops = [
            [mail.send(source, target, self.neighbours[way], self.open_end[way]) for source, target in pairs]
            for way in (UP, DOWN)
        ]
        self.over, self.cores = {}, []
        if share_own:
            self.over["own"] = [
                [mail.send(source, target, side) for source, target in pairs] for side in sides
            ]
        if sibling is not None:
            self.cores.append(
                (None, [mail.send(source, target, sibling) for source, target in pairs])
            )

    def where(self, way, step):
        z = self.at.z
        if way == UP:
            return z >= step + 1, self.at.z_off(-1 - step)
        return z + 1 + step < DEPTH, self.at.z_off(1 + step)

    def step(self, step):
        for way in (UP, DOWN):
            got, index = self.where(way, step)
            refs = self.place(index, 0)
            arrived = self.hops[way]
            onward = []
            if step < DEPTH - 2:
                more = got & self.open_end[way]
                onward = [self.mail.make(ref, ref, self.neighbours[way], more) for ref in refs]
            over = [[self.mail.make(ref, ref, side, got) for ref in refs] for side in self.sides]
            cores = []
            if self.sibling is not None:
                cores = [self.mail.make(ref, ref, self.sibling, got) for ref in refs]

            def pass_on(way=way, arrived=arrived, onward=onward, over=over, cores=cores):
                receive(arrived)
                pl.when(self.open_end[way])(lambda: start_all(onward))
                for copies in over:
                    start_all(copies)
                start_all(cores)

            pl.when(got)(pass_on)
            self.hops[way] = onward
            self.over[way, step] = over
            if cores:
                self.cores.append((got, cores))

    def side_step(self, key):
        got, index = (None, self.at.z) if key == "own" else self.where(*key)
        cores = []
        for j in range(1, len(self.sides) + 1):
            if self.sibling is not None:
                refs = self.place(index, j)
                cores += [self.mail.make(ref, ref, self.sibling, got) for ref in refs]

        def pass_on():
            for copies in self.over[key]:
                receive(copies)
            start_all(cores)

        guarded(got, pass_on)
        if cores:
            self.cores.append((got, cores))

    def side_steps(self, step):
        self.side_step((UP, step))
        self.side_step((DOWN, step))

    def finish(self):
        for got, cores in self.cores:
            guarded(got, lambda cores=cores: receive(cores))


class LineReduce:
    slots = 2 * (DEPTH - 1)

    def __init__(self, mail, at, pieces, part, land):
        self.mail, self.at, self.pieces, self.part, self.land = mail, at, pieces, part, land
        self.base = mail.reserve(self.slots * pieces)

    def copies(self, index, sources, device):
        slots = [self.base + index * self.pieces + i for i in range(self.pieces)]
        return [
            self.mail.describe(source, target, device, slot)
            for source, target, slot in zip(sources, self.land(index), slots)
        ]

    def pass_on(self, turn):
        z = self.at.z
        low = 1 - lax.div(z, jnp.int32(2))
        up = low if turn < 2 else 1 - lax.rem(z, jnp.int32(2))
        target = self.at.order()[turn]
        index = up * (target - 1) + (1 - up) * (DEPTH - 1 + target)
        device = self.at.device(z=z + 2 * up - 1)
        sources = self.part(target)
        copies = self.copies(index, sources, device)
        has_in = up * jnp.where(z > 0, 1, 0) + (1 - up) * jnp.where(z < DEPTH - 1, 1, 0)

        @pl.when(has_in > 0)
        def _():
            receive(copies)
            for source, landed in zip(sources, self.land(index)):
                add_into(source, landed)

        start_all(copies)
        self.mail.open += [(copy, None) for copy in copies]

    def last(self, use):
        z = self.at.z
        sources = self.part(z)
        for when, index, neighbour in (
            (z > 0, lax.max(z - 1, 0), self.at.z_off(-1)),
            (z < DEPTH - 1, lax.min(DEPTH - 1 + z, self.slots - 1), self.at.z_off(1)),
        ):
            copies = self.copies(index, sources, self.at.device(z=neighbour))

            @pl.when(when)
            def _(copies=copies, index=index):
                receive(copies)
                for i, landed in enumerate(self.land(index)):
                    use(i, landed)


def own_copies(pairs, sems, first=0):
    copies = [
        pltpu.make_async_copy(source, target, sems.at[first + i])
        for i, (source, target) in enumerate(pairs)
    ]
    start_all(copies)
    return copies


def finish_own(copies):
    for copy in copies:
        copy.wait()


def add_into(target, *others):
    total = target[...].astype(jnp.float32)
    for other in others:
        total = total + other[...].astype(jnp.float32)
    target[...] = total.astype(target.dtype)


def dot_nt(left_op, right_op):
    return lax.dot_general(
        left_op, right_op, (((1,), (1,)), ((), ())), preferred_element_type=jnp.float32
    )


def dot_tn(left_op, right_op):
    return lax.dot_general(
        left_op, right_op, (((0,), (0,)), ((), ())), preferred_element_type=jnp.float32
    )


def turned(values):
    return pltpu.roll(values, values.shape[-1] // 2, axis=values.ndim - 1)


def document_tables(seg_col, seg_row, head_dim):
    seq_len = seg_col.shape[0]
    rows = lax.broadcasted_iota(jnp.int32, (seq_len, seq_len), 0)
    cols = lax.broadcasted_iota(jnp.int32, (seq_len, seq_len), 1)
    same = seg_col == seg_row
    bias = jnp.where(same & (cols <= rows), 0.0, MASKED)
    before = jnp.where(same & (cols < rows), 1.0, 0.0)
    position = jnp.sum(before, axis=-1, keepdims=True)
    lane = lax.broadcasted_iota(jnp.int32, (1, head_dim), 1)
    half_dim = head_dim // 2
    slot = jnp.where(lane < half_dim, lane, lane - half_dim).astype(jnp.float32)
    frequency = jnp.exp(slot * (-2.0 * math.log(ROPE_BASE) / head_dim))
    angles = position * frequency
    sine = jnp.sin(angles)
    return bias, jnp.cos(angles), jnp.where(lane < half_dim, -sine, sine)


def matmul_tiles(left, right, write, tile=256):
    @pl.loop(0, right.shape[1] // tile)
    def _(index):
        columns = pl.ds(pl.multiple_of(index * tile, tile), tile)
        write(columns, matmul(left[...], right[:, columns]))


SAVED = 11


def forward_kernel(
    dp_size, w_q, w_k, w_v, w_o, w_g, w_u, w_d, cot, row_in, seg_col, seg_row,
    gain_one, gain_two, q_gain, k_gain,
    *refs,
):
    o_attn, o_ffn, o_c, o_n, o_mid = refs[:5]
    stored, held = refs[5 : 5 + SAVED], refs[6 + SAVED : 6 + 2 * SAVED]
    mid = refs[5 + SAVED]
    normed_one, query_raw, key_raw, values_half, queries, keys, context, log_total = held[:8]
    cosine, sine, bias = held[8:]
    full, own_part, outgoing, incoming, normed, own_sems, send_sems, recv_sems = refs[6 + 2 * SAVED :]
    at = Place(dp_size)
    z, y, c, x = at.z, at.y, at.c, at.x
    sibling, other = at.device(c=1 - c), at.device(x=1 - x)
    z_peers, y_peers = at.z_peers(), at.y_peers()
    meet([sibling, other] + z_peers + y_peers)

    mail = Mail(send_sems, recv_sems)
    rows = w_q.shape[0]
    head_dim = q_gain.shape[1]
    part = w_g.shape[1] // DEPTH
    tokens = mid.shape[0]
    here = at.rows(z, y, c, rows)
    spans, start = [], 0
    for weight in (w_q, w_k, w_v, w_o):
        spans.append(pl.ds(start, weight.shape[1]))
        start += weight.shape[1]
    q_span, k_span, v_span, o_span = spans
    ffn = [(weight, pl.ds(i * part, part)) for i, weight in enumerate((w_g, w_u, w_d))]

    def columns(index):
        return pl.ds(pl.multiple_of(index * part, part), part)

    def half_rows(index):
        return pl.ds(pl.multiple_of(index * tokens, tokens), tokens)

    mine = own_copies(
        [(weight, full.at[here, span]) for weight, span in zip((w_q, w_k, w_v, w_o), spans)],
        own_sems,
    )
    own_ffn = own_copies(
        [(weight.at[:, columns(z)], own_part.at[:, span]) for weight, span in ffn], own_sems, 4
    )
    own_cot = own_copies([(cot.at[half_rows(i)], o_c.at[z, i]) for i in range(2)], own_sems, 7)
    finish_own(mine)
    attn = LineGather(
        mail,
        at,
        (full.at[here],),
        lambda zb, j: [full.at[at.rows(zb, at.y_off(-j), c, rows)]],
        y_peers,
        sibling,
    )

    residual = row_in[...].astype(jnp.float32)
    normed_full, _ = rms_norm(residual, gain_one[...])
    normed_one[...] = normed_full.astype(jnp.bfloat16)
    bias_values, cosine[...], sine[...] = document_tables(seg_col[...], seg_row[...], head_dim)
    bias[...] = bias_values

    spread, crossing, to_sibling = {}, {}, []

    def start_spread():
        for k in range(1, DEPTH):
            target = at.z_flip(k)
            spread[k] = [
                mail.send(
                    weight.at[:, columns(target)], o_ffn.at[here, span], at.device(z=target)
                )
                for weight, span in ffn
            ]
        block = o_ffn.at[here]
        for j in range(1, at.wide):
            crossing[0, j] = mail.send(own_part, block, y_peers[j - 1])
        to_sibling.append(mail.send(own_part, block, sibling))

    def forward_spread(k):
        receive(spread[k])
        block = o_ffn.at[at.rows(at.z_flip(k), y, c, rows)]
        for j in range(1, at.wide):
            crossing[k, j] = mail.send(block, block, y_peers[j - 1])
        to_sibling.append(mail.send(block, block, sibling))

    def forward_crossing(k):
        for j in range(1, at.wide):
            crossing[k, j].wait_recv()
            block = o_ffn.at[at.rows(at.z_flip(k), at.y_off(-j), c, rows)]
            to_sibling.append(mail.send(block, block, sibling))

    def half_place(out):
        return lambda zb, j: [out.at[zb, x if j == 0 else 1 - x]]

    attn.step(0)
    finish_own(own_ffn)
    own_copy = own_copies([(own_part, o_ffn.at[here])], own_sems, 4)
    attn.side_step("own")
    attn.step(1)
    cots = LineGather(
        mail, at, (cot.at[half_rows(x)],), half_place(o_c), [other], share_own=False
    )
    attn.side_steps(0)
    attn.step(2)
    cots.step(0)
    attn.side_steps(1)
    cots.step(1)
    start_spread()
    attn.side_steps(2)
    attn.finish()
    saved = own_copies([(full, o_attn)], own_sems)

    def write_query(cols, block):
        query_raw[:, cols] = block

    def write_key(cols, block):
        key_raw[:, cols] = block

    def write_value(cols, block):
        values_half[:, cols] = block.astype(jnp.bfloat16)

    matmul_tiles(normed_one, full.at[:, q_span], write_query)
    matmul_tiles(normed_one, full.at[:, k_span], write_key)
    matmul_tiles(normed_one, full.at[:, v_span], write_value)

    def rotated(raw, gain):
        unit, _ = rms_norm(raw, gain)
        return (unit * cosine[...] + turned(unit) * sine[...]).astype(jnp.bfloat16)

    kv_heads = key_raw.shape[1] // head_dim
    group = query_raw.shape[1] // key_raw.shape[1]
    for j in range(kv_heads):
        kv_cols = pl.ds(j * head_dim, head_dim)
        keys[:, kv_cols] = rotated(key_raw[:, kv_cols], k_gain[...])
        for g in range(group):
            head = j * group + g
            cols = pl.ds(head * head_dim, head_dim)
            queries[:, cols] = rotated(query_raw[:, cols], q_gain[...])
            scores = dot_nt(queries[:, cols], keys[:, kv_cols]) * (1.0 / math.sqrt(head_dim))
            scores = scores + bias[...]
            row_max = jnp.max(scores, axis=-1, keepdims=True)
            weights = jnp.exp(scores - row_max)
            total = jnp.sum(weights, axis=-1, keepdims=True)
            log_total[:, head : head + 1] = row_max + jnp.log(total)
            probs = (weights * (1.0 / total)).astype(jnp.bfloat16)
            context[:, cols] = matmul(probs, values_half[:, kv_cols]).astype(jnp.bfloat16)
        if j == kv_heads // 2 - 1:
            cots.step(2)

    saved += own_copies(list(zip(held, stored)), own_sems, 11)
    given, kept = half_rows(1 - x), half_rows(x)
    width = row_in.shape[1]

    def project(token_rows, target):
        @pl.loop(0, width // TILE)
        def _(index):
            cols = pl.ds(pl.multiple_of(index * TILE, TILE), TILE)
            block = dot_nt(context[token_rows, :], full[cols, o_span])
            target[:, cols] = block.astype(target.dtype)

    project(given, outgoing)
    swap = mail.send(outgoing, incoming, other)
    project(kept, mid)
    swap.wait_recv()
    total = row_in[kept, :].astype(jnp.float32) + (mid[...] + incoming[...].astype(jnp.float32))
    mid[...] = total
    saved += own_copies([(mid, o_mid)], own_sems, 10)
    normed_mid, _ = rms_norm(total, gain_two[...])
    normed[...] = normed_mid.astype(jnp.bfloat16)
    last = own_copies([(normed, o_n.at[z, x])], own_sems, 9)
    strip = tokens // 2
    norms = []
    for i in range(2):
        rows_of = pl.ds(i * strip, strip)
        norms.append(
            LineGather(
                mail,
                at,
                (normed.at[rows_of],),
                lambda zb, j, rows_of=rows_of: [o_n.at[zb, x if j == 0 else 1 - x, rows_of]],
                [other],
            )
        )
    forward_spread(1)
    forward_crossing(0)
    for step in range(DEPTH - 1):
        if step < DEPTH - 2:
            forward_spread(step + 2)
        for line in norms:
            line.step(step)
        forward_crossing(step + 1)
    for step in range(DEPTH - 1):
        cots.side_steps(step)
    for line in norms:
        line.side_step("own")
        for step in range(DEPTH - 1):
            line.side_steps(step)
    receive(to_sibling)
    mail.finish()
    finish_own(saved + last + own_cot + own_copy)


def forward(dp_size, weights, cot, row_in, seg_row, gains):
    w_q, w_k, w_v, w_o, w_g, w_u, w_d = weights
    wide = dp_size // (DEPTH * CORES)
    seq_len, width = row_in.shape
    head_dim = gains[2].shape[1]
    tokens = seq_len // HALVES
    part = w_g.shape[1] // DEPTH
    half, whole = jnp.bfloat16, jnp.float32
    attn_cols = [w.shape[1] for w in (w_q, w_k, w_v, w_o)]
    shapes = [jax.ShapeDtypeStruct((width, cols), half) for cols in (sum(attn_cols), 3 * part)]
    shapes += [jax.ShapeDtypeStruct((DEPTH, HALVES, tokens, width), half)] * 2
    q_cols, kv_cols = attn_cols[0], attn_cols[1]
    for cols, kind in (
        (width, half), (q_cols, whole), (kv_cols, whole), (kv_cols, half), (q_cols, half),
        (kv_cols, half), (q_cols, half), (head_dim, whole), (head_dim, whole), (head_dim, whole),
        (seq_len, whole),
    ):
        shapes.append(jax.ShapeDtypeStruct((seq_len, cols), kind))
    shapes.insert(4, jax.ShapeDtypeStruct((tokens, width), whole))
    hops = 2 * (DEPTH - 1)
    spots = 1 + hops
    copies = (hops + spots * (2 * wide - 1)) + 3 * (2 * hops + 1) + 1
    copies += 9 + DEPTH * (2 * wide - 1)
    return pl.pallas_call(
        functools.partial(forward_kernel, dp_size),
        out_shape=shapes,
        in_specs=[ANY] * 7 + [VMEM] * 8,
        out_specs=[ANY] * (5 + SAVED),
        scratch_shapes=[pltpu.VMEM(shape.shape, shape.dtype) for shape in shapes[4:]]
        + [pltpu.VMEM((width, sum(attn_cols)), half)]
        + [pltpu.VMEM((w_g.shape[0], 3 * part), half)]
        + [pltpu.VMEM((tokens, width), half)] * 3
        + [
            pltpu.SemaphoreType.DMA((11 + SAVED,)),
            pltpu.SemaphoreType.DMA((copies,)),
            pltpu.SemaphoreType.DMA((copies,)),
        ],
        compiler_params=pltpu.CompilerParams(
            collective_id=0, has_side_effects=True, vmem_limit_bytes=56 * 2**20
        ),
    )(w_q, w_k, w_v, w_o, w_g, w_u, w_d, cot, row_in, seg_row[:, None], seg_row[None, :], *gains)


def mlp_kernel(
    dp_size, weights, n_all, c_all, a_mid, a_cot, gain,
    a_m, a_h, a_p, o_t, a_shares, d_g, d_u,
    mid, cot, o_m, o_h, shares, full, x_n, x_c, hidden, p_n, p_o, h_n, l_n, from_core, from_y,
    own_sems, send_sems, recv_sems,
):
    at = Place(dp_size)
    z, y, c, x = at.z, at.y, at.c, at.x
    other, sibling = at.device(x=1 - x), at.device(c=1 - c)
    y_peers = at.y_peers()
    order = at.order()
    tokens = mid.shape[0]
    block_rows = HALVES * tokens
    rows = from_core.shape[2]
    part = full.shape[1] // 3
    gate_up, down = pl.ds(0, 2 * part), pl.ds(2 * part, part)
    width = mid.shape[1]

    def band(index, size):
        return pl.ds(pl.multiple_of(index * size, size), size)

    loads = {}
    for i, name in enumerate("gud"):
        span = pl.ds(i * part, part)
        loads[name] = pltpu.make_async_copy(weights.at[:, span], full.at[:, span], own_sems.at[i])
    for i, index in enumerate(order):
        block = band(index, block_rows)
        loads["n", i] = pltpu.make_async_copy(n_all.at[block], x_n.at[block], own_sems.at[3 + i])
        loads["c", i] = pltpu.make_async_copy(c_all.at[block], x_c.at[block], own_sems.at[7 + i])
    for key in ("g", "u", ("n", 0), "d", ("c", 0)):
        loads[key].start()
    for i in range(1, DEPTH):
        loads["n", i].start()
        loads["c", i].start()
    late = own_copies([(a_mid, mid), (a_cot, cot)], own_sems, 11)
    meet([other, sibling] + at.z_peers() + y_peers)
    mail = Mail(send_sems, recv_sems)

    def half_rows(index, side):
        return band(index * HALVES + side, tokens)

    norm_line = LineReduce(
        mail, at, 1, lambda index: [p_n.at[half_rows(index, x)]], lambda slot: [l_n.at[slot]]
    )
    norm_swaps = []

    def compute(i):
        block = band(order[i], block_rows)
        if i == 0:
            for name in ("g", "u", "d"):
                loads[name].wait()
        loads["n", i].wait()
        loads["c", i].wait()

        @pl.loop(0, part // TILE)
        def _(index):
            g_cols, u_cols, d_cols = [
                pl.ds(pl.multiple_of(i * part + index * TILE, TILE), TILE) for i in range(3)
            ]
            gate = matmul(x_n[block, :], full[:, g_cols])
            up = matmul(x_n[block, :], full[:, u_cols])
            grad_act = matmul(x_c[block, :], full[:, d_cols])
            sigmoid_gate = 1.0 / (1.0 + jnp.exp(-gate))
            silu_val = gate * sigmoid_gate
            hidden[block, g_cols] = (
                grad_act * up * sigmoid_gate * (1.0 + gate * (1.0 - sigmoid_gate))
            ).astype(jnp.bfloat16)
            hidden[block, u_cols] = (grad_act * silu_val).astype(jnp.bfloat16)
            hidden[block, d_cols] = (silu_val * up).astype(jnp.bfloat16)

        @pl.loop(0, width // TILE)
        def _(index):
            cols = band(index, TILE)
            p_n[block, cols] = dot_nt(hidden[block, gate_up], full[cols, gate_up]).astype(jnp.bfloat16)

        norm_swaps.append(mail.send(p_n.at[half_rows(order[i], 1 - x)], h_n.at[i], other))

    def compute_out(i):
        block = band(order[i], block_rows)

        @pl.loop(0, width // TILE)
        def _(index):
            cols = band(index, TILE)
            p_o[block, cols] = dot_nt(hidden[block, down], full[cols, down]).astype(jnp.bfloat16)

        stores.extend(own_copies([(p_o.at[block], a_p.at[block])], own_sems, 7 + i))

    def norm_step(i):
        norm_swaps[i].wait_recv()
        add_into(p_n.at[half_rows(order[i], x)], h_n.at[i])
        norm_line.pass_on(i)

    def weight_grads(span, i):
        left = x_n if span is gate_up else x_c

        @pl.loop(0, width // DEPTH // TILE)
        def _(index):
            cols = pl.ds(pl.multiple_of(order[i] * (width // DEPTH) + index * TILE, TILE), TILE)
            full[cols, span] = matmul(left[:, cols].T, hidden[:, span]).astype(jnp.bfloat16)

        to_core[span.start, i] = [
            mail.send(
                full.at[at.rows(order[i], side, 1 - c, rows), span],
                from_core.at[order[i], side, :, span],
                sibling,
            )
            for side in range(at.wide)
        ]

    to_core, to_y = {}, {}

    def core_stage(span, i):
        receive(to_core[span.start, i])
        for side in range(at.wide):
            add_into(
                full.at[at.rows(order[i], side, c, rows), span], from_core.at[order[i], side, :, span]
            )
        to_y[span.start, i] = [
            mail.send(
                full.at[at.rows(order[i], at.y_off(j), c, rows), span],
                from_y.at[j - 1, order[i], :, span],
                y_peers[j - 1],
            )
            for j in range(1, at.wide)
        ]

    def y_stage(span, i):
        receive(to_y[span.start, i])
        total = full[at.rows(order[i], y, c, rows), span].astype(jnp.float32)
        for j in range(1, at.wide):
            total = total + from_y[j - 1, order[i], :, span].astype(jnp.float32)
        shares[order[i], :, span] = total.astype(jnp.bfloat16)

    spread_base = mail.reserve(2 * DEPTH)

    def spread_copies(i, source, target, device):
        return [
            pltpu.make_async_remote_copy(
                shares.at[target, :, pl.ds(w * part, part)],
                out.at[:, band(source, part)],
                mail.send_sems.at[spread_base + 2 * i + w],
                mail.recv_sems.at[spread_base + 2 * source + w],
                device_id=device,
                device_id_type=MESH,
            )
            for w, out in enumerate((d_g, d_u))
        ]

    def spread(i):
        copies = spread_copies(i, z, order[i], at.device(z=order[i]))
        start_all(copies)
        mail.open += [(copy, None) for copy in copies]

    stores = []
    compute(0)
    compute(1)
    compute(2)
    norm_step(0)
    compute(3)
    weight_grads(gate_up, 0)
    norm_step(1)
    weight_grads(gate_up, 1)
    core_stage(gate_up, 0)
    weight_grads(gate_up, 2)
    core_stage(gate_up, 1)
    norm_step(2)
    weight_grads(gate_up, 3)
    core_stage(gate_up, 2)
    compute_out(0)
    compute_out(1)
    core_stage(gate_up, 3)
    compute_out(2)
    compute_out(3)
    weight_grads(down, 0)
    weight_grads(down, 1)
    core_stage(down, 0)
    weight_grads(down, 2)
    core_stage(down, 1)
    y_stage(gate_up, 0)
    spread(0)
    weight_grads(down, 3)
    core_stage(down, 2)
    core_stage(down, 3)
    norm_swaps[3].wait_recv()
    finish_own(late)
    o_m[...] = p_n[half_rows(z, x), :].astype(jnp.float32) + h_n[3].astype(jnp.float32)

    def add_norm(_, landed):
        o_m[...] = o_m[...] + landed[...].astype(jnp.float32)

    norm_line.last(add_norm)
    grad_norm = o_m[...]
    values = mid[...]
    inv_rms = lax.rsqrt(jnp.mean(values * values, axis=-1, keepdims=True) + EPSILON)
    grad_values, terms = norm_back(grad_norm, values, inv_rms, gain[...])
    o_t[...] = jnp.sum(terms, axis=0, keepdims=True)
    kept = band(x, tokens)
    total = cot[kept, :].astype(jnp.float32) + grad_values
    o_m[...] = total
    o_h[kept, :] = total.astype(jnp.bfloat16)
    swap_h = mail.send(o_h.at[kept], o_h.at[kept], other)
    stores += own_copies([(o_m, a_m)], own_sems, 0)
    for i in range(1, DEPTH):
        y_stage(gate_up, i)
        if i < DEPTH - 1:
            spread(i)
    stores += own_copies(
        [
            (shares.at[z, :, pl.ds(w * part, part)], out.at[:, band(z, part)])
            for w, out in enumerate((d_g, d_u))
        ],
        own_sems,
        1,
    )
    for i in range(DEPTH):
        y_stage(down, i)
        stores += own_copies([(shares.at[order[i], :, down], a_shares.at[order[i]])], own_sems, 3 + i)
    swap_h.wait_recv()
    stores += own_copies([(o_h, a_h)], own_sems, 11)
    for k in range(1, DEPTH):
        source = at.z_off(-k)
        receive(spread_copies(0, source, z, at.device(z=source)))
    mail.finish()
    finish_own(stores)


def mlp(dp_size, weights, normed, cots, mid, cot, gain):
    wide = dp_size // (DEPTH * CORES)
    tokens, width = mid.shape
    cols = weights.shape[1]
    rows = width // dp_size
    every = DEPTH * HALVES * tokens
    half, full = jnp.bfloat16, jnp.float32
    copies = LineReduce.slots + DEPTH + 2 * DEPTH * (2 * wide - 1) + 1 + 2 * DEPTH
    shapes = [
        jax.ShapeDtypeStruct((tokens, width), full),
        jax.ShapeDtypeStruct((HALVES * tokens, width), half),
        jax.ShapeDtypeStruct((every, width), half),
        jax.ShapeDtypeStruct((1, width), full),
        jax.ShapeDtypeStruct((DEPTH, rows, cols // 3), half),
    ] + [jax.ShapeDtypeStruct((rows, DEPTH * cols // 3), half)] * 2
    return pl.pallas_call(
        functools.partial(mlp_kernel, dp_size),
        out_shape=shapes,
        in_specs=[ANY] * 5 + [VMEM],
        out_specs=[ANY] * 3 + [VMEM] + [ANY] * 3,
        scratch_shapes=[
            pltpu.VMEM((tokens, width), full),
            pltpu.VMEM((HALVES * tokens, width), half),
            pltpu.VMEM((tokens, width), full),
            pltpu.VMEM((HALVES * tokens, width), half),
            pltpu.VMEM((DEPTH, rows, cols), half),
        ]
        + [pltpu.VMEM((width, cols), half)]
        + [pltpu.VMEM((every, width), half)] * 2
        + [pltpu.VMEM((every, cols), half)]
        + [pltpu.VMEM((every, width), half)] * 2
        + [
            pltpu.VMEM((DEPTH, tokens, width), half),
            pltpu.VMEM((LineReduce.slots, tokens, width), half),
        ]
        + [
            pltpu.VMEM((DEPTH, wide, rows, cols), half),
            pltpu.VMEM((wide - 1, DEPTH, rows, cols), half),
            pltpu.SemaphoreType.DMA((13,)),
            pltpu.SemaphoreType.DMA((copies,)),
            pltpu.SemaphoreType.DMA((copies,)),
        ],
        compiler_params=pltpu.CompilerParams(
            collective_id=1, has_side_effects=True, vmem_limit_bytes=63 * 2**20
        ),
    )(weights, normed, cots, mid, cot, gain)


def backward_kernel(
    dp_size, shares, weights, a_mid, mid_half, a_out, a_part, t_m, gain_one, a_row, a_normed, a_query,
    a_key, a_values, a_queries, a_keys, context, a_log, a_cosine, a_sine, a_bias, q_gain, k_gain,
    o_l, o_i, sums, d_q, d_k, d_v, d_o, d_d,
    grad_mid, layer_mid, row_in, normed_one, query_raw, key_raw, values_half, queries, keys,
    log_total, cosine, sine, bias,
    full, head_grads, gains, from_other, totals, core_o, core_h, core_s, y_o, y_h, y_s, z_o, z_h, z_s,
    part_own, part_other, part_line, spare, context_grad, raw_half, raw_head, flipped, partial,
    outgoing, incoming, own_sems, send_sems, recv_sems,
):
    at = Place(dp_size)
    z, y, c, x = at.z, at.y, at.c, at.x
    other, sibling = at.device(x=1 - x), at.device(c=1 - c)
    y_peers, z_peers = at.y_peers(), at.z_peers()
    order = at.order()
    tokens, width = grad_mid.shape
    rows = d_q.shape[0]
    part = shares.shape[2]
    spans, start = [], 0
    for out in (d_q, d_k, d_v, d_o):
        spans.append(pl.ds(start, out.shape[1]))
        start += out.shape[1]
    q_span, k_span, v_span, o_span = spans
    qkv_span = pl.ds(0, start - d_o.shape[1])
    q_cols, kv_width = d_q.shape[1], d_k.shape[1]
    head_dim = q_gain.shape[1]

    def band(index, size):
        return pl.ds(pl.multiple_of(index * size, size), size)

    kept, given = band(x, tokens), band(1 - x, tokens)
    loads = own_copies(
        [(weights.at[:, span], full.at[:, span]) for span in (o_span, qkv_span)], own_sems
    )
    late = own_copies(
        [
            (a_normed, normed_one), (a_query, query_raw), (a_key, key_raw), (a_values, values_half),
            (a_queries, queries), (a_keys, keys), (a_log, log_total), (a_cosine, cosine),
            (a_sine, sine), (a_bias, bias), (a_out, layer_mid), (a_mid, grad_mid), (a_row, row_in),
        ],
        own_sems,
        2,
    )
    part_loads = own_copies(
        [(a_part.at[band(index * HALVES + x, tokens)], part_own.at[index]) for index in order],
        own_sems,
        16,
    )
    meet([other, sibling] + y_peers + z_peers)
    mail = Mail(send_sems, recv_sems)
    part_swaps = [
        mail.send(a_part.at[band(index * HALVES + 1 - x, tokens)], part_other.at[i], other)
        for i, index in enumerate(order)
    ]
    part_sums = LineReduce(
        mail, at, 1, lambda index: [part_own.at[index]], lambda slot: [part_line.at[slot]]
    )

    def part_step(i):
        part_swaps[i].wait_recv()
        part_loads[i].wait()
        add_into(part_own.at[order[i]], part_other.at[i])
        if i < DEPTH - 1:
            part_sums.pass_on(i)

    to_z = [
        mail.send(shares.at[at.z_off(k)], d_d.at[:, band(z, part)], z_peers[k - 1])
        for k in (2, 1, 3)
    ]
    kv_heads = key_raw.shape[1] // head_dim
    group = query_raw.shape[1] // key_raw.shape[1]
    q_part = group * head_dim

    def block_of(zb, side, core):
        return (zb * at.wide + side) * CORES + core

    class Sums:
        def __init__(self, held, core_land, y_land, z_land, outs):
            self.held, self.core_land, self.y_land, self.outs = held, core_land, y_land, outs
            self.line = LineReduce(
                mail, at, 1, lambda zb: [held(zb, y, c)], lambda slot: [z_land.at[slot]]
            )
            self.to_core, self.to_y = {}, {}

        def core_sends(self, i):
            self.to_core[i] = [
                mail.send(
                    self.held(order[i], side, 1 - c), self.core_land.at[order[i], side], sibling
                )
                for side in range(at.wide)
            ]

        def core_stage(self, i):
            receive(self.to_core[i])
            for side in range(at.wide):
                add_into(self.held(order[i], side, c), self.core_land.at[order[i], side])
            self.to_y[i] = [
                mail.send(
                    self.held(order[i], at.y_off(j), c), self.y_land.at[j - 1, order[i]], y_peers[j - 1]
                )
                for j in range(1, at.wide)
            ]

        def y_stage(self, i):
            receive(self.to_y[i])
            terms = [self.y_land.at[j - 1, order[i]] for j in range(1, at.wide)]
            own = self.held(order[i], y, c)
            if i < DEPTH - 1:
                add_into(own, *terms)
                return
            for out, span in self.outs:
                out[...] = own[:, span].astype(jnp.float32)
                add_into(out, *[term.at[:, span] for term in terms])

        def finish(self):
            def use(_, landed):
                for out, span in self.outs:
                    add_into(out, landed.at[:, span])

            self.line.last(use)

    out_sums = Sums(
        lambda zb, side, core: full.at[at.rows(zb, side, core, rows), o_span],
        core_o, y_o, z_o, [(d_o, pl.ds(0, d_o.shape[1]))],
    )
    head_sums = []
    for j in range(kv_heads):
        kv_cols = pl.ds(j * head_dim, head_dim)
        head_sums.append(
            Sums(
                lambda zb, side, core, j=j: head_grads.at[j, at.rows(zb, side, core, rows)],
                core_h.at[j], y_h.at[j], z_h.at[j],
                [
                    (d_q.at[:, pl.ds(j * q_part, q_part)], pl.ds(0, q_part)),
                    (d_k.at[:, kv_cols], pl.ds(q_part, head_dim)),
                    (d_v.at[:, kv_cols], pl.ds(q_part + head_dim, head_dim)),
                ],
            )
        )
    gain_sums = Sums(
        lambda zb, side, core: totals.at[block_of(zb, side, core)],
        core_s, y_s, z_s, [(sums, pl.ds(0, sums.shape[1]))],
    )

    gains[...] = jnp.zeros(gains.shape, jnp.float32)
    loads[0].wait()

    def write_context(cols, value):
        context_grad[:, cols] = value.astype(jnp.bfloat16)

    matmul_tiles(mid_half, full.at[:, o_span], write_context)

    quarter = width // DEPTH
    for i in range(DEPTH):

        @pl.loop(0, quarter // TILE)
        def _(index, i=i):
            cols = pl.ds(pl.multiple_of(order[i] * quarter + index * TILE, TILE), TILE)
            full[cols, o_span] = dot_tn(mid_half[:, cols], context[...]).astype(jnp.bfloat16)

        out_sums.core_sends(i)
    own_share = own_copies([(shares.at[z], spare)], own_sems, 15)
    for i in range(DEPTH):
        out_sums.core_stage(i)
    finish_own(late)
    finish_own(own_share)
    own_share = own_copies([(spare, d_d.at[:, band(z, part)])], own_sems, 15)
    flipped[...] = normed_one[...].T

    scale = 1.0 / math.sqrt(head_dim)

    def raw_grad(grad, raw, gain):
        back = grad * cosine[...] - turned(grad) * sine[...]
        inv_rms = lax.rsqrt(jnp.mean(raw * raw, axis=-1, keepdims=True) + EPSILON)
        grad_raw, terms = norm_back(back, raw, inv_rms, gain)
        return grad_raw.astype(jnp.bfloat16), jnp.sum(terms, axis=0, keepdims=True)

    for j in range(kv_heads):
        q_sum = jnp.zeros((1, head_dim), jnp.float32)
        k_sum = jnp.zeros((1, head_dim), jnp.float32)
        kv_cols = pl.ds(j * head_dim, head_dim)
        key_total = jnp.zeros((row_in.shape[0], head_dim), jnp.float32)
        value_total = jnp.zeros((row_in.shape[0], head_dim), jnp.float32)
        for g in range(group):
            head = j * group + g
            cols = pl.ds(head * head_dim, head_dim)
            scores = dot_nt(queries[:, cols], keys[:, kv_cols]) * scale + bias[...]
            probs = jnp.exp(scores - log_total[:, head : head + 1])
            grad_context = context_grad[:, cols]
            grad_probs = dot_nt(grad_context, values_half[:, kv_cols])
            delta = jnp.sum(
                grad_context.astype(jnp.float32) * context[:, cols].astype(jnp.float32),
                axis=-1,
                keepdims=True,
            )
            grad_scores = (probs * (grad_probs - delta) * scale).astype(jnp.bfloat16)
            grad_query, terms = raw_grad(
                matmul(grad_scores, keys[:, kv_cols]), query_raw[:, cols], q_gain[...]
            )
            raw_half[:, cols] = grad_query
            raw_head[:, pl.ds(g * head_dim, head_dim)] = grad_query
            q_sum = q_sum + terms
            key_total = key_total + dot_tn(grad_scores, queries[:, cols])
            value_total = value_total + dot_tn(probs.astype(jnp.bfloat16), grad_context)
        grad_key, terms = raw_grad(key_total, key_raw[:, kv_cols], k_gain[...])
        grad_value = value_total.astype(jnp.bfloat16)
        raw_half[:, pl.ds(q_cols + j * head_dim, head_dim)] = grad_key
        raw_half[:, pl.ds(q_cols + kv_width + j * head_dim, head_dim)] = grad_value
        raw_head[:, pl.ds(q_part, head_dim)] = grad_key
        raw_head[:, pl.ds(q_part + head_dim, head_dim)] = grad_value
        k_sum = k_sum + terms
        gains[0, 2:3, :head_dim] = gains[0, 2:3, :head_dim] + q_sum
        gains[0, 3:4, :head_dim] = gains[0, 3:4, :head_dim] + k_sum
        for i in range(DEPTH):

            @pl.loop(0, quarter // TILE)
            def _(index, i=i, j=j):
                cols = pl.ds(pl.multiple_of(order[i] * quarter + index * TILE, TILE), TILE)
                head_grads[j, cols, :] = matmul(flipped[cols, :], raw_head[...]).astype(jnp.bfloat16)

            head_sums[j].core_sends(i)
        if 1 <= j < DEPTH:
            out_sums.y_stage(j - 1)
            out_sums.line.pass_on(j - 1)
        if j == 0:
            part_step(0)
        if j == DEPTH - 2:
            part_step(1)
        if j > 0:
            for i in range(DEPTH):
                head_sums[j - 1].core_stage(i)
    for j in range(max(kv_heads - 1, 0), DEPTH - 1):
        out_sums.y_stage(j)
        out_sums.line.pass_on(j)
    out_sums.y_stage(DEPTH - 1)
    for i in range(DEPTH):
        head_sums[kv_heads - 1].core_stage(i)
    finish_own(loads[1:])

    def project(token_rows, target):
        @pl.loop(0, width // TILE)
        def _(index):
            cols = band(index, TILE)
            total = dot_nt(raw_half[token_rows, :], full[cols, qkv_span])
            partial[token_rows, cols] = total
            if target is not None:
                target[:, cols] = total.astype(target.dtype)

    project(given, outgoing)
    swap = mail.send(outgoing, incoming, other)
    project(kept, None)

    values = row_in[...].astype(jnp.float32)
    inv_rms = lax.rsqrt(jnp.mean(values * values, axis=-1, keepdims=True) + EPSILON)
    gain_terms = jnp.sum(partial[...] * values * inv_rms, axis=0, keepdims=True)
    blocks = gains.shape[0]
    share = width // blocks
    head_terms = gains[0, 2:4, :]
    for index in range(blocks):
        gains[index, 0:1, :share] = gain_terms[:, index * share : (index + 1) * share]
        gains[index, 1:2, :share] = t_m[:, index * share : (index + 1) * share]
        gains[index, 2:4, :] = head_terms
    swap_gains = mail.send(gains, from_other, other)
    swap.wait_recv()
    grad_norm = partial[kept, :] + incoming[...].astype(jnp.float32)
    values = row_in[kept, :].astype(jnp.float32)
    inv_rms = lax.rsqrt(jnp.mean(values * values, axis=-1, keepdims=True) + EPSILON)
    grad_values, _ = norm_back(grad_norm, values, inv_rms, gain_one[...])
    o_i[kept, :] = (grad_mid[...] + grad_values).astype(jnp.bfloat16)
    swap_back = mail.send(o_i.at[kept], o_i.at[kept], other)

    if kv_heads < DEPTH - 1:
        part_step(1)
    part_step(2)
    swap_gains.wait_recv()
    totals[...] = gains[...] + from_other[...]
    for i in range(DEPTH):
        gain_sums.core_sends(i)
    for i in range(DEPTH):
        gain_sums.core_stage(i)
    every = head_sums + [gain_sums]
    part_step(3)
    for index in range(len(every) + DEPTH - 2):
        if index < len(every):
            for i in range(DEPTH):
                every[index].y_stage(i)
        for turn in range(DEPTH - 1):
            if 0 <= index - turn < len(every):
                every[index - turn].line.pass_on(turn)
    out_sums.finish()
    layer_mid[...] = layer_mid[...] + part_own[z].astype(jnp.float32)

    def add_part(_, landed):
        layer_mid[...] = layer_mid[...] + landed[...].astype(jnp.float32)

    part_sums.last(add_part)
    o_l[kept, :] = layer_mid[...].astype(jnp.bfloat16)
    swap_l = mail.send(o_l.at[kept], o_l.at[kept], other)
    for one in every[:-1]:
        one.finish()
    every[-1].finish()
    receive([swap_l, swap_back] + to_z)
    finish_own(own_share)
    mail.finish()


def backward(dp_size, shares, weights, cols, grad_mid, mid_half, layer_mid, part_out, gain_terms, saved, gains):
    wide = dp_size // (DEPTH * CORES)
    tokens, width = grad_mid.shape
    seq_len = HALVES * tokens
    part = shares.shape[2]
    rows = width // dp_size
    half, full = jnp.bfloat16, jnp.float32
    every = sum(cols)
    kv_heads = cols[1] // gains[2].shape[1]
    head_cols = (every - cols[3]) // kv_heads
    passes = kv_heads + 2
    copies = 3 + 4 + DEPTH + LineReduce.slots + passes * (LineReduce.slots + DEPTH * (2 * wide - 1))
    shapes = [jax.ShapeDtypeStruct((seq_len, width), half)] * 2
    shapes += [jax.ShapeDtypeStruct((8, 128), full)]
    shapes += [jax.ShapeDtypeStruct((rows, col), full) for col in cols]
    shapes += [jax.ShapeDtypeStruct((rows, DEPTH * part), half)]
    lazy = [grad_mid, layer_mid] + [one for i, one in enumerate(saved) if i != 7]
    inputs = [grad_mid, mid_half, layer_mid, part_out, gain_terms, gains[0], *saved, *gains[2:]]
    return pl.pallas_call(
        functools.partial(backward_kernel, dp_size),
        out_shape=shapes,
        in_specs=[ANY] * 3 + [VMEM, ANY, ANY, VMEM, VMEM] + [ANY] * 7 + [VMEM] + [ANY] * 4 + [VMEM] * 2,
        out_specs=[VMEM] * 7 + [ANY],
        scratch_shapes=[pltpu.VMEM(one.shape, one.dtype) for one in lazy]
        + [
            pltpu.VMEM((width, every), half),
            pltpu.VMEM((kv_heads, width, head_cols), half),
            pltpu.VMEM((dp_size, 8, 128), full),
            pltpu.VMEM((dp_size, 8, 128), full),
            pltpu.VMEM((dp_size, 8, 128), full),
            pltpu.VMEM((DEPTH, wide, rows, cols[3]), half),
            pltpu.VMEM((kv_heads, DEPTH, wide, rows, head_cols), half),
            pltpu.VMEM((DEPTH, wide, 8, 128), full),
            pltpu.VMEM((wide - 1, DEPTH, rows, cols[3]), half),
            pltpu.VMEM((kv_heads, wide - 1, DEPTH, rows, head_cols), half),
            pltpu.VMEM((wide - 1, DEPTH, 8, 128), full),
            pltpu.VMEM((LineReduce.slots, rows, cols[3]), half),
            pltpu.VMEM((kv_heads, LineReduce.slots, rows, head_cols), half),
            pltpu.VMEM((LineReduce.slots, 8, 128), full),
            pltpu.VMEM((DEPTH, tokens, width), half),
            pltpu.VMEM((DEPTH, tokens, width), half),
            pltpu.VMEM((LineReduce.slots, tokens, width), half),
            pltpu.VMEM((rows, part), half),
            pltpu.VMEM((seq_len, cols[0]), half),
            pltpu.VMEM((seq_len, every - cols[3]), half),
            pltpu.VMEM((seq_len, head_cols), half),
            pltpu.VMEM((width, seq_len), half),
            pltpu.VMEM((seq_len, width), full),
            pltpu.VMEM((tokens, width), half),
            pltpu.VMEM((tokens, width), half),
            pltpu.SemaphoreType.DMA((20,)),
            pltpu.SemaphoreType.DMA((copies,)),
            pltpu.SemaphoreType.DMA((copies,)),
        ],
        compiler_params=pltpu.CompilerParams(
            collective_id=2, has_side_effects=True, vmem_limit_bytes=63 * 2**20
        ),
    )(shares, weights, *inputs)


def body(
    dp_size,
    layer_in,
    seg_ids,
    w_q,
    w_k,
    w_v,
    w_o,
    w_gate,
    w_up,
    w_down,
    attn_gain,
    mlp_gain,
    q_gain,
    k_gain,
    cotangent,
):
    row_in = layer_in[0]
    row_cot = cotangent[0]
    width = row_in.shape[1]
    gains = [gain[None, :] for gain in (attn_gain, mlp_gain, q_gain, k_gain)]
    outs = forward(
        dp_size, (w_q, w_k, w_v, w_o, w_gate, w_up, w_down), row_cot, row_in, seg_ids[0], gains
    )
    attn_full, ffn_full, cots, normed, mid = outs[:5]
    saved = outs[5:]
    outs = mlp(
        dp_size, ffn_full, normed.reshape(-1, width), cots.reshape(-1, width), mid, row_cot, gains[1]
    )
    grad_mid, mid_half, part_out, gain_terms, shares, *gate_up_grads = outs
    cols = [weight.shape[1] for weight in (w_q, w_k, w_v, w_o)]
    outs = backward(
        dp_size, shares, attn_full, cols, grad_mid, mid_half, mid, part_out, gain_terms,
        [row_in] + list(saved), gains,
    )
    out_row, in_grad, sums = outs[:3]
    share = width // dp_size
    gain_outs = [sums[0, :share], sums[1, :share]]
    for i, gain in enumerate((q_gain, k_gain)):
        share = gain.shape[0] // dp_size
        gain_outs.append(lax.dynamic_slice(sums[2 + i], (lax.axis_index("dp") * share,), (share,)))
    ffn_grads = [grad.astype(jnp.float32) for grad in (*gate_up_grads, outs[7])]
    return (out_row[None], in_grad[None], *outs[3:7], *ffn_grads, *gain_outs)


def solution(mesh):
    return jax.shard_map(
        functools.partial(body, mesh.shape["dp"]),
        mesh=mesh,
        in_specs=(
            P("dp", None, None),
            P("dp", None),
            P("dp", "mp"),
            P("dp", "mp"),
            P("dp", "mp"),
            P("dp", "mp"),
            P("dp", "mp"),
            P("dp", "mp"),
            P("dp", "mp"),
            P(),
            P(),
            P(),
            P(),
            P("dp", None, None),
        ),
        out_specs=(
            P("dp", None, None),
            P("dp", None, None),
            P("dp", "mp"),
            P("dp", "mp"),
            P("dp", "mp"),
            P("dp", "mp"),
            P("dp", "mp"),
            P("dp", "mp"),
            P("dp", "mp"),
            P("dp"),
            P("dp"),
            P("dp"),
            P("dp"),
        ),
        check_vma=False,
    )
```

```python
import functools
import math

import jax
import jax.numpy as jnp
from jax import lax
from jax.experimental import pallas as pl
from jax.experimental.pallas import tpu as pltpu
from jax.sharding import PartitionSpec as P

EPSILON = 1e-06
ROPE_BASE = 1000000.0
MASKED = -1e30


def matmul(left_op, right_op):
    return jnp.dot(left_op, right_op, preferred_element_type=jnp.float32)


def rms_norm(values, gain_vec):
    inv_rms = lax.rsqrt(jnp.mean(values * values, axis=-1, keepdims=True) + EPSILON)
    return (values * inv_rms * gain_vec, inv_rms)


def norm_back(grad_norm, values, inv_rms, gain_vec):
    scaled = grad_norm * gain_vec
    cubed = inv_rms * inv_rms * inv_rms
    grad_values = inv_rms * scaled - values * cubed * jnp.mean(
        scaled * values, axis=-1, keepdims=True
    )
    return (grad_values, grad_norm * values * inv_rms)


MESH = pl.DeviceIdType.MESH
ANY = pl.BlockSpec(memory_space=pl.ANY)
VMEM = pl.BlockSpec(memory_space=pltpu.VMEM)
DEPTH = 4
CORES = 2
HALVES = 2
UP, DOWN = 0, 1
TILE = 256


def split(index, size):
    size = jnp.int32(size)
    return lax.div(index, size), lax.rem(index, size)


class Place:
    def __init__(self, dp_size):
        self.wide = dp_size // (DEPTH * CORES)
        self.x = lax.axis_index("mp")
        rest, self.c = split(lax.axis_index("dp"), CORES)
        self.z, self.y = split(rest, self.wide)

    def device(self, z=None, y=None, c=None, x=None):
        z = self.z if z is None else z
        y = self.y if y is None else y
        c = self.c if c is None else c
        x = self.x if x is None else x
        return ((z * self.wide + y) * CORES + c, x)

    def z_off(self, step):
        return lax.rem(self.z + DEPTH + step, jnp.int32(DEPTH))

    def z_flip(self, bits):
        z = self.z
        if bits == DEPTH - 1:
            return DEPTH - 1 - z
        return z + bits - 2 * bits * lax.rem(lax.div(z, jnp.int32(bits)), jnp.int32(2))

    def y_off(self, step):
        return lax.rem(self.y + self.wide + step, jnp.int32(self.wide))

    def rows(self, z, y, c, count):
        return pl.ds(pl.multiple_of(((z * self.wide + y) * CORES + c) * count, count), count)

    def line(self):
        return [self.device(z=self.z_off(1)), self.device(z=self.z_off(-1))]

    def z_peers(self):
        return [self.device(z=self.z_off(k)) for k in range(1, DEPTH)]

    def y_peers(self):
        return [self.device(y=self.y_off(j)) for j in range(1, self.wide)]

    def order(self):
        low = 1 - lax.div(self.z, jnp.int32(2))
        return [3 * low, 1 + low, low * (1 - self.z) + (1 - low) * (5 - self.z), self.z]


def guarded(when, action):
    if when is None:
        action()
    else:
        pl.when(when)(action)


class Mail:
    def __init__(self, send_sems, recv_sems):
        self.send_sems, self.recv_sems = send_sems, recv_sems
        self.count = 0
        self.open = []

    def reserve(self, count):
        first = self.count
        self.count += count
        return first

    def describe(self, source, target, device, slot):
        return pltpu.make_async_remote_copy(
            source,
            target,
            self.send_sems.at[slot],
            self.recv_sems.at[slot],
            device_id=device,
            device_id_type=MESH,
        )

    def make(self, source, target, device, when=None, slot=None):
        copy = self.describe(source, target, device, self.reserve(1) if slot is None else slot)
        self.open.append((copy, when))
        return copy

    def send(self, source, target, device, when=None):
        copy = self.make(source, target, device, when)
        guarded(when, copy.start)
        return copy

    def finish(self):
        for copy, when in self.open:
            guarded(when, copy.wait_send)


def meet(devices):
    barrier = pltpu.get_barrier_semaphore()
    for device in devices:
        pl.semaphore_signal(barrier, inc=1, device_id=device, device_id_type=MESH)
    pl.semaphore_wait(barrier, len(devices))


def receive(copies):
    for copy in copies:
        copy.wait_recv()


def start_all(copies):
    for copy in copies:
        copy.start()


class LineGather:
    def __init__(self, mail, at, own, place, sides, sibling=None, share_own=True):
        self.mail, self.at, self.place = mail, at, place
        self.sides, self.sibling = sides, sibling
        self.neighbours = at.line()
        self.open_end = [at.z < DEPTH - 1, at.z > 0]
        pairs = list(zip(own, place(at.z, 0)))
        self.hops = [
            [mail.send(source, target, self.neighbours[way], self.open_end[way]) for source, target in pairs]
            for way in (UP, DOWN)
        ]
        self.over, self.cores = {}, []
        if share_own:
            self.over["own"] = [
                [mail.send(source, target, side) for source, target in pairs] for side in sides
            ]
        if sibling is not None:
            self.cores.append(
                (None, [mail.send(source, target, sibling) for source, target in pairs])
            )

    def where(self, way, step):
        z = self.at.z
        if way == UP:
            return z >= step + 1, self.at.z_off(-1 - step)
        return z + 1 + step < DEPTH, self.at.z_off(1 + step)

    def step(self, step):
        for way in (UP, DOWN):
            got, index = self.where(way, step)
            refs = self.place(index, 0)
            arrived = self.hops[way]
            onward = []
            if step < DEPTH - 2:
                more = got & self.open_end[way]
                onward = [self.mail.make(ref, ref, self.neighbours[way], more) for ref in refs]
            over = [[self.mail.make(ref, ref, side, got) for ref in refs] for side in self.sides]
            cores = []
            if self.sibling is not None:
                cores = [self.mail.make(ref, ref, self.sibling, got) for ref in refs]

            def pass_on(way=way, arrived=arrived, onward=onward, over=over, cores=cores):
                receive(arrived)
                pl.when(self.open_end[way])(lambda: start_all(onward))
                for copies in over:
                    start_all(copies)
                start_all(cores)

            pl.when(got)(pass_on)
            self.hops[way] = onward
            self.over[way, step] = over
            if cores:
                self.cores.append((got, cores))

    def side_step(self, key):
        got, index = (None, self.at.z) if key == "own" else self.where(*key)
        cores = []
        for j in range(1, len(self.sides) + 1):
            if self.sibling is not None:
                refs = self.place(index, j)
                cores += [self.mail.make(ref, ref, self.sibling, got) for ref in refs]

        def pass_on():
            for copies in self.over[key]:
                receive(copies)
            start_all(cores)

        guarded(got, pass_on)
        if cores:
            self.cores.append((got, cores))

    def side_steps(self, step):
        self.side_step((UP, step))
        self.side_step((DOWN, step))

    def finish(self):
        for got, cores in self.cores:
            guarded(got, lambda cores=cores: receive(cores))


class LineReduce:
    slots = 2 * (DEPTH - 1)

    def __init__(self, mail, at, pieces, part, land):
        self.mail, self.at, self.pieces, self.part, self.land = mail, at, pieces, part, land
        self.base = mail.reserve(self.slots * pieces)

    def copies(self, index, sources, device):
        slots = [self.base + index * self.pieces + i for i in range(self.pieces)]
        return [
            self.mail.describe(source, target, device, slot)
            for source, target, slot in zip(sources, self.land(index), slots)
        ]

    def pass_on(self, turn, part=None):
        z = self.at.z
        low = 1 - lax.div(z, jnp.int32(2))
        up = low if turn < 2 else 1 - lax.rem(z, jnp.int32(2))
        target = self.at.order()[turn]
        index = up * (target - 1) + (1 - up) * (DEPTH - 1 + target)
        device = self.at.device(z=z + 2 * up - 1)
        sources = self.part(target)
        copies = self.copies(index, sources, device)
        has_in = up * jnp.where(z > 0, 1, 0) + (1 - up) * jnp.where(z < DEPTH - 1, 1, 0)

        if part != 0:

            @pl.when(has_in > 0)
            def _():
                receive(copies)
                for source, landed in zip(sources, self.land(index)):
                    add_into(source, landed)
                if part == 1:
                    start_all(copies)

        if part == 0:
            pl.when(has_in == 0)(lambda: start_all(copies))
        elif part is None:
            start_all(copies)
        if part != 1:
            self.mail.open += [(copy, None) for copy in copies]

    def last(self, use):
        z = self.at.z
        sources = self.part(z)
        for when, index, neighbour in (
            (z > 0, lax.max(z - 1, 0), self.at.z_off(-1)),
            (z < DEPTH - 1, lax.min(DEPTH - 1 + z, self.slots - 1), self.at.z_off(1)),
        ):
            copies = self.copies(index, sources, self.at.device(z=neighbour))

            @pl.when(when)
            def _(copies=copies, index=index):
                receive(copies)
                for i, landed in enumerate(self.land(index)):
                    use(i, landed)


def own_copies(pairs, sems, first=0):
    copies = [
        pltpu.make_async_copy(source, target, sems.at[first + i])
        for i, (source, target) in enumerate(pairs)
    ]
    start_all(copies)
    return copies


def finish_own(copies):
    for copy in copies:
        copy.wait()


def add_into(target, *others):
    total = target[...].astype(jnp.float32)
    for other in others:
        total = total + other[...].astype(jnp.float32)
    target[...] = total.astype(target.dtype)


def dot_nt(left_op, right_op):
    return lax.dot_general(
        left_op, right_op, (((1,), (1,)), ((), ())), preferred_element_type=jnp.float32
    )


def dot_tn(left_op, right_op):
    return lax.dot_general(
        left_op, right_op, (((0,), (0,)), ((), ())), preferred_element_type=jnp.float32
    )


def turned(values):
    return pltpu.roll(values, values.shape[-1] // 2, axis=values.ndim - 1)


def document_tables(seg_col, seg_row, head_dim):
    seq_len = seg_col.shape[0]
    rows = lax.broadcasted_iota(jnp.int32, (seq_len, seq_len), 0)
    cols = lax.broadcasted_iota(jnp.int32, (seq_len, seq_len), 1)
    same = seg_col == seg_row
    bias = jnp.where(same & (cols <= rows), 0.0, MASKED)
    before = jnp.where(same & (cols < rows), 1.0, 0.0)
    position = jnp.sum(before, axis=-1, keepdims=True)
    lane = lax.broadcasted_iota(jnp.int32, (1, head_dim), 1)
    half_dim = head_dim // 2
    slot = jnp.where(lane < half_dim, lane, lane - half_dim).astype(jnp.float32)
    frequency = jnp.exp(slot * (-2.0 * math.log(ROPE_BASE) / head_dim))
    angles = position * frequency
    sine = jnp.sin(angles)
    return bias, jnp.cos(angles), jnp.where(lane < half_dim, -sine, sine)


def matmul_tiles(left, right, write, tile=256):
    @pl.loop(0, right.shape[1] // tile)
    def _(index):
        columns = pl.ds(pl.multiple_of(index * tile, tile), tile)
        write(columns, matmul(left[...], right[:, columns]))


SAVED = 11


def forward_kernel(
    dp_size, w_q, w_k, w_v, w_o, w_g, w_u, w_d, cot, row_in, seg_col, seg_row,
    gain_one, gain_two, q_gain, k_gain,
    *refs,
):
    o_attn, o_ffn, o_c, o_n, o_mid = refs[:5]
    stored, held = refs[5 : 5 + SAVED], refs[6 + SAVED : 6 + 2 * SAVED]
    mid = refs[5 + SAVED]
    normed_one, query_raw, key_raw, values_half, queries, keys, context, log_total = held[:8]
    cosine, sine, bias = held[8:]
    full, own_part, outgoing, incoming, normed, own_sems, send_sems, recv_sems = refs[6 + 2 * SAVED :]
    at = Place(dp_size)
    z, y, c, x = at.z, at.y, at.c, at.x
    sibling, other = at.device(c=1 - c), at.device(x=1 - x)
    z_peers, y_peers = at.z_peers(), at.y_peers()
    meet([sibling, other] + z_peers + y_peers)

    mail = Mail(send_sems, recv_sems)
    rows = w_q.shape[0]
    head_dim = q_gain.shape[1]
    part = w_g.shape[1] // DEPTH
    tokens = mid.shape[0]
    here = at.rows(z, y, c, rows)
    spans, start = [], 0
    for weight in (w_q, w_k, w_v, w_o):
        spans.append(pl.ds(start, weight.shape[1]))
        start += weight.shape[1]
    q_span, k_span, v_span, o_span = spans
    ffn = [(weight, pl.ds(i * part, part)) for i, weight in enumerate((w_g, w_u, w_d))]

    def columns(index):
        return pl.ds(pl.multiple_of(index * part, part), part)

    def half_rows(index):
        return pl.ds(pl.multiple_of(index * tokens, tokens), tokens)

    mine = own_copies(
        [(weight, full.at[here, span]) for weight, span in zip((w_q, w_k, w_v, w_o), spans)],
        own_sems,
    )
    own_ffn = own_copies(
        [(weight.at[:, columns(z)], own_part.at[:, span]) for weight, span in ffn], own_sems, 4
    )
    own_cot = own_copies([(cot.at[half_rows(i)], o_c.at[z, i]) for i in range(2)], own_sems, 7)
    finish_own(mine)
    attn = LineGather(
        mail,
        at,
        (full.at[here],),
        lambda zb, j: [full.at[at.rows(zb, at.y_off(-j), c, rows)]],
        y_peers,
        sibling,
    )

    residual = row_in[...].astype(jnp.float32)
    normed_full, _ = rms_norm(residual, gain_one[...])
    normed_one[...] = normed_full.astype(jnp.bfloat16)
    bias_values, cosine[...], sine[...] = document_tables(seg_col[...], seg_row[...], head_dim)
    bias[...] = bias_values

    spread, crossing, to_sibling = {}, {}, []

    def start_spread():
        for k in range(1, DEPTH):
            target = at.z_flip(k)
            spread[k] = [
                mail.send(
                    weight.at[:, columns(target)], o_ffn.at[here, span], at.device(z=target)
                )
                for weight, span in ffn
            ]
        block = o_ffn.at[here]
        for j in range(1, at.wide):
            crossing[0, j] = mail.send(own_part, block, y_peers[j - 1])
        to_sibling.append(mail.send(own_part, block, sibling))

    def forward_spread(k):
        receive(spread[k])
        block = o_ffn.at[at.rows(at.z_flip(k), y, c, rows)]
        for j in range(1, at.wide):
            crossing[k, j] = mail.send(block, block, y_peers[j - 1])
        to_sibling.append(mail.send(block, block, sibling))

    def forward_crossing(k):
        for j in range(1, at.wide):
            crossing[k, j].wait_recv()
            block = o_ffn.at[at.rows(at.z_flip(k), at.y_off(-j), c, rows)]
            to_sibling.append(mail.send(block, block, sibling))

    def half_place(out):
        return lambda zb, j: [out.at[zb, x if j == 0 else 1 - x]]

    attn.step(0)
    finish_own(own_ffn)
    own_copy = own_copies([(own_part, o_ffn.at[here])], own_sems, 4)
    attn.side_step("own")
    attn.step(1)
    cots = LineGather(
        mail, at, (cot.at[half_rows(x)],), half_place(o_c), [other], share_own=False
    )
    attn.side_steps(0)
    attn.step(2)
    cots.step(0)
    attn.side_steps(1)
    cots.step(1)
    start_spread()
    attn.side_steps(2)
    attn.finish()
    saved = own_copies([(full, o_attn)], own_sems)

    def write_query(cols, block):
        query_raw[:, cols] = block

    def write_key(cols, block):
        key_raw[:, cols] = block

    def write_value(cols, block):
        values_half[:, cols] = block.astype(jnp.bfloat16)

    matmul_tiles(normed_one, full.at[:, q_span], write_query)
    matmul_tiles(normed_one, full.at[:, k_span], write_key)
    matmul_tiles(normed_one, full.at[:, v_span], write_value)

    def rotated(raw, gain):
        unit, _ = rms_norm(raw, gain)
        return (unit * cosine[...] + turned(unit) * sine[...]).astype(jnp.bfloat16)

    kv_heads = key_raw.shape[1] // head_dim
    group = query_raw.shape[1] // key_raw.shape[1]
    for j in range(kv_heads):
        kv_cols = pl.ds(j * head_dim, head_dim)
        keys[:, kv_cols] = rotated(key_raw[:, kv_cols], k_gain[...])
        for g in range(group):
            head = j * group + g
            cols = pl.ds(head * head_dim, head_dim)
            queries[:, cols] = rotated(query_raw[:, cols], q_gain[...])
            scores = dot_nt(queries[:, cols], keys[:, kv_cols]) * (1.0 / math.sqrt(head_dim))
            scores = scores + bias[...]
            row_max = jnp.max(scores, axis=-1, keepdims=True)
            weights = jnp.exp(scores - row_max)
            total = jnp.sum(weights, axis=-1, keepdims=True)
            log_total[:, head : head + 1] = row_max + jnp.log(total)
            probs = (weights * (1.0 / total)).astype(jnp.bfloat16)
            context[:, cols] = matmul(probs, values_half[:, kv_cols]).astype(jnp.bfloat16)
        if j == kv_heads // 2 - 1:
            cots.step(2)

    saved += own_copies(list(zip(held, stored)), own_sems, 11)
    given, kept = half_rows(1 - x), half_rows(x)
    width = row_in.shape[1]

    def project(token_rows, target):
        @pl.loop(0, width // TILE)
        def _(index):
            cols = pl.ds(pl.multiple_of(index * TILE, TILE), TILE)
            block = dot_nt(context[token_rows, :], full[cols, o_span])
            target[:, cols] = block.astype(target.dtype)

    project(given, outgoing)
    swap = mail.send(outgoing, incoming, other)
    project(kept, mid)
    swap.wait_recv()
    total = row_in[kept, :].astype(jnp.float32) + (mid[...] + incoming[...].astype(jnp.float32))
    mid[...] = total
    saved += own_copies([(mid, o_mid)], own_sems, 10)
    normed_mid, _ = rms_norm(total, gain_two[...])
    normed[...] = normed_mid.astype(jnp.bfloat16)
    last = own_copies([(normed, o_n.at[z, x])], own_sems, 9)
    strip = tokens // 2
    norms = []
    for i in range(2):
        rows_of = pl.ds(i * strip, strip)
        norms.append(
            LineGather(
                mail,
                at,
                (normed.at[rows_of],),
                lambda zb, j, rows_of=rows_of: [o_n.at[zb, x if j == 0 else 1 - x, rows_of]],
                [other],
            )
        )
    forward_spread(1)
    forward_crossing(0)
    for step in range(DEPTH - 1):
        if step < DEPTH - 2:
            forward_spread(step + 2)
        for line in norms:
            line.step(step)
        forward_crossing(step + 1)
    for step in range(DEPTH - 1):
        cots.side_steps(step)
    for line in norms:
        line.side_step("own")
        for step in range(DEPTH - 1):
            line.side_steps(step)
    receive(to_sibling)
    mail.finish()
    finish_own(saved + last + own_cot + own_copy)


def forward(dp_size, weights, cot, row_in, seg_row, gains):
    w_q, w_k, w_v, w_o, w_g, w_u, w_d = weights
    wide = dp_size // (DEPTH * CORES)
    seq_len, width = row_in.shape
    head_dim = gains[2].shape[1]
    tokens = seq_len // HALVES
    part = w_g.shape[1] // DEPTH
    half, whole = jnp.bfloat16, jnp.float32
    attn_cols = [w.shape[1] for w in (w_q, w_k, w_v, w_o)]
    shapes = [jax.ShapeDtypeStruct((width, cols), half) for cols in (sum(attn_cols), 3 * part)]
    shapes += [jax.ShapeDtypeStruct((DEPTH, HALVES, tokens, width), half)] * 2
    q_cols, kv_cols = attn_cols[0], attn_cols[1]
    for cols, kind in (
        (width, half), (q_cols, whole), (kv_cols, whole), (kv_cols, half), (q_cols, half),
        (kv_cols, half), (q_cols, half), (head_dim, whole), (head_dim, whole), (head_dim, whole),
        (seq_len, whole),
    ):
        shapes.append(jax.ShapeDtypeStruct((seq_len, cols), kind))
    shapes.insert(4, jax.ShapeDtypeStruct((tokens, width), whole))
    hops = 2 * (DEPTH - 1)
    spots = 1 + hops
    copies = (hops + spots * (2 * wide - 1)) + 3 * (2 * hops + 1) + 1
    copies += 9 + DEPTH * (2 * wide - 1)
    return pl.pallas_call(
        functools.partial(forward_kernel, dp_size),
        out_shape=shapes,
        in_specs=[ANY] * 7 + [VMEM] * 8,
        out_specs=[ANY] * (5 + SAVED),
        scratch_shapes=[pltpu.VMEM(shape.shape, shape.dtype) for shape in shapes[4:]]
        + [pltpu.VMEM((width, sum(attn_cols)), half)]
        + [pltpu.VMEM((w_g.shape[0], 3 * part), half)]
        + [pltpu.VMEM((tokens, width), half)] * 3
        + [
            pltpu.SemaphoreType.DMA((11 + SAVED,)),
            pltpu.SemaphoreType.DMA((copies,)),
            pltpu.SemaphoreType.DMA((copies,)),
        ],
        compiler_params=pltpu.CompilerParams(
            collective_id=0, has_side_effects=True, vmem_limit_bytes=56 * 2**20
        ),
    )(w_q, w_k, w_v, w_o, w_g, w_u, w_d, cot, row_in, seg_row[:, None], seg_row[None, :], *gains)


def mlp_kernel(
    dp_size, weights, n_all, c_all, a_mid, a_cot, gain,
    a_m, a_h, a_p, o_t, a_shares, d_g, d_u,
    mid, cot, o_m, o_h, shares, full, x_n, x_c, hidden, p_n, p_o, h_n, l_n, from_core, from_y,
    own_sems, send_sems, recv_sems,
):
    at = Place(dp_size)
    z, y, c, x = at.z, at.y, at.c, at.x
    other, sibling = at.device(x=1 - x), at.device(c=1 - c)
    y_peers = at.y_peers()
    order = at.order()
    tokens = mid.shape[0]
    block_rows = HALVES * tokens
    rows = from_core.shape[2]
    part = full.shape[1] // 3
    gate_up, down = pl.ds(0, 2 * part), pl.ds(2 * part, part)
    width = mid.shape[1]

    def band(index, size):
        return pl.ds(pl.multiple_of(index * size, size), size)

    loads = {}
    for i, name in enumerate("gud"):
        span = pl.ds(i * part, part)
        loads[name] = pltpu.make_async_copy(weights.at[:, span], full.at[:, span], own_sems.at[i])
    for i, index in enumerate(order):
        block = band(index, block_rows)
        loads["n", i] = pltpu.make_async_copy(n_all.at[block], x_n.at[block], own_sems.at[3 + i])
        loads["c", i] = pltpu.make_async_copy(c_all.at[block], x_c.at[block], own_sems.at[7 + i])
    for key in ("g", "u", ("n", 0), "d", ("c", 0)):
        loads[key].start()
    for i in range(1, DEPTH):
        loads["n", i].start()
        loads["c", i].start()
    late = own_copies([(a_mid, mid), (a_cot, cot)], own_sems, 11)
    meet([other, sibling] + at.z_peers() + y_peers)
    mail = Mail(send_sems, recv_sems)

    def half_rows(index, side):
        return band(index * HALVES + side, tokens)

    norm_line = LineReduce(
        mail, at, 1, lambda index: [p_n.at[half_rows(index, x)]], lambda slot: [l_n.at[slot]]
    )
    norm_swaps = []

    def compute(i):
        block = band(order[i], block_rows)
        if i == 0:
            for name in ("g", "u", "d"):
                loads[name].wait()
        loads["n", i].wait()
        loads["c", i].wait()

        @pl.loop(0, part // TILE)
        def _(index):
            g_cols, u_cols, d_cols = [
                pl.ds(pl.multiple_of(i * part + index * TILE, TILE), TILE) for i in range(3)
            ]
            gate = matmul(x_n[block, :], full[:, g_cols])
            up = matmul(x_n[block, :], full[:, u_cols])
            grad_act = matmul(x_c[block, :], full[:, d_cols])
            sigmoid_gate = 1.0 / (1.0 + jnp.exp(-gate))
            silu_val = gate * sigmoid_gate
            hidden[block, g_cols] = (
                grad_act * up * sigmoid_gate * (1.0 + gate * (1.0 - sigmoid_gate))
            ).astype(jnp.bfloat16)
            hidden[block, u_cols] = (grad_act * silu_val).astype(jnp.bfloat16)
            hidden[block, d_cols] = (silu_val * up).astype(jnp.bfloat16)

        @pl.loop(0, width // TILE)
        def _(index):
            cols = band(index, TILE)
            p_n[block, cols] = dot_nt(hidden[block, gate_up], full[cols, gate_up]).astype(jnp.bfloat16)

        norm_swaps.append(mail.send(p_n.at[half_rows(order[i], 1 - x)], h_n.at[i], other))

    def compute_out(i):
        block = band(order[i], block_rows)

        @pl.loop(0, width // TILE)
        def _(index):
            cols = band(index, TILE)
            p_o[block, cols] = dot_nt(hidden[block, down], full[cols, down]).astype(jnp.bfloat16)

        stores.extend(own_copies([(p_o.at[block], a_p.at[block])], own_sems, 7 + i))

    def norm_step(i):
        norm_swaps[i].wait_recv()
        add_into(p_n.at[half_rows(order[i], x)], h_n.at[i])
        norm_line.pass_on(i, 0)

    def weight_grads(span, i):
        left = x_n if span is gate_up else x_c

        @pl.loop(0, width // DEPTH // TILE)
        def _(index):
            cols = pl.ds(pl.multiple_of(order[i] * (width // DEPTH) + index * TILE, TILE), TILE)
            full[cols, span] = matmul(left[:, cols].T, hidden[:, span]).astype(jnp.bfloat16)

        to_core[span.start, i] = [
            mail.send(
                full.at[at.rows(order[i], side, 1 - c, rows), span],
                from_core.at[order[i], side, :, span],
                sibling,
            )
            for side in range(at.wide)
        ]

    to_core, to_y = {}, {}

    def core_stage(span, i):
        receive(to_core[span.start, i])
        for side in range(at.wide):
            add_into(
                full.at[at.rows(order[i], side, c, rows), span], from_core.at[order[i], side, :, span]
            )
        to_y[span.start, i] = [
            mail.send(
                full.at[at.rows(order[i], at.y_off(j), c, rows), span],
                from_y.at[j - 1, order[i], :, span],
                y_peers[j - 1],
            )
            for j in range(1, at.wide)
        ]

    def y_stage(span, i):
        receive(to_y[span.start, i])
        total = full[at.rows(order[i], y, c, rows), span].astype(jnp.float32)
        for j in range(1, at.wide):
            total = total + from_y[j - 1, order[i], :, span].astype(jnp.float32)
        shares[order[i], :, span] = total.astype(jnp.bfloat16)

    spread_base = mail.reserve(2 * DEPTH)

    def spread_copies(i, source, target, device):
        return [
            pltpu.make_async_remote_copy(
                shares.at[target, :, pl.ds(w * part, part)],
                out.at[:, band(source, part)],
                mail.send_sems.at[spread_base + 2 * i + w],
                mail.recv_sems.at[spread_base + 2 * source + w],
                device_id=device,
                device_id_type=MESH,
            )
            for w, out in enumerate((d_g, d_u))
        ]

    def spread(i):
        copies = spread_copies(i, z, order[i], at.device(z=order[i]))
        start_all(copies)
        mail.open += [(copy, None) for copy in copies]

    stores = []
    compute(0)
    compute(1)
    compute(2)
    norm_step(0)
    compute(3)
    weight_grads(gate_up, 0)
    norm_step(1)
    weight_grads(gate_up, 1)
    norm_line.pass_on(0, 1)
    core_stage(gate_up, 0)
    weight_grads(gate_up, 2)
    core_stage(gate_up, 1)
    weight_grads(gate_up, 3)
    core_stage(gate_up, 2)
    compute_out(0)
    core_stage(gate_up, 3)
    compute_out(1)
    norm_step(2)
    norm_line.pass_on(1, 1)
    compute_out(2)
    norm_line.pass_on(2, 1)
    compute_out(3)
    weight_grads(down, 0)
    y_stage(gate_up, 0)
    spread(0)
    weight_grads(down, 1)
    core_stage(down, 0)
    weight_grads(down, 2)
    core_stage(down, 1)
    weight_grads(down, 3)
    core_stage(down, 2)
    core_stage(down, 3)
    norm_swaps[3].wait_recv()
    finish_own(late)
    o_m[...] = p_n[half_rows(z, x), :].astype(jnp.float32) + h_n[3].astype(jnp.float32)

    def add_norm(_, landed):
        o_m[...] = o_m[...] + landed[...].astype(jnp.float32)

    norm_line.last(add_norm)
    grad_norm = o_m[...]
    values = mid[...]
    inv_rms = lax.rsqrt(jnp.mean(values * values, axis=-1, keepdims=True) + EPSILON)
    grad_values, terms = norm_back(grad_norm, values, inv_rms, gain[...])
    o_t[...] = jnp.sum(terms, axis=0, keepdims=True)
    kept = band(x, tokens)
    total = cot[kept, :].astype(jnp.float32) + grad_values
    o_m[...] = total
    o_h[kept, :] = total.astype(jnp.bfloat16)
    swap_h = mail.send(o_h.at[kept], o_h.at[kept], other)
    stores += own_copies([(o_m, a_m)], own_sems, 0)
    for i in range(1, DEPTH):
        y_stage(gate_up, i)
        if i < DEPTH - 1:
            spread(i)
    stores += own_copies(
        [
            (shares.at[z, :, pl.ds(w * part, part)], out.at[:, band(z, part)])
            for w, out in enumerate((d_g, d_u))
        ],
        own_sems,
        1,
    )
    for i in range(DEPTH):
        y_stage(down, i)
        stores += own_copies([(shares.at[order[i], :, down], a_shares.at[order[i]])], own_sems, 3 + i)
    swap_h.wait_recv()
    stores += own_copies([(o_h, a_h)], own_sems, 11)
    for k in range(1, DEPTH):
        source = at.z_off(-k)
        receive(spread_copies(0, source, z, at.device(z=source)))
    mail.finish()
    finish_own(stores)


def mlp(dp_size, weights, normed, cots, mid, cot, gain):
    wide = dp_size // (DEPTH * CORES)
    tokens, width = mid.shape
    cols = weights.shape[1]
    rows = width // dp_size
    every = DEPTH * HALVES * tokens
    half, full = jnp.bfloat16, jnp.float32
    copies = LineReduce.slots + DEPTH + 2 * DEPTH * (2 * wide - 1) + 1 + 2 * DEPTH
    shapes = [
        jax.ShapeDtypeStruct((tokens, width), full),
        jax.ShapeDtypeStruct((HALVES * tokens, width), half),
        jax.ShapeDtypeStruct((every, width), half),
        jax.ShapeDtypeStruct((1, width), full),
        jax.ShapeDtypeStruct((DEPTH, rows, cols // 3), half),
    ] + [jax.ShapeDtypeStruct((rows, DEPTH * cols // 3), half)] * 2
    return pl.pallas_call(
        functools.partial(mlp_kernel, dp_size),
        out_shape=shapes,
        in_specs=[ANY] * 5 + [VMEM],
        out_specs=[ANY] * 3 + [VMEM] + [ANY] * 3,
        scratch_shapes=[
            pltpu.VMEM((tokens, width), full),
            pltpu.VMEM((HALVES * tokens, width), half),
            pltpu.VMEM((tokens, width), full),
            pltpu.VMEM((HALVES * tokens, width), half),
            pltpu.VMEM((DEPTH, rows, cols), half),
        ]
        + [pltpu.VMEM((width, cols), half)]
        + [pltpu.VMEM((every, width), half)] * 2
        + [pltpu.VMEM((every, cols), half)]
        + [pltpu.VMEM((every, width), half)] * 2
        + [
            pltpu.VMEM((DEPTH, tokens, width), half),
            pltpu.VMEM((LineReduce.slots, tokens, width), half),
        ]
        + [
            pltpu.VMEM((DEPTH, wide, rows, cols), half),
            pltpu.VMEM((wide - 1, DEPTH, rows, cols), half),
            pltpu.SemaphoreType.DMA((13,)),
            pltpu.SemaphoreType.DMA((copies,)),
            pltpu.SemaphoreType.DMA((copies,)),
        ],
        compiler_params=pltpu.CompilerParams(
            collective_id=1, has_side_effects=True, vmem_limit_bytes=63 * 2**20
        ),
    )(weights, normed, cots, mid, cot, gain)


def backward_kernel(
    dp_size, shares, weights, a_mid, mid_half, a_out, a_part, t_m, gain_one, a_row, a_normed, a_query,
    a_key, a_values, a_queries, a_keys, context, a_log, a_cosine, a_sine, a_bias, q_gain, k_gain,
    o_l, o_i, sums, d_q, d_k, d_v, d_o, d_d,
    grad_mid, layer_mid, row_in, normed_one, query_raw, key_raw, values_half, queries, keys,
    log_total, cosine, sine, bias,
    full, head_grads, gains, from_other, totals, core_o, core_h, core_s, y_o, y_h, y_s, z_o, z_h, z_s,
    part_own, part_other, part_line, spare, context_grad, raw_half, raw_head, flipped, partial,
    outgoing, incoming, own_sems, send_sems, recv_sems,
):
    at = Place(dp_size)
    z, y, c, x = at.z, at.y, at.c, at.x
    other, sibling = at.device(x=1 - x), at.device(c=1 - c)
    y_peers, z_peers = at.y_peers(), at.z_peers()
    order = at.order()
    tokens, width = grad_mid.shape
    rows = d_q.shape[0]
    part = shares.shape[2]
    spans, start = [], 0
    for out in (d_q, d_k, d_v, d_o):
        spans.append(pl.ds(start, out.shape[1]))
        start += out.shape[1]
    q_span, k_span, v_span, o_span = spans
    qkv_span = pl.ds(0, start - d_o.shape[1])
    q_cols, kv_width = d_q.shape[1], d_k.shape[1]
    head_dim = q_gain.shape[1]

    def band(index, size):
        return pl.ds(pl.multiple_of(index * size, size), size)

    kept, given = band(x, tokens), band(1 - x, tokens)
    loads = own_copies(
        [(weights.at[:, span], full.at[:, span]) for span in (o_span, qkv_span)], own_sems
    )
    late = own_copies(
        [
            (a_normed, normed_one), (a_query, query_raw), (a_key, key_raw), (a_values, values_half),
            (a_queries, queries), (a_keys, keys), (a_log, log_total), (a_cosine, cosine),
            (a_sine, sine), (a_bias, bias), (a_out, layer_mid), (a_mid, grad_mid), (a_row, row_in),
        ],
        own_sems,
        2,
    )
    part_loads = own_copies(
        [(a_part.at[band(index * HALVES + x, tokens)], part_own.at[index]) for index in order],
        own_sems,
        16,
    )
    meet([other, sibling] + y_peers + z_peers)
    mail = Mail(send_sems, recv_sems)
    part_swaps = [
        mail.send(a_part.at[band(index * HALVES + 1 - x, tokens)], part_other.at[i], other)
        for i, index in enumerate(order)
    ]
    part_sums = LineReduce(
        mail, at, 1, lambda index: [part_own.at[index]], lambda slot: [part_line.at[slot]]
    )

    def part_step(i):
        part_swaps[i].wait_recv()
        part_loads[i].wait()
        add_into(part_own.at[order[i]], part_other.at[i])
        if i < DEPTH - 1:
            part_sums.pass_on(i, 0)

    to_z = [
        mail.send(shares.at[at.z_off(k)], d_d.at[:, band(z, part)], z_peers[k - 1])
        for k in (2, 1, 3)
    ]
    kv_heads = key_raw.shape[1] // head_dim
    group = query_raw.shape[1] // key_raw.shape[1]
    q_part = group * head_dim

    def block_of(zb, side, core):
        return (zb * at.wide + side) * CORES + core

    class Sums:
        def __init__(self, held, core_land, y_land, z_land, outs):
            self.held, self.core_land, self.y_land, self.outs = held, core_land, y_land, outs
            self.line = LineReduce(
                mail, at, 1, lambda zb: [held(zb, y, c)], lambda slot: [z_land.at[slot]]
            )
            self.to_core, self.to_y = {}, {}

        def core_sends(self, i):
            self.to_core[i] = [
                mail.send(
                    self.held(order[i], side, 1 - c), self.core_land.at[order[i], side], sibling
                )
                for side in range(at.wide)
            ]

        def core_stage(self, i):
            receive(self.to_core[i])
            for side in range(at.wide):
                add_into(self.held(order[i], side, c), self.core_land.at[order[i], side])
            self.to_y[i] = [
                mail.send(
                    self.held(order[i], at.y_off(j), c), self.y_land.at[j - 1, order[i]], y_peers[j - 1]
                )
                for j in range(1, at.wide)
            ]

        def y_stage(self, i):
            receive(self.to_y[i])
            terms = [self.y_land.at[j - 1, order[i]] for j in range(1, at.wide)]
            own = self.held(order[i], y, c)
            if i < DEPTH - 1:
                add_into(own, *terms)
                return
            for out, span in self.outs:
                out[...] = own[:, span].astype(jnp.float32)
                add_into(out, *[term.at[:, span] for term in terms])

        def finish(self):
            def use(_, landed):
                for out, span in self.outs:
                    add_into(out, landed.at[:, span])

            self.line.last(use)

    out_sums = Sums(
        lambda zb, side, core: full.at[at.rows(zb, side, core, rows), o_span],
        core_o, y_o, z_o, [(d_o, pl.ds(0, d_o.shape[1]))],
    )
    head_sums = []
    for j in range(kv_heads):
        kv_cols = pl.ds(j * head_dim, head_dim)
        head_sums.append(
            Sums(
                lambda zb, side, core, j=j: head_grads.at[j, at.rows(zb, side, core, rows)],
                core_h.at[j], y_h.at[j], z_h.at[j],
                [
                    (d_q.at[:, pl.ds(j * q_part, q_part)], pl.ds(0, q_part)),
                    (d_k.at[:, kv_cols], pl.ds(q_part, head_dim)),
                    (d_v.at[:, kv_cols], pl.ds(q_part + head_dim, head_dim)),
                ],
            )
        )
    gain_sums = Sums(
        lambda zb, side, core: totals.at[block_of(zb, side, core)],
        core_s, y_s, z_s, [(sums, pl.ds(0, sums.shape[1]))],
    )

    gains[...] = jnp.zeros(gains.shape, jnp.float32)
    loads[0].wait()

    def write_context(cols, value):
        context_grad[:, cols] = value.astype(jnp.bfloat16)

    matmul_tiles(mid_half, full.at[:, o_span], write_context)

    quarter = width // DEPTH
    for i in range(DEPTH):

        @pl.loop(0, quarter // TILE)
        def _(index, i=i):
            cols = pl.ds(pl.multiple_of(order[i] * quarter + index * TILE, TILE), TILE)
            full[cols, o_span] = dot_tn(mid_half[:, cols], context[...]).astype(jnp.bfloat16)

        out_sums.core_sends(i)
    own_share = own_copies([(shares.at[z], spare)], own_sems, 15)
    for i in range(DEPTH):
        out_sums.core_stage(i)
    finish_own(late)
    finish_own(own_share)
    own_share = own_copies([(spare, d_d.at[:, band(z, part)])], own_sems, 15)
    flipped[...] = normed_one[...].T

    scale = 1.0 / math.sqrt(head_dim)

    def raw_grad(grad, raw, gain):
        back = grad * cosine[...] - turned(grad) * sine[...]
        inv_rms = lax.rsqrt(jnp.mean(raw * raw, axis=-1, keepdims=True) + EPSILON)
        grad_raw, terms = norm_back(back, raw, inv_rms, gain)
        return grad_raw.astype(jnp.bfloat16), jnp.sum(terms, axis=0, keepdims=True)

    for j in range(kv_heads):
        q_sum = jnp.zeros((1, head_dim), jnp.float32)
        k_sum = jnp.zeros((1, head_dim), jnp.float32)
        kv_cols = pl.ds(j * head_dim, head_dim)
        key_total = jnp.zeros((row_in.shape[0], head_dim), jnp.float32)
        value_total = jnp.zeros((row_in.shape[0], head_dim), jnp.float32)
        for g in range(group):
            head = j * group + g
            cols = pl.ds(head * head_dim, head_dim)
            scores = dot_nt(queries[:, cols], keys[:, kv_cols]) * scale + bias[...]
            probs = jnp.exp(scores - log_total[:, head : head + 1])
            grad_context = context_grad[:, cols]
            grad_probs = dot_nt(grad_context, values_half[:, kv_cols])
            delta = jnp.sum(
                grad_context.astype(jnp.float32) * context[:, cols].astype(jnp.float32),
                axis=-1,
                keepdims=True,
            )
            grad_scores = (probs * (grad_probs - delta) * scale).astype(jnp.bfloat16)
            grad_query, terms = raw_grad(
                matmul(grad_scores, keys[:, kv_cols]), query_raw[:, cols], q_gain[...]
            )
            raw_half[:, cols] = grad_query
            raw_head[:, pl.ds(g * head_dim, head_dim)] = grad_query
            q_sum = q_sum + terms
            key_total = key_total + dot_tn(grad_scores, queries[:, cols])
            value_total = value_total + dot_tn(probs.astype(jnp.bfloat16), grad_context)
        grad_key, terms = raw_grad(key_total, key_raw[:, kv_cols], k_gain[...])
        grad_value = value_total.astype(jnp.bfloat16)
        raw_half[:, pl.ds(q_cols + j * head_dim, head_dim)] = grad_key
        raw_half[:, pl.ds(q_cols + kv_width + j * head_dim, head_dim)] = grad_value
        raw_head[:, pl.ds(q_part, head_dim)] = grad_key
        raw_head[:, pl.ds(q_part + head_dim, head_dim)] = grad_value
        k_sum = k_sum + terms
        gains[0, 2:3, :head_dim] = gains[0, 2:3, :head_dim] + q_sum
        gains[0, 3:4, :head_dim] = gains[0, 3:4, :head_dim] + k_sum
        for i in range(DEPTH):

            @pl.loop(0, quarter // TILE)
            def _(index, i=i, j=j):
                cols = pl.ds(pl.multiple_of(order[i] * quarter + index * TILE, TILE), TILE)
                head_grads[j, cols, :] = matmul(flipped[cols, :], raw_head[...]).astype(jnp.bfloat16)

            head_sums[j].core_sends(i)
        if 1 <= j < DEPTH:
            out_sums.y_stage(j - 1)
            out_sums.line.pass_on(j - 1, 0)
        if j >= 2:
            out_sums.line.pass_on(j - 2, 1)
        if j == 0:
            part_step(0)
        if j == DEPTH - 2:
            part_step(1)
            part_sums.pass_on(0, 1)
        if j > 0:
            for i in range(DEPTH):
                head_sums[j - 1].core_stage(i)
    for j in range(max(kv_heads - 1, 0), DEPTH - 1):
        out_sums.y_stage(j)
        out_sums.line.pass_on(j, 0)
    for j in range(max(kv_heads - 2, 0), DEPTH - 2):
        out_sums.line.pass_on(j, 1)
    out_sums.y_stage(DEPTH - 1)
    for i in range(DEPTH):
        head_sums[kv_heads - 1].core_stage(i)
    finish_own(loads[1:])

    def project(token_rows, target):
        @pl.loop(0, width // TILE)
        def _(index):
            cols = band(index, TILE)
            total = dot_nt(raw_half[token_rows, :], full[cols, qkv_span])
            partial[token_rows, cols] = total
            if target is not None:
                target[:, cols] = total.astype(target.dtype)

    project(given, outgoing)
    swap = mail.send(outgoing, incoming, other)
    project(kept, None)

    values = row_in[...].astype(jnp.float32)
    inv_rms = lax.rsqrt(jnp.mean(values * values, axis=-1, keepdims=True) + EPSILON)
    gain_terms = jnp.sum(partial[...] * values * inv_rms, axis=0, keepdims=True)
    blocks = gains.shape[0]
    share = width // blocks
    head_terms = gains[0, 2:4, :]
    for index in range(blocks):
        gains[index, 0:1, :share] = gain_terms[:, index * share : (index + 1) * share]
        gains[index, 1:2, :share] = t_m[:, index * share : (index + 1) * share]
        gains[index, 2:4, :] = head_terms
    swap_gains = mail.send(gains, from_other, other)
    swap.wait_recv()
    grad_norm = partial[kept, :] + incoming[...].astype(jnp.float32)
    values = row_in[kept, :].astype(jnp.float32)
    inv_rms = lax.rsqrt(jnp.mean(values * values, axis=-1, keepdims=True) + EPSILON)
    grad_values, _ = norm_back(grad_norm, values, inv_rms, gain_one[...])
    o_i[kept, :] = (grad_mid[...] + grad_values).astype(jnp.bfloat16)
    swap_back = mail.send(o_i.at[kept], o_i.at[kept], other)

    if kv_heads < DEPTH - 1:
        part_step(1)
    part_sums.pass_on(1, 1)
    part_step(2)
    out_sums.line.pass_on(DEPTH - 2, 1)
    swap_gains.wait_recv()
    totals[...] = gains[...] + from_other[...]
    for i in range(DEPTH):
        gain_sums.core_sends(i)
    for i in range(DEPTH):
        gain_sums.core_stage(i)
    every = head_sums + [gain_sums]
    part_sums.pass_on(2, 1)
    part_step(3)
    for index in range(len(every) + DEPTH - 1):
        if index < len(every):
            for i in range(DEPTH):
                every[index].y_stage(i)
        for turn in range(DEPTH - 1):
            if 0 <= index - turn < len(every):
                every[index - turn].line.pass_on(turn, 0)
            if 0 <= index - turn - 1 < len(every):
                every[index - turn - 1].line.pass_on(turn, 1)
    out_sums.finish()
    layer_mid[...] = layer_mid[...] + part_own[z].astype(jnp.float32)

    def add_part(_, landed):
        layer_mid[...] = layer_mid[...] + landed[...].astype(jnp.float32)

    part_sums.last(add_part)
    o_l[kept, :] = layer_mid[...].astype(jnp.bfloat16)
    swap_l = mail.send(o_l.at[kept], o_l.at[kept], other)
    for one in every[:-1]:
        one.finish()
    every[-1].finish()
    receive([swap_l, swap_back] + to_z)
    finish_own(own_share)
    mail.finish()


def backward(dp_size, shares, weights, cols, grad_mid, mid_half, layer_mid, part_out, gain_terms, saved, gains):
    wide = dp_size // (DEPTH * CORES)
    tokens, width = grad_mid.shape
    seq_len = HALVES * tokens
    part = shares.shape[2]
    rows = width // dp_size
    half, full = jnp.bfloat16, jnp.float32
    every = sum(cols)
    kv_heads = cols[1] // gains[2].shape[1]
    head_cols = (every - cols[3]) // kv_heads
    passes = kv_heads + 2
    copies = 3 + 4 + DEPTH + LineReduce.slots + passes * (LineReduce.slots + DEPTH * (2 * wide - 1))
    shapes = [jax.ShapeDtypeStruct((seq_len, width), half)] * 2
    shapes += [jax.ShapeDtypeStruct((8, 128), full)]
    shapes += [jax.ShapeDtypeStruct((rows, col), full) for col in cols]
    shapes += [jax.ShapeDtypeStruct((rows, DEPTH * part), half)]
    lazy = [grad_mid, layer_mid] + [one for i, one in enumerate(saved) if i != 7]
    inputs = [grad_mid, mid_half, layer_mid, part_out, gain_terms, gains[0], *saved, *gains[2:]]
    return pl.pallas_call(
        functools.partial(backward_kernel, dp_size),
        out_shape=shapes,
        in_specs=[ANY] * 3 + [VMEM, ANY, ANY, VMEM, VMEM] + [ANY] * 7 + [VMEM] + [ANY] * 4 + [VMEM] * 2,
        out_specs=[VMEM] * 7 + [ANY],
        scratch_shapes=[pltpu.VMEM(one.shape, one.dtype) for one in lazy]
        + [
            pltpu.VMEM((width, every), half),
            pltpu.VMEM((kv_heads, width, head_cols), half),
            pltpu.VMEM((dp_size, 8, 128), full),
            pltpu.VMEM((dp_size, 8, 128), full),
            pltpu.VMEM((dp_size, 8, 128), full),
            pltpu.VMEM((DEPTH, wide, rows, cols[3]), half),
            pltpu.VMEM((kv_heads, DEPTH, wide, rows, head_cols), half),
            pltpu.VMEM((DEPTH, wide, 8, 128), full),
            pltpu.VMEM((wide - 1, DEPTH, rows, cols[3]), half),
            pltpu.VMEM((kv_heads, wide - 1, DEPTH, rows, head_cols), half),
            pltpu.VMEM((wide - 1, DEPTH, 8, 128), full),
            pltpu.VMEM((LineReduce.slots, rows, cols[3]), half),
            pltpu.VMEM((kv_heads, LineReduce.slots, rows, head_cols), half),
            pltpu.VMEM((LineReduce.slots, 8, 128), full),
            pltpu.VMEM((DEPTH, tokens, width), half),
            pltpu.VMEM((DEPTH, tokens, width), half),
            pltpu.VMEM((LineReduce.slots, tokens, width), half),
            pltpu.VMEM((rows, part), half),
            pltpu.VMEM((seq_len, cols[0]), half),
            pltpu.VMEM((seq_len, every - cols[3]), half),
            pltpu.VMEM((seq_len, head_cols), half),
            pltpu.VMEM((width, seq_len), half),
            pltpu.VMEM((seq_len, width), full),
            pltpu.VMEM((tokens, width), half),
            pltpu.VMEM((tokens, width), half),
            pltpu.SemaphoreType.DMA((20,)),
            pltpu.SemaphoreType.DMA((copies,)),
            pltpu.SemaphoreType.DMA((copies,)),
        ],
        compiler_params=pltpu.CompilerParams(
            collective_id=2, has_side_effects=True, vmem_limit_bytes=63 * 2**20
        ),
    )(shares, weights, *inputs)


def body(
    dp_size,
    layer_in,
    seg_ids,
    w_q,
    w_k,
    w_v,
    w_o,
    w_gate,
    w_up,
    w_down,
    attn_gain,
    mlp_gain,
    q_gain,
    k_gain,
    cotangent,
):
    row_in = layer_in[0]
    row_cot = cotangent[0]
    width = row_in.shape[1]
    gains = [gain[None, :] for gain in (attn_gain, mlp_gain, q_gain, k_gain)]
    outs = forward(
        dp_size, (w_q, w_k, w_v, w_o, w_gate, w_up, w_down), row_cot, row_in, seg_ids[0], gains
    )
    attn_full, ffn_full, cots, normed, mid = outs[:5]
    saved = outs[5:]
    outs = mlp(
        dp_size, ffn_full, normed.reshape(-1, width), cots.reshape(-1, width), mid, row_cot, gains[1]
    )
    grad_mid, mid_half, part_out, gain_terms, shares, *gate_up_grads = outs
    cols = [weight.shape[1] for weight in (w_q, w_k, w_v, w_o)]
    outs = backward(
        dp_size, shares, attn_full, cols, grad_mid, mid_half, mid, part_out, gain_terms,
        [row_in] + list(saved), gains,
    )
    out_row, in_grad, sums = outs[:3]
    share = width // dp_size
    gain_outs = [sums[0, :share], sums[1, :share]]
    for i, gain in enumerate((q_gain, k_gain)):
        share = gain.shape[0] // dp_size
        gain_outs.append(lax.dynamic_slice(sums[2 + i], (lax.axis_index("dp") * share,), (share,)))
    ffn_grads = [grad.astype(jnp.float32) for grad in (*gate_up_grads, outs[7])]
    return (out_row[None], in_grad[None], *outs[3:7], *ffn_grads, *gain_outs)


def solution(mesh):
    return jax.shard_map(
        functools.partial(body, mesh.shape["dp"]),
        mesh=mesh,
        in_specs=(
            P("dp", None, None),
            P("dp", None),
            P("dp", "mp"),
            P("dp", "mp"),
            P("dp", "mp"),
            P("dp", "mp"),
            P("dp", "mp"),
            P("dp", "mp"),
            P("dp", "mp"),
            P(),
            P(),
            P(),
            P(),
            P("dp", None, None),
        ),
        out_specs=(
            P("dp", None, None),
            P("dp", None, None),
            P("dp", "mp"),
            P("dp", "mp"),
            P("dp", "mp"),
            P("dp", "mp"),
            P("dp", "mp"),
            P("dp", "mp"),
            P("dp", "mp"),
            P("dp"),
            P("dp"),
            P("dp"),
            P("dp"),
        ),
        check_vma=False,
    )
```

```python
import functools
import math

import jax
import jax.numpy as jnp
from jax import lax
from jax.experimental import pallas as pl
from jax.experimental.pallas import tpu as pltpu
from jax.sharding import PartitionSpec as P

EPSILON = 1e-06
ROPE_BASE = 1000000.0
MASKED = -1e30


def matmul(left_op, right_op):
    return jnp.dot(left_op, right_op, preferred_element_type=jnp.float32)


def rms_norm(values, gain_vec):
    inv_rms = lax.rsqrt(jnp.mean(values * values, axis=-1, keepdims=True) + EPSILON)
    return (values * inv_rms * gain_vec, inv_rms)


def norm_back(grad_norm, values, inv_rms, gain_vec):
    scaled = grad_norm * gain_vec
    cubed = inv_rms * inv_rms * inv_rms
    grad_values = inv_rms * scaled - values * cubed * jnp.mean(
        scaled * values, axis=-1, keepdims=True
    )
    return (grad_values, grad_norm * values * inv_rms)


MESH = pl.DeviceIdType.MESH
ANY = pl.BlockSpec(memory_space=pl.ANY)
VMEM = pl.BlockSpec(memory_space=pltpu.VMEM)
DEPTH = 4
CORES = 2
HALVES = 2
UP, DOWN = 0, 1
TILE = 256


def split(index, size):
    size = jnp.int32(size)
    return lax.div(index, size), lax.rem(index, size)


class Place:
    def __init__(self, dp_size):
        self.wide = dp_size // (DEPTH * CORES)
        self.x = lax.axis_index("mp")
        rest, self.c = split(lax.axis_index("dp"), CORES)
        self.z, self.y = split(rest, self.wide)

    def device(self, z=None, y=None, c=None, x=None):
        z = self.z if z is None else z
        y = self.y if y is None else y
        c = self.c if c is None else c
        x = self.x if x is None else x
        return ((z * self.wide + y) * CORES + c, x)

    def z_off(self, step):
        return lax.rem(self.z + DEPTH + step, jnp.int32(DEPTH))

    def z_flip(self, bits):
        z = self.z
        if bits == DEPTH - 1:
            return DEPTH - 1 - z
        return z + bits - 2 * bits * lax.rem(lax.div(z, jnp.int32(bits)), jnp.int32(2))

    def y_off(self, step):
        return lax.rem(self.y + self.wide + step, jnp.int32(self.wide))

    def rows(self, z, y, c, count):
        return pl.ds(pl.multiple_of(((z * self.wide + y) * CORES + c) * count, count), count)

    def line(self):
        return [self.device(z=self.z_off(1)), self.device(z=self.z_off(-1))]

    def z_peers(self):
        return [self.device(z=self.z_off(k)) for k in range(1, DEPTH)]

    def y_peers(self):
        return [self.device(y=self.y_off(j)) for j in range(1, self.wide)]

    def order(self):
        low = 1 - lax.div(self.z, jnp.int32(2))
        return [3 * low, 1 + low, low * (1 - self.z) + (1 - low) * (5 - self.z), self.z]


def guarded(when, action):
    if when is None:
        action()
    else:
        pl.when(when)(action)


class Mail:
    def __init__(self, send_sems, recv_sems):
        self.send_sems, self.recv_sems = send_sems, recv_sems
        self.count = 0
        self.open = []

    def reserve(self, count):
        first = self.count
        self.count += count
        return first

    def describe(self, source, target, device, slot):
        return pltpu.make_async_remote_copy(
            source,
            target,
            self.send_sems.at[slot],
            self.recv_sems.at[slot],
            device_id=device,
            device_id_type=MESH,
        )

    def make(self, source, target, device, when=None, slot=None):
        copy = self.describe(source, target, device, self.reserve(1) if slot is None else slot)
        self.open.append((copy, when))
        return copy

    def send(self, source, target, device, when=None):
        copy = self.make(source, target, device, when)
        guarded(when, copy.start)
        return copy

    def finish(self):
        for copy, when in self.open:
            guarded(when, copy.wait_send)


def meet(devices):
    barrier = pltpu.get_barrier_semaphore()
    for device in devices:
        pl.semaphore_signal(barrier, inc=1, device_id=device, device_id_type=MESH)
    pl.semaphore_wait(barrier, len(devices))


def receive(copies):
    for copy in copies:
        copy.wait_recv()


def start_all(copies):
    for copy in copies:
        copy.start()


class LineGather:
    def __init__(self, mail, at, own, place, sides, sibling=None, share_own=True):
        self.mail, self.at, self.place = mail, at, place
        self.sides, self.sibling = sides, sibling
        self.neighbours = at.line()
        self.open_end = [at.z < DEPTH - 1, at.z > 0]
        pairs = list(zip(own, place(at.z, 0)))
        self.hops = [
            [mail.send(source, target, self.neighbours[way], self.open_end[way]) for source, target in pairs]
            for way in (UP, DOWN)
        ]
        self.over, self.cores = {}, []
        if share_own:
            self.over["own"] = [
                [mail.send(source, target, side) for source, target in pairs] for side in sides
            ]
        if sibling is not None:
            self.cores.append(
                (None, [mail.send(source, target, sibling) for source, target in pairs])
            )

    def where(self, way, step):
        z = self.at.z
        if way == UP:
            return z >= step + 1, self.at.z_off(-1 - step)
        return z + 1 + step < DEPTH, self.at.z_off(1 + step)

    def step(self, step):
        for way in (UP, DOWN):
            got, index = self.where(way, step)
            refs = self.place(index, 0)
            arrived = self.hops[way]
            onward = []
            if step < DEPTH - 2:
                more = got & self.open_end[way]
                onward = [self.mail.make(ref, ref, self.neighbours[way], more) for ref in refs]
            over = [[self.mail.make(ref, ref, side, got) for ref in refs] for side in self.sides]
            cores = []
            if self.sibling is not None:
                cores = [self.mail.make(ref, ref, self.sibling, got) for ref in refs]

            def pass_on(way=way, arrived=arrived, onward=onward, over=over, cores=cores):
                receive(arrived)
                pl.when(self.open_end[way])(lambda: start_all(onward))
                for copies in over:
                    start_all(copies)
                start_all(cores)

            pl.when(got)(pass_on)
            self.hops[way] = onward
            self.over[way, step] = over
            if cores:
                self.cores.append((got, cores))

    def side_step(self, key):
        got, index = (None, self.at.z) if key == "own" else self.where(*key)
        cores = []
        for j in range(1, len(self.sides) + 1):
            if self.sibling is not None:
                refs = self.place(index, j)
                cores += [self.mail.make(ref, ref, self.sibling, got) for ref in refs]

        def pass_on():
            for copies in self.over[key]:
                receive(copies)
            start_all(cores)

        guarded(got, pass_on)
        if cores:
            self.cores.append((got, cores))

    def side_steps(self, step):
        self.side_step((UP, step))
        self.side_step((DOWN, step))

    def finish(self):
        for got, cores in self.cores:
            guarded(got, lambda cores=cores: receive(cores))


class LineReduce:
    slots = 2 * (DEPTH - 1)

    def __init__(self, mail, at, pieces, part, land):
        self.mail, self.at, self.pieces, self.part, self.land = mail, at, pieces, part, land
        self.base = mail.reserve(self.slots * pieces)

    def copies(self, index, sources, device):
        slots = [self.base + index * self.pieces + i for i in range(self.pieces)]
        return [
            self.mail.describe(source, target, device, slot)
            for source, target, slot in zip(sources, self.land(index), slots)
        ]

    def pass_on(self, turn, part=None):
        z = self.at.z
        low = 1 - lax.div(z, jnp.int32(2))
        up = low if turn < 2 else 1 - lax.rem(z, jnp.int32(2))
        target = self.at.order()[turn]
        index = up * (target - 1) + (1 - up) * (DEPTH - 1 + target)
        device = self.at.device(z=z + 2 * up - 1)
        sources = self.part(target)
        copies = self.copies(index, sources, device)
        has_in = up * jnp.where(z > 0, 1, 0) + (1 - up) * jnp.where(z < DEPTH - 1, 1, 0)

        if part != 0:

            @pl.when(has_in > 0)
            def _():
                receive(copies)
                for source, landed in zip(sources, self.land(index)):
                    add_into(source, landed)
                if part == 1:
                    start_all(copies)

        if part == 0:
            pl.when(has_in == 0)(lambda: start_all(copies))
        elif part is None:
            start_all(copies)
        if part != 1:
            self.mail.open += [(copy, None) for copy in copies]

    def last(self, use):
        z = self.at.z
        sources = self.part(z)
        for when, index, neighbour in (
            (z > 0, lax.max(z - 1, 0), self.at.z_off(-1)),
            (z < DEPTH - 1, lax.min(DEPTH - 1 + z, self.slots - 1), self.at.z_off(1)),
        ):
            copies = self.copies(index, sources, self.at.device(z=neighbour))

            @pl.when(when)
            def _(copies=copies, index=index):
                receive(copies)
                for i, landed in enumerate(self.land(index)):
                    use(i, landed)


def own_copies(pairs, sems, first=0):
    copies = [
        pltpu.make_async_copy(source, target, sems.at[first + i])
        for i, (source, target) in enumerate(pairs)
    ]
    start_all(copies)
    return copies


def finish_own(copies):
    for copy in copies:
        copy.wait()


def add_into(target, *others):
    total = target[...].astype(jnp.float32)
    for other in others:
        total = total + other[...].astype(jnp.float32)
    target[...] = total.astype(target.dtype)


def dot_nt(left_op, right_op):
    return lax.dot_general(
        left_op, right_op, (((1,), (1,)), ((), ())), preferred_element_type=jnp.float32
    )


def dot_tn(left_op, right_op):
    return lax.dot_general(
        left_op, right_op, (((0,), (0,)), ((), ())), preferred_element_type=jnp.float32
    )


def turned(values):
    return pltpu.roll(values, values.shape[-1] // 2, axis=values.ndim - 1)


def document_tables(seg_col, seg_row, head_dim):
    seq_len = seg_col.shape[0]
    rows = lax.broadcasted_iota(jnp.int32, (seq_len, seq_len), 0)
    cols = lax.broadcasted_iota(jnp.int32, (seq_len, seq_len), 1)
    same = seg_col == seg_row
    bias = jnp.where(same & (cols <= rows), 0.0, MASKED)
    before = jnp.where(same & (cols < rows), 1.0, 0.0)
    position = jnp.sum(before, axis=-1, keepdims=True)
    lane = lax.broadcasted_iota(jnp.int32, (1, head_dim), 1)
    half_dim = head_dim // 2
    slot = jnp.where(lane < half_dim, lane, lane - half_dim).astype(jnp.float32)
    frequency = jnp.exp(slot * (-2.0 * math.log(ROPE_BASE) / head_dim))
    angles = position * frequency
    sine = jnp.sin(angles)
    return bias, jnp.cos(angles), jnp.where(lane < half_dim, -sine, sine)


def matmul_tiles(left, right, write, tile=256):
    @pl.loop(0, right.shape[1] // tile)
    def _(index):
        columns = pl.ds(pl.multiple_of(index * tile, tile), tile)
        write(columns, matmul(left[...], right[:, columns]))


SAVED = 11


def forward_kernel(
    dp_size, w_q, w_k, w_v, w_o, w_g, w_u, w_d, cot, row_in, seg_col, seg_row,
    gain_one, gain_two, q_gain, k_gain,
    *refs,
):
    o_attn, o_ffn, o_c, o_n, o_mid = refs[:5]
    stored, held = refs[5 : 5 + SAVED], refs[6 + SAVED : 6 + 2 * SAVED]
    mid = refs[5 + SAVED]
    normed_one, query_raw, key_raw, values_half, queries, keys, context, log_total = held[:8]
    cosine, sine, bias = held[8:]
    full, own_part, outgoing, incoming, normed, own_sems, send_sems, recv_sems = refs[6 + 2 * SAVED :]
    at = Place(dp_size)
    z, y, c, x = at.z, at.y, at.c, at.x
    sibling, other = at.device(c=1 - c), at.device(x=1 - x)
    z_peers, y_peers = at.z_peers(), at.y_peers()
    meet([sibling, other] + z_peers + y_peers)

    mail = Mail(send_sems, recv_sems)
    rows = w_q.shape[0]
    head_dim = q_gain.shape[1]
    part = w_g.shape[1] // DEPTH
    tokens = mid.shape[0]
    here = at.rows(z, y, c, rows)
    spans, start = [], 0
    for weight in (w_q, w_k, w_v, w_o):
        spans.append(pl.ds(start, weight.shape[1]))
        start += weight.shape[1]
    q_span, k_span, v_span, o_span = spans
    ffn = [(weight, pl.ds(i * part, part)) for i, weight in enumerate((w_g, w_u, w_d))]

    def columns(index):
        return pl.ds(pl.multiple_of(index * part, part), part)

    def half_rows(index):
        return pl.ds(pl.multiple_of(index * tokens, tokens), tokens)

    mine = own_copies(
        [(weight, full.at[here, span]) for weight, span in zip((w_q, w_k, w_v, w_o), spans)],
        own_sems,
    )
    own_ffn = own_copies(
        [(weight.at[:, columns(z)], own_part.at[:, span]) for weight, span in ffn], own_sems, 4
    )
    own_cot = own_copies([(cot.at[half_rows(i)], o_c.at[z, i]) for i in range(2)], own_sems, 7)
    finish_own(mine)
    attn = LineGather(
        mail,
        at,
        (full.at[here],),
        lambda zb, j: [full.at[at.rows(zb, at.y_off(-j), c, rows)]],
        y_peers,
        sibling,
    )

    residual = row_in[...].astype(jnp.float32)
    normed_full, _ = rms_norm(residual, gain_one[...])
    normed_one[...] = normed_full.astype(jnp.bfloat16)
    bias_values, cosine[...], sine[...] = document_tables(seg_col[...], seg_row[...], head_dim)
    bias[...] = bias_values

    spread, crossing, to_sibling = {}, {}, []

    def start_spread():
        for k in range(1, DEPTH):
            target = at.z_flip(k)
            spread[k] = [
                mail.send(
                    weight.at[:, columns(target)], o_ffn.at[here, span], at.device(z=target)
                )
                for weight, span in ffn
            ]
        block = o_ffn.at[here]
        for j in range(1, at.wide):
            crossing[0, j] = mail.send(own_part, block, y_peers[j - 1])
        to_sibling.append(mail.send(own_part, block, sibling))

    def forward_spread(k):
        receive(spread[k])
        block = o_ffn.at[at.rows(at.z_flip(k), y, c, rows)]
        for j in range(1, at.wide):
            crossing[k, j] = mail.send(block, block, y_peers[j - 1])
        to_sibling.append(mail.send(block, block, sibling))

    def forward_crossing(k):
        for j in range(1, at.wide):
            crossing[k, j].wait_recv()
            block = o_ffn.at[at.rows(at.z_flip(k), at.y_off(-j), c, rows)]
            to_sibling.append(mail.send(block, block, sibling))

    def half_place(out):
        return lambda zb, j: [out.at[zb, x if j == 0 else 1 - x]]

    attn.step(0)
    finish_own(own_ffn)
    own_copy = own_copies([(own_part, o_ffn.at[here])], own_sems, 4)
    attn.side_step("own")
    attn.step(1)
    cots = LineGather(
        mail, at, (cot.at[half_rows(x)],), half_place(o_c), [other], share_own=False
    )
    attn.side_steps(0)
    attn.step(2)
    cots.step(0)
    attn.side_steps(1)
    cots.step(1)
    start_spread()
    attn.side_steps(2)
    attn.finish()
    saved = own_copies([(full, o_attn)], own_sems)

    def write_query(cols, block):
        query_raw[:, cols] = block

    def write_key(cols, block):
        key_raw[:, cols] = block

    def write_value(cols, block):
        values_half[:, cols] = block.astype(jnp.bfloat16)

    matmul_tiles(normed_one, full.at[:, q_span], write_query)
    matmul_tiles(normed_one, full.at[:, k_span], write_key)
    matmul_tiles(normed_one, full.at[:, v_span], write_value)

    def rotated(raw, gain):
        unit, _ = rms_norm(raw, gain)
        return (unit * cosine[...] + turned(unit) * sine[...]).astype(jnp.bfloat16)

    kv_heads = key_raw.shape[1] // head_dim
    group = query_raw.shape[1] // key_raw.shape[1]
    for j in range(kv_heads):
        kv_cols = pl.ds(j * head_dim, head_dim)
        keys[:, kv_cols] = rotated(key_raw[:, kv_cols], k_gain[...])
        for g in range(group):
            head = j * group + g
            cols = pl.ds(head * head_dim, head_dim)
            queries[:, cols] = rotated(query_raw[:, cols], q_gain[...])
            scores = dot_nt(queries[:, cols], keys[:, kv_cols]) * (1.0 / math.sqrt(head_dim))
            scores = scores + bias[...]
            row_max = jnp.max(scores, axis=-1, keepdims=True)
            weights = jnp.exp(scores - row_max)
            total = jnp.sum(weights, axis=-1, keepdims=True)
            log_total[:, head : head + 1] = row_max + jnp.log(total)
            probs = (weights * (1.0 / total)).astype(jnp.bfloat16)
            context[:, cols] = matmul(probs, values_half[:, kv_cols]).astype(jnp.bfloat16)
        if j == kv_heads // 2 - 1:
            cots.step(2)

    saved += own_copies(list(zip(held, stored)), own_sems, 11)
    given, kept = half_rows(1 - x), half_rows(x)
    width = row_in.shape[1]

    def project(token_rows, target):
        @pl.loop(0, width // TILE)
        def _(index):
            cols = pl.ds(pl.multiple_of(index * TILE, TILE), TILE)
            block = dot_nt(context[token_rows, :], full[cols, o_span])
            target[:, cols] = block.astype(target.dtype)

    project(given, outgoing)
    swap = mail.send(outgoing, incoming, other)
    project(kept, mid)
    swap.wait_recv()
    total = row_in[kept, :].astype(jnp.float32) + (mid[...] + incoming[...].astype(jnp.float32))
    mid[...] = total
    saved += own_copies([(mid, o_mid)], own_sems, 10)
    normed_mid, _ = rms_norm(total, gain_two[...])
    normed[...] = normed_mid.astype(jnp.bfloat16)
    last = own_copies([(normed, o_n.at[z, x])], own_sems, 9)
    strip = tokens // 2
    norms = []
    for i in range(2):
        rows_of = pl.ds(i * strip, strip)
        norms.append(
            LineGather(
                mail,
                at,
                (normed.at[rows_of],),
                lambda zb, j, rows_of=rows_of: [o_n.at[zb, x if j == 0 else 1 - x, rows_of]],
                [other],
            )
        )
    forward_spread(1)
    forward_crossing(0)
    for step in range(DEPTH - 1):
        if step < DEPTH - 2:
            forward_spread(step + 2)
        for line in norms:
            line.step(step)
        forward_crossing(step + 1)
    for step in range(DEPTH - 1):
        cots.side_steps(step)
    for line in norms:
        line.side_step("own")
        for step in range(DEPTH - 1):
            line.side_steps(step)
    receive(to_sibling)
    mail.finish()
    finish_own(saved + last + own_cot + own_copy)


def forward(dp_size, weights, cot, row_in, seg_row, gains):
    w_q, w_k, w_v, w_o, w_g, w_u, w_d = weights
    wide = dp_size // (DEPTH * CORES)
    seq_len, width = row_in.shape
    head_dim = gains[2].shape[1]
    tokens = seq_len // HALVES
    part = w_g.shape[1] // DEPTH
    half, whole = jnp.bfloat16, jnp.float32
    attn_cols = [w.shape[1] for w in (w_q, w_k, w_v, w_o)]
    shapes = [jax.ShapeDtypeStruct((width, cols), half) for cols in (sum(attn_cols), 3 * part)]
    shapes += [jax.ShapeDtypeStruct((DEPTH, HALVES, tokens, width), half)] * 2
    q_cols, kv_cols = attn_cols[0], attn_cols[1]
    for cols, kind in (
        (width, half), (q_cols, whole), (kv_cols, whole), (kv_cols, half), (q_cols, half),
        (kv_cols, half), (q_cols, half), (head_dim, whole), (head_dim, whole), (head_dim, whole),
        (seq_len, whole),
    ):
        shapes.append(jax.ShapeDtypeStruct((seq_len, cols), kind))
    shapes.insert(4, jax.ShapeDtypeStruct((tokens, width), whole))
    hops = 2 * (DEPTH - 1)
    spots = 1 + hops
    copies = (hops + spots * (2 * wide - 1)) + 3 * (2 * hops + 1) + 1
    copies += 9 + DEPTH * (2 * wide - 1)
    return pl.pallas_call(
        functools.partial(forward_kernel, dp_size),
        out_shape=shapes,
        in_specs=[ANY] * 7 + [VMEM] * 8,
        out_specs=[ANY] * (5 + SAVED),
        scratch_shapes=[pltpu.VMEM(shape.shape, shape.dtype) for shape in shapes[4:]]
        + [pltpu.VMEM((width, sum(attn_cols)), half)]
        + [pltpu.VMEM((w_g.shape[0], 3 * part), half)]
        + [pltpu.VMEM((tokens, width), half)] * 3
        + [
            pltpu.SemaphoreType.DMA((11 + SAVED,)),
            pltpu.SemaphoreType.DMA((copies,)),
            pltpu.SemaphoreType.DMA((copies,)),
        ],
        compiler_params=pltpu.CompilerParams(
            collective_id=0, has_side_effects=True, vmem_limit_bytes=56 * 2**20
        ),
    )(w_q, w_k, w_v, w_o, w_g, w_u, w_d, cot, row_in, seg_row[:, None], seg_row[None, :], *gains)


def mlp_kernel(
    dp_size, weights, n_all, c_all, a_mid, a_cot, gain,
    a_m, a_h, a_p, o_t, a_shares, d_g, d_u,
    mid, cot, o_m, o_h, shares, full, x_n, x_c, hidden, p_n, p_o, h_n, l_n, from_core, from_y,
    own_sems, send_sems, recv_sems,
):
    at = Place(dp_size)
    z, y, c, x = at.z, at.y, at.c, at.x
    other, sibling = at.device(x=1 - x), at.device(c=1 - c)
    y_peers = at.y_peers()
    order = at.order()
    tokens = mid.shape[0]
    block_rows = HALVES * tokens
    rows = from_core.shape[2]
    part = full.shape[1] // 3
    gate_up, down = pl.ds(0, 2 * part), pl.ds(2 * part, part)
    width = mid.shape[1]

    def band(index, size):
        return pl.ds(pl.multiple_of(index * size, size), size)

    loads = {}
    for i, name in enumerate("gud"):
        span = pl.ds(i * part, part)
        loads[name] = pltpu.make_async_copy(weights.at[:, span], full.at[:, span], own_sems.at[i])
    for i, index in enumerate(order):
        block = band(index, block_rows)
        loads["n", i] = pltpu.make_async_copy(n_all.at[block], x_n.at[block], own_sems.at[3 + i])
        loads["c", i] = pltpu.make_async_copy(c_all.at[block], x_c.at[block], own_sems.at[7 + i])
    for key in ("g", "u", ("n", 0), "d", ("c", 0)):
        loads[key].start()
    for i in range(1, DEPTH):
        loads["n", i].start()
        loads["c", i].start()
    late = own_copies([(a_mid, mid), (a_cot, cot)], own_sems, 11)
    meet([other, sibling] + at.z_peers() + y_peers)
    mail = Mail(send_sems, recv_sems)

    def half_rows(index, side):
        return band(index * HALVES + side, tokens)

    norm_line = LineReduce(
        mail, at, 1, lambda index: [p_n.at[half_rows(index, x)]], lambda slot: [l_n.at[slot]]
    )
    norm_swaps = []

    def compute(i):
        block = band(order[i], block_rows)
        if i == 0:
            for name in ("g", "u", "d"):
                loads[name].wait()
        loads["n", i].wait()
        loads["c", i].wait()

        @pl.loop(0, part // TILE)
        def _(index):
            g_cols, u_cols, d_cols = [
                pl.ds(pl.multiple_of(i * part + index * TILE, TILE), TILE) for i in range(3)
            ]
            gate = matmul(x_n[block, :], full[:, g_cols])
            up = matmul(x_n[block, :], full[:, u_cols])
            grad_act = matmul(x_c[block, :], full[:, d_cols])
            sigmoid_gate = 1.0 / (1.0 + jnp.exp(-gate))
            silu_val = gate * sigmoid_gate
            hidden[block, g_cols] = (
                grad_act * up * sigmoid_gate * (1.0 + gate * (1.0 - sigmoid_gate))
            ).astype(jnp.bfloat16)
            hidden[block, u_cols] = (grad_act * silu_val).astype(jnp.bfloat16)
            hidden[block, d_cols] = (silu_val * up).astype(jnp.bfloat16)

        @pl.loop(0, width // TILE)
        def _(index):
            cols = band(index, TILE)
            p_n[block, cols] = dot_nt(hidden[block, gate_up], full[cols, gate_up]).astype(jnp.bfloat16)

        norm_swaps.append(mail.send(p_n.at[half_rows(order[i], 1 - x)], h_n.at[i], other))

    def compute_out(i):
        block = band(order[i], block_rows)

        @pl.loop(0, width // TILE)
        def _(index):
            cols = band(index, TILE)
            p_o[block, cols] = dot_nt(hidden[block, down], full[cols, down]).astype(jnp.bfloat16)

        stores.extend(own_copies([(p_o.at[block], a_p.at[block])], own_sems, 7 + i))

    def norm_step(i):
        norm_swaps[i].wait_recv()
        add_into(p_n.at[half_rows(order[i], x)], h_n.at[i])
        norm_line.pass_on(i, 0)

    def weight_grads(span, i):
        left = x_n if span is gate_up else x_c

        @pl.loop(0, width // DEPTH // TILE)
        def _(index):
            cols = pl.ds(pl.multiple_of(order[i] * (width // DEPTH) + index * TILE, TILE), TILE)
            full[cols, span] = matmul(left[:, cols].T, hidden[:, span]).astype(jnp.bfloat16)

        to_core[span.start, i] = [
            mail.send(
                full.at[at.rows(order[i], side, 1 - c, rows), span],
                from_core.at[order[i], side, :, span],
                sibling,
            )
            for side in range(at.wide)
        ]

    to_core, to_y = {}, {}

    def core_stage(span, i):
        receive(to_core[span.start, i])
        for side in range(at.wide):
            add_into(
                full.at[at.rows(order[i], side, c, rows), span], from_core.at[order[i], side, :, span]
            )
        to_y[span.start, i] = [
            mail.send(
                full.at[at.rows(order[i], at.y_off(j), c, rows), span],
                from_y.at[j - 1, order[i], :, span],
                y_peers[j - 1],
            )
            for j in range(1, at.wide)
        ]

    def y_stage(span, i):
        receive(to_y[span.start, i])
        total = full[at.rows(order[i], y, c, rows), span].astype(jnp.float32)
        for j in range(1, at.wide):
            total = total + from_y[j - 1, order[i], :, span].astype(jnp.float32)
        shares[order[i], :, span] = total.astype(jnp.bfloat16)

    spread_base = mail.reserve(2 * DEPTH)

    def spread_copies(i, source, target, device):
        return [
            pltpu.make_async_remote_copy(
                shares.at[target, :, pl.ds(w * part, part)],
                out.at[:, band(source, part)],
                mail.send_sems.at[spread_base + 2 * i + w],
                mail.recv_sems.at[spread_base + 2 * source + w],
                device_id=device,
                device_id_type=MESH,
            )
            for w, out in enumerate((d_g, d_u))
        ]

    def spread(i):
        copies = spread_copies(i, z, order[i], at.device(z=order[i]))
        start_all(copies)
        mail.open += [(copy, None) for copy in copies]

    stores = []
    compute(0)
    compute(1)
    compute(2)
    norm_step(0)
    compute(3)
    weight_grads(gate_up, 0)
    norm_step(1)
    weight_grads(gate_up, 1)
    norm_line.pass_on(0, 1)
    core_stage(gate_up, 0)
    weight_grads(gate_up, 2)
    core_stage(gate_up, 1)
    weight_grads(gate_up, 3)
    core_stage(gate_up, 2)
    compute_out(0)
    core_stage(gate_up, 3)
    compute_out(1)
    norm_step(2)
    norm_line.pass_on(1, 1)
    compute_out(2)
    norm_line.pass_on(2, 1)
    compute_out(3)
    weight_grads(down, 0)
    y_stage(gate_up, 0)
    spread(0)
    weight_grads(down, 1)
    core_stage(down, 0)
    weight_grads(down, 2)
    core_stage(down, 1)
    weight_grads(down, 3)
    core_stage(down, 2)
    core_stage(down, 3)
    y_stage(gate_up, 1)
    spread(1)
    y_stage(gate_up, 2)
    spread(2)
    norm_swaps[3].wait_recv()
    finish_own(late)
    o_m[...] = p_n[half_rows(z, x), :].astype(jnp.float32) + h_n[3].astype(jnp.float32)

    def add_norm(_, landed):
        o_m[...] = o_m[...] + landed[...].astype(jnp.float32)

    norm_line.last(add_norm)
    grad_norm = o_m[...]
    values = mid[...]
    inv_rms = lax.rsqrt(jnp.mean(values * values, axis=-1, keepdims=True) + EPSILON)
    grad_values, terms = norm_back(grad_norm, values, inv_rms, gain[...])
    o_t[...] = jnp.sum(terms, axis=0, keepdims=True)
    kept = band(x, tokens)
    total = cot[kept, :].astype(jnp.float32) + grad_values
    o_m[...] = total
    o_h[kept, :] = total.astype(jnp.bfloat16)
    swap_h = mail.send(o_h.at[kept], o_h.at[kept], other)
    stores += own_copies([(o_m, a_m)], own_sems, 0)
    y_stage(gate_up, DEPTH - 1)
    stores += own_copies(
        [
            (shares.at[z, :, pl.ds(w * part, part)], out.at[:, band(z, part)])
            for w, out in enumerate((d_g, d_u))
        ],
        own_sems,
        1,
    )
    for i in range(DEPTH):
        y_stage(down, i)
        stores += own_copies([(shares.at[order[i], :, down], a_shares.at[order[i]])], own_sems, 3 + i)
    swap_h.wait_recv()
    stores += own_copies([(o_h, a_h)], own_sems, 11)
    for k in range(1, DEPTH):
        source = at.z_off(-k)
        receive(spread_copies(0, source, z, at.device(z=source)))
    mail.finish()
    finish_own(stores)


def mlp(dp_size, weights, normed, cots, mid, cot, gain):
    wide = dp_size // (DEPTH * CORES)
    tokens, width = mid.shape
    cols = weights.shape[1]
    rows = width // dp_size
    every = DEPTH * HALVES * tokens
    half, full = jnp.bfloat16, jnp.float32
    copies = LineReduce.slots + DEPTH + 2 * DEPTH * (2 * wide - 1) + 1 + 2 * DEPTH
    shapes = [
        jax.ShapeDtypeStruct((tokens, width), full),
        jax.ShapeDtypeStruct((HALVES * tokens, width), half),
        jax.ShapeDtypeStruct((every, width), half),
        jax.ShapeDtypeStruct((1, width), full),
        jax.ShapeDtypeStruct((DEPTH, rows, cols // 3), half),
    ] + [jax.ShapeDtypeStruct((rows, DEPTH * cols // 3), half)] * 2
    return pl.pallas_call(
        functools.partial(mlp_kernel, dp_size),
        out_shape=shapes,
        in_specs=[ANY] * 5 + [VMEM],
        out_specs=[ANY] * 3 + [VMEM] + [ANY] * 3,
        scratch_shapes=[
            pltpu.VMEM((tokens, width), full),
            pltpu.VMEM((HALVES * tokens, width), half),
            pltpu.VMEM((tokens, width), full),
            pltpu.VMEM((HALVES * tokens, width), half),
            pltpu.VMEM((DEPTH, rows, cols), half),
        ]
        + [pltpu.VMEM((width, cols), half)]
        + [pltpu.VMEM((every, width), half)] * 2
        + [pltpu.VMEM((every, cols), half)]
        + [pltpu.VMEM((every, width), half)] * 2
        + [
            pltpu.VMEM((DEPTH, tokens, width), half),
            pltpu.VMEM((LineReduce.slots, tokens, width), half),
        ]
        + [
            pltpu.VMEM((DEPTH, wide, rows, cols), half),
            pltpu.VMEM((wide - 1, DEPTH, rows, cols), half),
            pltpu.SemaphoreType.DMA((13,)),
            pltpu.SemaphoreType.DMA((copies,)),
            pltpu.SemaphoreType.DMA((copies,)),
        ],
        compiler_params=pltpu.CompilerParams(
            collective_id=1, has_side_effects=True, vmem_limit_bytes=63 * 2**20
        ),
    )(weights, normed, cots, mid, cot, gain)


def backward_kernel(
    dp_size, shares, weights, a_mid, mid_half, a_out, a_part, t_m, gain_one, a_row, a_normed, a_query,
    a_key, a_values, a_queries, a_keys, context, a_log, a_cosine, a_sine, a_bias, q_gain, k_gain,
    o_l, o_i, sums, d_q, d_k, d_v, d_o, d_d,
    grad_mid, layer_mid, row_in, normed_one, query_raw, key_raw, values_half, queries, keys,
    log_total, cosine, sine, bias,
    full, head_grads, gains, from_other, totals, core_o, core_h, core_s, y_o, y_h, y_s, z_o, z_h, z_s,
    part_own, part_other, part_line, spare, context_grad, raw_half, raw_head, flipped, partial,
    outgoing, incoming, own_sems, send_sems, recv_sems,
):
    at = Place(dp_size)
    z, y, c, x = at.z, at.y, at.c, at.x
    other, sibling = at.device(x=1 - x), at.device(c=1 - c)
    y_peers, z_peers = at.y_peers(), at.z_peers()
    order = at.order()
    tokens, width = grad_mid.shape
    rows = d_q.shape[0]
    part = shares.shape[2]
    spans, start = [], 0
    for out in (d_q, d_k, d_v, d_o):
        spans.append(pl.ds(start, out.shape[1]))
        start += out.shape[1]
    q_span, k_span, v_span, o_span = spans
    qkv_span = pl.ds(0, start - d_o.shape[1])
    q_cols, kv_width = d_q.shape[1], d_k.shape[1]
    head_dim = q_gain.shape[1]

    def band(index, size):
        return pl.ds(pl.multiple_of(index * size, size), size)

    kept, given = band(x, tokens), band(1 - x, tokens)
    loads = own_copies(
        [(weights.at[:, span], full.at[:, span]) for span in (o_span, qkv_span)], own_sems
    )
    late = own_copies(
        [
            (a_normed, normed_one), (a_query, query_raw), (a_key, key_raw), (a_values, values_half),
            (a_queries, queries), (a_keys, keys), (a_log, log_total), (a_cosine, cosine),
            (a_sine, sine), (a_bias, bias), (a_out, layer_mid), (a_mid, grad_mid), (a_row, row_in),
        ],
        own_sems,
        2,
    )
    part_loads = own_copies(
        [(a_part.at[band(index * HALVES + x, tokens)], part_own.at[index]) for index in order],
        own_sems,
        16,
    )
    meet([other, sibling] + y_peers + z_peers)
    mail = Mail(send_sems, recv_sems)
    part_swaps = [
        mail.send(a_part.at[band(index * HALVES + 1 - x, tokens)], part_other.at[i], other)
        for i, index in enumerate(order)
    ]
    part_sums = LineReduce(
        mail, at, 1, lambda index: [part_own.at[index]], lambda slot: [part_line.at[slot]]
    )

    def part_step(i):
        part_swaps[i].wait_recv()
        part_loads[i].wait()
        add_into(part_own.at[order[i]], part_other.at[i])
        if i < DEPTH - 1:
            part_sums.pass_on(i, 0)

    to_z = [
        mail.send(shares.at[at.z_off(k)], d_d.at[:, band(z, part)], z_peers[k - 1])
        for k in (2, 1, 3)
    ]
    kv_heads = key_raw.shape[1] // head_dim
    group = query_raw.shape[1] // key_raw.shape[1]
    q_part = group * head_dim

    def block_of(zb, side, core):
        return (zb * at.wide + side) * CORES + core

    class Sums:
        def __init__(self, held, core_land, y_land, z_land, outs):
            self.held, self.core_land, self.y_land, self.outs = held, core_land, y_land, outs
            self.line = LineReduce(
                mail, at, 1, lambda zb: [held(zb, y, c)], lambda slot: [z_land.at[slot]]
            )
            self.to_core, self.to_y = {}, {}

        def core_sends(self, i):
            self.to_core[i] = [
                mail.send(
                    self.held(order[i], side, 1 - c), self.core_land.at[order[i], side], sibling
                )
                for side in range(at.wide)
            ]

        def core_stage(self, i):
            receive(self.to_core[i])
            for side in range(at.wide):
                add_into(self.held(order[i], side, c), self.core_land.at[order[i], side])
            self.to_y[i] = [
                mail.send(
                    self.held(order[i], at.y_off(j), c), self.y_land.at[j - 1, order[i]], y_peers[j - 1]
                )
                for j in range(1, at.wide)
            ]

        def y_stage(self, i):
            receive(self.to_y[i])
            terms = [self.y_land.at[j - 1, order[i]] for j in range(1, at.wide)]
            own = self.held(order[i], y, c)
            if i < DEPTH - 1:
                add_into(own, *terms)
                return
            for out, span in self.outs:
                out[...] = own[:, span].astype(jnp.float32)
                add_into(out, *[term.at[:, span] for term in terms])

        def finish(self):
            def use(_, landed):
                for out, span in self.outs:
                    add_into(out, landed.at[:, span])

            self.line.last(use)

    out_sums = Sums(
        lambda zb, side, core: full.at[at.rows(zb, side, core, rows), o_span],
        core_o, y_o, z_o, [(d_o, pl.ds(0, d_o.shape[1]))],
    )
    head_sums = []
    for j in range(kv_heads):
        kv_cols = pl.ds(j * head_dim, head_dim)
        head_sums.append(
            Sums(
                lambda zb, side, core, j=j: head_grads.at[j, at.rows(zb, side, core, rows)],
                core_h.at[j], y_h.at[j], z_h.at[j],
                [
                    (d_q.at[:, pl.ds(j * q_part, q_part)], pl.ds(0, q_part)),
                    (d_k.at[:, kv_cols], pl.ds(q_part, head_dim)),
                    (d_v.at[:, kv_cols], pl.ds(q_part + head_dim, head_dim)),
                ],
            )
        )
    gain_sums = Sums(
        lambda zb, side, core: totals.at[block_of(zb, side, core)],
        core_s, y_s, z_s, [(sums, pl.ds(0, sums.shape[1]))],
    )

    gains[...] = jnp.zeros(gains.shape, jnp.float32)
    loads[0].wait()

    def write_context(cols, value):
        context_grad[:, cols] = value.astype(jnp.bfloat16)

    matmul_tiles(mid_half, full.at[:, o_span], write_context)

    quarter = width // DEPTH
    for i in range(DEPTH):

        @pl.loop(0, quarter // TILE)
        def _(index, i=i):
            cols = pl.ds(pl.multiple_of(order[i] * quarter + index * TILE, TILE), TILE)
            full[cols, o_span] = dot_tn(mid_half[:, cols], context[...]).astype(jnp.bfloat16)

        out_sums.core_sends(i)
    own_share = own_copies([(shares.at[z], spare)], own_sems, 15)
    for i in range(DEPTH):
        out_sums.core_stage(i)
    finish_own(late)
    finish_own(own_share)
    own_share = own_copies([(spare, d_d.at[:, band(z, part)])], own_sems, 15)
    flipped[...] = normed_one[...].T

    scale = 1.0 / math.sqrt(head_dim)

    def raw_grad(grad, raw, gain):
        back = grad * cosine[...] - turned(grad) * sine[...]
        inv_rms = lax.rsqrt(jnp.mean(raw * raw, axis=-1, keepdims=True) + EPSILON)
        grad_raw, terms = norm_back(back, raw, inv_rms, gain)
        return grad_raw.astype(jnp.bfloat16), jnp.sum(terms, axis=0, keepdims=True)

    for j in range(kv_heads):
        q_sum = jnp.zeros((1, head_dim), jnp.float32)
        k_sum = jnp.zeros((1, head_dim), jnp.float32)
        kv_cols = pl.ds(j * head_dim, head_dim)
        key_total = jnp.zeros((row_in.shape[0], head_dim), jnp.float32)
        value_total = jnp.zeros((row_in.shape[0], head_dim), jnp.float32)
        for g in range(group):
            head = j * group + g
            cols = pl.ds(head * head_dim, head_dim)
            scores = dot_nt(queries[:, cols], keys[:, kv_cols]) * scale + bias[...]
            probs = jnp.exp(scores - log_total[:, head : head + 1])
            grad_context = context_grad[:, cols]
            grad_probs = dot_nt(grad_context, values_half[:, kv_cols])
            delta = jnp.sum(
                grad_context.astype(jnp.float32) * context[:, cols].astype(jnp.float32),
                axis=-1,
                keepdims=True,
            )
            grad_scores = (probs * (grad_probs - delta) * scale).astype(jnp.bfloat16)
            grad_query, terms = raw_grad(
                matmul(grad_scores, keys[:, kv_cols]), query_raw[:, cols], q_gain[...]
            )
            raw_half[:, cols] = grad_query
            raw_head[:, pl.ds(g * head_dim, head_dim)] = grad_query
            q_sum = q_sum + terms
            key_total = key_total + dot_tn(grad_scores, queries[:, cols])
            value_total = value_total + dot_tn(probs.astype(jnp.bfloat16), grad_context)
        grad_key, terms = raw_grad(key_total, key_raw[:, kv_cols], k_gain[...])
        grad_value = value_total.astype(jnp.bfloat16)
        raw_half[:, pl.ds(q_cols + j * head_dim, head_dim)] = grad_key
        raw_half[:, pl.ds(q_cols + kv_width + j * head_dim, head_dim)] = grad_value
        raw_head[:, pl.ds(q_part, head_dim)] = grad_key
        raw_head[:, pl.ds(q_part + head_dim, head_dim)] = grad_value
        k_sum = k_sum + terms
        gains[0, 2:3, :head_dim] = gains[0, 2:3, :head_dim] + q_sum
        gains[0, 3:4, :head_dim] = gains[0, 3:4, :head_dim] + k_sum
        for i in range(DEPTH):

            @pl.loop(0, quarter // TILE)
            def _(index, i=i, j=j):
                cols = pl.ds(pl.multiple_of(order[i] * quarter + index * TILE, TILE), TILE)
                head_grads[j, cols, :] = matmul(flipped[cols, :], raw_head[...]).astype(jnp.bfloat16)

            head_sums[j].core_sends(i)
        if 1 <= j < DEPTH:
            out_sums.y_stage(j - 1)
            out_sums.line.pass_on(j - 1, 0)
        if j >= 2:
            out_sums.line.pass_on(j - 2, 1)
        if j == 0:
            part_step(0)
        if j == DEPTH - 2:
            part_step(1)
            part_sums.pass_on(0, 1)
        if j > 0:
            for i in range(DEPTH):
                head_sums[j - 1].core_stage(i)
    for j in range(max(kv_heads - 1, 0), DEPTH - 1):
        out_sums.y_stage(j)
        out_sums.line.pass_on(j, 0)
    for j in range(max(kv_heads - 2, 0), DEPTH - 2):
        out_sums.line.pass_on(j, 1)
    out_sums.y_stage(DEPTH - 1)
    for i in range(DEPTH):
        head_sums[kv_heads - 1].core_stage(i)
    finish_own(loads[1:])

    def project(token_rows, target):
        @pl.loop(0, width // TILE)
        def _(index):
            cols = band(index, TILE)
            total = dot_nt(raw_half[token_rows, :], full[cols, qkv_span])
            partial[token_rows, cols] = total
            if target is not None:
                target[:, cols] = total.astype(target.dtype)

    project(given, outgoing)
    swap = mail.send(outgoing, incoming, other)
    project(kept, None)

    values = row_in[...].astype(jnp.float32)
    inv_rms = lax.rsqrt(jnp.mean(values * values, axis=-1, keepdims=True) + EPSILON)
    gain_terms = jnp.sum(partial[...] * values * inv_rms, axis=0, keepdims=True)
    blocks = gains.shape[0]
    share = width // blocks
    head_terms = gains[0, 2:4, :]
    for index in range(blocks):
        gains[index, 0:1, :share] = gain_terms[:, index * share : (index + 1) * share]
        gains[index, 1:2, :share] = t_m[:, index * share : (index + 1) * share]
        gains[index, 2:4, :] = head_terms
    swap_gains = mail.send(gains, from_other, other)
    swap.wait_recv()
    grad_norm = partial[kept, :] + incoming[...].astype(jnp.float32)
    values = row_in[kept, :].astype(jnp.float32)
    inv_rms = lax.rsqrt(jnp.mean(values * values, axis=-1, keepdims=True) + EPSILON)
    grad_values, _ = norm_back(grad_norm, values, inv_rms, gain_one[...])
    o_i[kept, :] = (grad_mid[...] + grad_values).astype(jnp.bfloat16)
    swap_back = mail.send(o_i.at[kept], o_i.at[kept], other)

    if kv_heads < DEPTH - 1:
        part_step(1)
    part_sums.pass_on(1, 1)
    part_step(2)
    out_sums.line.pass_on(DEPTH - 2, 1)
    swap_gains.wait_recv()
    totals[...] = gains[...] + from_other[...]
    for i in range(DEPTH):
        gain_sums.core_sends(i)
    for i in range(DEPTH):
        gain_sums.core_stage(i)
    every = head_sums + [gain_sums]
    part_sums.pass_on(2, 1)
    part_step(3)
    for index in range(len(every) + DEPTH - 1):
        if index < len(every):
            for i in range(DEPTH):
                every[index].y_stage(i)
        for turn in range(DEPTH - 1):
            if 0 <= index - turn < len(every):
                every[index - turn].line.pass_on(turn, 0)
            if 0 <= index - turn - 1 < len(every):
                every[index - turn - 1].line.pass_on(turn, 1)
    out_sums.finish()
    layer_mid[...] = layer_mid[...] + part_own[z].astype(jnp.float32)

    def add_part(_, landed):
        layer_mid[...] = layer_mid[...] + landed[...].astype(jnp.float32)

    part_sums.last(add_part)
    o_l[kept, :] = layer_mid[...].astype(jnp.bfloat16)
    swap_l = mail.send(o_l.at[kept], o_l.at[kept], other)
    for one in every[:-1]:
        one.finish()
    every[-1].finish()
    receive([swap_l, swap_back] + to_z)
    finish_own(own_share)
    mail.finish()


def backward(dp_size, shares, weights, cols, grad_mid, mid_half, layer_mid, part_out, gain_terms, saved, gains):
    wide = dp_size // (DEPTH * CORES)
    tokens, width = grad_mid.shape
    seq_len = HALVES * tokens
    part = shares.shape[2]
    rows = width // dp_size
    half, full = jnp.bfloat16, jnp.float32
    every = sum(cols)
    kv_heads = cols[1] // gains[2].shape[1]
    head_cols = (every - cols[3]) // kv_heads
    passes = kv_heads + 2
    copies = 3 + 4 + DEPTH + LineReduce.slots + passes * (LineReduce.slots + DEPTH * (2 * wide - 1))
    shapes = [jax.ShapeDtypeStruct((seq_len, width), half)] * 2
    shapes += [jax.ShapeDtypeStruct((8, 128), full)]
    shapes += [jax.ShapeDtypeStruct((rows, col), full) for col in cols]
    shapes += [jax.ShapeDtypeStruct((rows, DEPTH * part), half)]
    lazy = [grad_mid, layer_mid] + [one for i, one in enumerate(saved) if i != 7]
    inputs = [grad_mid, mid_half, layer_mid, part_out, gain_terms, gains[0], *saved, *gains[2:]]
    return pl.pallas_call(
        functools.partial(backward_kernel, dp_size),
        out_shape=shapes,
        in_specs=[ANY] * 3 + [VMEM, ANY, ANY, VMEM, VMEM] + [ANY] * 7 + [VMEM] + [ANY] * 4 + [VMEM] * 2,
        out_specs=[VMEM] * 7 + [ANY],
        scratch_shapes=[pltpu.VMEM(one.shape, one.dtype) for one in lazy]
        + [
            pltpu.VMEM((width, every), half),
            pltpu.VMEM((kv_heads, width, head_cols), half),
            pltpu.VMEM((dp_size, 8, 128), full),
            pltpu.VMEM((dp_size, 8, 128), full),
            pltpu.VMEM((dp_size, 8, 128), full),
            pltpu.VMEM((DEPTH, wide, rows, cols[3]), half),
            pltpu.VMEM((kv_heads, DEPTH, wide, rows, head_cols), half),
            pltpu.VMEM((DEPTH, wide, 8, 128), full),
            pltpu.VMEM((wide - 1, DEPTH, rows, cols[3]), half),
            pltpu.VMEM((kv_heads, wide - 1, DEPTH, rows, head_cols), half),
            pltpu.VMEM((wide - 1, DEPTH, 8, 128), full),
            pltpu.VMEM((LineReduce.slots, rows, cols[3]), half),
            pltpu.VMEM((kv_heads, LineReduce.slots, rows, head_cols), half),
            pltpu.VMEM((LineReduce.slots, 8, 128), full),
            pltpu.VMEM((DEPTH, tokens, width), half),
            pltpu.VMEM((DEPTH, tokens, width), half),
            pltpu.VMEM((LineReduce.slots, tokens, width), half),
            pltpu.VMEM((rows, part), half),
            pltpu.VMEM((seq_len, cols[0]), half),
            pltpu.VMEM((seq_len, every - cols[3]), half),
            pltpu.VMEM((seq_len, head_cols), half),
            pltpu.VMEM((width, seq_len), half),
            pltpu.VMEM((seq_len, width), full),
            pltpu.VMEM((tokens, width), half),
            pltpu.VMEM((tokens, width), half),
            pltpu.SemaphoreType.DMA((20,)),
            pltpu.SemaphoreType.DMA((copies,)),
            pltpu.SemaphoreType.DMA((copies,)),
        ],
        compiler_params=pltpu.CompilerParams(
            collective_id=2, has_side_effects=True, vmem_limit_bytes=63 * 2**20
        ),
    )(shares, weights, *inputs)


def body(
    dp_size,
    layer_in,
    seg_ids,
    w_q,
    w_k,
    w_v,
    w_o,
    w_gate,
    w_up,
    w_down,
    attn_gain,
    mlp_gain,
    q_gain,
    k_gain,
    cotangent,
):
    row_in = layer_in[0]
    row_cot = cotangent[0]
    width = row_in.shape[1]
    gains = [gain[None, :] for gain in (attn_gain, mlp_gain, q_gain, k_gain)]
    outs = forward(
        dp_size, (w_q, w_k, w_v, w_o, w_gate, w_up, w_down), row_cot, row_in, seg_ids[0], gains
    )
    attn_full, ffn_full, cots, normed, mid = outs[:5]
    saved = outs[5:]
    outs = mlp(
        dp_size, ffn_full, normed.reshape(-1, width), cots.reshape(-1, width), mid, row_cot, gains[1]
    )
    grad_mid, mid_half, part_out, gain_terms, shares, *gate_up_grads = outs
    cols = [weight.shape[1] for weight in (w_q, w_k, w_v, w_o)]
    outs = backward(
        dp_size, shares, attn_full, cols, grad_mid, mid_half, mid, part_out, gain_terms,
        [row_in] + list(saved), gains,
    )
    out_row, in_grad, sums = outs[:3]
    share = width // dp_size
    gain_outs = [sums[0, :share], sums[1, :share]]
    for i, gain in enumerate((q_gain, k_gain)):
        share = gain.shape[0] // dp_size
        gain_outs.append(lax.dynamic_slice(sums[2 + i], (lax.axis_index("dp") * share,), (share,)))
    ffn_grads = [grad.astype(jnp.float32) for grad in (*gate_up_grads, outs[7])]
    return (out_row[None], in_grad[None], *outs[3:7], *ffn_grads, *gain_outs)


def solution(mesh):
    return jax.shard_map(
        functools.partial(body, mesh.shape["dp"]),
        mesh=mesh,
        in_specs=(
            P("dp", None, None),
            P("dp", None),
            P("dp", "mp"),
            P("dp", "mp"),
            P("dp", "mp"),
            P("dp", "mp"),
            P("dp", "mp"),
            P("dp", "mp"),
            P("dp", "mp"),
            P(),
            P(),
            P(),
            P(),
            P("dp", None, None),
        ),
        out_specs=(
            P("dp", None, None),
            P("dp", None, None),
            P("dp", "mp"),
            P("dp", "mp"),
            P("dp", "mp"),
            P("dp", "mp"),
            P("dp", "mp"),
            P("dp", "mp"),
            P("dp", "mp"),
            P("dp"),
            P("dp"),
            P("dp"),
            P("dp"),
        ),
        check_vma=False,
    )
```

```python
import functools
import math

import jax
import jax.numpy as jnp
from jax import lax
from jax.experimental import pallas as pl
from jax.experimental.pallas import tpu as pltpu
from jax.sharding import PartitionSpec as P

EPSILON = 1e-06
ROPE_BASE = 1000000.0
MASKED = -1e30


def matmul(left_op, right_op):
    return jnp.dot(left_op, right_op, preferred_element_type=jnp.float32)


def rms_norm(values, gain_vec):
    inv_rms = lax.rsqrt(jnp.mean(values * values, axis=-1, keepdims=True) + EPSILON)
    return (values * inv_rms * gain_vec, inv_rms)


def norm_back(grad_norm, values, inv_rms, gain_vec):
    scaled = grad_norm * gain_vec
    cubed = inv_rms * inv_rms * inv_rms
    grad_values = inv_rms * scaled - values * cubed * jnp.mean(
        scaled * values, axis=-1, keepdims=True
    )
    return (grad_values, grad_norm * values * inv_rms)


MESH = pl.DeviceIdType.MESH
ANY = pl.BlockSpec(memory_space=pl.ANY)
VMEM = pl.BlockSpec(memory_space=pltpu.VMEM)
DEPTH = 4
CORES = 2
HALVES = 2
UP, DOWN = 0, 1
TILE = 256


def split(index, size):
    size = jnp.int32(size)
    return lax.div(index, size), lax.rem(index, size)


class Place:
    def __init__(self, dp_size):
        self.wide = dp_size // (DEPTH * CORES)
        self.x = lax.axis_index("mp")
        rest, self.c = split(lax.axis_index("dp"), CORES)
        self.z, self.y = split(rest, self.wide)

    def device(self, z=None, y=None, c=None, x=None):
        z = self.z if z is None else z
        y = self.y if y is None else y
        c = self.c if c is None else c
        x = self.x if x is None else x
        return ((z * self.wide + y) * CORES + c, x)

    def z_off(self, step):
        return lax.rem(self.z + DEPTH + step, jnp.int32(DEPTH))

    def z_flip(self, bits):
        z = self.z
        if bits == DEPTH - 1:
            return DEPTH - 1 - z
        return z + bits - 2 * bits * lax.rem(lax.div(z, jnp.int32(bits)), jnp.int32(2))

    def y_off(self, step):
        return lax.rem(self.y + self.wide + step, jnp.int32(self.wide))

    def rows(self, z, y, c, count):
        return pl.ds(pl.multiple_of(((z * self.wide + y) * CORES + c) * count, count), count)

    def line(self):
        return [self.device(z=self.z_off(1)), self.device(z=self.z_off(-1))]

    def z_peers(self):
        return [self.device(z=self.z_off(k)) for k in range(1, DEPTH)]

    def y_peers(self):
        return [self.device(y=self.y_off(j)) for j in range(1, self.wide)]

    def order(self):
        low = 1 - lax.div(self.z, jnp.int32(2))
        return [3 * low, 1 + low, low * (1 - self.z) + (1 - low) * (5 - self.z), self.z]


def guarded(when, action):
    if when is None:
        action()
    else:
        pl.when(when)(action)


class Mail:
    def __init__(self, send_sems, recv_sems):
        self.send_sems, self.recv_sems = send_sems, recv_sems
        self.count = 0
        self.open = []

    def reserve(self, count):
        first = self.count
        self.count += count
        return first

    def describe(self, source, target, device, slot):
        return pltpu.make_async_remote_copy(
            source,
            target,
            self.send_sems.at[slot],
            self.recv_sems.at[slot],
            device_id=device,
            device_id_type=MESH,
        )

    def make(self, source, target, device, when=None, slot=None):
        copy = self.describe(source, target, device, self.reserve(1) if slot is None else slot)
        self.open.append((copy, when))
        return copy

    def send(self, source, target, device, when=None):
        copy = self.make(source, target, device, when)
        guarded(when, copy.start)
        return copy

    def finish(self):
        for copy, when in self.open:
            guarded(when, copy.wait_send)


def meet(devices):
    barrier = pltpu.get_barrier_semaphore()
    for device in devices:
        pl.semaphore_signal(barrier, inc=1, device_id=device, device_id_type=MESH)
    pl.semaphore_wait(barrier, len(devices))


def receive(copies):
    for copy in copies:
        copy.wait_recv()


def start_all(copies):
    for copy in copies:
        copy.start()


class LineGather:
    def __init__(self, mail, at, own, place, sides, sibling=None, share_own=True):
        self.mail, self.at, self.place = mail, at, place
        self.sides, self.sibling = sides, sibling
        self.neighbours = at.line()
        self.open_end = [at.z < DEPTH - 1, at.z > 0]
        pairs = list(zip(own, place(at.z, 0)))
        self.hops = [
            [mail.send(source, target, self.neighbours[way], self.open_end[way]) for source, target in pairs]
            for way in (UP, DOWN)
        ]
        self.over, self.cores = {}, []
        if share_own:
            self.over["own"] = [
                [mail.send(source, target, side) for source, target in pairs] for side in sides
            ]
        if sibling is not None:
            self.cores.append(
                (None, [mail.send(source, target, sibling) for source, target in pairs])
            )

    def where(self, way, step):
        z = self.at.z
        if way == UP:
            return z >= step + 1, self.at.z_off(-1 - step)
        return z + 1 + step < DEPTH, self.at.z_off(1 + step)

    def step(self, step):
        for way in (UP, DOWN):
            got, index = self.where(way, step)
            refs = self.place(index, 0)
            arrived = self.hops[way]
            onward = []
            if step < DEPTH - 2:
                more = got & self.open_end[way]
                onward = [self.mail.make(ref, ref, self.neighbours[way], more) for ref in refs]
            over = [[self.mail.make(ref, ref, side, got) for ref in refs] for side in self.sides]
            cores = []
            if self.sibling is not None:
                cores = [self.mail.make(ref, ref, self.sibling, got) for ref in refs]

            def pass_on(way=way, arrived=arrived, onward=onward, over=over, cores=cores):
                receive(arrived)
                pl.when(self.open_end[way])(lambda: start_all(onward))
                for copies in over:
                    start_all(copies)
                start_all(cores)

            pl.when(got)(pass_on)
            self.hops[way] = onward
            self.over[way, step] = over
            if cores:
                self.cores.append((got, cores))

    def side_step(self, key):
        got, index = (None, self.at.z) if key == "own" else self.where(*key)
        cores = []
        for j in range(1, len(self.sides) + 1):
            if self.sibling is not None:
                refs = self.place(index, j)
                cores += [self.mail.make(ref, ref, self.sibling, got) for ref in refs]

        def pass_on():
            for copies in self.over[key]:
                receive(copies)
            start_all(cores)

        guarded(got, pass_on)
        if cores:
            self.cores.append((got, cores))

    def side_steps(self, step):
        self.side_step((UP, step))
        self.side_step((DOWN, step))

    def finish(self):
        for got, cores in self.cores:
            guarded(got, lambda cores=cores: receive(cores))


class LineReduce:
    slots = 2 * (DEPTH - 1)

    def __init__(self, mail, at, pieces, part, land):
        self.mail, self.at, self.pieces, self.part, self.land = mail, at, pieces, part, land
        self.base = mail.reserve(self.slots * pieces)

    def copies(self, index, sources, device):
        slots = [self.base + index * self.pieces + i for i in range(self.pieces)]
        return [
            self.mail.describe(source, target, device, slot)
            for source, target, slot in zip(sources, self.land(index), slots)
        ]

    def pass_on(self, turn, part=None):
        z = self.at.z
        low = 1 - lax.div(z, jnp.int32(2))
        up = low if turn < 2 else 1 - lax.rem(z, jnp.int32(2))
        target = self.at.order()[turn]
        index = up * (target - 1) + (1 - up) * (DEPTH - 1 + target)
        device = self.at.device(z=z + 2 * up - 1)
        sources = self.part(target)
        copies = self.copies(index, sources, device)
        has_in = up * jnp.where(z > 0, 1, 0) + (1 - up) * jnp.where(z < DEPTH - 1, 1, 0)

        if part != 0:

            @pl.when(has_in > 0)
            def _():
                receive(copies)
                for source, landed in zip(sources, self.land(index)):
                    add_into(source, landed)
                if part == 1:
                    start_all(copies)

        if part == 0:
            pl.when(has_in == 0)(lambda: start_all(copies))
        elif part is None:
            start_all(copies)
        if part != 1:
            self.mail.open += [(copy, None) for copy in copies]

    def last(self, use):
        z = self.at.z
        sources = self.part(z)
        for when, index, neighbour in (
            (z > 0, lax.max(z - 1, 0), self.at.z_off(-1)),
            (z < DEPTH - 1, lax.min(DEPTH - 1 + z, self.slots - 1), self.at.z_off(1)),
        ):
            copies = self.copies(index, sources, self.at.device(z=neighbour))

            @pl.when(when)
            def _(copies=copies, index=index):
                receive(copies)
                for i, landed in enumerate(self.land(index)):
                    use(i, landed)


def own_copies(pairs, sems, first=0):
    copies = [
        pltpu.make_async_copy(source, target, sems.at[first + i])
        for i, (source, target) in enumerate(pairs)
    ]
    start_all(copies)
    return copies


def finish_own(copies):
    for copy in copies:
        copy.wait()


def add_into(target, *others):
    total = target[...].astype(jnp.float32)
    for other in others:
        total = total + other[...].astype(jnp.float32)
    target[...] = total.astype(target.dtype)


def dot_nt(left_op, right_op):
    return lax.dot_general(
        left_op, right_op, (((1,), (1,)), ((), ())), preferred_element_type=jnp.float32
    )


def dot_tn(left_op, right_op):
    return lax.dot_general(
        left_op, right_op, (((0,), (0,)), ((), ())), preferred_element_type=jnp.float32
    )


def turned(values):
    return pltpu.roll(values, values.shape[-1] // 2, axis=values.ndim - 1)


def document_tables(seg_col, seg_row, head_dim):
    seq_len = seg_col.shape[0]
    rows = lax.broadcasted_iota(jnp.int32, (seq_len, seq_len), 0)
    cols = lax.broadcasted_iota(jnp.int32, (seq_len, seq_len), 1)
    same = seg_col == seg_row
    bias = jnp.where(same & (cols <= rows), 0.0, MASKED)
    before = jnp.where(same & (cols < rows), 1.0, 0.0)
    position = jnp.sum(before, axis=-1, keepdims=True)
    lane = lax.broadcasted_iota(jnp.int32, (1, head_dim), 1)
    half_dim = head_dim // 2
    slot = jnp.where(lane < half_dim, lane, lane - half_dim).astype(jnp.float32)
    frequency = jnp.exp(slot * (-2.0 * math.log(ROPE_BASE) / head_dim))
    angles = position * frequency
    sine = jnp.sin(angles)
    return bias, jnp.cos(angles), jnp.where(lane < half_dim, -sine, sine)


def matmul_tiles(left, right, write, tile=256):
    @pl.loop(0, right.shape[1] // tile)
    def _(index):
        columns = pl.ds(pl.multiple_of(index * tile, tile), tile)
        write(columns, matmul(left[...], right[:, columns]))


SAVED = 11


def forward_kernel(
    dp_size, w_q, w_k, w_v, w_o, w_g, w_u, w_d, cot, row_in, seg_col, seg_row,
    gain_one, gain_two, q_gain, k_gain,
    *refs,
):
    o_attn, o_ffn, o_c, o_n, o_mid = refs[:5]
    stored, held = refs[5 : 5 + SAVED], refs[6 + SAVED : 6 + 2 * SAVED]
    mid = refs[5 + SAVED]
    normed_one, query_raw, key_raw, values_half, queries, keys, context, log_total = held[:8]
    cosine, sine, bias = held[8:]
    full, own_part, outgoing, incoming, normed, own_sems, send_sems, recv_sems = refs[6 + 2 * SAVED :]
    at = Place(dp_size)
    z, y, c, x = at.z, at.y, at.c, at.x
    sibling, other = at.device(c=1 - c), at.device(x=1 - x)
    z_peers, y_peers = at.z_peers(), at.y_peers()
    meet([sibling, other] + z_peers + y_peers)

    mail = Mail(send_sems, recv_sems)
    rows = w_q.shape[0]
    head_dim = q_gain.shape[1]
    part = w_g.shape[1] // DEPTH
    tokens = mid.shape[0]
    here = at.rows(z, y, c, rows)
    spans, start = [], 0
    for weight in (w_q, w_k, w_v, w_o):
        spans.append(pl.ds(start, weight.shape[1]))
        start += weight.shape[1]
    q_span, k_span, v_span, o_span = spans
    ffn = [(weight, pl.ds(i * part, part)) for i, weight in enumerate((w_g, w_u, w_d))]

    def columns(index):
        return pl.ds(pl.multiple_of(index * part, part), part)

    def half_rows(index):
        return pl.ds(pl.multiple_of(index * tokens, tokens), tokens)

    mine = own_copies(
        [(weight, full.at[here, span]) for weight, span in zip((w_q, w_k, w_v, w_o), spans)],
        own_sems,
    )
    own_ffn = own_copies(
        [(weight.at[:, columns(z)], own_part.at[:, span]) for weight, span in ffn], own_sems, 4
    )
    own_cot = own_copies([(cot.at[half_rows(i)], o_c.at[z, i]) for i in range(2)], own_sems, 7)
    finish_own(mine)
    attn = LineGather(
        mail,
        at,
        (full.at[here],),
        lambda zb, j: [full.at[at.rows(zb, at.y_off(-j), c, rows)]],
        y_peers,
        sibling,
    )

    residual = row_in[...].astype(jnp.float32)
    normed_full, _ = rms_norm(residual, gain_one[...])
    normed_one[...] = normed_full.astype(jnp.bfloat16)
    bias_values, cosine[...], sine[...] = document_tables(seg_col[...], seg_row[...], head_dim)
    bias[...] = bias_values

    spread, crossing, to_sibling = {}, {}, []

    def start_spread():
        for k in range(1, DEPTH):
            target = at.z_flip(k)
            spread[k] = [
                mail.send(
                    weight.at[:, columns(target)], o_ffn.at[here, span], at.device(z=target)
                )
                for weight, span in ffn
            ]
        block = o_ffn.at[here]
        for j in range(1, at.wide):
            crossing[0, j] = mail.send(own_part, block, y_peers[j - 1])
        to_sibling.append(mail.send(own_part, block, sibling))

    def forward_spread(k):
        receive(spread[k])
        block = o_ffn.at[at.rows(at.z_flip(k), y, c, rows)]
        for j in range(1, at.wide):
            crossing[k, j] = mail.send(block, block, y_peers[j - 1])
        to_sibling.append(mail.send(block, block, sibling))

    def forward_crossing(k):
        for j in range(1, at.wide):
            crossing[k, j].wait_recv()
            block = o_ffn.at[at.rows(at.z_flip(k), at.y_off(-j), c, rows)]
            to_sibling.append(mail.send(block, block, sibling))

    def half_place(out):
        return lambda zb, j: [out.at[zb, x if j == 0 else 1 - x]]

    attn.step(0)
    finish_own(own_ffn)
    own_copy = own_copies([(own_part, o_ffn.at[here])], own_sems, 4)
    attn.side_step("own")
    attn.step(1)
    cots = LineGather(
        mail, at, (cot.at[half_rows(x)],), half_place(o_c), [other], share_own=False
    )
    attn.side_steps(0)
    attn.step(2)
    cots.step(0)
    attn.side_steps(1)
    cots.step(1)
    start_spread()
    attn.side_steps(2)
    attn.finish()
    saved = own_copies([(full, o_attn)], own_sems)

    def write_query(cols, block):
        query_raw[:, cols] = block

    def write_key(cols, block):
        key_raw[:, cols] = block

    def write_value(cols, block):
        values_half[:, cols] = block.astype(jnp.bfloat16)

    matmul_tiles(normed_one, full.at[:, q_span], write_query)
    matmul_tiles(normed_one, full.at[:, k_span], write_key)
    matmul_tiles(normed_one, full.at[:, v_span], write_value)

    def rotated(raw, gain):
        unit, _ = rms_norm(raw, gain)
        return (unit * cosine[...] + turned(unit) * sine[...]).astype(jnp.bfloat16)

    kv_heads = key_raw.shape[1] // head_dim
    group = query_raw.shape[1] // key_raw.shape[1]
    for j in range(kv_heads):
        kv_cols = pl.ds(j * head_dim, head_dim)
        keys[:, kv_cols] = rotated(key_raw[:, kv_cols], k_gain[...])
        for g in range(group):
            head = j * group + g
            cols = pl.ds(head * head_dim, head_dim)
            queries[:, cols] = rotated(query_raw[:, cols], q_gain[...])
            scores = dot_nt(queries[:, cols], keys[:, kv_cols]) * (1.0 / math.sqrt(head_dim))
            scores = scores + bias[...]
            row_max = jnp.max(scores, axis=-1, keepdims=True)
            weights = jnp.exp(scores - row_max)
            total = jnp.sum(weights, axis=-1, keepdims=True)
            log_total[:, head : head + 1] = row_max + jnp.log(total)
            probs = (weights * (1.0 / total)).astype(jnp.bfloat16)
            context[:, cols] = matmul(probs, values_half[:, kv_cols]).astype(jnp.bfloat16)
        if j == kv_heads // 2 - 1:
            cots.step(2)

    saved += own_copies(list(zip(held, stored)), own_sems, 11)
    given, kept = half_rows(1 - x), half_rows(x)
    width = row_in.shape[1]

    def project(token_rows, target):
        @pl.loop(0, width // TILE)
        def _(index):
            cols = pl.ds(pl.multiple_of(index * TILE, TILE), TILE)
            block = dot_nt(context[token_rows, :], full[cols, o_span])
            target[:, cols] = block.astype(target.dtype)

    project(given, outgoing)
    swap = mail.send(outgoing, incoming, other)
    project(kept, mid)
    swap.wait_recv()
    total = row_in[kept, :].astype(jnp.float32) + (mid[...] + incoming[...].astype(jnp.float32))
    mid[...] = total
    saved += own_copies([(mid, o_mid)], own_sems, 10)
    normed_mid, _ = rms_norm(total, gain_two[...])
    normed[...] = normed_mid.astype(jnp.bfloat16)
    last = own_copies([(normed, o_n.at[z, x])], own_sems, 9)
    strip = tokens // 2
    norms = []
    for i in range(2):
        rows_of = pl.ds(i * strip, strip)
        norms.append(
            LineGather(
                mail,
                at,
                (normed.at[rows_of],),
                lambda zb, j, rows_of=rows_of: [o_n.at[zb, x if j == 0 else 1 - x, rows_of]],
                [other],
            )
        )
    forward_spread(1)
    forward_crossing(0)
    for step in range(DEPTH - 1):
        if step < DEPTH - 2:
            forward_spread(step + 2)
        for line in norms:
            line.step(step)
        forward_crossing(step + 1)
    for step in range(DEPTH - 1):
        cots.side_steps(step)
    for line in norms:
        line.side_step("own")
        for step in range(DEPTH - 1):
            line.side_steps(step)
    receive(to_sibling)
    mail.finish()
    finish_own(saved + last + own_cot + own_copy)


def forward(dp_size, weights, cot, row_in, seg_row, gains):
    w_q, w_k, w_v, w_o, w_g, w_u, w_d = weights
    wide = dp_size // (DEPTH * CORES)
    seq_len, width = row_in.shape
    head_dim = gains[2].shape[1]
    tokens = seq_len // HALVES
    part = w_g.shape[1] // DEPTH
    half, whole = jnp.bfloat16, jnp.float32
    attn_cols = [w.shape[1] for w in (w_q, w_k, w_v, w_o)]
    shapes = [jax.ShapeDtypeStruct((width, cols), half) for cols in (sum(attn_cols), 3 * part)]
    shapes += [jax.ShapeDtypeStruct((DEPTH, HALVES, tokens, width), half)] * 2
    q_cols, kv_cols = attn_cols[0], attn_cols[1]
    for cols, kind in (
        (width, half), (q_cols, whole), (kv_cols, whole), (kv_cols, half), (q_cols, half),
        (kv_cols, half), (q_cols, half), (head_dim, whole), (head_dim, whole), (head_dim, whole),
        (seq_len, whole),
    ):
        shapes.append(jax.ShapeDtypeStruct((seq_len, cols), kind))
    shapes.insert(4, jax.ShapeDtypeStruct((tokens, width), whole))
    hops = 2 * (DEPTH - 1)
    spots = 1 + hops
    copies = (hops + spots * (2 * wide - 1)) + 3 * (2 * hops + 1) + 1
    copies += 9 + DEPTH * (2 * wide - 1)
    return pl.pallas_call(
        functools.partial(forward_kernel, dp_size),
        out_shape=shapes,
        in_specs=[ANY] * 7 + [VMEM] * 8,
        out_specs=[ANY] * (5 + SAVED),
        scratch_shapes=[pltpu.VMEM(shape.shape, shape.dtype) for shape in shapes[4:]]
        + [pltpu.VMEM((width, sum(attn_cols)), half)]
        + [pltpu.VMEM((w_g.shape[0], 3 * part), half)]
        + [pltpu.VMEM((tokens, width), half)] * 3
        + [
            pltpu.SemaphoreType.DMA((11 + SAVED,)),
            pltpu.SemaphoreType.DMA((copies,)),
            pltpu.SemaphoreType.DMA((copies,)),
        ],
        compiler_params=pltpu.CompilerParams(
            collective_id=0, has_side_effects=True, vmem_limit_bytes=56 * 2**20
        ),
    )(w_q, w_k, w_v, w_o, w_g, w_u, w_d, cot, row_in, seg_row[:, None], seg_row[None, :], *gains)


def mlp_kernel(
    dp_size, weights, n_all, c_all, a_mid, a_cot, gain,
    a_m, a_h, a_p, o_t, a_shares, d_g, d_u,
    mid, cot, o_m, o_h, shares, full, x_n, x_c, hidden, p_n, p_o, h_n, l_n, from_core, from_y,
    own_sems, send_sems, recv_sems,
):
    at = Place(dp_size)
    z, y, c, x = at.z, at.y, at.c, at.x
    other, sibling = at.device(x=1 - x), at.device(c=1 - c)
    y_peers = at.y_peers()
    order = at.order()
    tokens = mid.shape[0]
    block_rows = HALVES * tokens
    rows = from_core.shape[2]
    part = full.shape[1] // 3
    gate_up, down = pl.ds(0, 2 * part), pl.ds(2 * part, part)
    width = mid.shape[1]

    def band(index, size):
        return pl.ds(pl.multiple_of(index * size, size), size)

    loads = {}
    for i, name in enumerate("gud"):
        span = pl.ds(i * part, part)
        loads[name] = pltpu.make_async_copy(weights.at[:, span], full.at[:, span], own_sems.at[i])
    for i, index in enumerate(order):
        block = band(index, block_rows)
        loads["n", i] = pltpu.make_async_copy(n_all.at[block], x_n.at[block], own_sems.at[3 + i])
        loads["c", i] = pltpu.make_async_copy(c_all.at[block], x_c.at[block], own_sems.at[7 + i])
    for key in ("g", "u", ("n", 0), "d", ("c", 0)):
        loads[key].start()
    for i in range(1, DEPTH):
        loads["n", i].start()
        loads["c", i].start()
    late = own_copies([(a_mid, mid), (a_cot, cot)], own_sems, 11)
    meet([other, sibling] + at.z_peers() + y_peers)
    mail = Mail(send_sems, recv_sems)

    def half_rows(index, side):
        return band(index * HALVES + side, tokens)

    norm_line = LineReduce(
        mail, at, 1, lambda index: [p_n.at[half_rows(index, x)]], lambda slot: [l_n.at[slot]]
    )
    norm_swaps = []

    def compute(i):
        block = band(order[i], block_rows)
        if i == 0:
            for name in ("g", "u", "d"):
                loads[name].wait()
        loads["n", i].wait()
        loads["c", i].wait()

        @pl.loop(0, part // TILE)
        def _(index):
            g_cols, u_cols, d_cols = [
                pl.ds(pl.multiple_of(i * part + index * TILE, TILE), TILE) for i in range(3)
            ]
            gate = matmul(x_n[block, :], full[:, g_cols])
            up = matmul(x_n[block, :], full[:, u_cols])
            grad_act = matmul(x_c[block, :], full[:, d_cols])
            sigmoid_gate = 1.0 / (1.0 + jnp.exp(-gate))
            silu_val = gate * sigmoid_gate
            hidden[block, g_cols] = (
                grad_act * up * sigmoid_gate * (1.0 + gate * (1.0 - sigmoid_gate))
            ).astype(jnp.bfloat16)
            hidden[block, u_cols] = (grad_act * silu_val).astype(jnp.bfloat16)
            hidden[block, d_cols] = (silu_val * up).astype(jnp.bfloat16)

        @pl.loop(0, width // TILE)
        def _(index):
            cols = band(index, TILE)
            p_n[block, cols] = dot_nt(hidden[block, gate_up], full[cols, gate_up]).astype(jnp.bfloat16)

        norm_swaps.append(mail.send(p_n.at[half_rows(order[i], 1 - x)], h_n.at[i], other))

    def compute_out(i):
        block = band(order[i], block_rows)

        @pl.loop(0, width // TILE)
        def _(index):
            cols = band(index, TILE)
            p_o[block, cols] = dot_nt(hidden[block, down], full[cols, down]).astype(jnp.bfloat16)

        stores.extend(own_copies([(p_o.at[block], a_p.at[block])], own_sems, 7 + i))

    def norm_step(i):
        norm_swaps[i].wait_recv()
        add_into(p_n.at[half_rows(order[i], x)], h_n.at[i])
        norm_line.pass_on(i, 0)

    def weight_grads(span, i):
        left = x_n if span is gate_up else x_c

        @pl.loop(0, width // DEPTH // TILE)
        def _(index):
            cols = pl.ds(pl.multiple_of(order[i] * (width // DEPTH) + index * TILE, TILE), TILE)
            full[cols, span] = matmul(left[:, cols].T, hidden[:, span]).astype(jnp.bfloat16)

        to_core[span.start, i] = [
            mail.send(
                full.at[at.rows(order[i], side, 1 - c, rows), span],
                from_core.at[order[i], side, :, span],
                sibling,
            )
            for side in range(at.wide)
        ]

    to_core, to_y = {}, {}

    def core_stage(span, i):
        receive(to_core[span.start, i])
        for side in range(at.wide):
            add_into(
                full.at[at.rows(order[i], side, c, rows), span], from_core.at[order[i], side, :, span]
            )
        to_y[span.start, i] = [
            mail.send(
                full.at[at.rows(order[i], at.y_off(j), c, rows), span],
                from_y.at[j - 1, order[i], :, span],
                y_peers[j - 1],
            )
            for j in range(1, at.wide)
        ]

    def y_stage(span, i):
        receive(to_y[span.start, i])
        total = full[at.rows(order[i], y, c, rows), span].astype(jnp.float32)
        for j in range(1, at.wide):
            total = total + from_y[j - 1, order[i], :, span].astype(jnp.float32)
        shares[order[i], :, span] = total.astype(jnp.bfloat16)

    spread_base = mail.reserve(2 * DEPTH)

    def spread_copies(i, source, target, device):
        return [
            pltpu.make_async_remote_copy(
                shares.at[target, :, pl.ds(w * part, part)],
                out.at[:, band(source, part)],
                mail.send_sems.at[spread_base + 2 * i + w],
                mail.recv_sems.at[spread_base + 2 * source + w],
                device_id=device,
                device_id_type=MESH,
            )
            for w, out in enumerate((d_g, d_u))
        ]

    def spread(i):
        copies = spread_copies(i, z, order[i], at.device(z=order[i]))
        start_all(copies)
        mail.open += [(copy, None) for copy in copies]

    stores = []
    compute(0)
    compute(1)
    compute(2)
    norm_step(0)
    compute(3)
    weight_grads(gate_up, 0)
    norm_step(1)
    weight_grads(gate_up, 1)
    norm_line.pass_on(0, 1)
    core_stage(gate_up, 0)
    weight_grads(gate_up, 2)
    core_stage(gate_up, 1)
    weight_grads(gate_up, 3)
    core_stage(gate_up, 2)
    compute_out(0)
    core_stage(gate_up, 3)
    compute_out(1)
    norm_step(2)
    norm_line.pass_on(1, 1)
    compute_out(2)
    norm_line.pass_on(2, 1)
    compute_out(3)
    weight_grads(down, 0)
    y_stage(gate_up, 0)
    spread(0)
    weight_grads(down, 1)
    core_stage(down, 0)
    weight_grads(down, 2)
    core_stage(down, 1)
    y_stage(gate_up, 1)
    spread(1)
    weight_grads(down, 3)
    core_stage(down, 2)
    core_stage(down, 3)
    y_stage(gate_up, 2)
    spread(2)
    norm_swaps[3].wait_recv()
    finish_own(late)
    o_m[...] = p_n[half_rows(z, x), :].astype(jnp.float32) + h_n[3].astype(jnp.float32)

    def add_norm(_, landed):
        o_m[...] = o_m[...] + landed[...].astype(jnp.float32)

    norm_line.last(add_norm)
    grad_norm = o_m[...]
    values = mid[...]
    inv_rms = lax.rsqrt(jnp.mean(values * values, axis=-1, keepdims=True) + EPSILON)
    grad_values, terms = norm_back(grad_norm, values, inv_rms, gain[...])
    o_t[...] = jnp.sum(terms, axis=0, keepdims=True)
    kept = band(x, tokens)
    total = cot[kept, :].astype(jnp.float32) + grad_values
    o_m[...] = total
    o_h[kept, :] = total.astype(jnp.bfloat16)
    swap_h = mail.send(o_h.at[kept], o_h.at[kept], other)
    stores += own_copies([(o_m, a_m)], own_sems, 0)
    y_stage(gate_up, DEPTH - 1)
    stores += own_copies(
        [
            (shares.at[z, :, pl.ds(w * part, part)], out.at[:, band(z, part)])
            for w, out in enumerate((d_g, d_u))
        ],
        own_sems,
        1,
    )
    for i in range(DEPTH):
        y_stage(down, i)
        stores += own_copies([(shares.at[order[i], :, down], a_shares.at[order[i]])], own_sems, 3 + i)
    swap_h.wait_recv()
    stores += own_copies([(o_h, a_h)], own_sems, 11)
    for k in range(1, DEPTH):
        source = at.z_off(-k)
        receive(spread_copies(0, source, z, at.device(z=source)))
    mail.finish()
    finish_own(stores)


def mlp(dp_size, weights, normed, cots, mid, cot, gain):
    wide = dp_size // (DEPTH * CORES)
    tokens, width = mid.shape
    cols = weights.shape[1]
    rows = width // dp_size
    every = DEPTH * HALVES * tokens
    half, full = jnp.bfloat16, jnp.float32
    copies = LineReduce.slots + DEPTH + 2 * DEPTH * (2 * wide - 1) + 1 + 2 * DEPTH
    shapes = [
        jax.ShapeDtypeStruct((tokens, width), full),
        jax.ShapeDtypeStruct((HALVES * tokens, width), half),
        jax.ShapeDtypeStruct((every, width), half),
        jax.ShapeDtypeStruct((1, width), full),
        jax.ShapeDtypeStruct((DEPTH, rows, cols // 3), half),
    ] + [jax.ShapeDtypeStruct((rows, DEPTH * cols // 3), half)] * 2
    return pl.pallas_call(
        functools.partial(mlp_kernel, dp_size),
        out_shape=shapes,
        in_specs=[ANY] * 5 + [VMEM],
        out_specs=[ANY] * 3 + [VMEM] + [ANY] * 3,
        scratch_shapes=[
            pltpu.VMEM((tokens, width), full),
            pltpu.VMEM((HALVES * tokens, width), half),
            pltpu.VMEM((tokens, width), full),
            pltpu.VMEM((HALVES * tokens, width), half),
            pltpu.VMEM((DEPTH, rows, cols), half),
        ]
        + [pltpu.VMEM((width, cols), half)]
        + [pltpu.VMEM((every, width), half)] * 2
        + [pltpu.VMEM((every, cols), half)]
        + [pltpu.VMEM((every, width), half)] * 2
        + [
            pltpu.VMEM((DEPTH, tokens, width), half),
            pltpu.VMEM((LineReduce.slots, tokens, width), half),
        ]
        + [
            pltpu.VMEM((DEPTH, wide, rows, cols), half),
            pltpu.VMEM((wide - 1, DEPTH, rows, cols), half),
            pltpu.SemaphoreType.DMA((13,)),
            pltpu.SemaphoreType.DMA((copies,)),
            pltpu.SemaphoreType.DMA((copies,)),
        ],
        compiler_params=pltpu.CompilerParams(
            collective_id=1, has_side_effects=True, vmem_limit_bytes=63 * 2**20
        ),
    )(weights, normed, cots, mid, cot, gain)


def backward_kernel(
    dp_size, shares, weights, a_mid, mid_half, a_out, a_part, t_m, gain_one, a_row, a_normed, a_query,
    a_key, a_values, a_queries, a_keys, context, a_log, a_cosine, a_sine, a_bias, q_gain, k_gain,
    o_l, o_i, sums, d_q, d_k, d_v, d_o, d_d,
    grad_mid, layer_mid, row_in, normed_one, query_raw, key_raw, values_half, queries, keys,
    log_total, cosine, sine, bias,
    full, head_grads, gains, from_other, totals, core_o, core_h, core_s, y_o, y_h, y_s, z_o, z_h, z_s,
    part_own, part_other, part_line, spare, context_grad, raw_half, raw_head, flipped, partial,
    outgoing, incoming, own_sems, send_sems, recv_sems,
):
    at = Place(dp_size)
    z, y, c, x = at.z, at.y, at.c, at.x
    other, sibling = at.device(x=1 - x), at.device(c=1 - c)
    y_peers, z_peers = at.y_peers(), at.z_peers()
    order = at.order()
    tokens, width = grad_mid.shape
    rows = d_q.shape[0]
    part = shares.shape[2]
    spans, start = [], 0
    for out in (d_q, d_k, d_v, d_o):
        spans.append(pl.ds(start, out.shape[1]))
        start += out.shape[1]
    q_span, k_span, v_span, o_span = spans
    qkv_span = pl.ds(0, start - d_o.shape[1])
    q_cols, kv_width = d_q.shape[1], d_k.shape[1]
    head_dim = q_gain.shape[1]

    def band(index, size):
        return pl.ds(pl.multiple_of(index * size, size), size)

    kept, given = band(x, tokens), band(1 - x, tokens)
    loads = own_copies(
        [(weights.at[:, span], full.at[:, span]) for span in (o_span, qkv_span)], own_sems
    )
    late = own_copies(
        [
            (a_normed, normed_one), (a_query, query_raw), (a_key, key_raw), (a_values, values_half),
            (a_queries, queries), (a_keys, keys), (a_log, log_total), (a_cosine, cosine),
            (a_sine, sine), (a_bias, bias), (a_out, layer_mid), (a_mid, grad_mid), (a_row, row_in),
        ],
        own_sems,
        2,
    )
    part_loads = own_copies(
        [(a_part.at[band(index * HALVES + x, tokens)], part_own.at[index]) for index in order],
        own_sems,
        16,
    )
    meet([other, sibling] + y_peers + z_peers)
    mail = Mail(send_sems, recv_sems)
    part_swaps = [
        mail.send(a_part.at[band(index * HALVES + 1 - x, tokens)], part_other.at[i], other)
        for i, index in enumerate(order)
    ]
    part_sums = LineReduce(
        mail, at, 1, lambda index: [part_own.at[index]], lambda slot: [part_line.at[slot]]
    )

    def part_step(i):
        part_swaps[i].wait_recv()
        part_loads[i].wait()
        add_into(part_own.at[order[i]], part_other.at[i])
        if i < DEPTH - 1:
            part_sums.pass_on(i, 0)

    to_z = [
        mail.send(shares.at[at.z_off(k)], d_d.at[:, band(z, part)], z_peers[k - 1])
        for k in (2, 1, 3)
    ]
    kv_heads = key_raw.shape[1] // head_dim
    group = query_raw.shape[1] // key_raw.shape[1]
    q_part = group * head_dim

    def block_of(zb, side, core):
        return (zb * at.wide + side) * CORES + core

    class Sums:
        def __init__(self, held, core_land, y_land, z_land, outs):
            self.held, self.core_land, self.y_land, self.outs = held, core_land, y_land, outs
            self.line = LineReduce(
                mail, at, 1, lambda zb: [held(zb, y, c)], lambda slot: [z_land.at[slot]]
            )
            self.to_core, self.to_y = {}, {}

        def core_sends(self, i):
            self.to_core[i] = [
                mail.send(
                    self.held(order[i], side, 1 - c), self.core_land.at[order[i], side], sibling
                )
                for side in range(at.wide)
            ]

        def core_stage(self, i):
            receive(self.to_core[i])
            for side in range(at.wide):
                add_into(self.held(order[i], side, c), self.core_land.at[order[i], side])
            self.to_y[i] = [
                mail.send(
                    self.held(order[i], at.y_off(j), c), self.y_land.at[j - 1, order[i]], y_peers[j - 1]
                )
                for j in range(1, at.wide)
            ]

        def y_stage(self, i):
            receive(self.to_y[i])
            terms = [self.y_land.at[j - 1, order[i]] for j in range(1, at.wide)]
            own = self.held(order[i], y, c)
            if i < DEPTH - 1:
                add_into(own, *terms)
                return
            for out, span in self.outs:
                out[...] = own[:, span].astype(jnp.float32)
                add_into(out, *[term.at[:, span] for term in terms])

        def finish(self):
            def use(_, landed):
                for out, span in self.outs:
                    add_into(out, landed.at[:, span])

            self.line.last(use)

    out_sums = Sums(
        lambda zb, side, core: full.at[at.rows(zb, side, core, rows), o_span],
        core_o, y_o, z_o, [(d_o, pl.ds(0, d_o.shape[1]))],
    )
    head_sums = []
    for j in range(kv_heads):
        kv_cols = pl.ds(j * head_dim, head_dim)
        head_sums.append(
            Sums(
                lambda zb, side, core, j=j: head_grads.at[j, at.rows(zb, side, core, rows)],
                core_h.at[j], y_h.at[j], z_h.at[j],
                [
                    (d_q.at[:, pl.ds(j * q_part, q_part)], pl.ds(0, q_part)),
                    (d_k.at[:, kv_cols], pl.ds(q_part, head_dim)),
                    (d_v.at[:, kv_cols], pl.ds(q_part + head_dim, head_dim)),
                ],
            )
        )
    gain_sums = Sums(
        lambda zb, side, core: totals.at[block_of(zb, side, core)],
        core_s, y_s, z_s, [(sums, pl.ds(0, sums.shape[1]))],
    )

    gains[...] = jnp.zeros(gains.shape, jnp.float32)
    loads[0].wait()

    def write_context(cols, value):
        context_grad[:, cols] = value.astype(jnp.bfloat16)

    matmul_tiles(mid_half, full.at[:, o_span], write_context)

    quarter = width // DEPTH
    for i in range(DEPTH):

        @pl.loop(0, quarter // TILE)
        def _(index, i=i):
            cols = pl.ds(pl.multiple_of(order[i] * quarter + index * TILE, TILE), TILE)
            full[cols, o_span] = dot_tn(mid_half[:, cols], context[...]).astype(jnp.bfloat16)

        out_sums.core_sends(i)
    own_share = own_copies([(shares.at[z], spare)], own_sems, 15)
    for i in range(DEPTH):
        out_sums.core_stage(i)
    finish_own(late)
    finish_own(own_share)
    own_share = own_copies([(spare, d_d.at[:, band(z, part)])], own_sems, 15)
    flipped[...] = normed_one[...].T

    scale = 1.0 / math.sqrt(head_dim)

    def raw_grad(grad, raw, gain):
        back = grad * cosine[...] - turned(grad) * sine[...]
        inv_rms = lax.rsqrt(jnp.mean(raw * raw, axis=-1, keepdims=True) + EPSILON)
        grad_raw, terms = norm_back(back, raw, inv_rms, gain)
        return grad_raw.astype(jnp.bfloat16), jnp.sum(terms, axis=0, keepdims=True)

    for j in range(kv_heads):
        q_sum = jnp.zeros((1, head_dim), jnp.float32)
        k_sum = jnp.zeros((1, head_dim), jnp.float32)
        kv_cols = pl.ds(j * head_dim, head_dim)
        key_total = jnp.zeros((row_in.shape[0], head_dim), jnp.float32)
        value_total = jnp.zeros((row_in.shape[0], head_dim), jnp.float32)
        for g in range(group):
            head = j * group + g
            cols = pl.ds(head * head_dim, head_dim)
            scores = dot_nt(queries[:, cols], keys[:, kv_cols]) * scale + bias[...]
            probs = jnp.exp(scores - log_total[:, head : head + 1])
            grad_context = context_grad[:, cols]
            grad_probs = dot_nt(grad_context, values_half[:, kv_cols])
            delta = jnp.sum(
                grad_context.astype(jnp.float32) * context[:, cols].astype(jnp.float32),
                axis=-1,
                keepdims=True,
            )
            grad_scores = (probs * (grad_probs - delta) * scale).astype(jnp.bfloat16)
            grad_query, terms = raw_grad(
                matmul(grad_scores, keys[:, kv_cols]), query_raw[:, cols], q_gain[...]
            )
            raw_half[:, cols] = grad_query
            raw_head[:, pl.ds(g * head_dim, head_dim)] = grad_query
            q_sum = q_sum + terms
            key_total = key_total + dot_tn(grad_scores, queries[:, cols])
            value_total = value_total + dot_tn(probs.astype(jnp.bfloat16), grad_context)
        grad_key, terms = raw_grad(key_total, key_raw[:, kv_cols], k_gain[...])
        grad_value = value_total.astype(jnp.bfloat16)
        raw_half[:, pl.ds(q_cols + j * head_dim, head_dim)] = grad_key
        raw_half[:, pl.ds(q_cols + kv_width + j * head_dim, head_dim)] = grad_value
        raw_head[:, pl.ds(q_part, head_dim)] = grad_key
        raw_head[:, pl.ds(q_part + head_dim, head_dim)] = grad_value
        k_sum = k_sum + terms
        gains[0, 2:3, :head_dim] = gains[0, 2:3, :head_dim] + q_sum
        gains[0, 3:4, :head_dim] = gains[0, 3:4, :head_dim] + k_sum
        for i in range(DEPTH):

            @pl.loop(0, quarter // TILE)
            def _(index, i=i, j=j):
                cols = pl.ds(pl.multiple_of(order[i] * quarter + index * TILE, TILE), TILE)
                head_grads[j, cols, :] = matmul(flipped[cols, :], raw_head[...]).astype(jnp.bfloat16)

            head_sums[j].core_sends(i)
        if 1 <= j < DEPTH:
            out_sums.y_stage(j - 1)
            out_sums.line.pass_on(j - 1, 0)
        if j >= 2:
            out_sums.line.pass_on(j - 2, 1)
        if j == 0:
            part_step(0)
        if j == DEPTH - 2:
            part_step(1)
            part_sums.pass_on(0, 1)
        if j > 0:
            for i in range(DEPTH):
                head_sums[j - 1].core_stage(i)
    for j in range(max(kv_heads - 1, 0), DEPTH - 1):
        out_sums.y_stage(j)
        out_sums.line.pass_on(j, 0)
    for j in range(max(kv_heads - 2, 0), DEPTH - 2):
        out_sums.line.pass_on(j, 1)
    out_sums.y_stage(DEPTH - 1)
    for i in range(DEPTH):
        head_sums[kv_heads - 1].core_stage(i)
    finish_own(loads[1:])

    def project(token_rows, target):
        @pl.loop(0, width // TILE)
        def _(index):
            cols = band(index, TILE)
            total = dot_nt(raw_half[token_rows, :], full[cols, qkv_span])
            partial[token_rows, cols] = total
            if target is not None:
                target[:, cols] = total.astype(target.dtype)

    project(given, outgoing)
    swap = mail.send(outgoing, incoming, other)
    project(kept, None)

    values = row_in[...].astype(jnp.float32)
    inv_rms = lax.rsqrt(jnp.mean(values * values, axis=-1, keepdims=True) + EPSILON)
    gain_terms = jnp.sum(partial[...] * values * inv_rms, axis=0, keepdims=True)
    blocks = gains.shape[0]
    share = width // blocks
    head_terms = gains[0, 2:4, :]
    for index in range(blocks):
        gains[index, 0:1, :share] = gain_terms[:, index * share : (index + 1) * share]
        gains[index, 1:2, :share] = t_m[:, index * share : (index + 1) * share]
        gains[index, 2:4, :] = head_terms
    swap_gains = mail.send(gains, from_other, other)
    swap.wait_recv()
    grad_norm = partial[kept, :] + incoming[...].astype(jnp.float32)
    values = row_in[kept, :].astype(jnp.float32)
    inv_rms = lax.rsqrt(jnp.mean(values * values, axis=-1, keepdims=True) + EPSILON)
    grad_values, _ = norm_back(grad_norm, values, inv_rms, gain_one[...])
    o_i[kept, :] = (grad_mid[...] + grad_values).astype(jnp.bfloat16)
    swap_back = mail.send(o_i.at[kept], o_i.at[kept], other)

    if kv_heads < DEPTH - 1:
        part_step(1)
    part_sums.pass_on(1, 1)
    part_step(2)
    out_sums.line.pass_on(DEPTH - 2, 1)
    swap_gains.wait_recv()
    totals[...] = gains[...] + from_other[...]
    for i in range(DEPTH):
        gain_sums.core_sends(i)
    for i in range(DEPTH):
        gain_sums.core_stage(i)
    every = head_sums + [gain_sums]
    part_sums.pass_on(2, 1)
    part_step(3)
    for index in range(len(every) + DEPTH - 1):
        if index < len(every):
            for i in range(DEPTH):
                every[index].y_stage(i)
        for turn in range(DEPTH - 1):
            if 0 <= index - turn < len(every):
                every[index - turn].line.pass_on(turn, 0)
            if 0 <= index - turn - 1 < len(every):
                every[index - turn - 1].line.pass_on(turn, 1)
    out_sums.finish()
    layer_mid[...] = layer_mid[...] + part_own[z].astype(jnp.float32)

    def add_part(_, landed):
        layer_mid[...] = layer_mid[...] + landed[...].astype(jnp.float32)

    part_sums.last(add_part)
    o_l[kept, :] = layer_mid[...].astype(jnp.bfloat16)
    swap_l = mail.send(o_l.at[kept], o_l.at[kept], other)
    for one in every[:-1]:
        one.finish()
    every[-1].finish()
    receive([swap_l, swap_back] + to_z)
    finish_own(own_share)
    mail.finish()


def backward(dp_size, shares, weights, cols, grad_mid, mid_half, layer_mid, part_out, gain_terms, saved, gains):
    wide = dp_size // (DEPTH * CORES)
    tokens, width = grad_mid.shape
    seq_len = HALVES * tokens
    part = shares.shape[2]
    rows = width // dp_size
    half, full = jnp.bfloat16, jnp.float32
    every = sum(cols)
    kv_heads = cols[1] // gains[2].shape[1]
    head_cols = (every - cols[3]) // kv_heads
    passes = kv_heads + 2
    copies = 3 + 4 + DEPTH + LineReduce.slots + passes * (LineReduce.slots + DEPTH * (2 * wide - 1))
    shapes = [jax.ShapeDtypeStruct((seq_len, width), half)] * 2
    shapes += [jax.ShapeDtypeStruct((8, 128), full)]
    shapes += [jax.ShapeDtypeStruct((rows, col), full) for col in cols]
    shapes += [jax.ShapeDtypeStruct((rows, DEPTH * part), half)]
    lazy = [grad_mid, layer_mid] + [one for i, one in enumerate(saved) if i != 7]
    inputs = [grad_mid, mid_half, layer_mid, part_out, gain_terms, gains[0], *saved, *gains[2:]]
    return pl.pallas_call(
        functools.partial(backward_kernel, dp_size),
        out_shape=shapes,
        in_specs=[ANY] * 3 + [VMEM, ANY, ANY, VMEM, VMEM] + [ANY] * 7 + [VMEM] + [ANY] * 4 + [VMEM] * 2,
        out_specs=[VMEM] * 7 + [ANY],
        scratch_shapes=[pltpu.VMEM(one.shape, one.dtype) for one in lazy]
        + [
            pltpu.VMEM((width, every), half),
            pltpu.VMEM((kv_heads, width, head_cols), half),
            pltpu.VMEM((dp_size, 8, 128), full),
            pltpu.VMEM((dp_size, 8, 128), full),
            pltpu.VMEM((dp_size, 8, 128), full),
            pltpu.VMEM((DEPTH, wide, rows, cols[3]), half),
            pltpu.VMEM((kv_heads, DEPTH, wide, rows, head_cols), half),
            pltpu.VMEM((DEPTH, wide, 8, 128), full),
            pltpu.VMEM((wide - 1, DEPTH, rows, cols[3]), half),
            pltpu.VMEM((kv_heads, wide - 1, DEPTH, rows, head_cols), half),
            pltpu.VMEM((wide - 1, DEPTH, 8, 128), full),
            pltpu.VMEM((LineReduce.slots, rows, cols[3]), half),
            pltpu.VMEM((kv_heads, LineReduce.slots, rows, head_cols), half),
            pltpu.VMEM((LineReduce.slots, 8, 128), full),
            pltpu.VMEM((DEPTH, tokens, width), half),
            pltpu.VMEM((DEPTH, tokens, width), half),
            pltpu.VMEM((LineReduce.slots, tokens, width), half),
            pltpu.VMEM((rows, part), half),
            pltpu.VMEM((seq_len, cols[0]), half),
            pltpu.VMEM((seq_len, every - cols[3]), half),
            pltpu.VMEM((seq_len, head_cols), half),
            pltpu.VMEM((width, seq_len), half),
            pltpu.VMEM((seq_len, width), full),
            pltpu.VMEM((tokens, width), half),
            pltpu.VMEM((tokens, width), half),
            pltpu.SemaphoreType.DMA((20,)),
            pltpu.SemaphoreType.DMA((copies,)),
            pltpu.SemaphoreType.DMA((copies,)),
        ],
        compiler_params=pltpu.CompilerParams(
            collective_id=2, has_side_effects=True, vmem_limit_bytes=63 * 2**20
        ),
    )(shares, weights, *inputs)


def body(
    dp_size,
    layer_in,
    seg_ids,
    w_q,
    w_k,
    w_v,
    w_o,
    w_gate,
    w_up,
    w_down,
    attn_gain,
    mlp_gain,
    q_gain,
    k_gain,
    cotangent,
):
    row_in = layer_in[0]
    row_cot = cotangent[0]
    width = row_in.shape[1]
    gains = [gain[None, :] for gain in (attn_gain, mlp_gain, q_gain, k_gain)]
    outs = forward(
        dp_size, (w_q, w_k, w_v, w_o, w_gate, w_up, w_down), row_cot, row_in, seg_ids[0], gains
    )
    attn_full, ffn_full, cots, normed, mid = outs[:5]
    saved = outs[5:]
    outs = mlp(
        dp_size, ffn_full, normed.reshape(-1, width), cots.reshape(-1, width), mid, row_cot, gains[1]
    )
    grad_mid, mid_half, part_out, gain_terms, shares, *gate_up_grads = outs
    cols = [weight.shape[1] for weight in (w_q, w_k, w_v, w_o)]
    outs = backward(
        dp_size, shares, attn_full, cols, grad_mid, mid_half, mid, part_out, gain_terms,
        [row_in] + list(saved), gains,
    )
    out_row, in_grad, sums = outs[:3]
    share = width // dp_size
    gain_outs = [sums[0, :share], sums[1, :share]]
    for i, gain in enumerate((q_gain, k_gain)):
        share = gain.shape[0] // dp_size
        gain_outs.append(lax.dynamic_slice(sums[2 + i], (lax.axis_index("dp") * share,), (share,)))
    ffn_grads = [grad.astype(jnp.float32) for grad in (*gate_up_grads, outs[7])]
    return (out_row[None], in_grad[None], *outs[3:7], *ffn_grads, *gain_outs)


def solution(mesh):
    return jax.shard_map(
        functools.partial(body, mesh.shape["dp"]),
        mesh=mesh,
        in_specs=(
            P("dp", None, None),
            P("dp", None),
            P("dp", "mp"),
            P("dp", "mp"),
            P("dp", "mp"),
            P("dp", "mp"),
            P("dp", "mp"),
            P("dp", "mp"),
            P("dp", "mp"),
            P(),
            P(),
            P(),
            P(),
            P("dp", None, None),
        ),
        out_specs=(
            P("dp", None, None),
            P("dp", None, None),
            P("dp", "mp"),
            P("dp", "mp"),
            P("dp", "mp"),
            P("dp", "mp"),
            P("dp", "mp"),
            P("dp", "mp"),
            P("dp", "mp"),
            P("dp"),
            P("dp"),
            P("dp"),
            P("dp"),
        ),
        check_vma=False,
    )
```
